256 devices in a mesh: gx: 32 (over y, z), gy: 8 (over x, core).
Axes of the slice: x: 4, y: 4, z: 8, core: 2. Of those that a mesh axis runs over, the one named last changes fastest.
Arguments:
- load_nodes: float32 [4096, 512], P(('gx', 'gy')), may hold values from -6 to 6
- metric: float32 [4096, 3, 512], P(('gx', 'gy')), may hold values from 0.005 to 0.05
- mass_nodes: float32 [4096, 512], P(('gx', 'gy')), may hold values from 0.1 to 1
- smoother: float32 [10, 10], replicated, may hold values from -0.08 to 1.2, as said below
- element_order: int32 [4096], P(('gx', 'gy')), may hold values from 0 to 15, as said below
Outputs:
- pressure: float32 [4096, 512], P(('gx', 'gy'))
- residual: float32 [4096, 512], P(('gx', 'gy'))
The draws below stay inside these ranges and needn't reach their ends.
Inputs may be any that keep to these rules, and one draw needn't show every extreme that they name: `element_order`: each aligned block of 16 stored elements holds every brick position once. `smoother`: Symmetric, with a diagonal larger than the sum of the magnitudes of the rest of its row.
All inputs are finite; a program needn't handle non-finite values.
Results may differ from the reference program's by a relative error of at most 0.0008.
Values sent between devices are 32-bit elements; how exact they have to be, the bound alone decides.
A program may use at most 64 MiB of HBM per device.

```python
import math
from functools import partial
import jax
import jax.numpy as jnp
import numpy as np
from jax import lax

NODES = 8
EX = 2
EY = 2
EZ = 4
ITERS = 3
E_DEV = 16
ELEMS = 4096
N_GX = 32
N_GY = 8


def draw_element_order(key, part):
    key = jax.random.fold_in(key, 11)
    block_keys = jax.random.split(key, ELEMS // E_DEV)
    orders = jax.vmap(lambda single_key: jax.random.permutation(single_key, E_DEV))(block_keys)
    return orders.reshape(ELEMS).astype(jnp.int32)


def draw_load_nodes(key, part):
    key = jax.random.fold_in(key, 12)
    block_total = ELEMS // E_DEV
    position = (jnp.arange(ELEMS) // E_DEV).astype(jnp.float32) / max(block_total - 1, 1)
    rough_part = jnp.clip(jax.random.normal(key, (ELEMS, NODES ** 3), jnp.float32), -4.0, 4.0)
    scaling = 0.5 * (1.0 + 2.0 * position)
    return rough_part * scaling[:, None]


def draw_smoother(key, part):
    key = jax.random.fold_in(key, 13)
    first_key, second_key = jax.random.split(key)
    size_box = NODES + 2
    raw_entries = jax.random.uniform(first_key, (size_box, size_box), jnp.float32, -0.08, 0.08)
    mirror = 0.5 * (raw_entries + raw_entries.T)
    diagonal = jax.random.uniform(second_key, (size_box,), jnp.float32, 0.8, 1.2)
    identity = jnp.eye(size_box, dtype=jnp.float32)
    return mirror * (1.0 - identity) + identity * diagonal[None, :]


def steps_of(stream_key, shape, cuts, smallest, top_value):
    gain = 1.0
    for axis_at, parts in cuts:
        steps = jax.random.uniform(jax.random.fold_in(jax.random.fold_in(stream_key, 6), axis_at), (parts,), jnp.float32, smallest / len(cuts), top_value / len(cuts))
        gain = gain * jnp.repeat(jnp.exp(steps), shape[axis_at] // parts).reshape((-1,) + (1,) * (len(shape) - 1 - axis_at))
    return gain


def setup_inputs(seed: int = 0) -> dict:
    key_of = jax.random.split(jax.random.key(seed), 6)
    load_nodes = draw_load_nodes(jax.random.fold_in(key_of[5], 71), 0)
    metric = jnp.clip(jnp.exp(math.log(0.05) - 2.3025851 * jax.random.uniform(key_of[1], (ELEMS, 3, NODES ** 3), jnp.float32) ** steps_of(key_of[1], (ELEMS, 3, NODES ** 3), ((0, 256),), -0.2, 0.2)), 0.005, 0.05)
    mass_nodes = jnp.clip(jnp.exp(math.log(1.0) - 2.3025851 * jax.random.uniform(key_of[2], (ELEMS, NODES ** 3), jnp.float32) ** steps_of(key_of[2], (ELEMS, NODES ** 3), ((0, 256),), -0.2, 0.2)), 0.1, 1.0)
    smoother = draw_smoother(jax.random.fold_in(key_of[5], 71), 0)
    element_order = draw_element_order(jax.random.fold_in(key_of[5], 71), 0)
    return dict(load_nodes=load_nodes, metric=metric, mass_nodes=mass_nodes, smoother=smoother, element_order=element_order)


def derivative_table(node_count):
    degree = node_count - 1
    points = np.cos(np.pi * np.arange(node_count) / degree)
    weights = np.ones(node_count)
    weights[0] = 2.0
    weights[-1] = 2.0
    matrix = np.zeros((node_count, node_count))
    for row_index in range(node_count):
        for col_index in range(node_count):
            if row_index != col_index:
                matrix[row_index, col_index] = weights[row_index] / weights[col_index] * (-1.0) ** (row_index + col_index) / (points[row_index] - points[col_index])
        matrix[row_index, row_index] = -np.sum(matrix[row_index])
    return matrix


def cut_blocks(values_grid, axis_pos, block_width):
    step_size = NODES - 1
    leading = jnp.moveaxis(values_grid, axis_pos, 0)
    block_count = (leading.shape[0] - block_width + step_size) // step_size
    extra_rows = block_width - step_size
    head_rows = leading[:step_size * block_count].reshape((block_count, step_size) + leading.shape[1:])
    tail_rows = jnp.concatenate([head_rows[1:, :extra_rows], leading[step_size * block_count:][None]], axis=0)
    blocks = jnp.concatenate([head_rows, tail_rows], axis=1)
    return jnp.moveaxis(blocks, (0, 1), (axis_pos, axis_pos + 1))


def join_blocks(blocks, axis_pos):
    step_size = NODES - 1
    leading = jnp.moveaxis(blocks, (axis_pos, axis_pos + 1), (0, 1))
    block_count = leading.shape[0]
    extra_rows = leading.shape[1] - step_size
    head_rows = leading[:, :step_size]
    tail_rows = leading[:, step_size:]
    carried = jnp.concatenate([jnp.zeros_like(tail_rows[:1]), tail_rows[:-1]], axis=0)
    head_rows = jnp.concatenate([head_rows[:, :extra_rows] + carried, head_rows[:, extra_rows:]], axis=1)
    joined = jnp.concatenate([head_rows.reshape((step_size * block_count,) + leading.shape[2:]), tail_rows[-1]], axis=0)
    return jnp.moveaxis(joined, 0, axis_pos)


def to_elements(values_grid):
    return cut_blocks(cut_blocks(cut_blocks(values_grid, 0, NODES), 2, NODES), 4, NODES)


def to_grid(element_grid):
    return join_blocks(join_blocks(join_blocks(element_grid, 4), 2), 0)


def to_brick_rows(node_rows, element_order, groups_x, groups_y):
    per_device = EX * EY * EZ
    row_count = node_rows.shape[0]
    offsets = (jnp.arange(row_count, dtype=jnp.int32) // per_device) * per_device + element_order
    placed = jnp.zeros_like(node_rows).at[offsets].set(node_rows)
    shaped = placed.reshape(groups_x, groups_y, EX, EY, EZ, NODES, NODES, NODES)
    shaped = shaped.transpose(0, 2, 5, 1, 3, 6, 4, 7)
    return shaped.reshape(groups_x * EX, NODES, groups_y * EY, NODES, EZ, NODES)


def from_brick_rows(element_grid, element_order, groups_x, groups_y):
    per_device = EX * EY * EZ
    shaped = element_grid.reshape(groups_x, EX, NODES, groups_y, EY, NODES, EZ, NODES)
    shaped = shaped.transpose(0, 3, 1, 4, 6, 2, 5, 7)
    node_rows = shaped.reshape(-1, NODES ** 3)
    row_count = node_rows.shape[0]
    offsets = (jnp.arange(row_count, dtype=jnp.int32) // per_device) * per_device + element_order
    return node_rows[offsets]


def element_apply(values, metric_grid, mass_grid, derivative):
    highest = lax.Precision.HIGHEST
    grad_x = jnp.einsum("pa,iajbkc->ipjbkc", derivative, values, precision=highest)
    grad_y = jnp.einsum("pb,iajbkc->iajpkc", derivative, values, precision=highest)
    grad_z = jnp.einsum("pc,iajbkc->iajbkp", derivative, values, precision=highest)
    result = jnp.einsum("pa,ipjbkc->iajbkc", derivative, metric_grid[0] * grad_x, precision=highest)
    result = result + jnp.einsum("pb,iajpkc->iajbkc", derivative, metric_grid[1] * grad_y, precision=highest)
    result = result + jnp.einsum("pc,iajbkp->iajbkc", derivative, metric_grid[2] * grad_z, precision=highest)
    return result + mass_grid * values


def smooth_boxes(boxes, smoother):
    highest = lax.Precision.HIGHEST
    result = jnp.einsum("pa,iajbkc->ipjbkc", smoother, boxes, precision=highest)
    result = jnp.einsum("pb,iajbkc->iajpkc", smoother, result, precision=highest)
    return jnp.einsum("pc,iajbkc->iajbkp", smoother, result, precision=highest)


def reference(load_nodes, metric, mass_nodes, smoother, element_order):
    derivative = jnp.asarray(derivative_table(NODES), jnp.float32)
    bricked = partial(to_brick_rows, element_order=element_order, groups_x=N_GX, groups_y=N_GY)
    metric_grid = jnp.stack([bricked(metric[:, direction, :]) for direction in range(3)])
    mass_grid = bricked(mass_nodes)

    def operate(values_grid):
        return to_grid(element_apply(to_elements(values_grid), metric_grid, mass_grid, derivative))

    def precondition(values_grid):
        widened = jnp.pad(values_grid, 1)
        boxes = cut_blocks(cut_blocks(cut_blocks(widened, 0, NODES + 2), 2, NODES + 2), 4, NODES + 2)
        joined = join_blocks(join_blocks(join_blocks(smooth_boxes(boxes, smoother), 4), 2), 0)
        return joined[1:-1, 1:-1, 1:-1]

    right_side = to_grid(bricked(load_nodes))
    solution = jnp.zeros_like(right_side)
    residual = right_side
    search = precondition(residual)
    inner_now = jnp.sum(residual * search)
    direction = search
    for iteration in range(ITERS):
        image = operate(direction)
        step_length = inner_now / jnp.sum(direction * image)
        solution = solution + step_length * direction
        residual = residual - step_length * image
        if iteration + 1 < ITERS:
            search = precondition(residual)
            inner_next = jnp.sum(residual * search)
            direction = search + (inner_next / inner_now) * direction
            inner_now = inner_next
    back_rows = partial(from_brick_rows, element_order=element_order, groups_x=N_GX, groups_y=N_GY)
    return back_rows(to_elements(solution)), back_rows(to_elements(residual))
```

```python
import functools

import jax
import jax.numpy as jnp
import ml_dtypes
import numpy as np
from jax import lax
from jax.experimental import pallas as pl
from jax.experimental.pallas import tpu as pltpu
from jax.sharding import PartitionSpec as P

NODES = 8
BF16 = ml_dtypes.bfloat16
MESH = pl.DeviceIdType.MESH


def derivative_table(node_count):
    degree = node_count - 1
    points = np.cos(np.pi * np.arange(node_count) / degree)
    weights = np.ones(node_count)
    weights[0] = 2.0
    weights[-1] = 2.0
    matrix = np.zeros((node_count, node_count))
    for row in range(node_count):
        for col in range(node_count):
            if row != col:
                matrix[row, col] = (
                    weights[row]
                    / weights[col]
                    * (-1.0) ** (row + col)
                    / (points[row] - points[col])
                )
        matrix[row, row] = -np.sum(matrix[row])
    return matrix


def split_const(matrix):
    full = np.asarray(matrix, np.float32)
    high = full.astype(BF16)
    return high, (full - high.astype(np.float32)).astype(BF16)


@functools.lru_cache(None)
def tables():
    node = np.array([7 * i + a for i in range(2) for a in range(8)])
    incidence = {}
    for box in (-1, 0, 1, 2):
        block = np.zeros((10, 16))
        for at in range(16):
            idx = node[at] - 7 * box + 1
            if 0 <= idx < 10:
                block[idx, at] = 1.0
        incidence[box] = block
    dims = 64
    uc = np.zeros((24, dims))
    rv = np.zeros((dims, 16))
    re = np.zeros((16, dims))
    ae = np.zeros((dims, 24))
    for at in range(16):
        for slot, box in enumerate((-1, 0, 1, 2)):
            uc[at, slot * 10:slot * 10 + 10] = incidence[box][:, at]
            rv[slot * 10:slot * 10 + 10, at] = incidence[box][:, at]
        re[at, 10:20] = incidence[0][:, at]
        re[at, 20:30] = incidence[1][:, at]
        re[at, 40 + at] = 1.0
        ae[40 + at, at] = 1.0
        for dim, where in ((56, 0), (57, 1), (58, 13), (59, 14)):
            rv[dim, at] = float(node[at] == where)
            re[at, dim] = float(node[at] == where)
    uc[16, 20 + 8] = uc[17, 20 + 9] = uc[18, 58] = uc[19, 59] = 1.0
    uc[20, 10 + 0] = uc[21, 10 + 1] = uc[22, 56] = uc[23, 57] = 1.0
    ae[56, 16] = ae[57, 17] = ae[10 + 0, 18] = ae[10 + 1, 19] = 1.0
    ae[58, 20] = ae[59, 21] = ae[20 + 8, 22] = ae[20 + 9, 23] = 1.0
    assemble = np.zeros((24, 16))
    assemble[:16] = node[:, None] == node[None, :]
    assemble[16] = node == 14
    assemble[21] = node == 0

    lane = np.arange(256)
    xi = (lane // 128) * 8 + (lane // 8) % 8
    eta = ((lane // 64) % 2) * 8 + lane % 8
    mx, my = [], []
    for side in (16, 20):
        for q in range(4):
            for e in range(16):
                mx.append(side + q)
                my.append(e)
    for side in (16, 20):
        for e in range(16):
            for q in range(4):
                mx.append(e)
                my.append(side + q)
    for sx in (16, 20):
        for sy in (16, 20):
            for qx in range(4):
                for qy in range(4):
                    mx.append(sx + qx)
                    my.append(sy + qy)
    mx, my = np.array(mx), np.array(my)

    def padded(rows, index):
        return np.concatenate([rows[index], np.zeros((64,) + rows.shape[1:])], axis=0)

    allx = np.concatenate([xi, mx])
    ally = np.concatenate([eta, my])
    ucx, ucy = padded(uc, allx), padded(uc, ally)
    rvx, rvy = rv[:, xi], rv[:, eta]
    rex, rey = re[xi], re[eta]
    aex, aey = padded(ae.T, mx).T, padded(ae.T, my).T
    asm = padded(assemble, allx)[:, xi] * padded(assemble, ally)[:, eta]

    edges = np.zeros((8, 384))
    edges[0, :320] = (mx >= 16) & (mx < 20)
    edges[1, :320] = mx >= 20
    edges[2, :320] = (my >= 16) & (my < 20)
    edges[3, :320] = my >= 20

    tile = np.zeros((64, 128))
    for block in range(4):
        for idx in range(10):
            tile[block * 10 + idx, idx] = 1.0
    same = np.zeros((64, 64))
    for block in range(4):
        same[block * 10:block * 10 + 10, block * 10:block * 10 + 10] = 1.0
    fixed = np.diag((np.arange(64) >= 40).astype(float))
    znode = np.array([7 * k + c for k in range(4) for c in range(8)])
    rz = np.zeros((64, 32))
    for block in range(4):
        for at in range(32):
            idx = znode[at] - 7 * block + 1
            if 0 <= idx < 10:
                rz[block * 10 + idx, at] = 1.0
    az = (znode[:, None] == znode[None, :]).astype(float)

    d = derivative_table(NODES).astype(np.float32)
    eye8 = np.eye(8)
    dx = np.kron(np.eye(4), np.kron(d.T, eye8))
    dy = np.kron(np.eye(4), np.kron(eye8, d.T))
    dxy_hi, dxy_lo = split_const(np.concatenate([dx, dy], axis=1))
    dz = np.kron(np.eye(4), d)
    dz_hi, dz_lo = split_const(dz)
    dzt_hi, dzt_lo = split_const(dz.T)

    sel = np.zeros((512, 512))
    at = np.arange(512)
    sel[at, (at % 8) * 64 + at // 8] = 1.0
    b = lambda m: np.asarray(m, BF16)
    return dict(
        sel=b(sel),
        dxy_hi=dxy_hi,
        dxy_lo=dxy_lo,
        dxyt_hi=np.ascontiguousarray(dxy_hi.T),
        dxyt_lo=np.ascontiguousarray(dxy_lo.T),
        dz=np.concatenate([dz_hi, dz_hi, dz_lo], axis=1),
        dzt=np.concatenate([dzt_hi, dzt_hi, dzt_lo], axis=1),
        az=b(np.concatenate([az, az], axis=1)),
        uc=b(np.stack([np.concatenate([ucx, ucx], 1), np.concatenate([ucy, ucy], 1)])),
        rv=np.asarray(np.stack([rvx, rvy]), np.float32),
        re=b(np.stack([np.concatenate([rex, rex], 1), np.concatenate([rey, rey], 1)])),
        ae=np.asarray(np.stack([aex, aey]), np.float32),
        asm=b(asm),
        edges=np.asarray(edges, np.float32),
        tile=np.asarray(tile, np.float32),
        same=np.asarray(same, np.float32),
        fixed=np.asarray(fixed, np.float32),
        rz=np.asarray(np.concatenate([rz, rz, rz], axis=1), np.float32),
        rzt=np.asarray(rz.T, np.float32),
    )


NAMES = (
    "sel", "dxy_hi", "dxy_lo", "dxyt_hi", "dxyt_lo", "dz", "dzt", "az", "uc", "rv", "re", "ae",
    "asm", "edges", "tile", "same", "fixed", "rz", "rzt",
)


def fdot(left, right):
    return jnp.dot(left, right, preferred_element_type=jnp.float32)


def exact_dot(left, right):
    return jnp.dot(
        left, right, preferred_element_type=jnp.float32, precision=lax.Precision.HIGHEST
    )


def split(value):
    high = value.astype(jnp.bfloat16)
    low = (value - high.astype(jnp.float32)).astype(jnp.bfloat16)
    return high, low


def right_dot(value, w_hi, w_lo):
    rows = value.shape[0]
    high, low = split(value)
    both = fdot(jnp.concatenate([high, low], axis=0), w_hi)
    return both[:rows] + both[rows:] + fdot(high, w_lo)


def left_dot(stacked, value):
    high, low = split(value)
    return fdot(stacked, jnp.concatenate([high, low, high], axis=0))


def iota(shape, dim):
    return lax.broadcasted_iota(jnp.int32, shape, dim)


def half_roll(value):
    return pltpu.roll(value, 64, 1)


def local_sum(first, second):
    t = first * second
    t = t[0:8] + t[8:16] + t[16:24] + t[24:32]
    return t[:, :128] + t[:, 128:]


def kernel(
    nx, ny, lo,
    load_ref, metric_ref, mass_ref, smoother_ref, order_ref, *refs,
):
    c = dict(zip(NAMES, refs[:len(NAMES)]))
    (
        pressure_ref, residual_ref,
        k_hi, k_lo, e_hi, e_lo, s_pad,
        halo_out, halo_in, halo_send, halo_recv,
        sums, sum_send, sum_recv,
    ) = refs[len(NAMES):]
    gx = lax.axis_index("gx")
    gy = lax.axis_index("gy")
    hi = nx // lo
    x_low, x_high = lax.rem(gx + nx - 1, nx), lax.rem(gx + 1, nx)
    y_low, y_high = lax.rem(gy + ny - 1, ny), lax.rem(gy + 1, ny)
    neighbours = (
        ((x_low, gy), 0), ((x_high, gy), 1),
        ((gx, y_low), 2), ((gx, y_high), 3),
        ((x_low, y_low), 4), ((x_low, y_high), 4),
        ((x_high, y_low), 4), ((x_high, y_high), 4),
    )
    z_at, y_at = lax.rem(gx, lo), lax.div(gx, lo)
    rounds = [
        [(gx, lax.rem(gy + d, ny)) for d in range(1, ny)],
        [(y_at * lo + lax.rem(z_at + d, lo), gy) for d in range(1, lo)],
        [(lax.rem(y_at + d, hi) * lo + z_at, gy) for d in range(1, hi)],
    ]
    greeted = [n for n, _ in neighbours] + [peer for group in rounds for peer in group]

    barrier = pltpu.get_barrier_semaphore()
    for peer in greeted:
        pl.semaphore_signal(barrier, inc=1, device_id=peer, device_id_type=MESH)

    row = iota((128, 128), 0)
    lane = iota((128, 128), 1)
    wanted = jnp.zeros((128, 128), jnp.int32)
    for s in range(16):
        wanted = jnp.where((lane & 15) == s, order_ref[s], wanted)
    place = (
        ((row >> 3) == wanted) & (((row & 7) >> 1) == ((lane & 63) >> 4))
    ).astype(jnp.float32).astype(jnp.bfloat16)
    row_t = iota((64, 128), 0)
    lane_t = iota((64, 128), 1)
    wanted_t = jnp.zeros((64, 128), jnp.int32)
    for s in range(16):
        wanted_t = jnp.where((row_t & 15) == s, order_ref[s], wanted_t)
    unplace = (
        ((lane_t >> 3) == wanted_t) & (((lane_t & 7) >> 1) == (row_t >> 4))
    ).astype(jnp.float32).astype(jnp.bfloat16)

    row32 = iota((32, 128), 0)
    lane32 = iota((32, 128), 1)
    parity = row32 & 1
    left_half = lane32 < 64

    def from_rows(fields):
        count = len(fields)
        parts = [split(f) for f in fields]
        stacked = jnp.concatenate([p[0] for p in parts] + [p[1] for p in parts], axis=0)
        moved = fdot(stacked, c["sel"][...]).astype(jnp.bfloat16)
        out = []
        for f in range(count):
            pieces = []
            for part in range(2):
                z = moved[(part * count + f) * 16:(part * count + f) * 16 + 16]
                pieces += [z[:, u * 128:u * 128 + 128] for u in range(4)]
            v = fdot(place, jnp.concatenate(pieces, axis=0))
            tiles = []
            for pair in range(2):
                picked = []
                for odd in range(2):
                    at = (pair * 2 + odd) * 32
                    block = v[at:at + 32]
                    picked.append(jnp.where(parity == odd, block, half_roll(block)))
                tiles.append(jnp.where(left_half, picked[0], picked[1]))
            out.append(jnp.concatenate(tiles, axis=1))
        return out

    def to_rows(values):
        count = len(values)
        highs, lows = [], []
        for value in values:
            blocks = []
            for ij in range(4):
                block = value[:, (ij // 2) * 128:(ij // 2) * 128 + 128]
                block = jnp.where(parity == (ij & 1), block, half_roll(block))
                blocks.append(jnp.where((lane32 >> 6) == parity, block, 0.0))
            high, low = split(jnp.concatenate(blocks, axis=0))
            highs.append(high)
            lows.append(low)
        o = fdot(unplace, jnp.concatenate(highs + lows, axis=1)).astype(jnp.bfloat16)
        rows = []
        for v in range(2 * count):
            rows.append(
                jnp.concatenate(
                    [o[u * 16:u * 16 + 16, v * 128:v * 128 + 128] for u in range(4)], axis=1
                )
            )
        n = lax.dot_general(
            jnp.concatenate(rows, axis=0), c["sel"][...], (((1,), (1,)), ((), ())),
            preferred_element_type=jnp.float32,
        )
        return [
            n[v * 16:v * 16 + 16] + n[(count + v) * 16:(count + v) * 16 + 16]
            for v in range(count)
        ]

    s_pad[...] = jnp.zeros((128, 128), jnp.float32)
    s_pad[0:10, 0:10] = smoother_ref[...]
    tile = c["tile"][...]
    spread = exact_dot(tile, s_pad[...])
    base = lax.dot_general(
        spread, tile, (((1,), (1,)), ((), ())),
        preferred_element_type=jnp.float32, precision=lax.Precision.HIGHEST,
    ) * c["same"][...] + c["fixed"][...]

    def expanded(left, right):
        high, low = split(right)
        return fdot(left, jnp.concatenate([high, low], axis=0))

    enc = expanded(c["re"][0], exact_dot(base, c["ae"][0])) * expanded(
        c["re"][1], exact_dot(base, c["ae"][1])
    )
    high, low = split(enc)
    e_hi[...] = high
    e_lo[...] = low

    r0, = from_rows([load_ref[...]])

    low_x = (gx == 0).astype(jnp.float32)
    high_x = (gx == nx - 1).astype(jnp.float32)
    low_y = (gy == 0).astype(jnp.float32)
    high_y = (gy == ny - 1).astype(jnp.float32)
    edges = c["edges"][...]
    arrives = (1.0 - edges[0:1] * high_x - edges[1:2] * low_x) * (
        1.0 - edges[2:3] * high_y - edges[3:4] * low_y
    )

    lane16 = iota((16, 128), 1)
    left16 = lane16 < 64
    quarter = (lane16 & 63) >> 4

    pl.semaphore_wait(barrier, len(greeted))

    def exchange_start(stage, value):
        m = right_dot(value, e_hi[...], e_lo[...])
        for pair in range(2):
            t = m[:, pair * 128:pair * 128 + 128]
            top, bottom = t[0:16], t[16:32]
            halo_out[stage, 2 * pair] = jnp.where(left16, top, half_roll(bottom))
            halo_out[stage, 2 * pair + 1] = jnp.where(left16, half_roll(top), bottom)
        t = m[:, 256:384]
        halo_out[stage, 4] = jnp.where(left16, t[0:16], half_roll(t[16:32]))
        copies = []
        for slot, (peer, part) in enumerate(neighbours):
            copy = pltpu.make_async_remote_copy(
                src_ref=halo_out.at[stage, part],
                dst_ref=halo_in.at[stage, slot],
                send_sem=halo_send.at[stage, slot],
                recv_sem=halo_recv.at[stage, slot],
                device_id=peer,
                device_id_type=MESH,
            )
            copy.start()
            copies.append(copy)
        return copies

    def exchange_end(stage, copies):
        for copy in copies:
            copy.wait_recv()
        tiles = []
        for pair in range(2):
            a, b = halo_in[stage, 2 * pair], halo_in[stage, 2 * pair + 1]
            tiles.append(
                jnp.concatenate(
                    [jnp.where(left16, a, half_roll(b)), jnp.where(left16, half_roll(a), b)],
                    axis=0,
                )
            )
        corner = jnp.where(
            quarter == 0, halo_in[stage, 4],
            jnp.where(
                quarter == 1, halo_in[stage, 5],
                jnp.where(quarter == 2, halo_in[stage, 6], halo_in[stage, 7]),
            ),
        )
        tiles.append(jnp.concatenate([corner, half_roll(corner)], axis=0))
        return jnp.concatenate(tiles, axis=1) * arrives

    def sum_round_start(which, at, value):
        sums[which, at, 0] = value
        copies = []
        for d, peer in enumerate(rounds[at]):
            copy = pltpu.make_async_remote_copy(
                src_ref=sums.at[which, at, 0],
                dst_ref=sums.at[which, at, d + 1],
                send_sem=sum_send.at[which, at, d],
                recv_sem=sum_recv.at[which, at, d],
                device_id=peer,
                device_id_type=MESH,
            )
            copy.start()
            copies.append(copy)
        return copies

    def sum_round_end(which, at, copies):
        for copy in copies:
            copy.wait_recv()
        total = sums[which, at, 0]
        for d in range(len(copies)):
            total = total + sums[which, at, d + 1]
        return total

    row8 = iota((8, 128), 0)

    def partial_tile(r, w, u):
        first = local_sum(r, u)
        second = local_sum(w, u)
        return jnp.where(
            row8 < 4, first + pltpu.roll(first, 4, 0), second + pltpu.roll(second, 4, 0)
        )

    def both_sums(total):
        first = jnp.sum(jnp.where(row8 < 4, total, 0.0), axis=1, keepdims=True)
        second = jnp.sum(jnp.where(row8 < 4, 0.0, total), axis=1, keepdims=True)
        return jnp.sum(first, axis=0, keepdims=True), jnp.sum(second, axis=0, keepdims=True)

    sent = []
    halo = exchange_start(0, r0)
    sent += halo

    row64 = iota((64, 64), 0)
    for axis, low_edge, high_edge in ((0, low_x, high_x), (1, low_y, high_y)):
        masked = base * (
            1.0
            - low_edge * (row64 < 10).astype(jnp.float32)
            - high_edge * ((row64 >= 30) & (row64 < 40)).astype(jnp.float32)
        )
        wide = expanded(c["uc"][axis], exact_dot(masked, c["rv"][axis]))
        kxy = wide if axis == 0 else kxy * wide
    high, low = split(kxy)
    k_hi[...] = high
    k_lo[...] = low
    tz = exact_dot(c["rzt"][...], exact_dot(base, c["rz"][...]))
    tz_hi, tz_lo = split(tz)
    tz = jnp.where(iota((32, 96), 1) < 64, tz_hi.astype(jnp.float32), tz_lo.astype(jnp.float32))
    tz = tz.astype(jnp.bfloat16)

    m0, m1, m2, mass = from_rows(
        [metric_ref[:, 0, :], metric_ref[:, 1, :], metric_ref[:, 2, :], mass_ref[...]]
    )
    m01 = jnp.concatenate([m0, m1], axis=1)

    def own_part(value):
        return right_dot(value, k_hi[0:256], k_lo[0:256])

    def precondition(own, arrived):
        return left_dot(tz, own + right_dot(arrived, k_hi[256:640], k_lo[256:640]))

    def operate(u):
        slope = m01 * right_dot(u, c["dxy_hi"][...], c["dxy_lo"][...])
        slope_z = m2 * left_dot(c["dz"][...], u)
        return (
            right_dot(slope, c["dxyt_hi"][...], c["dxyt_lo"][...])
            + left_dot(c["dzt"][...], slope_z)
            + mass * u
        )

    def assembled(value, arrived):
        both = jnp.concatenate([value, arrived], axis=1)
        high, low = split(both)
        t = fdot(jnp.concatenate([high, low], axis=0), c["asm"][...])
        t = t[:32] + t[32:]
        high, low = split(t)
        return fdot(c["az"][...], jnp.concatenate([high, low], axis=0))

    own = own_part(r0)
    arrived_r0 = exchange_end(0, halo)
    z0 = precondition(own, arrived_r0)
    w0 = operate(z0)

    halo = exchange_start(1, w0)
    sent += halo
    ring = sum_round_start(0, 0, partial_tile(r0, w0, z0))
    sent += ring
    own = own_part(w0)
    arrived_w0 = exchange_end(1, halo)
    total = sum_round_end(0, 0, ring)
    ring = sum_round_start(0, 1, total)
    sent += ring
    z1 = precondition(own, arrived_w0)
    total = sum_round_end(0, 1, ring)
    ring = sum_round_start(0, 2, total)
    sent += ring
    w1 = operate(z1)
    halo = exchange_start(2, w1)
    sent += halo
    total = sum_round_end(0, 2, ring)
    gamma0, delta0 = both_sums(total)
    alpha0 = gamma0 / delta0

    r1 = r0 - alpha0 * w0
    u1 = z0 - alpha0 * z1
    v1 = w0 - alpha0 * w1
    ring = sum_round_start(1, 0, partial_tile(r1, v1, u1))
    sent += ring
    own = own_part(w1)
    arrived_w1 = exchange_end(2, halo)
    total = sum_round_end(1, 0, ring)
    ring = sum_round_start(1, 1, total)
    sent += ring
    z2 = precondition(own, arrived_w1)
    total = sum_round_end(1, 1, ring)
    ring = sum_round_start(1, 2, total)
    sent += ring
    w2 = operate(z2)
    halo = exchange_start(3, w2)
    sent += halo
    total = sum_round_end(1, 2, ring)
    gamma1, delta1 = both_sums(total)
    beta1 = gamma1 / gamma0
    alpha1 = gamma1 / (delta1 - beta1 * gamma1 / alpha0)

    def advance(r0, z0, z1, z2, w0, w1, w2):
        p1 = (z0 - alpha0 * z1) + beta1 * z0
        q1 = (z1 - alpha0 * z2) + beta1 * z1
        u2 = (z0 - alpha0 * z1) - alpha1 * q1
        x2 = alpha0 * z0 + alpha1 * p1
        v1 = w0 - alpha0 * w1
        s1 = v1 + beta1 * w0
        y1 = (w1 - alpha0 * w2) + beta1 * w1
        r2 = (r0 - alpha0 * w0) - alpha1 * s1
        v2 = v1 - alpha1 * y1
        return r2, u2, v2, x2, p1, s1

    r2, u2, v2, x2, p1, s1 = advance(r0, z0, z1, z2, w0, w1, w2)
    ring = sum_round_start(2, 0, partial_tile(r2, v2, u2))
    sent += ring

    rows_u2, rows_x2, rows_p1, rows_r0, rows_w0, rows_w1 = to_rows(
        [
            u2, x2, p1, assembled(r0, arrived_r0), assembled(w0, arrived_w0),
            assembled(w1, arrived_w1),
        ]
    )
    total = sum_round_end(2, 0, ring)
    ring = sum_round_start(2, 1, total)
    sent += ring
    arrived_w2 = exchange_end(3, halo)
    rows_w2, = to_rows([assembled(w2, arrived_w2)])
    rows_v1 = rows_w0 - alpha0 * rows_w1
    rows_s1 = rows_v1 + beta1 * rows_w0
    rows_y1 = (rows_w1 - alpha0 * rows_w2) + beta1 * rows_w1
    rows_r2 = (rows_r0 - alpha0 * rows_w0) - alpha1 * rows_s1
    rows_v2 = rows_v1 - alpha1 * rows_y1
    total = sum_round_end(2, 1, ring)
    ring = sum_round_start(2, 2, total)
    sent += ring
    total = sum_round_end(2, 2, ring)
    gamma2, delta2 = both_sums(total)
    beta2 = gamma2 / gamma1
    alpha2 = gamma2 / (delta2 - beta2 * gamma2 / alpha1)
    pressure_ref[...] = rows_x2 + alpha2 * (rows_u2 + beta2 * rows_p1)
    residual_ref[...] = rows_r2 - alpha2 * (rows_v2 + beta2 * rows_s1)
    for copy in sent:
        copy.wait_send()


def solution(mesh):
    nx, ny = mesh.shape["gx"], mesh.shape["gy"]
    lo = 8 if nx % 8 == 0 else 2
    consts = tables()
    vmem = pl.BlockSpec(memory_space=pltpu.VMEM)
    rows = jax.ShapeDtypeStruct((16, 512), jnp.float32)
    longest = max(ny, lo)
    call = pl.pallas_call(
        functools.partial(kernel, nx, ny, lo),
        out_shape=(rows, rows),
        in_specs=[vmem] * 4 + [pl.BlockSpec(memory_space=pltpu.SMEM)] + [vmem] * len(NAMES),
        out_specs=(vmem, vmem),
        scratch_shapes=[
            pltpu.VMEM((640, 256), jnp.bfloat16),
            pltpu.VMEM((640, 256), jnp.bfloat16),
            pltpu.VMEM((256, 384), jnp.bfloat16),
            pltpu.VMEM((256, 384), jnp.bfloat16),
            pltpu.VMEM((128, 128), jnp.float32),
            pltpu.VMEM((4, 5, 16, 128), jnp.float32),
            pltpu.VMEM((4, 8, 16, 128), jnp.float32),
            pltpu.SemaphoreType.DMA((4, 8)),
            pltpu.SemaphoreType.DMA((4, 8)),
            pltpu.VMEM((3, 3, longest, 8, 128), jnp.float32),
            pltpu.SemaphoreType.DMA((3, 3, longest)),
            pltpu.SemaphoreType.DMA((3, 3, longest)),
        ],
        compiler_params=pltpu.CompilerParams(
            collective_id=0, has_side_effects=True, vmem_limit_bytes=32 * 1024 * 1024
        ),
    )

    def on_device(load_nodes, metric, mass_nodes, smoother, element_order):
        return call(
            load_nodes, metric, mass_nodes, smoother, element_order,
            *[jnp.asarray(consts[name]) for name in NAMES],
        )

    return jax.shard_map(
        on_device,
        mesh=mesh,
        in_specs=(
            P(("gx", "gy"), None),
            P(("gx", "gy"), None, None),
            P(("gx", "gy"), None),
            P(),
            P(("gx", "gy")),
        ),
        out_specs=(P(("gx", "gy"), None), P(("gx", "gy"), None)),
        check_vma=False,
    )
```

```python
import functools

import jax
import jax.numpy as jnp
import ml_dtypes
import numpy as np
from jax import lax
from jax.experimental import pallas as pl
from jax.experimental.pallas import tpu as pltpu
from jax.sharding import PartitionSpec as P

NODES = 8
BF16 = ml_dtypes.bfloat16
MESH = pl.DeviceIdType.MESH


def derivative_table(node_count):
    degree = node_count - 1
    points = np.cos(np.pi * np.arange(node_count) / degree)
    weights = np.ones(node_count)
    weights[0] = 2.0
    weights[-1] = 2.0
    matrix = np.zeros((node_count, node_count))
    for row in range(node_count):
        for col in range(node_count):
            if row != col:
                matrix[row, col] = (
                    weights[row]
                    / weights[col]
                    * (-1.0) ** (row + col)
                    / (points[row] - points[col])
                )
        matrix[row, row] = -np.sum(matrix[row])
    return matrix


def split_const(matrix):
    full = np.asarray(matrix, np.float32)
    high = full.astype(BF16)
    return high, (full - high.astype(np.float32)).astype(BF16)


@functools.lru_cache(None)
def tables():
    node = np.array([7 * i + a for i in range(2) for a in range(8)])
    incidence = {}
    for box in (-1, 0, 1, 2):
        block = np.zeros((10, 16))
        for at in range(16):
            idx = node[at] - 7 * box + 1
            if 0 <= idx < 10:
                block[idx, at] = 1.0
        incidence[box] = block
    dims = 64
    uc = np.zeros((24, dims))
    rv = np.zeros((dims, 16))
    re = np.zeros((16, dims))
    ae = np.zeros((dims, 24))
    for at in range(16):
        for slot, box in enumerate((-1, 0, 1, 2)):
            uc[at, slot * 10:slot * 10 + 10] = incidence[box][:, at]
            rv[slot * 10:slot * 10 + 10, at] = incidence[box][:, at]
        re[at, 10:20] = incidence[0][:, at]
        re[at, 20:30] = incidence[1][:, at]
        re[at, 40 + at] = 1.0
        ae[40 + at, at] = 1.0
        for dim, where in ((56, 0), (57, 1), (58, 13), (59, 14)):
            rv[dim, at] = float(node[at] == where)
            re[at, dim] = float(node[at] == where)
    uc[16, 20 + 8] = uc[17, 20 + 9] = uc[18, 58] = uc[19, 59] = 1.0
    uc[20, 10 + 0] = uc[21, 10 + 1] = uc[22, 56] = uc[23, 57] = 1.0
    ae[56, 16] = ae[57, 17] = ae[10 + 0, 18] = ae[10 + 1, 19] = 1.0
    ae[58, 20] = ae[59, 21] = ae[20 + 8, 22] = ae[20 + 9, 23] = 1.0
    assemble = np.zeros((24, 16))
    assemble[:16] = node[:, None] == node[None, :]
    assemble[16] = node == 14
    assemble[21] = node == 0

    lane = np.arange(256)
    xi = (lane // 128) * 8 + (lane // 8) % 8
    eta = ((lane // 64) % 2) * 8 + lane % 8
    mx, my = [], []
    for side in (16, 20):
        for q in range(4):
            for e in range(16):
                mx.append(side + q)
                my.append(e)
    for side in (16, 20):
        for e in range(16):
            for q in range(4):
                mx.append(e)
                my.append(side + q)
    for sx in (16, 20):
        for sy in (16, 20):
            for qx in range(4):
                for qy in range(4):
                    mx.append(sx + qx)
                    my.append(sy + qy)
    mx, my = np.array(mx), np.array(my)

    def padded(rows, index):
        return np.concatenate([rows[index], np.zeros((64,) + rows.shape[1:])], axis=0)

    allx = np.concatenate([xi, mx])
    ally = np.concatenate([eta, my])
    ucx, ucy = padded(uc, allx), padded(uc, ally)
    rvx, rvy = rv[:, xi], rv[:, eta]
    rex, rey = re[xi], re[eta]
    aex, aey = padded(ae.T, mx).T, padded(ae.T, my).T
    asm = padded(assemble, allx)[:, xi] * padded(assemble, ally)[:, eta]

    edges = np.zeros((8, 384))
    edges[0, :320] = (mx >= 16) & (mx < 20)
    edges[1, :320] = mx >= 20
    edges[2, :320] = (my >= 16) & (my < 20)
    edges[3, :320] = my >= 20

    tile = np.zeros((64, 128))
    for block in range(4):
        for idx in range(10):
            tile[block * 10 + idx, idx] = 1.0
    same = np.zeros((64, 64))
    for block in range(4):
        same[block * 10:block * 10 + 10, block * 10:block * 10 + 10] = 1.0
    fixed = np.diag((np.arange(64) >= 40).astype(float))
    znode = np.array([7 * k + c for k in range(4) for c in range(8)])
    rz = np.zeros((64, 32))
    for block in range(4):
        for at in range(32):
            idx = znode[at] - 7 * block + 1
            if 0 <= idx < 10:
                rz[block * 10 + idx, at] = 1.0
    az = (znode[:, None] == znode[None, :]).astype(float)

    d = derivative_table(NODES).astype(np.float32)
    eye8 = np.eye(8)
    dx = np.kron(np.eye(4), np.kron(d.T, eye8))
    dy = np.kron(np.eye(4), np.kron(eye8, d.T))
    dxy_hi, dxy_lo = split_const(np.concatenate([dx, dy], axis=1))
    dz = np.kron(np.eye(4), d)
    dz_hi, dz_lo = split_const(dz)
    dzt_hi, dzt_lo = split_const(dz.T)

    sel = np.zeros((512, 512))
    at = np.arange(512)
    sel[at, (at % 8) * 64 + at // 8] = 1.0
    b = lambda m: np.asarray(m, BF16)
    return dict(
        sel=b(sel),
        dxy_hi=dxy_hi,
        dxy_lo=dxy_lo,
        dxyt_hi=np.ascontiguousarray(dxy_hi.T),
        dxyt_lo=np.ascontiguousarray(dxy_lo.T),
        dz=np.concatenate([dz_hi, dz_hi, dz_lo], axis=1),
        dzt=np.concatenate([dzt_hi, dzt_hi, dzt_lo], axis=1),
        az=b(np.concatenate([az, az], axis=1)),
        uc=b(np.stack([np.concatenate([ucx, ucx], 1), np.concatenate([ucy, ucy], 1)])),
        rv=np.asarray(np.stack([rvx, rvy]), np.float32),
        re=b(np.stack([np.concatenate([rex, rex], 1), np.concatenate([rey, rey], 1)])),
        ae=np.asarray(np.stack([aex, aey]), np.float32),
        asm=b(asm),
        edges=np.asarray(edges, np.float32),
        tile=np.asarray(tile, np.float32),
        same=np.asarray(same, np.float32),
        fixed=np.asarray(fixed, np.float32),
        rz=np.asarray(np.concatenate([rz, rz, rz], axis=1), np.float32),
        rzt=np.asarray(rz.T, np.float32),
    )


FETCHED = (
    "smoother", "tile", "same", "fixed", "load", "sel", "ae", "re", "edges", "rv", "uc", "rz",
    "rzt", "metric", "mass", "dxy_hi", "dxy_lo", "dz", "dxyt_hi", "dxyt_lo", "dzt", "asm", "az",
)


def fdot(left, right):
    return jnp.dot(left, right, preferred_element_type=jnp.float32)


def exact_dot(left, right):
    return jnp.dot(
        left, right, preferred_element_type=jnp.float32, precision=lax.Precision.HIGHEST
    )


def split(value):
    high = value.astype(jnp.bfloat16)
    low = (value - high.astype(jnp.float32)).astype(jnp.bfloat16)
    return high, low


def right_dot(value, w_hi, w_lo):
    rows = value.shape[0]
    high, low = split(value)
    both = fdot(jnp.concatenate([high, low], axis=0), w_hi)
    return both[:rows] + both[rows:] + fdot(high, w_lo)


def left_dot(stacked, value):
    high, low = split(value)
    return fdot(stacked, jnp.concatenate([high, low, high], axis=0))


def iota(shape, dim):
    return lax.broadcasted_iota(jnp.int32, shape, dim)


def half_roll(value):
    return pltpu.roll(value, 64, 1)


def local_sum(first, second):
    t = first * second
    t = t[0:8] + t[8:16] + t[16:24] + t[24:32]
    return t[:, :128] + t[:, 128:]


def kernel(
    nx, ny, lo,
    order_ref, *refs,
):
    count = len(FETCHED)
    far = dict(zip(FETCHED, refs[:count]))
    near = dict(zip(FETCHED, refs[count + 2:2 * count + 2]))
    pressure_ref, residual_ref = refs[count:count + 2]
    (
        fetch_sem, k_hi, k_lo, e_hi, e_lo, s_pad,
        halo_out, halo_in, halo_send, halo_recv,
        sums, sum_send, sum_recv,
    ) = refs[2 * count + 2:]
    fetches = {}
    for at, name in enumerate(FETCHED):
        fetches[name] = pltpu.make_async_copy(far[name], near[name], fetch_sem.at[at])
        fetches[name].start()

    def c(name):
        if name in fetches:
            fetches.pop(name).wait()
        return near[name]

    gx = lax.axis_index("gx")
    gy = lax.axis_index("gy")
    hi = nx // lo
    x_low, x_high = lax.rem(gx + nx - 1, nx), lax.rem(gx + 1, nx)
    y_low, y_high = lax.rem(gy + ny - 1, ny), lax.rem(gy + 1, ny)
    neighbours = (
        ((x_low, gy), 0), ((x_high, gy), 1),
        ((gx, y_low), 2), ((gx, y_high), 3),
        ((x_low, y_low), 4), ((x_low, y_high), 4),
        ((x_high, y_low), 4), ((x_high, y_high), 4),
    )
    z_at, y_at = lax.rem(gx, lo), lax.div(gx, lo)
    rounds = [
        [(gx, lax.rem(gy + d, ny)) for d in range(1, ny)],
        [(y_at * lo + lax.rem(z_at + d, lo), gy) for d in range(1, lo)],
        [(lax.rem(y_at + d, hi) * lo + z_at, gy) for d in range(1, hi)],
    ]
    greeted = [n for n, _ in neighbours] + [peer for group in rounds for peer in group]

    barrier = pltpu.get_barrier_semaphore()
    for peer in greeted:
        pl.semaphore_signal(barrier, inc=1, device_id=peer, device_id_type=MESH)

    row = iota((128, 128), 0)
    lane = iota((128, 128), 1)
    wanted = jnp.zeros((128, 128), jnp.int32)
    for s in range(16):
        wanted = jnp.where((lane & 15) == s, order_ref[s], wanted)
    place = (
        ((row >> 3) == wanted) & (((row & 7) >> 1) == ((lane & 63) >> 4))
    ).astype(jnp.float32).astype(jnp.bfloat16)
    row_t = iota((64, 128), 0)
    lane_t = iota((64, 128), 1)
    wanted_t = jnp.zeros((64, 128), jnp.int32)
    for s in range(16):
        wanted_t = jnp.where((row_t & 15) == s, order_ref[s], wanted_t)
    unplace = (
        ((lane_t >> 3) == wanted_t) & (((lane_t & 7) >> 1) == (row_t >> 4))
    ).astype(jnp.float32).astype(jnp.bfloat16)

    row32 = iota((32, 128), 0)
    lane32 = iota((32, 128), 1)
    parity = row32 & 1
    left_half = lane32 < 64

    def from_rows(fields):
        count = len(fields)
        parts = [split(f) for f in fields]
        stacked = jnp.concatenate([p[0] for p in parts] + [p[1] for p in parts], axis=0)
        moved = fdot(stacked, c("sel")[...]).astype(jnp.bfloat16)
        out = []
        for f in range(count):
            pieces = []
            for part in range(2):
                z = moved[(part * count + f) * 16:(part * count + f) * 16 + 16]
                pieces += [z[:, u * 128:u * 128 + 128] for u in range(4)]
            v = fdot(place, jnp.concatenate(pieces, axis=0))
            tiles = []
            for pair in range(2):
                picked = []
                for odd in range(2):
                    at = (pair * 2 + odd) * 32
                    block = v[at:at + 32]
                    picked.append(jnp.where(parity == odd, block, half_roll(block)))
                tiles.append(jnp.where(left_half, picked[0], picked[1]))
            out.append(jnp.concatenate(tiles, axis=1))
        return out

    def to_rows(values):
        count = len(values)
        highs, lows = [], []
        for value in values:
            blocks = []
            for ij in range(4):
                block = value[:, (ij // 2) * 128:(ij // 2) * 128 + 128]
                block = jnp.where(parity == (ij & 1), block, half_roll(block))
                blocks.append(jnp.where((lane32 >> 6) == parity, block, 0.0))
            high, low = split(jnp.concatenate(blocks, axis=0))
            highs.append(high)
            lows.append(low)
        o = fdot(unplace, jnp.concatenate(highs + lows, axis=1)).astype(jnp.bfloat16)
        rows = []
        for v in range(2 * count):
            rows.append(
                jnp.concatenate(
                    [o[u * 16:u * 16 + 16, v * 128:v * 128 + 128] for u in range(4)], axis=1
                )
            )
        n = lax.dot_general(
            jnp.concatenate(rows, axis=0), c("sel")[...], (((1,), (1,)), ((), ())),
            preferred_element_type=jnp.float32,
        )
        return [
            n[v * 16:v * 16 + 16] + n[(count + v) * 16:(count + v) * 16 + 16]
            for v in range(count)
        ]

    s_pad[...] = jnp.zeros((128, 128), jnp.float32)
    s_pad[0:10, 0:10] = c("smoother")[...]
    tile = c("tile")[...]
    spread = exact_dot(tile, s_pad[...])
    base = lax.dot_general(
        spread, tile, (((1,), (1,)), ((), ())),
        preferred_element_type=jnp.float32, precision=lax.Precision.HIGHEST,
    ) * c("same")[...] + c("fixed")[...]

    def expanded(left, right):
        high, low = split(right)
        return fdot(left, jnp.concatenate([high, low], axis=0))

    enc = expanded(c("re")[0], exact_dot(base, c("ae")[0])) * expanded(
        c("re")[1], exact_dot(base, c("ae")[1])
    )
    high, low = split(enc)
    e_hi[...] = high
    e_lo[...] = low

    r0, = from_rows([c("load")[...]])

    low_x = (gx == 0).astype(jnp.float32)
    high_x = (gx == nx - 1).astype(jnp.float32)
    low_y = (gy == 0).astype(jnp.float32)
    high_y = (gy == ny - 1).astype(jnp.float32)
    edges = c("edges")[...]
    arrives = (1.0 - edges[0:1] * high_x - edges[1:2] * low_x) * (
        1.0 - edges[2:3] * high_y - edges[3:4] * low_y
    )

    lane16 = iota((16, 128), 1)
    left16 = lane16 < 64
    quarter = (lane16 & 63) >> 4

    pl.semaphore_wait(barrier, len(greeted))

    def exchange_start(stage, value):
        m = right_dot(value, e_hi[...], e_lo[...])
        for pair in range(2):
            t = m[:, pair * 128:pair * 128 + 128]
            top, bottom = t[0:16], t[16:32]
            halo_out[stage, 2 * pair] = jnp.where(left16, top, half_roll(bottom))
            halo_out[stage, 2 * pair + 1] = jnp.where(left16, half_roll(top), bottom)
        t = m[:, 256:384]
        halo_out[stage, 4] = jnp.where(left16, t[0:16], half_roll(t[16:32]))
        copies = []
        for slot, (peer, part) in enumerate(neighbours):
            copy = pltpu.make_async_remote_copy(
                src_ref=halo_out.at[stage, part],
                dst_ref=halo_in.at[stage, slot],
                send_sem=halo_send.at[stage, slot],
                recv_sem=halo_recv.at[stage, slot],
                device_id=peer,
                device_id_type=MESH,
            )
            copy.start()
            copies.append(copy)
        return copies

    def exchange_end(stage, copies):
        for copy in copies:
            copy.wait_recv()
        tiles = []
        for pair in range(2):
            a, b = halo_in[stage, 2 * pair], halo_in[stage, 2 * pair + 1]
            tiles.append(
                jnp.concatenate(
                    [jnp.where(left16, a, half_roll(b)), jnp.where(left16, half_roll(a), b)],
                    axis=0,
                )
            )
        corner = jnp.where(
            quarter == 0, halo_in[stage, 4],
            jnp.where(
                quarter == 1, halo_in[stage, 5],
                jnp.where(quarter == 2, halo_in[stage, 6], halo_in[stage, 7]),
            ),
        )
        tiles.append(jnp.concatenate([corner, half_roll(corner)], axis=0))
        return jnp.concatenate(tiles, axis=1) * arrives

    def sum_round_start(which, at, value):
        sums[which, at, 0] = value
        copies = []
        for d, peer in enumerate(rounds[at]):
            copy = pltpu.make_async_remote_copy(
                src_ref=sums.at[which, at, 0],
                dst_ref=sums.at[which, at, d + 1],
                send_sem=sum_send.at[which, at, d],
                recv_sem=sum_recv.at[which, at, d],
                device_id=peer,
                device_id_type=MESH,
            )
            copy.start()
            copies.append(copy)
        return copies

    def sum_round_end(which, at, copies):
        for copy in copies:
            copy.wait_recv()
        total = sums[which, at, 0]
        for d in range(len(copies)):
            total = total + sums[which, at, d + 1]
        return total

    row8 = iota((8, 128), 0)

    def partial_tile(pairs):
        tile = jnp.zeros((8, 128), jnp.float32)
        for q, (first, second) in enumerate(pairs):
            t = local_sum(first, second)
            for shift in (4, 2, 1):
                t = t + pltpu.roll(t, shift, 0)
            tile = jnp.where(row8 == q, t, tile)
        return tile

    def scalars(total, number):
        column = jnp.sum(total, axis=1, keepdims=True)
        return [column[q:q + 1] for q in range(number)]

    sent = []
    halo = exchange_start(0, r0)
    sent += halo

    row64 = iota((64, 64), 0)
    for axis, low_edge, high_edge in ((0, low_x, high_x), (1, low_y, high_y)):
        masked = base * (
            1.0
            - low_edge * (row64 < 10).astype(jnp.float32)
            - high_edge * ((row64 >= 30) & (row64 < 40)).astype(jnp.float32)
        )
        wide = expanded(c("uc")[axis], exact_dot(masked, c("rv")[axis]))
        kxy = wide if axis == 0 else kxy * wide
    high, low = split(kxy)
    k_hi[...] = high
    k_lo[...] = low
    tz = exact_dot(c("rzt")[...], exact_dot(base, c("rz")[...]))
    tz_hi, tz_lo = split(tz)
    tz = jnp.where(iota((32, 96), 1) < 64, tz_hi.astype(jnp.float32), tz_lo.astype(jnp.float32))
    tz = tz.astype(jnp.bfloat16)

    metric = c("metric")
    m0, m1, m2, mass = from_rows(
        [metric[:, 0, :], metric[:, 1, :], metric[:, 2, :], c("mass")[...]]
    )
    m01 = jnp.concatenate([m0, m1], axis=1)

    def own_part(value):
        return right_dot(value, k_hi[0:256], k_lo[0:256])

    def precondition(own, arrived):
        return left_dot(tz, own + right_dot(arrived, k_hi[256:640], k_lo[256:640]))

    def operate(u):
        slope = m01 * right_dot(u, c("dxy_hi")[...], c("dxy_lo")[...])
        slope_z = m2 * left_dot(c("dz")[...], u)
        return (
            right_dot(slope, c("dxyt_hi")[...], c("dxyt_lo")[...])
            + left_dot(c("dzt")[...], slope_z)
            + mass * u
        )

    def assembled(value, arrived):
        both = jnp.concatenate([value, arrived], axis=1)
        high, low = split(both)
        t = fdot(jnp.concatenate([high, low], axis=0), c("asm")[...])
        t = t[:32] + t[32:]
        high, low = split(t)
        return fdot(c("az")[...], jnp.concatenate([high, low], axis=0))

    own = own_part(r0)
    arrived_r0 = exchange_end(0, halo)
    z0 = precondition(own, arrived_r0)
    w0 = operate(z0)

    halo = exchange_start(1, w0)
    sent += halo
    ring = sum_round_start(0, 0, partial_tile([(r0, z0), (w0, z0)]))
    sent += ring
    own = own_part(w0)
    arrived_w0 = exchange_end(1, halo)
    z1 = precondition(own, arrived_w0)
    w1 = operate(z1)
    halo = exchange_start(2, w1)
    sent += halo
    total = sum_round_end(0, 0, ring)
    ring = sum_round_start(0, 1, total)
    sent += ring
    own = own_part(w1)
    rows_z0, rows_z1, rows_r0, rows_w0 = to_rows(
        [z0, z1, assembled(r0, arrived_r0), assembled(w0, arrived_w0)]
    )
    total = sum_round_end(0, 1, ring)
    ring = sum_round_start(0, 2, total)
    sent += ring
    arrived_w1 = exchange_end(2, halo)
    z2 = precondition(own, arrived_w1)
    w2 = operate(z2)
    halo = exchange_start(3, w2)
    sent += halo
    total = sum_round_end(0, 2, ring)
    gamma0, delta0 = scalars(total, 2)
    alpha0 = gamma0 / delta0

    r1 = r0 - alpha0 * w0
    u1 = z0 - alpha0 * z1
    v1 = w0 - alpha0 * w1
    q = z1 - alpha0 * z2
    y = w1 - alpha0 * w2
    ring = sum_round_start(
        1, 0,
        partial_tile(
            [(r1, u1), (v1, u1), (v1, q), (v1, z1), (w0, z1), (y, q), (y, z1), (w1, z1)]
        ),
    )
    sent += ring
    rows_z2, rows_w1 = to_rows([z2, assembled(w1, arrived_w1)])
    rows_r1 = rows_r0 - alpha0 * rows_w0
    rows_u1 = rows_z0 - alpha0 * rows_z1
    rows_v1 = rows_w0 - alpha0 * rows_w1
    rows_q = rows_z1 - alpha0 * rows_z2
    rows_x1 = alpha0 * rows_z0
    total = sum_round_end(1, 0, ring)
    ring = sum_round_start(1, 1, total)
    sent += ring
    arrived_w2 = exchange_end(3, halo)
    rows_w2, = to_rows([assembled(w2, arrived_w2)])
    rows_y = rows_w1 - alpha0 * rows_w2
    total = sum_round_end(1, 1, ring)
    ring = sum_round_start(1, 2, total)
    sent += ring
    total = sum_round_end(1, 2, ring)
    gamma1, delta1, vq, vz, wz0, yq, yz, wz1 = scalars(total, 8)

    beta1 = gamma1 / gamma0
    alpha1 = gamma1 / (delta1 - beta1 * gamma1 / alpha0)
    uz = -gamma1 / alpha0
    gamma2 = (
        gamma1 - 2.0 * alpha1 * (delta1 + beta1 * uz)
        + alpha1 * alpha1 * (vq + beta1 * (2.0 * vz + beta1 * wz0))
    )
    delta2 = (
        delta1 - 2.0 * alpha1 * (vq + beta1 * vz)
        + alpha1 * alpha1 * (yq + beta1 * (2.0 * yz + beta1 * wz1))
    )
    beta2 = gamma2 / gamma1
    alpha2 = gamma2 / (delta2 - beta2 * gamma2 / alpha1)
    rows_p1 = rows_u1 + beta1 * rows_z0
    rows_u2 = rows_u1 - alpha1 * (rows_q + beta1 * rows_z1)
    rows_s1 = rows_v1 + beta1 * rows_w0
    rows_v2 = rows_v1 - alpha1 * (rows_y + beta1 * rows_w1)
    pressure_ref[...] = rows_x1 + alpha1 * rows_p1 + alpha2 * (rows_u2 + beta2 * rows_p1)
    residual_ref[...] = rows_r1 - alpha1 * rows_s1 - alpha2 * (rows_v2 + beta2 * rows_s1)
    for copy in sent:
        copy.wait_send()


def solution(mesh):
    nx, ny = mesh.shape["gx"], mesh.shape["gy"]
    lo = 8 if nx % 8 == 0 else 2
    consts = tables()
    vmem = pl.BlockSpec(memory_space=pltpu.VMEM)
    rows = jax.ShapeDtypeStruct((16, 512), jnp.float32)
    longest = max(ny, lo)
    shapes = dict(
        consts,
        load=rows,
        metric=jax.ShapeDtypeStruct((16, 3, 512), jnp.float32),
        mass=rows,
        smoother=jax.ShapeDtypeStruct((10, 10), jnp.float32),
    )
    call = pl.pallas_call(
        functools.partial(kernel, nx, ny, lo),
        out_shape=(rows, rows),
        in_specs=[pl.BlockSpec(memory_space=pltpu.SMEM)]
        + [pl.BlockSpec(memory_space=pltpu.HBM)] * len(FETCHED),
        out_specs=(vmem, vmem),
        scratch_shapes=[pltpu.VMEM(shapes[name].shape, shapes[name].dtype) for name in FETCHED]
        + [
            pltpu.SemaphoreType.DMA((len(FETCHED),)),
            pltpu.VMEM((640, 256), jnp.bfloat16),
            pltpu.VMEM((640, 256), jnp.bfloat16),
            pltpu.VMEM((256, 384), jnp.bfloat16),
            pltpu.VMEM((256, 384), jnp.bfloat16),
            pltpu.VMEM((128, 128), jnp.float32),
            pltpu.VMEM((4, 5, 16, 128), jnp.float32),
            pltpu.VMEM((4, 8, 16, 128), jnp.float32),
            pltpu.SemaphoreType.DMA((4, 8)),
            pltpu.SemaphoreType.DMA((4, 8)),
            pltpu.VMEM((2, 3, longest, 8, 128), jnp.float32),
            pltpu.SemaphoreType.DMA((2, 3, longest)),
            pltpu.SemaphoreType.DMA((2, 3, longest)),
        ],
        compiler_params=pltpu.CompilerParams(
            collective_id=0, has_side_effects=True, vmem_limit_bytes=32 * 1024 * 1024
        ),
    )

    def on_device(load_nodes, metric, mass_nodes, smoother, element_order):
        given = dict(
            consts, load=load_nodes, metric=metric, mass=mass_nodes, smoother=smoother
        )
        return call(element_order, *[jnp.asarray(given[name]) for name in FETCHED])

    return jax.shard_map(
        on_device,
        mesh=mesh,
        in_specs=(
            P(("gx", "gy"), None),
            P(("gx", "gy"), None, None),
            P(("gx", "gy"), None),
            P(),
            P(("gx", "gy")),
        ),
        out_specs=(P(("gx", "gy"), None), P(("gx", "gy"), None)),
        check_vma=False,
    )
```

```python
import functools

import jax
import jax.numpy as jnp
import ml_dtypes
import numpy as np
from jax import lax
from jax.experimental import pallas as pl
from jax.experimental.pallas import tpu as pltpu
from jax.sharding import PartitionSpec as P

NODES = 8
BF16 = ml_dtypes.bfloat16
MESH = pl.DeviceIdType.MESH


def derivative_table(node_count):
    degree = node_count - 1
    points = np.cos(np.pi * np.arange(node_count) / degree)
    weights = np.ones(node_count)
    weights[0] = 2.0
    weights[-1] = 2.0
    matrix = np.zeros((node_count, node_count))
    for row in range(node_count):
        for col in range(node_count):
            if row != col:
                matrix[row, col] = (
                    weights[row]
                    / weights[col]
                    * (-1.0) ** (row + col)
                    / (points[row] - points[col])
                )
        matrix[row, row] = -np.sum(matrix[row])
    return matrix


def split_const(matrix):
    full = np.asarray(matrix, np.float32)
    high = full.astype(BF16)
    return high, (full - high.astype(np.float32)).astype(BF16)


@functools.lru_cache(None)
def tables():
    node = np.array([7 * i + a for i in range(2) for a in range(8)])
    incidence = {}
    for box in (-1, 0, 1, 2):
        block = np.zeros((10, 16))
        for at in range(16):
            idx = node[at] - 7 * box + 1
            if 0 <= idx < 10:
                block[idx, at] = 1.0
        incidence[box] = block
    uc = np.zeros((24, 4, 16))
    uci = np.zeros((24, 16))
    rv = np.zeros((4, 16, 16))
    rvi = np.zeros((16, 16))
    re = np.zeros((16, 2, 16))
    rei = np.zeros((16, 32))
    ae = np.zeros((2, 16, 24))
    aei = np.zeros((32, 24))
    for at in range(16):
        for slot, box in enumerate((-1, 0, 1, 2)):
            uc[at, slot, :10] = incidence[box][:, at]
            rv[slot, :10, at] = incidence[box][:, at]
        re[at, 0, :10] = incidence[0][:, at]
        re[at, 1, :10] = incidence[1][:, at]
        rei[at, at] = 1.0
        aei[at, at] = 1.0
        for dim, where in enumerate((0, 1, 13, 14)):
            rvi[dim, at] = float(node[at] == where)
            rei[at, 16 + dim] = float(node[at] == where)
    uc[16, 2, 8] = uc[17, 2, 9] = uci[18, 2] = uci[19, 3] = 1.0
    uc[20, 1, 0] = uc[21, 1, 1] = uci[22, 0] = uci[23, 1] = 1.0
    aei[16, 16] = aei[17, 17] = ae[0, 0, 18] = ae[0, 1, 19] = 1.0
    aei[18, 20] = aei[19, 21] = ae[1, 8, 22] = ae[1, 9, 23] = 1.0
    assemble = np.zeros((24, 16))
    assemble[:16] = node[:, None] == node[None, :]
    assemble[16] = node == 14
    assemble[21] = node == 0

    lane = np.arange(256)
    xi = (lane // 128) * 8 + (lane // 8) % 8
    eta = ((lane // 64) % 2) * 8 + lane % 8
    mx, my = [], []
    for side in (16, 20):
        for q in range(4):
            for e in range(16):
                mx.append(side + q)
                my.append(e)
    for side in (16, 20):
        for e in range(16):
            for q in range(4):
                mx.append(e)
                my.append(side + q)
    for sx in (16, 20):
        for sy in (16, 20):
            for qx in range(4):
                for qy in range(4):
                    mx.append(sx + qx)
                    my.append(sy + qy)
    mx, my = np.array(mx), np.array(my)

    def padded(rows, index):
        return np.concatenate([rows[index], np.zeros((64,) + rows.shape[1:])], axis=0)

    allx = np.concatenate([xi, mx])
    ally = np.concatenate([eta, my])
    def kernel_side(index):
        rows = uc.reshape(24, 64)
        return padded(np.concatenate([rows, rows, uci], axis=1), index)

    def sending_side(index):
        rows = re.reshape(16, 32)[index]
        return np.concatenate([rows, rows, rei[index]], axis=1)

    spread_e = [padded(ae[box].T, m).T for m in (mx, my) for box in range(2)]
    spread_k = [rv[box][:, at] for at in (xi, eta) for box in range(4)]
    asm = padded(assemble, allx)[:, xi] * padded(assemble, ally)[:, eta]

    edges = np.zeros((8, 384))
    edges[0, :320] = (mx >= 16) & (mx < 20)
    edges[1, :320] = mx >= 20
    edges[2, :320] = (my >= 16) & (my < 20)
    edges[3, :320] = my >= 20

    znode = np.array([7 * k + c for k in range(4) for c in range(8)])
    rz = np.zeros((4, 16, 32))
    for block in range(4):
        for at in range(32):
            idx = znode[at] - 7 * block + 1
            if 0 <= idx < 10:
                rz[block, idx, at] = 1.0
    spread_z = [np.concatenate([block] * 4, axis=1) for block in rz]
    rzt = rz.reshape(64, 32).T
    az = (znode[:, None] == znode[None, :]).astype(float)

    d = derivative_table(NODES).astype(np.float32)
    eye8 = np.eye(8)
    dx = np.kron(np.eye(4), np.kron(d.T, eye8))
    dy = np.kron(np.eye(4), np.kron(eye8, d.T))
    dxy_hi, dxy_lo = split_const(np.concatenate([dx, dy], axis=1))
    dz = np.kron(np.eye(4), d)
    dz_hi, dz_lo = split_const(dz)
    dzt_hi, dzt_lo = split_const(dz.T)

    b = lambda m: np.asarray(m, BF16)
    return dict(
        dxy_hi=dxy_hi,
        dxy_lo=dxy_lo,
        dxyt_hi=np.ascontiguousarray(dxy_hi.T),
        dxyt_lo=np.ascontiguousarray(dxy_lo.T),
        dz=np.concatenate([dz_hi, dz_hi, dz_lo], axis=1),
        dzt=np.concatenate([dzt_hi, dzt_hi, dzt_lo], axis=1),
        az=b(np.concatenate([az, az], axis=1)),
        uc=b(np.stack([kernel_side(allx), kernel_side(ally)])),
        rvi=b(np.stack([rvi[:, xi], rvi[:, eta]])),
        re=b(np.stack([sending_side(xi), sending_side(eta)])),
        aei=b(np.stack([padded(aei.T, mx).T, padded(aei.T, my).T])),
        spread_e=b(np.concatenate(spread_e, axis=1)),
        spread_k=b(np.concatenate(spread_k + spread_z, axis=1)),
        rzt=b(np.concatenate([rzt, rzt], axis=1)),
        asm=b(asm),
        edges=np.asarray(edges, np.float32),
    )


FETCHED = (
    "smoother", "load", "spread_e", "aei", "re", "edges", "spread_k", "rvi", "uc", "rzt",
    "metric", "mass", "dxy_hi", "dxy_lo", "dz", "dxyt_hi", "dxyt_lo", "dzt", "asm", "az",
)


def fdot(left, right):
    return jnp.dot(left, right, preferred_element_type=jnp.float32)


def split(value):
    high = value.astype(jnp.bfloat16)
    low = (value - high.astype(jnp.float32)).astype(jnp.bfloat16)
    return high, low


def right_dot(value, w_hi, w_lo):
    rows = value.shape[0]
    high, low = split(value)
    both = fdot(jnp.concatenate([high, low], axis=0), w_hi)
    return both[:rows] + both[rows:] + fdot(high, w_lo)


def left_dot(stacked, value):
    high, low = split(value)
    return fdot(stacked, jnp.concatenate([high, low, high], axis=0))


def iota(shape, dim):
    return lax.broadcasted_iota(jnp.int32, shape, dim)


def half_roll(value):
    return pltpu.roll(value, 64, 1)


def local_sum(first, second):
    t = first * second
    t = t[0:8] + t[8:16] + t[16:24] + t[24:32]
    return t[:, :128] + t[:, 128:]


def kernel(
    nx, ny, lo,
    order_ref, *refs,
):
    count = len(FETCHED)
    far = dict(zip(FETCHED, refs[:count]))
    near = dict(zip(FETCHED, refs[count + 2:2 * count + 2]))
    pressure_ref, residual_ref = refs[count:count + 2]
    (
        fetch_sem, sel, k_hi, k_lo, e_hi, e_lo, s_pad,
        halo_out, halo_in, halo_send, halo_recv,
        sums, sum_send, sum_recv,
    ) = refs[2 * count + 2:]
    fetches = {}
    for at, name in enumerate(FETCHED):
        fetches[name] = pltpu.make_async_copy(far[name], near[name], fetch_sem.at[at])
        fetches[name].start()

    def c(name):
        if name in fetches:
            fetches.pop(name).wait()
        return near[name]

    gx = lax.axis_index("gx")
    gy = lax.axis_index("gy")
    hi = nx // lo
    x_low, x_high = lax.rem(gx + nx - 1, nx), lax.rem(gx + 1, nx)
    y_low, y_high = lax.rem(gy + ny - 1, ny), lax.rem(gy + 1, ny)
    neighbours = (
        ((x_low, gy), 0), ((x_high, gy), 1),
        ((gx, y_low), 2), ((gx, y_high), 3),
        ((x_low, y_low), 4), ((x_low, y_high), 4),
        ((x_high, y_low), 4), ((x_high, y_high), 4),
    )
    z_at, y_at = lax.rem(gx, lo), lax.div(gx, lo)
    rounds = [
        [(gx, lax.rem(gy + d, ny)) for d in range(1, ny)],
        [(y_at * lo + lax.rem(z_at + d, lo), gy) for d in range(1, lo)],
        [(lax.rem(y_at + d, hi) * lo + z_at, gy) for d in range(1, hi)],
    ]
    greeted = [n for n, _ in neighbours] + [peer for group in rounds for peer in group]

    barrier = pltpu.get_barrier_semaphore()
    for peer in greeted:
        pl.semaphore_signal(barrier, inc=1, device_id=peer, device_id_type=MESH)

    col = iota((64, 512), 1)
    for block in range(8):
        at = iota((64, 512), 0) + block * 64
        sel[block * 64:block * 64 + 64] = (
            ((at & 7) * 64 + (at >> 3)) == col
        ).astype(jnp.float32).astype(jnp.bfloat16)

    lane1 = iota((1, 128), 1)
    row16 = iota((16, 128), 0)
    along_lanes = jnp.zeros((1, 128), jnp.int32)
    along_rows = jnp.zeros((16, 128), jnp.int32)
    for at in range(16):
        along_lanes = jnp.where((lane1 & 15) == at, order_ref[at], along_lanes)
        along_rows = jnp.where(row16 == at, order_ref[at], along_rows)
    row = iota((128, 128), 0)
    place = (
        ((row >> 3) == along_lanes) & (((row & 7) >> 1) == ((lane1 & 63) >> 4))
    ).astype(jnp.float32).astype(jnp.bfloat16)
    lane16 = iota((16, 128), 1)
    unplace = jnp.concatenate(
        [((lane16 >> 3) == along_rows) & (((lane16 & 7) >> 1) == u) for u in range(4)], axis=0
    ).astype(jnp.float32).astype(jnp.bfloat16)

    row32 = iota((32, 128), 0)
    lane32 = iota((32, 128), 1)
    parity = row32 & 1
    left_half = lane32 < 64

    def from_rows(fields):
        count = len(fields)
        parts = [split(f) for f in fields]
        stacked = jnp.concatenate([p[0] for p in parts] + [p[1] for p in parts], axis=0)
        moved = fdot(stacked, sel[...]).astype(jnp.bfloat16)
        out = []
        for f in range(count):
            pieces = []
            for part in range(2):
                z = moved[(part * count + f) * 16:(part * count + f) * 16 + 16]
                pieces += [z[:, u * 128:u * 128 + 128] for u in range(4)]
            v = fdot(place, jnp.concatenate(pieces, axis=0))
            tiles = []
            for pair in range(2):
                picked = []
                for odd in range(2):
                    at = (pair * 2 + odd) * 32
                    block = v[at:at + 32]
                    picked.append(jnp.where(parity == odd, block, half_roll(block)))
                tiles.append(jnp.where(left_half, picked[0], picked[1]))
            out.append(jnp.concatenate(tiles, axis=1))
        return out

    def to_rows(values):
        count = len(values)
        highs, lows = [], []
        for value in values:
            blocks = []
            for ij in range(4):
                block = value[:, (ij // 2) * 128:(ij // 2) * 128 + 128]
                block = jnp.where(parity == (ij & 1), block, half_roll(block))
                blocks.append(jnp.where((lane32 >> 6) == parity, block, 0.0))
            high, low = split(jnp.concatenate(blocks, axis=0))
            highs.append(high)
            lows.append(low)
        o = fdot(unplace, jnp.concatenate(highs + lows, axis=1)).astype(jnp.bfloat16)
        rows = []
        for v in range(2 * count):
            rows.append(
                jnp.concatenate(
                    [o[u * 16:u * 16 + 16, v * 128:v * 128 + 128] for u in range(4)], axis=1
                )
            )
        n = lax.dot_general(
            jnp.concatenate(rows, axis=0), sel[...], (((1,), (1,)), ((), ())),
            preferred_element_type=jnp.float32,
        )
        return [
            n[v * 16:v * 16 + 16] + n[(count + v) * 16:(count + v) * 16 + 16]
            for v in range(count)
        ]

    for name in ("smoother", "load", "spread_e", "aei", "re", "edges"):
        c(name)
    s_pad[...] = jnp.zeros((16, 128), jnp.float32)
    s_pad[0:10, 0:10] = c("smoother")[...]
    both_parts = jnp.concatenate(split(s_pad[...]), axis=0)[:, 0:16]
    entries = fdot(both_parts, c("spread_e")[...]).astype(jnp.bfloat16)

    def stacked_entries(entries, at, width, number):
        blocks = [entries[:, at + b * width:at + (b + 1) * width] for b in range(number)]
        return [block[0:16] for block in blocks] + [block[16:32] for block in blocks]

    for axis in range(2):
        wide = fdot(
            c("re")[axis],
            jnp.concatenate(
                stacked_entries(entries, axis * 768, 384, 2) + [c("aei")[axis]], axis=0
            ),
        )
        enc = wide if axis == 0 else enc * wide
    high, low = split(enc)
    e_hi[...] = high
    e_lo[...] = low

    r0, = from_rows([c("load")[...]])

    low_x = (gx == 0).astype(jnp.float32)
    high_x = (gx == nx - 1).astype(jnp.float32)
    low_y = (gy == 0).astype(jnp.float32)
    high_y = (gy == ny - 1).astype(jnp.float32)
    edges = c("edges")[...]
    arrives = (1.0 - edges[0:1] * high_x - edges[1:2] * low_x) * (
        1.0 - edges[2:3] * high_y - edges[3:4] * low_y
    )

    left16 = lane16 < 64
    quarter = (lane16 & 63) >> 4

    pl.semaphore_wait(barrier, len(greeted))

    def exchange_start(stage, value):
        m = right_dot(value, e_hi[...], e_lo[...])
        for pair in range(2):
            t = m[:, pair * 128:pair * 128 + 128]
            top, bottom = t[0:16], t[16:32]
            halo_out[stage, 2 * pair] = jnp.where(left16, top, half_roll(bottom))
            halo_out[stage, 2 * pair + 1] = jnp.where(left16, half_roll(top), bottom)
        t = m[:, 256:384]
        halo_out[stage, 4] = jnp.where(left16, t[0:16], half_roll(t[16:32]))
        copies = []
        for slot, (peer, part) in enumerate(neighbours):
            copy = pltpu.make_async_remote_copy(
                src_ref=halo_out.at[stage, part],
                dst_ref=halo_in.at[stage, slot],
                send_sem=halo_send.at[stage, slot],
                recv_sem=halo_recv.at[stage, slot],
                device_id=peer,
                device_id_type=MESH,
            )
            copy.start()
            copies.append(copy)
        return copies

    def exchange_end(stage, copies):
        for copy in copies:
            copy.wait_recv()
        tiles = []
        for pair in range(2):
            a, b = halo_in[stage, 2 * pair], halo_in[stage, 2 * pair + 1]
            tiles.append(
                jnp.concatenate(
                    [jnp.where(left16, a, half_roll(b)), jnp.where(left16, half_roll(a), b)],
                    axis=0,
                )
            )
        corner = jnp.where(
            quarter == 0, halo_in[stage, 4],
            jnp.where(
                quarter == 1, halo_in[stage, 5],
                jnp.where(quarter == 2, halo_in[stage, 6], halo_in[stage, 7]),
            ),
        )
        tiles.append(jnp.concatenate([corner, half_roll(corner)], axis=0))
        return jnp.concatenate(tiles, axis=1) * arrives

    def sum_round_start(which, at, value):
        sums[which, at, 0] = value
        copies = []
        for d, peer in enumerate(rounds[at]):
            copy = pltpu.make_async_remote_copy(
                src_ref=sums.at[which, at, 0],
                dst_ref=sums.at[which, at, d + 1],
                send_sem=sum_send.at[which, at, d],
                recv_sem=sum_recv.at[which, at, d],
                device_id=peer,
                device_id_type=MESH,
            )
            copy.start()
            copies.append(copy)
        return copies

    def sum_round_end(which, at, copies):
        for copy in copies:
            copy.wait_recv()
        total = sums[which, at, 0]
        for d in range(len(copies)):
            total = total + sums[which, at, d + 1]
        return total

    row8 = iota((8, 128), 0)

    def partial_tile(pairs):
        tile = jnp.zeros((8, 128), jnp.float32)
        for q, (first, second) in enumerate(pairs):
            t = local_sum(first, second)
            for shift in (4, 2, 1):
                t = t + pltpu.roll(t, shift, 0)
            tile = jnp.where(row8 == q, t, tile)
        return tile

    def scalars(total, number):
        column = jnp.sum(total, axis=1, keepdims=True)
        return [column[q:q + 1] for q in range(number)]

    sent = []
    halo = exchange_start(0, r0)
    sent += halo

    for name in ("spread_k", "rvi", "uc", "rzt", "metric", "mass"):
        c(name)
    entries = fdot(both_parts, c("spread_k")[...]).astype(jnp.bfloat16)
    for axis, low_edge, high_edge in ((0, low_x, high_x), (1, low_y, high_y)):
        blocks = stacked_entries(entries, axis * 1024, 256, 4)
        for at in (0, 4):
            blocks[at] = blocks[at] * (1.0 - low_edge).astype(jnp.bfloat16)
            blocks[at + 3] = blocks[at + 3] * (1.0 - high_edge).astype(jnp.bfloat16)
        wide = fdot(c("uc")[axis], jnp.concatenate(blocks + [c("rvi")[axis]], axis=0))
        kxy = wide if axis == 0 else kxy * wide
    high, low = split(kxy)
    k_hi[...] = high
    k_lo[...] = low
    tz = fdot(c("rzt")[...], jnp.concatenate(stacked_entries(entries, 2048, 128, 4), axis=0))
    tz_hi, tz_lo = split(tz[:, 0:96])
    tz = jnp.where(iota((32, 96), 1) < 64, tz_hi.astype(jnp.float32), tz_lo.astype(jnp.float32))
    tz = tz.astype(jnp.bfloat16)

    metric = c("metric")
    m0, m1, m2, mass = from_rows(
        [metric[0], metric[1], metric[2], c("mass")[...]]
    )
    m01 = jnp.concatenate([m0, m1], axis=1)

    def own_part(value):
        return right_dot(value, k_hi[0:256], k_lo[0:256])

    def precondition(own, arrived):
        return left_dot(tz, own + right_dot(arrived, k_hi[256:640], k_lo[256:640]))

    def operate(u):
        slope = m01 * right_dot(u, c("dxy_hi")[...], c("dxy_lo")[...])
        slope_z = m2 * left_dot(c("dz")[...], u)
        return (
            right_dot(slope, c("dxyt_hi")[...], c("dxyt_lo")[...])
            + left_dot(c("dzt")[...], slope_z)
            + mass * u
        )

    def assembled(value, arrived):
        both = jnp.concatenate([value, arrived], axis=1)
        high, low = split(both)
        t = fdot(jnp.concatenate([high, low], axis=0), c("asm")[...])
        t = t[:32] + t[32:]
        high, low = split(t)
        return fdot(c("az")[...], jnp.concatenate([high, low], axis=0))

    own = own_part(r0)
    arrived_r0 = exchange_end(0, halo)
    z0 = precondition(own, arrived_r0)
    w0 = operate(z0)

    halo = exchange_start(1, w0)
    sent += halo
    ring = sum_round_start(0, 0, partial_tile([(r0, z0), (w0, z0)]))
    sent += ring
    own = own_part(w0)
    arrived_w0 = exchange_end(1, halo)
    z1 = precondition(own, arrived_w0)
    w1 = operate(z1)
    halo = exchange_start(2, w1)
    sent += halo
    total = sum_round_end(0, 0, ring)
    ring = sum_round_start(0, 1, total)
    sent += ring
    own = own_part(w1)
    rows_z0, rows_z1, rows_r0, rows_w0 = to_rows(
        [z0, z1, assembled(r0, arrived_r0), assembled(w0, arrived_w0)]
    )
    total = sum_round_end(0, 1, ring)
    ring = sum_round_start(0, 2, total)
    sent += ring
    arrived_w1 = exchange_end(2, halo)
    z2 = precondition(own, arrived_w1)
    w2 = operate(z2)
    halo = exchange_start(3, w2)
    sent += halo
    total = sum_round_end(0, 2, ring)
    gamma0, delta0 = scalars(total, 2)
    alpha0 = gamma0 / delta0

    r1 = r0 - alpha0 * w0
    u1 = z0 - alpha0 * z1
    v1 = w0 - alpha0 * w1
    q = z1 - alpha0 * z2
    y = w1 - alpha0 * w2
    ring = sum_round_start(
        1, 0,
        partial_tile(
            [(r1, u1), (v1, u1), (v1, q), (v1, z1), (w0, z1), (y, q), (y, z1), (w1, z1)]
        ),
    )
    sent += ring
    rows_z2, rows_w1 = to_rows([z2, assembled(w1, arrived_w1)])
    rows_r1 = rows_r0 - alpha0 * rows_w0
    rows_u1 = rows_z0 - alpha0 * rows_z1
    rows_v1 = rows_w0 - alpha0 * rows_w1
    rows_q = rows_z1 - alpha0 * rows_z2
    rows_x1 = alpha0 * rows_z0
    total = sum_round_end(1, 0, ring)
    ring = sum_round_start(1, 1, total)
    sent += ring
    arrived_w2 = exchange_end(3, halo)
    rows_w2, = to_rows([assembled(w2, arrived_w2)])
    rows_y = rows_w1 - alpha0 * rows_w2
    total = sum_round_end(1, 1, ring)
    ring = sum_round_start(1, 2, total)
    sent += ring
    total = sum_round_end(1, 2, ring)
    gamma1, delta1, vq, vz, wz0, yq, yz, wz1 = scalars(total, 8)

    beta1 = gamma1 / gamma0
    alpha1 = gamma1 / (delta1 - beta1 * gamma1 / alpha0)
    uz = -gamma1 / alpha0
    gamma2 = (
        gamma1 - 2.0 * alpha1 * (delta1 + beta1 * uz)
        + alpha1 * alpha1 * (vq + beta1 * (2.0 * vz + beta1 * wz0))
    )
    delta2 = (
        delta1 - 2.0 * alpha1 * (vq + beta1 * vz)
        + alpha1 * alpha1 * (yq + beta1 * (2.0 * yz + beta1 * wz1))
    )
    beta2 = gamma2 / gamma1
    alpha2 = gamma2 / (delta2 - beta2 * gamma2 / alpha1)
    rows_p1 = rows_u1 + beta1 * rows_z0
    rows_u2 = rows_u1 - alpha1 * (rows_q + beta1 * rows_z1)
    rows_s1 = rows_v1 + beta1 * rows_w0
    rows_v2 = rows_v1 - alpha1 * (rows_y + beta1 * rows_w1)
    pressure_ref[...] = rows_x1 + alpha1 * rows_p1 + alpha2 * (rows_u2 + beta2 * rows_p1)
    residual_ref[...] = rows_r1 - alpha1 * rows_s1 - alpha2 * (rows_v2 + beta2 * rows_s1)
    for copy in sent:
        copy.wait_send()


def solution(mesh):
    nx, ny = mesh.shape["gx"], mesh.shape["gy"]
    lo = 8 if nx % 8 == 0 else 2
    consts = tables()
    vmem = pl.BlockSpec(memory_space=pltpu.VMEM)
    rows = jax.ShapeDtypeStruct((16, 512), jnp.float32)
    longest = max(ny, lo)
    shapes = dict(
        consts,
        load=rows,
        metric=jax.ShapeDtypeStruct((3, 16, 512), jnp.float32),
        mass=rows,
        smoother=jax.ShapeDtypeStruct((10, 10), jnp.float32),
    )
    call = pl.pallas_call(
        functools.partial(kernel, nx, ny, lo),
        out_shape=(rows, rows),
        in_specs=[pl.BlockSpec(memory_space=pltpu.SMEM)]
        + [pl.BlockSpec(memory_space=pltpu.HBM)] * len(FETCHED),
        out_specs=(vmem, vmem),
        scratch_shapes=[pltpu.VMEM(shapes[name].shape, shapes[name].dtype) for name in FETCHED]
        + [
            pltpu.SemaphoreType.DMA((len(FETCHED),)),
            pltpu.VMEM((512, 512), jnp.bfloat16),
            pltpu.VMEM((640, 256), jnp.bfloat16),
            pltpu.VMEM((640, 256), jnp.bfloat16),
            pltpu.VMEM((256, 384), jnp.bfloat16),
            pltpu.VMEM((256, 384), jnp.bfloat16),
            pltpu.VMEM((16, 128), jnp.float32),
            pltpu.VMEM((4, 5, 16, 128), jnp.float32),
            pltpu.VMEM((4, 8, 16, 128), jnp.float32),
            pltpu.SemaphoreType.DMA((4, 8)),
            pltpu.SemaphoreType.DMA((4, 8)),
            pltpu.VMEM((2, 3, longest, 8, 128), jnp.float32),
            pltpu.SemaphoreType.DMA((2, 3, longest)),
            pltpu.SemaphoreType.DMA((2, 3, longest)),
        ],
        compiler_params=pltpu.CompilerParams(
            collective_id=0, has_side_effects=True, vmem_limit_bytes=60 * 1024 * 1024
        ),
    )

    def on_device(load_nodes, metric, mass_nodes, smoother, element_order):
        given = dict(
            consts, load=load_nodes, metric=metric.transpose(1, 0, 2), mass=mass_nodes, smoother=smoother
        )
        return call(element_order, *[jnp.asarray(given[name]) for name in FETCHED])

    return jax.shard_map(
        on_device,
        mesh=mesh,
        in_specs=(
            P(("gx", "gy"), None),
            P(("gx", "gy"), None, None),
            P(("gx", "gy"), None),
            P(),
            P(("gx", "gy")),
        ),
        out_specs=(P(("gx", "gy"), None), P(("gx", "gy"), None)),
        check_vma=False,
    )
```

```python
import functools

import jax
import jax.numpy as jnp
import ml_dtypes
import numpy as np
from jax import lax
from jax.experimental import pallas as pl
from jax.experimental.pallas import tpu as pltpu
from jax.sharding import PartitionSpec as P

NODES = 8
BF16 = ml_dtypes.bfloat16
MESH = pl.DeviceIdType.MESH


def derivative_table(node_count):
    degree = node_count - 1
    points = np.cos(np.pi * np.arange(node_count) / degree)
    weights = np.ones(node_count)
    weights[0] = 2.0
    weights[-1] = 2.0
    matrix = np.zeros((node_count, node_count))
    for row in range(node_count):
        for col in range(node_count):
            if row != col:
                matrix[row, col] = (
                    weights[row]
                    / weights[col]
                    * (-1.0) ** (row + col)
                    / (points[row] - points[col])
                )
        matrix[row, row] = -np.sum(matrix[row])
    return matrix


def split_const(matrix):
    full = np.asarray(matrix, np.float32)
    high = full.astype(BF16)
    return high, (full - high.astype(np.float32)).astype(BF16)


@functools.lru_cache(None)
def tables():
    node = np.array([7 * i + a for i in range(2) for a in range(8)])
    incidence = {}
    for box in (-1, 0, 1, 2):
        block = np.zeros((10, 16))
        for at in range(16):
            idx = node[at] - 7 * box + 1
            if 0 <= idx < 10:
                block[idx, at] = 1.0
        incidence[box] = block
    uc = np.zeros((24, 4, 16))
    uci = np.zeros((24, 16))
    rv = np.zeros((4, 16, 16))
    rvi = np.zeros((16, 16))
    re = np.zeros((16, 2, 16))
    rei = np.zeros((16, 32))
    ae = np.zeros((2, 16, 24))
    aei = np.zeros((32, 24))
    for at in range(16):
        for slot, box in enumerate((-1, 0, 1, 2)):
            uc[at, slot, :10] = incidence[box][:, at]
            rv[slot, :10, at] = incidence[box][:, at]
        re[at, 0, :10] = incidence[0][:, at]
        re[at, 1, :10] = incidence[1][:, at]
        rei[at, at] = 1.0
        aei[at, at] = 1.0
        for dim, where in enumerate((0, 1, 13, 14)):
            rvi[dim, at] = float(node[at] == where)
            rei[at, 16 + dim] = float(node[at] == where)
    uc[16, 2, 8] = uc[17, 2, 9] = uci[18, 2] = uci[19, 3] = 1.0
    uc[20, 1, 0] = uc[21, 1, 1] = uci[22, 0] = uci[23, 1] = 1.0
    aei[16, 16] = aei[17, 17] = ae[0, 0, 18] = ae[0, 1, 19] = 1.0
    aei[18, 20] = aei[19, 21] = ae[1, 8, 22] = ae[1, 9, 23] = 1.0
    assemble = np.zeros((24, 16))
    assemble[:16] = node[:, None] == node[None, :]
    assemble[16] = node == 14
    assemble[21] = node == 0

    lane = np.arange(256)
    xi = (lane // 128) * 8 + (lane // 8) % 8
    eta = ((lane // 64) % 2) * 8 + lane % 8
    mx, my = [], []
    for side in (16, 20):
        for q in range(4):
            for e in range(16):
                mx.append(side + q)
                my.append(e)
    for side in (16, 20):
        for e in range(16):
            for q in range(4):
                mx.append(e)
                my.append(side + q)
    for sx in (16, 20):
        for sy in (16, 20):
            for qx in range(4):
                for qy in range(4):
                    mx.append(sx + qx)
                    my.append(sy + qy)
    mx, my = np.array(mx), np.array(my)

    def padded(rows, index):
        return np.concatenate([rows[index], np.zeros((64,) + rows.shape[1:])], axis=0)

    allx = np.concatenate([xi, mx])
    ally = np.concatenate([eta, my])
    def kernel_side(index):
        rows = uc.reshape(24, 64)
        return padded(np.concatenate([rows, rows, uci], axis=1), index)

    def sending_side(index):
        rows = re.reshape(16, 32)[index]
        return np.concatenate([rows, rows, rei[index]], axis=1)

    spread_e = [padded(ae[box].T, m).T for m in (mx, my) for box in range(2)]
    spread_k = [rv[box][:, at] for at in (xi, eta) for box in range(4)]
    asm = padded(assemble, allx)[:, xi] * padded(assemble, ally)[:, eta]

    edges = np.zeros((8, 384))
    edges[0, :320] = (mx >= 16) & (mx < 20)
    edges[1, :320] = mx >= 20
    edges[2, :320] = (my >= 16) & (my < 20)
    edges[3, :320] = my >= 20

    znode = np.array([7 * k + c for k in range(4) for c in range(8)])
    rz = np.zeros((4, 16, 32))
    for block in range(4):
        for at in range(32):
            idx = znode[at] - 7 * block + 1
            if 0 <= idx < 10:
                rz[block, idx, at] = 1.0
    spread_z = [np.concatenate([block] * 4, axis=1) for block in rz]
    rzt = rz.reshape(64, 32).T
    az = (znode[:, None] == znode[None, :]).astype(float)

    d = derivative_table(NODES).astype(np.float32)
    eye8 = np.eye(8)
    dx = np.kron(np.eye(2), np.kron(d.T, eye8))
    dy = np.kron(np.eye(2), np.kron(eye8, d.T))
    dxy_hi, dxy_lo = split_const(np.concatenate([dx, dy], axis=1))
    dz = np.kron(np.eye(4), d)
    dz_hi, dz_lo = split_const(dz)
    dzt_hi, dzt_lo = split_const(dz.T)

    b = lambda m: np.asarray(m, BF16)
    return dict(
        dxy_hi=dxy_hi,
        dxy_lo=dxy_lo,
        dxyt_hi=np.ascontiguousarray(dxy_hi.T),
        dxyt_lo=np.ascontiguousarray(dxy_lo.T),
        dz=np.concatenate([dz_hi, dz_hi, dz_lo], axis=1),
        dzt=np.concatenate([dzt_hi, dzt_hi, dzt_lo], axis=1),
        az=b(np.concatenate([az, az], axis=1)),
        uc=b(np.stack([kernel_side(allx), kernel_side(ally)])),
        rvi=b(np.stack([rvi[:, xi], rvi[:, eta]])),
        re=b(np.stack([sending_side(xi), sending_side(eta)])),
        aei=b(np.stack([padded(aei.T, mx).T, padded(aei.T, my).T])),
        spread_e=b(np.concatenate(spread_e, axis=1)),
        spread_k=b(np.concatenate(spread_k + spread_z, axis=1)),
        rzt=b(np.concatenate([rzt, rzt], axis=1)),
        asm=b(asm),
        edges=np.asarray(edges, np.float32),
    )


FETCHED = (
    "smoother", "load", "spread_e", "aei", "re", "edges", "spread_k", "rvi", "uc", "rzt",
    "metric", "mass", "dxy_hi", "dxy_lo", "dz", "dxyt_hi", "dxyt_lo", "dzt", "asm", "az",
)


def fdot(left, right):
    return jnp.dot(left, right, preferred_element_type=jnp.float32)


def split(value):
    high = value.astype(jnp.bfloat16)
    low = (value - high.astype(jnp.float32)).astype(jnp.bfloat16)
    return high, low


def right_dot(value, w_hi, w_lo):
    rows = value.shape[0]
    high, low = split(value)
    both = fdot(jnp.concatenate([high, low], axis=0), w_hi)
    return both[:rows] + both[rows:] + fdot(high, w_lo)


def left_dot(stacked, value):
    high, low = split(value)
    return fdot(stacked, jnp.concatenate([high, low, high], axis=0))


def offsets(first, second):
    def far(pair):
        return -min(pair[0], first - pair[0]) - min(pair[1], second - pair[1])

    pairs = [(a, b) for a in range(first) for b in range(second)]
    return sorted(pairs[1:], key=far)


def iota(shape, dim):
    return lax.broadcasted_iota(jnp.int32, shape, dim)


def half_roll(value):
    return pltpu.roll(value, 64, 1)


def local_sum(first, second):
    t = first * second
    t = t[0:8] + t[8:16] + t[16:24] + t[24:32]
    return t[:, :128] + t[:, 128:]


def kernel(
    nx, ny, lo,
    order_ref, *refs,
):
    count = len(FETCHED)
    far = dict(zip(FETCHED, refs[:count]))
    near = dict(zip(FETCHED, refs[count + 2:2 * count + 2]))
    pressure_ref, residual_ref = refs[count:count + 2]
    (
        fetch_sem, sel, k_hi, k_lo, e_hi, e_lo, s_pad,
        halo_out, halo_in, halo_send, halo_recv,
        sums, sum_send, sum_recv,
    ) = refs[2 * count + 2:]
    fetches = {}
    for at, name in enumerate(FETCHED):
        fetches[name] = pltpu.make_async_copy(far[name], near[name], fetch_sem.at[at])
        fetches[name].start()

    def c(name):
        if name in fetches:
            fetches.pop(name).wait()
        return near[name]

    gx = lax.axis_index("gx")
    gy = lax.axis_index("gy")
    hi = nx // lo
    x_low, x_high = lax.rem(gx + nx - 1, nx), lax.rem(gx + 1, nx)
    y_low, y_high = lax.rem(gy + ny - 1, ny), lax.rem(gy + 1, ny)
    neighbours = (
        ((x_low, gy), 0), ((x_high, gy), 1),
        ((gx, y_low), 2), ((gx, y_high), 3),
        ((x_low, y_low), 4), ((x_low, y_high), 4),
        ((x_high, y_low), 4), ((x_high, y_high), 4),
    )
    z_at, y_at = lax.rem(gx, lo), lax.div(gx, lo)
    x_at, core = lax.div(gy, 2), lax.rem(gy, 2)
    rounds = [
        [
            (lax.rem(y_at + a, hi) * lo + z_at, lax.rem(x_at + b, ny // 2) * 2 + core)
            for a, b in offsets(hi, ny // 2)
        ],
        [
            (y_at * lo + lax.rem(z_at + a, lo), x_at * 2 + lax.rem(core + b, 2))
            for a, b in offsets(lo, 2)
        ],
    ]
    greeted = [n for n, _ in neighbours] + [peer for group in rounds for peer in group]

    barrier = pltpu.get_barrier_semaphore()
    for peer in greeted:
        pl.semaphore_signal(barrier, inc=1, device_id=peer, device_id_type=MESH)

    col = iota((64, 512), 1)
    for block in range(8):
        at = iota((64, 512), 0) + block * 64
        sel[block * 64:block * 64 + 64] = (
            ((at & 7) * 64 + (at >> 3)) == col
        ).astype(jnp.float32).astype(jnp.bfloat16)

    lane1 = iota((1, 128), 1)
    row16 = iota((16, 128), 0)
    along_lanes = jnp.zeros((1, 128), jnp.int32)
    along_rows = jnp.zeros((16, 128), jnp.int32)
    for at in range(16):
        along_lanes = jnp.where((lane1 & 15) == at, order_ref[at], along_lanes)
        along_rows = jnp.where(row16 == at, order_ref[at], along_rows)
    row = iota((128, 128), 0)
    place = (
        ((row >> 3) == along_lanes) & (((row & 7) >> 1) == ((lane1 & 63) >> 4))
    ).astype(jnp.float32).astype(jnp.bfloat16)
    lane16 = iota((16, 128), 1)
    unplace = jnp.concatenate(
        [((lane16 >> 3) == along_rows) & (((lane16 & 7) >> 1) == u) for u in range(4)], axis=0
    ).astype(jnp.float32).astype(jnp.bfloat16)

    row32 = iota((32, 128), 0)
    lane32 = iota((32, 128), 1)
    parity = row32 & 1
    left_half = lane32 < 64

    def from_rows(fields):
        count = len(fields)
        parts = [split(f) for f in fields]
        stacked = jnp.concatenate([p[0] for p in parts] + [p[1] for p in parts], axis=0)
        moved = fdot(stacked, sel[...]).astype(jnp.bfloat16)
        out = []
        for f in range(count):
            pieces = []
            for part in range(2):
                z = moved[(part * count + f) * 16:(part * count + f) * 16 + 16]
                pieces += [z[:, u * 128:u * 128 + 128] for u in range(4)]
            v = fdot(place, jnp.concatenate(pieces, axis=0))
            tiles = []
            for pair in range(2):
                picked = []
                for odd in range(2):
                    at = (pair * 2 + odd) * 32
                    block = v[at:at + 32]
                    picked.append(jnp.where(parity == odd, block, half_roll(block)))
                tiles.append(jnp.where(left_half, picked[0], picked[1]))
            out.append(jnp.concatenate(tiles, axis=1))
        return out

    def to_rows(values):
        count = len(values)
        highs, lows = [], []
        for value in values:
            blocks = []
            for ij in range(4):
                block = value[:, (ij // 2) * 128:(ij // 2) * 128 + 128]
                block = jnp.where(parity == (ij & 1), block, half_roll(block))
                blocks.append(jnp.where((lane32 >> 6) == parity, block, 0.0))
            high, low = split(jnp.concatenate(blocks, axis=0))
            highs.append(high)
            lows.append(low)
        o = fdot(unplace, jnp.concatenate(highs + lows, axis=1)).astype(jnp.bfloat16)
        rows = []
        for v in range(2 * count):
            rows.append(
                jnp.concatenate(
                    [o[u * 16:u * 16 + 16, v * 128:v * 128 + 128] for u in range(4)], axis=1
                )
            )
        n = lax.dot_general(
            jnp.concatenate(rows, axis=0), sel[...], (((1,), (1,)), ((), ())),
            preferred_element_type=jnp.float32,
        )
        return [
            n[v * 16:v * 16 + 16] + n[(count + v) * 16:(count + v) * 16 + 16]
            for v in range(count)
        ]

    for name in ("smoother", "load", "spread_e", "aei", "re", "edges"):
        c(name)
    s_pad[...] = jnp.zeros((16, 128), jnp.float32)
    s_pad[0:10, 0:10] = c("smoother")[...]
    both_parts = jnp.concatenate(split(s_pad[...]), axis=0)[:, 0:16]
    entries = fdot(both_parts, c("spread_e")[...]).astype(jnp.bfloat16)

    def stacked_entries(entries, at, width, number):
        blocks = [entries[:, at + b * width:at + (b + 1) * width] for b in range(number)]
        return [block[0:16] for block in blocks] + [block[16:32] for block in blocks]

    for axis in range(2):
        wide = fdot(
            c("re")[axis],
            jnp.concatenate(
                stacked_entries(entries, axis * 768, 384, 2) + [c("aei")[axis]], axis=0
            ),
        )
        enc = wide if axis == 0 else enc * wide
    high, low = split(enc)
    e_hi[...] = high
    e_lo[...] = low

    r0, = from_rows([c("load")[...]])

    low_x = (gx == 0).astype(jnp.float32)
    high_x = (gx == nx - 1).astype(jnp.float32)
    low_y = (gy == 0).astype(jnp.float32)
    high_y = (gy == ny - 1).astype(jnp.float32)
    edges = c("edges")[...]
    arrives = (1.0 - edges[0:1] * high_x - edges[1:2] * low_x) * (
        1.0 - edges[2:3] * high_y - edges[3:4] * low_y
    )

    left16 = lane16 < 64
    quarter = (lane16 & 63) >> 4

    pl.semaphore_wait(barrier, len(greeted))

    def exchange_start(stage, value):
        m = right_dot(value, e_hi[...], e_lo[...])
        for pair in range(2):
            t = m[:, pair * 128:pair * 128 + 128]
            top, bottom = t[0:16], t[16:32]
            halo_out[stage, 2 * pair] = jnp.where(left16, top, half_roll(bottom))
            halo_out[stage, 2 * pair + 1] = jnp.where(left16, half_roll(top), bottom)
        t = m[:, 256:384]
        halo_out[stage, 4] = jnp.where(left16, t[0:16], half_roll(t[16:32]))
        copies = []
        for slot, (peer, part) in enumerate(neighbours):
            copy = pltpu.make_async_remote_copy(
                src_ref=halo_out.at[stage, part],
                dst_ref=halo_in.at[stage, slot],
                send_sem=halo_send.at[stage, slot],
                recv_sem=halo_recv.at[stage, slot],
                device_id=peer,
                device_id_type=MESH,
            )
            copy.start()
            copies.append(copy)
        return copies

    def exchange_end(stage, copies):
        for copy in copies:
            copy.wait_recv()
        tiles = []
        for pair in range(2):
            a, b = halo_in[stage, 2 * pair], halo_in[stage, 2 * pair + 1]
            tiles.append(
                jnp.concatenate(
                    [jnp.where(left16, a, half_roll(b)), jnp.where(left16, half_roll(a), b)],
                    axis=0,
                )
            )
        corner = jnp.where(
            quarter == 0, halo_in[stage, 4],
            jnp.where(
                quarter == 1, halo_in[stage, 5],
                jnp.where(quarter == 2, halo_in[stage, 6], halo_in[stage, 7]),
            ),
        )
        tiles.append(jnp.concatenate([corner, half_roll(corner)], axis=0))
        return jnp.concatenate(tiles, axis=1) * arrives

    def sum_round_start(which, at, value):
        sums[which, at, 0] = value
        copies = []
        for d, peer in enumerate(rounds[at]):
            copy = pltpu.make_async_remote_copy(
                src_ref=sums.at[which, at, 0],
                dst_ref=sums.at[which, at, d + 1],
                send_sem=sum_send.at[which, at, d],
                recv_sem=sum_recv.at[which, at, d],
                device_id=peer,
                device_id_type=MESH,
            )
            copy.start()
            copies.append(copy)
        return copies

    def sum_round_end(which, at, copies):
        for copy in copies:
            copy.wait_recv()
        total = sums[which, at, 0]
        for d in range(len(copies)):
            total = total + sums[which, at, d + 1]
        return total

    row8 = iota((8, 128), 0)

    def partial_tile(pairs):
        tile = jnp.zeros((8, 128), jnp.float32)
        for q, (first, second) in enumerate(pairs):
            t = local_sum(first, second)
            for shift in (4, 2, 1):
                t = t + pltpu.roll(t, shift, 0)
            tile = jnp.where(row8 == q, t, tile)
        return tile

    def scalars(total, number):
        column = jnp.sum(total, axis=1, keepdims=True)
        return [column[q:q + 1] for q in range(number)]

    sent = []
    halo = exchange_start(0, r0)
    sent += halo

    for name in ("spread_k", "rvi", "uc", "rzt", "metric", "mass"):
        c(name)
    entries = fdot(both_parts, c("spread_k")[...]).astype(jnp.bfloat16)
    for axis, low_edge, high_edge in ((0, low_x, high_x), (1, low_y, high_y)):
        blocks = stacked_entries(entries, axis * 1024, 256, 4)
        for at in (0, 4):
            blocks[at] = blocks[at] * (1.0 - low_edge).astype(jnp.bfloat16)
            blocks[at + 3] = blocks[at + 3] * (1.0 - high_edge).astype(jnp.bfloat16)
        wide = fdot(c("uc")[axis], jnp.concatenate(blocks + [c("rvi")[axis]], axis=0))
        kxy = wide if axis == 0 else kxy * wide
    high, low = split(kxy)
    k_hi[...] = high
    k_lo[...] = low
    tz = fdot(c("rzt")[...], jnp.concatenate(stacked_entries(entries, 2048, 128, 4), axis=0))
    tz_hi, tz_lo = split(tz[:, 0:96])
    tz = jnp.where(iota((32, 96), 1) < 64, tz_hi.astype(jnp.float32), tz_lo.astype(jnp.float32))
    tz = tz.astype(jnp.bfloat16)

    metric = c("metric")
    m0, m1, m2, mass = from_rows(
        [metric[0], metric[1], metric[2], c("mass")[...]]
    )
    m01 = jnp.concatenate(
        [
            jnp.concatenate([m0[:, :128], m1[:, :128]], axis=1),
            jnp.concatenate([m0[:, 128:], m1[:, 128:]], axis=1),
        ],
        axis=0,
    )

    def own_part(value):
        return right_dot(value, k_hi[0:256], k_lo[0:256])

    def precondition(own, arrived):
        return left_dot(tz, own + right_dot(arrived, k_hi[256:640], k_lo[256:640]))

    def operate(u):
        tall = jnp.concatenate([u[:, :128], u[:, 128:]], axis=0)
        slope = m01 * right_dot(tall, c("dxy_hi")[...], c("dxy_lo")[...])
        slope_z = m2 * left_dot(c("dz")[...], u)
        tall = right_dot(slope, c("dxyt_hi")[...], c("dxyt_lo")[...])
        return (
            jnp.concatenate([tall[:32], tall[32:]], axis=1)
            + left_dot(c("dzt")[...], slope_z)
            + mass * u
        )

    def assembled(value, arrived):
        both = jnp.concatenate([value, arrived], axis=1)
        high, low = split(both)
        t = fdot(jnp.concatenate([high, low], axis=0), c("asm")[...])
        t = t[:32] + t[32:]
        high, low = split(t)
        return fdot(c("az")[...], jnp.concatenate([high, low], axis=0))

    own = own_part(r0)
    arrived_r0 = exchange_end(0, halo)
    z0 = precondition(own, arrived_r0)
    w0 = operate(z0)

    halo = exchange_start(1, w0)
    sent += halo
    ring = sum_round_start(0, 0, partial_tile([(r0, z0), (w0, z0)]))
    sent += ring
    own = own_part(w0)
    arrived_w0 = exchange_end(1, halo)
    total = sum_round_end(0, 0, ring)
    ring = sum_round_start(0, 1, total)
    sent += ring
    z1 = precondition(own, arrived_w0)
    w1 = operate(z1)
    halo = exchange_start(2, w1)
    sent += halo
    own = own_part(w1)
    rows_z0, rows_z1, rows_r0, rows_w0 = to_rows(
        [z0, z1, assembled(r0, arrived_r0), assembled(w0, arrived_w0)]
    )
    total = sum_round_end(0, 1, ring)
    gamma0, delta0 = scalars(total, 2)
    alpha0 = gamma0 / delta0

    r1 = r0 - alpha0 * w0
    u1 = z0 - alpha0 * z1
    v1 = w0 - alpha0 * w1
    rows_r1 = rows_r0 - alpha0 * rows_w0
    rows_u1 = rows_z0 - alpha0 * rows_z1
    rows_x1 = alpha0 * rows_z0
    arrived_w1 = exchange_end(2, halo)
    z2 = precondition(own, arrived_w1)
    w2 = operate(z2)
    halo = exchange_start(3, w2)
    sent += halo
    q = z1 - alpha0 * z2
    y = w1 - alpha0 * w2
    ring = sum_round_start(
        1, 0,
        partial_tile(
            [(r1, u1), (v1, u1), (v1, q), (v1, z1), (w0, z1), (y, q), (y, z1), (w1, z1)]
        ),
    )
    sent += ring
    rows_z2, rows_w1 = to_rows([z2, assembled(w1, arrived_w1)])
    rows_v1 = rows_w0 - alpha0 * rows_w1
    rows_q = rows_z1 - alpha0 * rows_z2
    total = sum_round_end(1, 0, ring)
    ring = sum_round_start(1, 1, total)
    sent += ring
    arrived_w2 = exchange_end(3, halo)
    rows_w2, = to_rows([assembled(w2, arrived_w2)])
    rows_y = rows_w1 - alpha0 * rows_w2
    total = sum_round_end(1, 1, ring)
    gamma1, delta1, vq, vz, wz0, yq, yz, wz1 = scalars(total, 8)

    beta1 = gamma1 / gamma0
    alpha1 = gamma1 / (delta1 - beta1 * gamma1 / alpha0)
    uz = -gamma1 / alpha0
    gamma2 = (
        gamma1 - 2.0 * alpha1 * (delta1 + beta1 * uz)
        + alpha1 * alpha1 * (vq + beta1 * (2.0 * vz + beta1 * wz0))
    )
    delta2 = (
        delta1 - 2.0 * alpha1 * (vq + beta1 * vz)
        + alpha1 * alpha1 * (yq + beta1 * (2.0 * yz + beta1 * wz1))
    )
    beta2 = gamma2 / gamma1
    alpha2 = gamma2 / (delta2 - beta2 * gamma2 / alpha1)
    rows_p1 = rows_u1 + beta1 * rows_z0
    rows_u2 = rows_u1 - alpha1 * (rows_q + beta1 * rows_z1)
    rows_s1 = rows_v1 + beta1 * rows_w0
    rows_v2 = rows_v1 - alpha1 * (rows_y + beta1 * rows_w1)
    pressure_ref[...] = rows_x1 + alpha1 * rows_p1 + alpha2 * (rows_u2 + beta2 * rows_p1)
    residual_ref[...] = rows_r1 - alpha1 * rows_s1 - alpha2 * (rows_v2 + beta2 * rows_s1)
    for copy in sent:
        copy.wait_send()


def solution(mesh):
    nx, ny = mesh.shape["gx"], mesh.shape["gy"]
    lo = 8 if nx % 8 == 0 else 2
    consts = tables()
    vmem = pl.BlockSpec(memory_space=pltpu.VMEM)
    rows = jax.ShapeDtypeStruct((16, 512), jnp.float32)
    longest = max(nx // lo * (ny // 2), 2 * lo)
    shapes = dict(
        consts,
        load=rows,
        metric=jax.ShapeDtypeStruct((3, 16, 512), jnp.float32),
        mass=rows,
        smoother=jax.ShapeDtypeStruct((10, 10), jnp.float32),
    )
    call = pl.pallas_call(
        functools.partial(kernel, nx, ny, lo),
        out_shape=(rows, rows),
        in_specs=[pl.BlockSpec(memory_space=pltpu.SMEM)]
        + [pl.BlockSpec(memory_space=pltpu.HBM)] * len(FETCHED),
        out_specs=(vmem, vmem),
        scratch_shapes=[pltpu.VMEM(shapes[name].shape, shapes[name].dtype) for name in FETCHED]
        + [
            pltpu.SemaphoreType.DMA((len(FETCHED),)),
            pltpu.VMEM((512, 512), jnp.bfloat16),
            pltpu.VMEM((640, 256), jnp.bfloat16),
            pltpu.VMEM((640, 256), jnp.bfloat16),
            pltpu.VMEM((256, 384), jnp.bfloat16),
            pltpu.VMEM((256, 384), jnp.bfloat16),
            pltpu.VMEM((16, 128), jnp.float32),
            pltpu.VMEM((4, 5, 16, 128), jnp.float32),
            pltpu.VMEM((4, 8, 16, 128), jnp.float32),
            pltpu.SemaphoreType.DMA((4, 8)),
            pltpu.SemaphoreType.DMA((4, 8)),
            pltpu.VMEM((2, 2, longest, 8, 128), jnp.float32),
            pltpu.SemaphoreType.DMA((2, 2, longest)),
            pltpu.SemaphoreType.DMA((2, 2, longest)),
        ],
        compiler_params=pltpu.CompilerParams(
            collective_id=0, has_side_effects=True, vmem_limit_bytes=60 * 1024 * 1024
        ),
    )

    def on_device(load_nodes, metric, mass_nodes, smoother, element_order):
        given = dict(
            consts, load=load_nodes, metric=metric.transpose(1, 0, 2), mass=mass_nodes, smoother=smoother
        )
        return call(element_order, *[jnp.asarray(given[name]) for name in FETCHED])

    return jax.shard_map(
        on_device,
        mesh=mesh,
        in_specs=(
            P(("gx", "gy"), None),
            P(("gx", "gy"), None, None),
            P(("gx", "gy"), None),
            P(),
            P(("gx", "gy")),
        ),
        out_specs=(P(("gx", "gy"), None), P(("gx", "gy"), None)),
        check_vma=False,
    )
```

```python
import functools

import jax
import jax.numpy as jnp
import ml_dtypes
import numpy as np
from jax import lax
from jax.experimental import pallas as pl
from jax.experimental.pallas import tpu as pltpu
from jax.sharding import PartitionSpec as P

NODES = 8
BF16 = ml_dtypes.bfloat16
MESH = pl.DeviceIdType.MESH


def derivative_table(node_count):
    degree = node_count - 1
    points = np.cos(np.pi * np.arange(node_count) / degree)
    weights = np.ones(node_count)
    weights[0] = 2.0
    weights[-1] = 2.0
    matrix = np.zeros((node_count, node_count))
    for row in range(node_count):
        for col in range(node_count):
            if row != col:
                matrix[row, col] = (
                    weights[row]
                    / weights[col]
                    * (-1.0) ** (row + col)
                    / (points[row] - points[col])
                )
        matrix[row, row] = -np.sum(matrix[row])
    return matrix


def split_const(matrix):
    full = np.asarray(matrix, np.float32)
    high = full.astype(BF16)
    return high, (full - high.astype(np.float32)).astype(BF16)


@functools.lru_cache(None)
def tables():
    node = np.array([7 * i + a for i in range(2) for a in range(8)])
    incidence = {}
    for box in (-1, 0, 1, 2):
        block = np.zeros((10, 16))
        for at in range(16):
            idx = node[at] - 7 * box + 1
            if 0 <= idx < 10:
                block[idx, at] = 1.0
        incidence[box] = block
    uc = np.zeros((24, 4, 16))
    uci = np.zeros((24, 16))
    rv = np.zeros((4, 16, 16))
    rvi = np.zeros((16, 16))
    re = np.zeros((16, 2, 16))
    rei = np.zeros((16, 32))
    ae = np.zeros((2, 16, 24))
    aei = np.zeros((32, 24))
    for at in range(16):
        for slot, box in enumerate((-1, 0, 1, 2)):
            uc[at, slot, :10] = incidence[box][:, at]
            rv[slot, :10, at] = incidence[box][:, at]
        re[at, 0, :10] = incidence[0][:, at]
        re[at, 1, :10] = incidence[1][:, at]
        rei[at, at] = 1.0
        aei[at, at] = 1.0
        for dim, where in enumerate((0, 1, 13, 14)):
            rvi[dim, at] = float(node[at] == where)
            rei[at, 16 + dim] = float(node[at] == where)
    uc[16, 2, 8] = uc[17, 2, 9] = uci[18, 2] = uci[19, 3] = 1.0
    uc[20, 1, 0] = uc[21, 1, 1] = uci[22, 0] = uci[23, 1] = 1.0
    aei[16, 16] = aei[17, 17] = ae[0, 0, 18] = ae[0, 1, 19] = 1.0
    aei[18, 20] = aei[19, 21] = ae[1, 8, 22] = ae[1, 9, 23] = 1.0
    assemble = np.zeros((24, 16))
    assemble[:16] = node[:, None] == node[None, :]
    assemble[16] = node == 14
    assemble[21] = node == 0

    lane = np.arange(256)
    xi = (lane // 128) * 8 + (lane // 8) % 8
    eta = ((lane // 64) % 2) * 8 + lane % 8
    mx, my = [], []
    for side in (16, 20):
        for q in range(4):
            for e in range(16):
                mx.append(side + q)
                my.append(e)
    for side in (16, 20):
        for e in range(16):
            for q in range(4):
                mx.append(e)
                my.append(side + q)
    for sx in (16, 20):
        for sy in (16, 20):
            for qx in range(4):
                for qy in range(4):
                    mx.append(sx + qx)
                    my.append(sy + qy)
    mx, my = np.array(mx), np.array(my)

    def padded(rows, index):
        return np.concatenate([rows[index], np.zeros((64,) + rows.shape[1:])], axis=0)

    allx = np.concatenate([xi, mx])
    ally = np.concatenate([eta, my])
    def kernel_side(index):
        rows = uc.reshape(24, 64)
        return padded(np.concatenate([rows, rows, uci], axis=1), index)

    def sending_side(index):
        rows = re.reshape(16, 32)[index]
        return np.concatenate([rows, rows, rei[index]], axis=1)

    spread_e = [padded(ae[box].T, m).T for m in (mx, my) for box in range(2)]
    spread_k = [rv[box][:, at] for at in (xi, eta) for box in range(4)]
    asm = padded(assemble, allx)[:, xi] * padded(assemble, ally)[:, eta]

    edges = np.zeros((8, 384))
    edges[0, :320] = (mx >= 16) & (mx < 20)
    edges[1, :320] = mx >= 20
    edges[2, :320] = (my >= 16) & (my < 20)
    edges[3, :320] = my >= 20

    znode = np.array([7 * k + c for k in range(4) for c in range(8)])
    rz = np.zeros((4, 16, 32))
    for block in range(4):
        for at in range(32):
            idx = znode[at] - 7 * block + 1
            if 0 <= idx < 10:
                rz[block, idx, at] = 1.0
    spread_z = [np.concatenate([block] * 4, axis=1) for block in rz]
    rzt = rz.reshape(64, 32).T
    az = (znode[:, None] == znode[None, :]).astype(float)

    d = derivative_table(NODES).astype(np.float32)
    eye8 = np.eye(8)
    dx = np.kron(np.eye(2), np.kron(d.T, eye8))
    dy = np.kron(np.eye(2), np.kron(eye8, d.T))
    dxy_hi, dxy_lo = split_const(np.concatenate([dx, dy], axis=1))
    dz = np.kron(np.eye(4), d)
    dz_hi, dz_lo = split_const(dz)
    dzt_hi, dzt_lo = split_const(dz.T)

    b = lambda m: np.asarray(m, BF16)
    return dict(
        dxy_hi=dxy_hi,
        dxy_lo=dxy_lo,
        dxyt_hi=np.ascontiguousarray(dxy_hi.T),
        dxyt_lo=np.ascontiguousarray(dxy_lo.T),
        dz=np.concatenate([dz_hi, dz_hi, dz_lo], axis=1),
        dzt=np.concatenate([dzt_hi, dzt_hi, dzt_lo], axis=1),
        az=b(np.concatenate([az, az], axis=1)),
        uc=b(np.stack([kernel_side(allx), kernel_side(ally)])),
        rvi=b(np.stack([rvi[:, xi], rvi[:, eta]])),
        re=b(np.stack([sending_side(xi), sending_side(eta)])),
        aei=b(np.stack([padded(aei.T, mx).T, padded(aei.T, my).T])),
        spread_e=b(np.concatenate(spread_e, axis=1)),
        spread_k=b(np.concatenate(spread_k + spread_z, axis=1)),
        rzt=b(np.concatenate([rzt, rzt], axis=1)),
        asm=b(asm),
        edges=np.asarray(edges, np.float32),
    )


FETCHED = (
    "order", "smoother", "load", "spread_e", "aei", "re", "edges", "spread_k", "rvi", "uc", "rzt",
    "metric", "mass", "dxy_hi", "dxy_lo", "dz", "dxyt_hi", "dxyt_lo", "dzt", "asm", "az",
)


def fdot(left, right):
    return jnp.dot(left, right, preferred_element_type=jnp.float32)


def split(value):
    high = value.astype(jnp.bfloat16)
    low = (value - high.astype(jnp.float32)).astype(jnp.bfloat16)
    return high, low


def right_dot(value, w_hi, w_lo):
    rows = value.shape[0]
    high, low = split(value)
    both = fdot(jnp.concatenate([high, low], axis=0), w_hi)
    return both[:rows] + both[rows:] + fdot(high, w_lo)


def left_dot(stacked, value):
    high, low = split(value)
    return fdot(stacked, jnp.concatenate([high, low, high], axis=0))


def offsets(first, second):
    def far(pair):
        return -min(pair[0], first - pair[0]) - min(pair[1], second - pair[1])

    pairs = [(a, b) for a in range(first) for b in range(second)]
    return sorted(pairs[1:], key=far)


def iota(shape, dim):
    return lax.broadcasted_iota(jnp.int32, shape, dim)


def half_roll(value):
    return pltpu.roll(value, 64, 1)


def local_sum(pairs):
    t = sum(first * second for first, second in pairs)
    t = t[0:8] + t[8:16] + t[16:24] + t[24:32]
    return t[:, :128] + t[:, 128:]


def kernel(
    nx, ny, lo,
    *refs,
):
    count = len(FETCHED)
    far = dict(zip(FETCHED, refs[:count]))
    near = dict(zip(FETCHED, refs[count + 2:2 * count + 2]))
    pressure_ref, residual_ref = refs[count:count + 2]
    (
        fetch_sem, sel, k_hi, k_lo, e_hi, e_lo, s_pad,
        halo_out, halo_in, halo_send, halo_recv,
        sums, sum_send, sum_recv,
    ) = refs[2 * count + 2:]
    gx = lax.axis_index("gx")
    gy = lax.axis_index("gy")
    hi = nx // lo
    x_low, x_high = lax.rem(gx + nx - 1, nx), lax.rem(gx + 1, nx)
    y_low, y_high = lax.rem(gy + ny - 1, ny), lax.rem(gy + 1, ny)
    neighbours = (
        ((x_low, gy), 0), ((x_high, gy), 1),
        ((gx, y_low), 2), ((gx, y_high), 3),
        ((x_low, y_low), 4), ((x_low, y_high), 4),
        ((x_high, y_low), 4), ((x_high, y_high), 4),
    )
    z_at, y_at = lax.rem(gx, lo), lax.div(gx, lo)
    x_at, core = lax.div(gy, 2), lax.rem(gy, 2)
    rounds = [
        [
            (lax.rem(y_at + a, hi) * lo + z_at, lax.rem(x_at + b, ny // 2) * 2 + core)
            for a, b in offsets(hi, ny // 2)
        ],
        [
            (y_at * lo + lax.rem(z_at + a, lo), x_at * 2 + lax.rem(core + b, 2))
            for a, b in offsets(lo, 2)
        ],
    ]
    greeted = rounds[1] + [n for n, _ in neighbours[::-1]] + rounds[0]
    barrier = pltpu.get_barrier_semaphore()
    for peer in greeted:
        pl.semaphore_signal(barrier, inc=1, device_id=peer, device_id_type=MESH)

    fetches = {}
    for at, name in enumerate(FETCHED):
        fetches[name] = pltpu.make_async_copy(far[name], near[name], fetch_sem.at[at])
        fetches[name].start()

    def c(name):
        if name in fetches:
            fetches.pop(name).wait()
        return near[name]

    col = iota((64, 512), 1)
    for block in range(8):
        at = iota((64, 512), 0) + block * 64
        sel[block * 64:block * 64 + 64] = (
            ((at & 7) * 64 + (at >> 3)) == col
        ).astype(jnp.float32).astype(jnp.bfloat16)

    lane1 = iota((1, 128), 1)
    order_ref = c("order")
    row16 = iota((16, 128), 0)
    along_lanes = jnp.zeros((1, 128), jnp.int32)
    along_rows = jnp.zeros((16, 128), jnp.int32)
    for at in range(16):
        along_lanes = jnp.where((lane1 & 15) == at, order_ref[at], along_lanes)
        along_rows = jnp.where(row16 == at, order_ref[at], along_rows)
    row = iota((128, 128), 0)
    place = (
        ((row >> 3) == along_lanes) & (((row & 7) >> 1) == ((lane1 & 63) >> 4))
    ).astype(jnp.float32).astype(jnp.bfloat16)
    lane16 = iota((16, 128), 1)
    unplace = jnp.concatenate(
        [((lane16 >> 3) == along_rows) & (((lane16 & 7) >> 1) == u) for u in range(4)], axis=0
    ).astype(jnp.float32).astype(jnp.bfloat16)

    row32 = iota((32, 128), 0)
    lane32 = iota((32, 128), 1)
    parity = row32 & 1
    left_half = lane32 < 64

    def from_rows(fields):
        count = len(fields)
        parts = [split(f) for f in fields]
        stacked = jnp.concatenate([p[0] for p in parts] + [p[1] for p in parts], axis=0)
        moved = fdot(stacked, sel[...]).astype(jnp.bfloat16)
        out = []
        for f in range(count):
            pieces = []
            for part in range(2):
                z = moved[(part * count + f) * 16:(part * count + f) * 16 + 16]
                pieces += [z[:, u * 128:u * 128 + 128] for u in range(4)]
            v = fdot(place, jnp.concatenate(pieces, axis=0))
            tiles = []
            for pair in range(2):
                picked = []
                for odd in range(2):
                    at = (pair * 2 + odd) * 32
                    block = v[at:at + 32]
                    picked.append(jnp.where(parity == odd, block, half_roll(block)))
                tiles.append(jnp.where(left_half, picked[0], picked[1]))
            out.append(jnp.concatenate(tiles, axis=1))
        return out

    def to_rows(values):
        count = len(values)
        highs, lows = [], []
        for value in values:
            blocks = []
            for ij in range(4):
                block = value[:, (ij // 2) * 128:(ij // 2) * 128 + 128]
                block = jnp.where(parity == (ij & 1), block, half_roll(block))
                blocks.append(jnp.where((lane32 >> 6) == parity, block, 0.0))
            high, low = split(jnp.concatenate(blocks, axis=0))
            highs.append(high)
            lows.append(low)
        o = fdot(unplace, jnp.concatenate(highs + lows, axis=1)).astype(jnp.bfloat16)
        rows = []
        for v in range(2 * count):
            rows.append(
                jnp.concatenate(
                    [o[u * 16:u * 16 + 16, v * 128:v * 128 + 128] for u in range(4)], axis=1
                )
            )
        n = lax.dot_general(
            jnp.concatenate(rows, axis=0), sel[...], (((1,), (1,)), ((), ())),
            preferred_element_type=jnp.float32,
        )
        return [
            n[v * 16:v * 16 + 16] + n[(count + v) * 16:(count + v) * 16 + 16]
            for v in range(count)
        ]

    for name in ("smoother", "load", "spread_e", "aei", "re", "edges"):
        c(name)
    s_pad[...] = jnp.zeros((16, 128), jnp.float32)
    s_pad[0:10, 0:10] = c("smoother")[...]
    both_parts = jnp.concatenate(split(s_pad[...]), axis=0)[:, 0:16]
    entries = fdot(both_parts, c("spread_e")[...]).astype(jnp.bfloat16)

    def stacked_entries(entries, at, width, number):
        blocks = [entries[:, at + b * width:at + (b + 1) * width] for b in range(number)]
        return [block[0:16] for block in blocks] + [block[16:32] for block in blocks]

    for axis in range(2):
        wide = fdot(
            c("re")[axis],
            jnp.concatenate(
                stacked_entries(entries, axis * 768, 384, 2) + [c("aei")[axis]], axis=0
            ),
        )
        enc = wide if axis == 0 else enc * wide
    high, low = split(enc)
    e_hi[...] = high
    e_lo[...] = low

    r0, = from_rows([c("load")[...]])

    low_x = (gx == 0).astype(jnp.float32)
    high_x = (gx == nx - 1).astype(jnp.float32)
    low_y = (gy == 0).astype(jnp.float32)
    high_y = (gy == ny - 1).astype(jnp.float32)
    edges = c("edges")[...]
    arrives = (1.0 - edges[0:1] * high_x - edges[1:2] * low_x) * (
        1.0 - edges[2:3] * high_y - edges[3:4] * low_y
    )

    left16 = lane16 < 64
    quarter = (lane16 & 63) >> 4

    pl.semaphore_wait(barrier, len(greeted))

    def exchange_start(stage, value):
        m = right_dot(value, e_hi[...], e_lo[...])
        for pair in range(2):
            t = m[:, pair * 128:pair * 128 + 128]
            top, bottom = t[0:16], t[16:32]
            halo_out[stage, 2 * pair] = jnp.where(left16, top, half_roll(bottom))
            halo_out[stage, 2 * pair + 1] = jnp.where(left16, half_roll(top), bottom)
        t = m[:, 256:384]
        halo_out[stage, 4] = jnp.where(left16, t[0:16], half_roll(t[16:32]))
        copies = []
        for slot, (peer, part) in enumerate(neighbours):
            copy = pltpu.make_async_remote_copy(
                src_ref=halo_out.at[stage, part],
                dst_ref=halo_in.at[stage, slot],
                send_sem=halo_send.at[stage, slot],
                recv_sem=halo_recv.at[stage, slot],
                device_id=peer,
                device_id_type=MESH,
            )
            copy.start()
            copies.append(copy)
        return copies

    def exchange_end(stage, copies):
        for copy in copies:
            copy.wait_recv()
        tiles = []
        for pair in range(2):
            a, b = halo_in[stage, 2 * pair], halo_in[stage, 2 * pair + 1]
            tiles.append(
                jnp.concatenate(
                    [jnp.where(left16, a, half_roll(b)), jnp.where(left16, half_roll(a), b)],
                    axis=0,
                )
            )
        corner = jnp.where(
            quarter == 0, halo_in[stage, 4],
            jnp.where(
                quarter == 1, halo_in[stage, 5],
                jnp.where(quarter == 2, halo_in[stage, 6], halo_in[stage, 7]),
            ),
        )
        tiles.append(jnp.concatenate([corner, half_roll(corner)], axis=0))
        return jnp.concatenate(tiles, axis=1) * arrives

    def sum_round_start(which, at, value):
        sums[which, at, 0] = value
        copies = []
        for d, peer in enumerate(rounds[at]):
            copy = pltpu.make_async_remote_copy(
                src_ref=sums.at[which, at, 0],
                dst_ref=sums.at[which, at, d + 1],
                send_sem=sum_send.at[which, at, d],
                recv_sem=sum_recv.at[which, at, d],
                device_id=peer,
                device_id_type=MESH,
            )
            copy.start()
            copies.append(copy)
        return copies

    def sum_round_end(which, at, copies):
        for copy in copies:
            copy.wait_recv()
        total = sums[which, at, 0]
        for d in range(len(copies)):
            total = total + sums[which, at, d + 1]
        return total

    row8 = iota((8, 128), 0)

    def partial_tile(pairs):
        tile = jnp.zeros((8, 128), jnp.float32)
        for q, products in enumerate(pairs):
            t = local_sum(products)
            for shift in (4, 2, 1):
                t = t + pltpu.roll(t, shift, 0)
            tile = jnp.where(row8 == q, t, tile)
        return tile

    def scalars(total, number):
        column = jnp.sum(total, axis=1, keepdims=True)
        return [column[q:q + 1] for q in range(number)]

    sent = []
    halo = exchange_start(0, r0)
    sent += halo

    for name in ("spread_k", "rvi", "uc", "rzt", "metric", "mass"):
        c(name)
    entries = fdot(both_parts, c("spread_k")[...]).astype(jnp.bfloat16)
    for axis, low_edge, high_edge in ((0, low_x, high_x), (1, low_y, high_y)):
        blocks = stacked_entries(entries, axis * 1024, 256, 4)
        for at in (0, 4):
            blocks[at] = blocks[at] * (1.0 - low_edge).astype(jnp.bfloat16)
            blocks[at + 3] = blocks[at + 3] * (1.0 - high_edge).astype(jnp.bfloat16)
        wide = fdot(c("uc")[axis], jnp.concatenate(blocks + [c("rvi")[axis]], axis=0))
        kxy = wide if axis == 0 else kxy * wide
    high, low = split(kxy)
    k_hi[...] = high
    k_lo[...] = low
    tz = fdot(c("rzt")[...], jnp.concatenate(stacked_entries(entries, 2048, 128, 4), axis=0))
    tz_hi, tz_lo = split(tz[:, 0:96])
    tz = jnp.where(iota((32, 96), 1) < 64, tz_hi.astype(jnp.float32), tz_lo.astype(jnp.float32))
    tz = tz.astype(jnp.bfloat16)

    metric = c("metric")
    m0, m1, m2, mass = from_rows(
        [metric[0], metric[1], metric[2], c("mass")[...]]
    )
    m01 = jnp.concatenate(
        [
            jnp.concatenate([m0[:, :128], m1[:, :128]], axis=1),
            jnp.concatenate([m0[:, 128:], m1[:, 128:]], axis=1),
        ],
        axis=0,
    )

    def own_part(value):
        return right_dot(value, k_hi[0:256], k_lo[0:256])

    def precondition(own, arrived):
        return left_dot(tz, own + right_dot(arrived, k_hi[256:640], k_lo[256:640]))

    def slopes(u):
        tall = jnp.concatenate([u[:, :128], u[:, 128:]], axis=0)
        return right_dot(tall, c("dxy_hi")[...], c("dxy_lo")[...]), left_dot(c("dz")[...], u)

    def operate(u, grad):
        slope = m01 * grad[0]
        slope_z = m2 * grad[1]
        tall = right_dot(slope, c("dxyt_hi")[...], c("dxyt_lo")[...])
        return (
            jnp.concatenate([tall[:32], tall[32:]], axis=1)
            + left_dot(c("dzt")[...], slope_z)
            + mass * u
        )

    def assembled(value, arrived):
        both = jnp.concatenate([value, arrived], axis=1)
        high, low = split(both)
        t = fdot(jnp.concatenate([high, low], axis=0), c("asm")[...])
        t = t[:32] + t[32:]
        high, low = split(t)
        return fdot(c("az")[...], jnp.concatenate([high, low], axis=0))

    own = own_part(r0)
    arrived_r0 = exchange_end(0, halo)
    z0 = precondition(own, arrived_r0)
    w0 = operate(z0, slopes(z0))

    halo = exchange_start(1, w0)
    sent += halo
    ring = sum_round_start(0, 0, partial_tile([[(r0, z0)], [(w0, z0)]]))
    sent += ring
    own = own_part(w0)
    arrived_w0 = exchange_end(1, halo)
    z1 = precondition(own, arrived_w0)
    grad1 = slopes(z1)
    w1 = operate(z1, grad1)
    halo = exchange_start(2, w1)
    sent += halo
    total = sum_round_end(0, 0, ring)
    ring = sum_round_start(0, 1, total)
    sent += ring
    own = own_part(w1)
    rows_z0, rows_z1, rows_r0, rows_w0 = to_rows(
        [z0, z1, assembled(r0, arrived_r0), assembled(w0, arrived_w0)]
    )
    arrived_w1 = exchange_end(2, halo)
    z2 = precondition(own, arrived_w1)
    grad2 = slopes(z2)
    total = sum_round_end(0, 1, ring)
    gamma0, delta0 = scalars(total, 2)
    alpha0 = gamma0 / delta0

    r1 = r0 - alpha0 * w0
    u1 = z0 - alpha0 * z1
    v1 = w0 - alpha0 * w1
    q = z1 - alpha0 * z2
    grad_q = grad1[0] - alpha0 * grad2[0]
    grad_qz = grad1[1] - alpha0 * grad2[1]
    slope_q = m01 * grad_q
    ring = sum_round_start(
        1, 0,
        partial_tile(
            [
                [(r1, u1)], [(v1, u1)], [(v1, q)], [(v1, z1)], [(w0, z1)],
                [
                    (slope_q[:32], grad_q[:32]), (slope_q[32:], grad_q[32:]),
                    (m2 * grad_qz, grad_qz), (mass * q, q),
                ],
                [(w1, q)], [(w1, z1)],
            ]
        ),
    )
    sent += ring
    w2 = operate(z2, grad2)
    halo = exchange_start(3, w2)
    sent += halo
    rows_r1 = rows_r0 - alpha0 * rows_w0
    rows_u1 = rows_z0 - alpha0 * rows_z1
    rows_x1 = alpha0 * rows_z0
    rows_z2, rows_w1 = to_rows([z2, assembled(w1, arrived_w1)])
    rows_v1 = rows_w0 - alpha0 * rows_w1
    rows_q = rows_z1 - alpha0 * rows_z2
    total = sum_round_end(1, 0, ring)
    ring = sum_round_start(1, 1, total)
    sent += ring
    arrived_w2 = exchange_end(3, halo)
    rows_w2, = to_rows([assembled(w2, arrived_w2)])
    rows_y = rows_w1 - alpha0 * rows_w2
    total = sum_round_end(1, 1, ring)
    gamma1, delta1, vq, vz, wz0, yq, yz, wz1 = scalars(total, 8)

    beta1 = gamma1 / gamma0
    alpha1 = gamma1 / (delta1 - beta1 * gamma1 / alpha0)
    uz = -gamma1 / alpha0
    gamma2 = (
        gamma1 - 2.0 * alpha1 * (delta1 + beta1 * uz)
        + alpha1 * alpha1 * (vq + beta1 * (2.0 * vz + beta1 * wz0))
    )
    delta2 = (
        delta1 - 2.0 * alpha1 * (vq + beta1 * vz)
        + alpha1 * alpha1 * (yq + beta1 * (2.0 * yz + beta1 * wz1))
    )
    beta2 = gamma2 / gamma1
    alpha2 = gamma2 / (delta2 - beta2 * gamma2 / alpha1)
    rows_p1 = rows_u1 + beta1 * rows_z0
    rows_u2 = rows_u1 - alpha1 * (rows_q + beta1 * rows_z1)
    rows_s1 = rows_v1 + beta1 * rows_w0
    rows_v2 = rows_v1 - alpha1 * (rows_y + beta1 * rows_w1)
    pressure_ref[...] = rows_x1 + alpha1 * rows_p1 + alpha2 * (rows_u2 + beta2 * rows_p1)
    residual_ref[...] = rows_r1 - alpha1 * rows_s1 - alpha2 * (rows_v2 + beta2 * rows_s1)
    for copy in sent:
        copy.wait_send()


def solution(mesh):
    nx, ny = mesh.shape["gx"], mesh.shape["gy"]
    lo = 8 if nx % 8 == 0 else 2
    consts = tables()
    vmem = pl.BlockSpec(memory_space=pltpu.VMEM)
    rows = jax.ShapeDtypeStruct((16, 512), jnp.float32)
    longest = max(nx // lo * (ny // 2), 2 * lo)
    shapes = dict(
        consts,
        load=rows,
        metric=jax.ShapeDtypeStruct((3, 16, 512), jnp.float32),
        mass=rows,
        smoother=jax.ShapeDtypeStruct((10, 10), jnp.float32),
        order=jax.ShapeDtypeStruct((16,), jnp.int32),
    )
    call = pl.pallas_call(
        functools.partial(kernel, nx, ny, lo),
        out_shape=(rows, rows),
        in_specs=[pl.BlockSpec(memory_space=pltpu.HBM)] * len(FETCHED),
        out_specs=(vmem, vmem),
        scratch_shapes=[
            (pltpu.SMEM if name == "order" else pltpu.VMEM)(shapes[name].shape, shapes[name].dtype)
            for name in FETCHED
        ]
        + [
            pltpu.SemaphoreType.DMA((len(FETCHED),)),
            pltpu.VMEM((512, 512), jnp.bfloat16),
            pltpu.VMEM((640, 256), jnp.bfloat16),
            pltpu.VMEM((640, 256), jnp.bfloat16),
            pltpu.VMEM((256, 384), jnp.bfloat16),
            pltpu.VMEM((256, 384), jnp.bfloat16),
            pltpu.VMEM((16, 128), jnp.float32),
            pltpu.VMEM((4, 5, 16, 128), jnp.float32),
            pltpu.VMEM((4, 8, 16, 128), jnp.float32),
            pltpu.SemaphoreType.DMA((4, 8)),
            pltpu.SemaphoreType.DMA((4, 8)),
            pltpu.VMEM((2, 2, longest, 8, 128), jnp.float32),
            pltpu.SemaphoreType.DMA((2, 2, longest)),
            pltpu.SemaphoreType.DMA((2, 2, longest)),
        ],
        compiler_params=pltpu.CompilerParams(
            collective_id=0, has_side_effects=True, vmem_limit_bytes=60 * 1024 * 1024
        ),
    )

    def on_device(load_nodes, metric, mass_nodes, smoother, element_order):
        given = dict(
            consts, load=load_nodes, metric=metric.transpose(1, 0, 2), mass=mass_nodes, smoother=smoother,
            order=element_order,
        )
        return call(*[jnp.asarray(given[name]) for name in FETCHED])

    return jax.shard_map(
        on_device,
        mesh=mesh,
        in_specs=(
            P(("gx", "gy"), None),
            P(("gx", "gy"), None, None),
            P(("gx", "gy"), None),
            P(),
            P(("gx", "gy")),
        ),
        out_specs=(P(("gx", "gy"), None), P(("gx", "gy"), None)),
        check_vma=False,
    )
```

```python
import functools

import jax
import jax.numpy as jnp
import ml_dtypes
import numpy as np
from jax import lax
from jax.experimental import pallas as pl
from jax.experimental.pallas import tpu as pltpu
from jax.sharding import PartitionSpec as P

NODES = 8
BF16 = ml_dtypes.bfloat16
MESH = pl.DeviceIdType.MESH


def derivative_table(node_count):
    degree = node_count - 1
    points = np.cos(np.pi * np.arange(node_count) / degree)
    weights = np.ones(node_count)
    weights[0] = 2.0
    weights[-1] = 2.0
    matrix = np.zeros((node_count, node_count))
    for row in range(node_count):
        for col in range(node_count):
            if row != col:
                matrix[row, col] = (
                    weights[row]
                    / weights[col]
                    * (-1.0) ** (row + col)
                    / (points[row] - points[col])
                )
        matrix[row, row] = -np.sum(matrix[row])
    return matrix


def split_const(matrix):
    full = np.asarray(matrix, np.float32)
    high = full.astype(BF16)
    return high, (full - high.astype(np.float32)).astype(BF16)


@functools.lru_cache(None)
def tables():
    node = np.array([7 * i + a for i in range(2) for a in range(8)])
    incidence = {}
    for box in (-1, 0, 1, 2):
        block = np.zeros((10, 16))
        for at in range(16):
            idx = node[at] - 7 * box + 1
            if 0 <= idx < 10:
                block[idx, at] = 1.0
        incidence[box] = block
    uc = np.zeros((24, 4, 16))
    uci = np.zeros((24, 16))
    rv = np.zeros((4, 16, 16))
    rvi = np.zeros((16, 16))
    re = np.zeros((16, 2, 16))
    rei = np.zeros((16, 32))
    ae = np.zeros((2, 16, 24))
    aei = np.zeros((32, 24))
    for at in range(16):
        for slot, box in enumerate((-1, 0, 1, 2)):
            uc[at, slot, :10] = incidence[box][:, at]
            rv[slot, :10, at] = incidence[box][:, at]
        re[at, 0, :10] = incidence[0][:, at]
        re[at, 1, :10] = incidence[1][:, at]
        rei[at, at] = 1.0
        aei[at, at] = 1.0
        for dim, where in enumerate((0, 1, 13, 14)):
            rvi[dim, at] = float(node[at] == where)
            rei[at, 16 + dim] = float(node[at] == where)
    uc[16, 2, 8] = uc[17, 2, 9] = uci[18, 2] = uci[19, 3] = 1.0
    uc[20, 1, 0] = uc[21, 1, 1] = uci[22, 0] = uci[23, 1] = 1.0
    aei[16, 16] = aei[17, 17] = ae[0, 0, 18] = ae[0, 1, 19] = 1.0
    aei[18, 20] = aei[19, 21] = ae[1, 8, 22] = ae[1, 9, 23] = 1.0
    assemble = np.zeros((24, 16))
    assemble[:16] = node[:, None] == node[None, :]
    assemble[16] = node == 14
    assemble[21] = node == 0

    lane = np.arange(256)
    xi = (lane // 128) * 8 + (lane // 8) % 8
    eta = ((lane // 64) % 2) * 8 + lane % 8
    mx, my = [], []
    for side in (16, 20):
        for q in range(4):
            for e in range(16):
                mx.append(side + q)
                my.append(e)
    for side in (16, 20):
        for e in range(16):
            for q in range(4):
                mx.append(e)
                my.append(side + q)
    for sx in (16, 20):
        for sy in (16, 20):
            for qx in range(4):
                for qy in range(4):
                    mx.append(sx + qx)
                    my.append(sy + qy)
    mx, my = np.array(mx), np.array(my)

    def padded(rows, index):
        return np.concatenate([rows[index], np.zeros((64,) + rows.shape[1:])], axis=0)

    allx = np.concatenate([xi, mx])
    ally = np.concatenate([eta, my])
    def kernel_side(index):
        rows = uc.reshape(24, 64)
        return padded(np.concatenate([rows, rows, uci], axis=1), index)

    def sending_side(index):
        rows = re.reshape(16, 32)[index]
        return np.concatenate([rows, rows, rei[index]], axis=1)

    spread_e = [padded(ae[box].T, m).T for m in (mx, my) for box in range(2)]
    spread_k = [rv[box][:, at] for at in (xi, eta) for box in range(4)]
    asm = padded(assemble, allx)[:, xi] * padded(assemble, ally)[:, eta]

    edges = np.zeros((8, 384))
    edges[0, :320] = (mx >= 16) & (mx < 20)
    edges[1, :320] = mx >= 20
    edges[2, :320] = (my >= 16) & (my < 20)
    edges[3, :320] = my >= 20

    znode = np.array([7 * k + c for k in range(4) for c in range(8)])
    rz = np.zeros((4, 16, 32))
    for block in range(4):
        for at in range(32):
            idx = znode[at] - 7 * block + 1
            if 0 <= idx < 10:
                rz[block, idx, at] = 1.0
    spread_z = [np.concatenate([block] * 4, axis=1) for block in rz]
    rzt = rz.reshape(64, 32).T
    az = (znode[:, None] == znode[None, :]).astype(float)

    d = derivative_table(NODES).astype(np.float32)
    eye8 = np.eye(8)
    dx = np.kron(np.eye(2), np.kron(d.T, eye8))
    dy = np.kron(np.eye(2), np.kron(eye8, d.T))
    dxy_hi, dxy_lo = split_const(np.concatenate([dx, dy], axis=1))
    dz = np.kron(np.eye(4), d)
    dz_hi, dz_lo = split_const(dz)
    dzt_hi, dzt_lo = split_const(dz.T)

    b = lambda m: np.asarray(m, BF16)
    return dict(
        dxy_hi=dxy_hi,
        dxy_lo=dxy_lo,
        dxyt_hi=np.ascontiguousarray(dxy_hi.T),
        dxyt_lo=np.ascontiguousarray(dxy_lo.T),
        dz=np.concatenate([dz_hi, dz_hi, dz_lo], axis=1),
        dzt=np.concatenate([dzt_hi, dzt_hi, dzt_lo], axis=1),
        az=b(np.concatenate([az, az], axis=1)),
        uc=b(np.stack([kernel_side(allx), kernel_side(ally)])),
        rvi=b(np.stack([rvi[:, xi], rvi[:, eta]])),
        re=b(np.stack([sending_side(xi), sending_side(eta)])),
        aei=b(np.stack([padded(aei.T, mx).T, padded(aei.T, my).T])),
        spread_e=b(np.concatenate(spread_e, axis=1)),
        spread_k=b(np.concatenate(spread_k + spread_z, axis=1)),
        rzt=b(np.concatenate([rzt, rzt], axis=1)),
        asm=b(asm),
        edges=np.asarray(edges, np.float32),
    )


FETCHED = (
    "order", "smoother", "load", "spread_e", "aei", "re", "edges", "spread_k", "rvi", "uc", "rzt",
    "metric", "mass", "dxy_hi", "dxy_lo", "dz", "dxyt_hi", "dxyt_lo", "dzt", "asm", "az",
)


def fdot(left, right):
    return jnp.dot(left, right, preferred_element_type=jnp.float32)


def split(value):
    high = value.astype(jnp.bfloat16)
    low = (value - high.astype(jnp.float32)).astype(jnp.bfloat16)
    return high, low


def right_dot(value, w_hi, w_lo):
    rows = value.shape[0]
    high, low = split(value)
    both = fdot(jnp.concatenate([high, low], axis=0), w_hi)
    return both[:rows] + both[rows:] + fdot(high, w_lo)


def left_dot(stacked, value):
    high, low = split(value)
    return fdot(stacked, jnp.concatenate([high, low, high], axis=0))


def offsets(first, second):
    def far(pair):
        return -min(pair[0], first - pair[0]) - min(pair[1], second - pair[1])

    pairs = [(a, b) for a in range(first) for b in range(second)]
    return sorted(pairs[1:], key=far)


def iota(shape, dim):
    return lax.broadcasted_iota(jnp.int32, shape, dim)


def half_roll(value):
    return pltpu.roll(value, 64, 1)


def local_sum(pairs):
    t = sum(first * second for first, second in pairs)
    t = t[0:8] + t[8:16] + t[16:24] + t[24:32]
    return t[:, :128] + t[:, 128:]


def kernel(
    nx, ny, lo,
    *refs,
):
    count = len(FETCHED)
    far = dict(zip(FETCHED, refs[:count]))
    near = dict(zip(FETCHED, refs[count + 2:2 * count + 2]))
    pressure_ref, residual_ref = refs[count:count + 2]
    (
        fetch_sem, sel, k_hi, k_lo, e_hi, e_lo, s_pad,
        slopes_ref, geometry, tz_ref, own_ref, rows_ref,
        halo_out, halo_in, halo_send, halo_recv,
        sums, sum_send, sum_recv,
    ) = refs[2 * count + 2:]
    gx = lax.axis_index("gx")
    gy = lax.axis_index("gy")
    hi = nx // lo
    x_low, x_high = lax.rem(gx + nx - 1, nx), lax.rem(gx + 1, nx)
    y_low, y_high = lax.rem(gy + ny - 1, ny), lax.rem(gy + 1, ny)
    neighbours = (
        ((x_low, gy), 0), ((x_high, gy), 1),
        ((gx, y_low), 2), ((gx, y_high), 3),
        ((x_low, y_low), 4), ((x_low, y_high), 4),
        ((x_high, y_low), 4), ((x_high, y_high), 4),
    )
    z_at, y_at = lax.rem(gx, lo), lax.div(gx, lo)
    x_at, core = lax.div(gy, 2), lax.rem(gy, 2)
    rounds = [
        [
            (lax.rem(y_at + a, hi) * lo + z_at, lax.rem(x_at + b, ny // 2) * 2 + core)
            for a, b in offsets(hi, ny // 2)
        ],
        [
            (y_at * lo + lax.rem(z_at + a, lo), x_at * 2 + lax.rem(core + b, 2))
            for a, b in offsets(lo, 2)
        ],
    ]
    greeted = rounds[1] + [n for n, _ in neighbours[::-1]] + rounds[0]
    barrier = pltpu.get_barrier_semaphore()
    for peer in greeted:
        pl.semaphore_signal(barrier, inc=1, device_id=peer, device_id_type=MESH)

    fetches = {}
    for at, name in enumerate(FETCHED):
        fetches[name] = pltpu.make_async_copy(far[name], near[name], fetch_sem.at[at])
        fetches[name].start()

    def c(name):
        if name in fetches:
            fetches.pop(name).wait()
        return near[name]

    col = iota((64, 512), 1)
    for block in range(8):
        at = iota((64, 512), 0) + block * 64
        sel[block * 64:block * 64 + 64] = (
            ((at & 7) * 64 + (at >> 3)) == col
        ).astype(jnp.float32).astype(jnp.bfloat16)

    lane1 = iota((1, 128), 1)
    order_ref = c("order")
    row16 = iota((16, 128), 0)
    along_lanes = jnp.zeros((1, 128), jnp.int32)
    along_rows = jnp.zeros((16, 128), jnp.int32)
    for at in range(16):
        along_lanes = jnp.where((lane1 & 15) == at, order_ref[at], along_lanes)
        along_rows = jnp.where(row16 == at, order_ref[at], along_rows)
    row = iota((128, 128), 0)
    place = (
        ((row >> 3) == along_lanes) & (((row & 7) >> 1) == ((lane1 & 63) >> 4))
    ).astype(jnp.float32).astype(jnp.bfloat16)
    lane16 = iota((16, 128), 1)
    unplace = jnp.concatenate(
        [((lane16 >> 3) == along_rows) & (((lane16 & 7) >> 1) == u) for u in range(4)], axis=0
    ).astype(jnp.float32).astype(jnp.bfloat16)

    row32 = iota((32, 128), 0)
    lane32 = iota((32, 128), 1)
    parity = row32 & 1
    left_half = lane32 < 64

    def from_rows(fields):
        count = len(fields)
        parts = [split(f) for f in fields]
        stacked = jnp.concatenate([p[0] for p in parts] + [p[1] for p in parts], axis=0)
        moved = fdot(stacked, sel[...]).astype(jnp.bfloat16)
        out = []
        for f in range(count):
            pieces = []
            for part in range(2):
                z = moved[(part * count + f) * 16:(part * count + f) * 16 + 16]
                pieces += [z[:, u * 128:u * 128 + 128] for u in range(4)]
            v = fdot(place, jnp.concatenate(pieces, axis=0))
            tiles = []
            for pair in range(2):
                picked = []
                for odd in range(2):
                    at = (pair * 2 + odd) * 32
                    block = v[at:at + 32]
                    picked.append(jnp.where(parity == odd, block, half_roll(block)))
                tiles.append(jnp.where(left_half, picked[0], picked[1]))
            out.append(jnp.concatenate(tiles, axis=1))
        return out

    def to_rows(values):
        count = len(values)
        highs, lows = [], []
        for value in values:
            blocks = []
            for ij in range(4):
                block = value[:, (ij // 2) * 128:(ij // 2) * 128 + 128]
                block = jnp.where(parity == (ij & 1), block, half_roll(block))
                blocks.append(jnp.where((lane32 >> 6) == parity, block, 0.0))
            high, low = split(jnp.concatenate(blocks, axis=0))
            highs.append(high)
            lows.append(low)
        o = fdot(unplace, jnp.concatenate(highs + lows, axis=1)).astype(jnp.bfloat16)
        rows = []
        for v in range(2 * count):
            rows.append(
                jnp.concatenate(
                    [o[u * 16:u * 16 + 16, v * 128:v * 128 + 128] for u in range(4)], axis=1
                )
            )
        n = lax.dot_general(
            jnp.concatenate(rows, axis=0), sel[...], (((1,), (1,)), ((), ())),
            preferred_element_type=jnp.float32,
        )
        return [
            n[v * 16:v * 16 + 16] + n[(count + v) * 16:(count + v) * 16 + 16]
            for v in range(count)
        ]

    for name in ("smoother", "load", "spread_e", "aei", "re", "edges"):
        c(name)
    s_pad[...] = jnp.zeros((16, 128), jnp.float32)
    s_pad[0:10, 0:10] = c("smoother")[...]
    both_parts = jnp.concatenate(split(s_pad[...]), axis=0)[:, 0:16]
    entries = fdot(both_parts, c("spread_e")[...]).astype(jnp.bfloat16)

    def stacked_entries(entries, at, width, number):
        blocks = [entries[:, at + b * width:at + (b + 1) * width] for b in range(number)]
        return [block[0:16] for block in blocks] + [block[16:32] for block in blocks]

    for axis in range(2):
        wide = fdot(
            c("re")[axis],
            jnp.concatenate(
                stacked_entries(entries, axis * 768, 384, 2) + [c("aei")[axis]], axis=0
            ),
        )
        enc = wide if axis == 0 else enc * wide
    high, low = split(enc)
    e_hi[...] = high
    e_lo[...] = low

    r0, = from_rows([c("load")[...]])

    low_x = (gx == 0).astype(jnp.float32)
    high_x = (gx == nx - 1).astype(jnp.float32)
    low_y = (gy == 0).astype(jnp.float32)
    high_y = (gy == ny - 1).astype(jnp.float32)
    edges = c("edges")[...]
    arrives = (1.0 - edges[0:1] * high_x - edges[1:2] * low_x) * (
        1.0 - edges[2:3] * high_y - edges[3:4] * low_y
    )

    left16 = lane16 < 64
    quarter = (lane16 & 63) >> 4

    pl.semaphore_wait(barrier, len(greeted))

    def exchange_start(stage, value):
        m = right_dot(value, e_hi[...], e_lo[...])
        for pair in range(2):
            t = m[:, pair * 128:pair * 128 + 128]
            top, bottom = t[0:16], t[16:32]
            halo_out[stage, 2 * pair] = jnp.where(left16, top, half_roll(bottom))
            halo_out[stage, 2 * pair + 1] = jnp.where(left16, half_roll(top), bottom)
        t = m[:, 256:384]
        halo_out[stage, 4] = jnp.where(left16, t[0:16], half_roll(t[16:32]))
        copies = []
        for slot, (peer, part) in enumerate(neighbours):
            copy = pltpu.make_async_remote_copy(
                src_ref=halo_out.at[stage, part],
                dst_ref=halo_in.at[stage, slot],
                send_sem=halo_send.at[stage, slot],
                recv_sem=halo_recv.at[stage, slot],
                device_id=peer,
                device_id_type=MESH,
            )
            copy.start()
            copies.append(copy)
        return copies

    def exchange_end(stage, copies):
        for copy in copies:
            copy.wait_recv()
        tiles = []
        for pair in range(2):
            a, b = halo_in[stage, 2 * pair], halo_in[stage, 2 * pair + 1]
            tiles.append(
                jnp.concatenate(
                    [jnp.where(left16, a, half_roll(b)), jnp.where(left16, half_roll(a), b)],
                    axis=0,
                )
            )
        corner = jnp.where(
            quarter == 0, halo_in[stage, 4],
            jnp.where(
                quarter == 1, halo_in[stage, 5],
                jnp.where(quarter == 2, halo_in[stage, 6], halo_in[stage, 7]),
            ),
        )
        tiles.append(jnp.concatenate([corner, half_roll(corner)], axis=0))
        return jnp.concatenate(tiles, axis=1) * arrives

    def sum_round_start(which, at, value):
        sums[which, at, 0] = value
        copies = []
        for d, peer in enumerate(rounds[at]):
            copy = pltpu.make_async_remote_copy(
                src_ref=sums.at[which, at, 0],
                dst_ref=sums.at[which, at, d + 1],
                send_sem=sum_send.at[which, at, d],
                recv_sem=sum_recv.at[which, at, d],
                device_id=peer,
                device_id_type=MESH,
            )
            copy.start()
            copies.append(copy)
        return copies

    def sum_round_end(which, at, copies):
        for copy in copies:
            copy.wait_recv()
        total = sums[which, at, 0]
        for d in range(len(copies)):
            total = total + sums[which, at, d + 1]
        return total

    row8 = iota((8, 128), 0)

    def partial_tile(pairs):
        tile = jnp.zeros((8, 128), jnp.float32)
        for q, products in enumerate(pairs):
            t = local_sum(products)
            for shift in (4, 2, 1):
                t = t + pltpu.roll(t, shift, 0)
            tile = jnp.where(row8 == q, t, tile)
        return tile

    def scalars(total, number):
        column = jnp.sum(total, axis=1, keepdims=True)
        return [column[q:q + 1] for q in range(number)]

    sent = []
    halo = exchange_start(0, r0)
    sent += halo

    for name in ("spread_k", "rvi", "uc", "rzt", "metric", "mass"):
        c(name)
    entries = fdot(both_parts, c("spread_k")[...]).astype(jnp.bfloat16)
    for axis, low_edge, high_edge in ((0, low_x, high_x), (1, low_y, high_y)):
        blocks = stacked_entries(entries, axis * 1024, 256, 4)
        for at in (0, 4):
            blocks[at] = blocks[at] * (1.0 - low_edge).astype(jnp.bfloat16)
            blocks[at + 3] = blocks[at + 3] * (1.0 - high_edge).astype(jnp.bfloat16)
        wide = fdot(c("uc")[axis], jnp.concatenate(blocks + [c("rvi")[axis]], axis=0))
        kxy = wide if axis == 0 else kxy * wide
    high, low = split(kxy)
    k_hi[...] = high
    k_lo[...] = low
    tz = fdot(c("rzt")[...], jnp.concatenate(stacked_entries(entries, 2048, 128, 4), axis=0))
    tz_hi, tz_lo = split(tz[:, 0:96])
    tz = jnp.where(iota((32, 96), 1) < 64, tz_hi.astype(jnp.float32), tz_lo.astype(jnp.float32))
    tz_ref[...] = tz.astype(jnp.bfloat16)

    metric = c("metric")
    m0, m1, m2, mass = from_rows(
        [metric[0], metric[1], metric[2], c("mass")[...]]
    )
    slopes_ref[...] = jnp.concatenate(
        [
            jnp.concatenate([m0[:, :128], m1[:, :128]], axis=1),
            jnp.concatenate([m0[:, 128:], m1[:, 128:]], axis=1),
        ],
        axis=0,
    )

    geometry[0] = m2
    geometry[1] = mass

    def own_part(stage, value):
        own_ref[stage] = right_dot(value, k_hi[0:256], k_lo[0:256])

    def precondition(stage, arrived):
        return left_dot(
            tz_ref[...], own_ref[stage] + right_dot(arrived, k_hi[256:640], k_lo[256:640])
        )

    def slopes(u):
        tall = jnp.concatenate([u[:, :128], u[:, 128:]], axis=0)
        return right_dot(tall, c("dxy_hi")[...], c("dxy_lo")[...]), left_dot(c("dz")[...], u)

    def operate(u, grad):
        slope = slopes_ref[...] * grad[0]
        slope_z = geometry[0] * grad[1]
        tall = right_dot(slope, c("dxyt_hi")[...], c("dxyt_lo")[...])
        return (
            jnp.concatenate([tall[:32], tall[32:]], axis=1)
            + left_dot(c("dzt")[...], slope_z)
            + geometry[1] * u
        )

    def assembled(value, arrived):
        both = jnp.concatenate([value, arrived], axis=1)
        high, low = split(both)
        t = fdot(jnp.concatenate([high, low], axis=0), c("asm")[...])
        t = t[:32] + t[32:]
        high, low = split(t)
        return fdot(c("az")[...], jnp.concatenate([high, low], axis=0))

    own_part(0, r0)
    arrived_r0 = exchange_end(0, halo)
    z0 = precondition(0, arrived_r0)
    w0 = operate(z0, slopes(z0))

    halo = exchange_start(1, w0)
    sent += halo
    ring = sum_round_start(0, 0, partial_tile([[(r0, z0)], [(w0, z0)]]))
    sent += ring
    own_part(1, w0)
    arrived_w0 = exchange_end(1, halo)
    z1 = precondition(1, arrived_w0)
    grad1 = slopes(z1)
    w1 = operate(z1, grad1)
    halo = exchange_start(2, w1)
    sent += halo
    total = sum_round_end(0, 0, ring)
    ring = sum_round_start(0, 1, total)
    sent += ring
    own_part(2, w1)
    for at, value in enumerate(
        to_rows([z0, z1, assembled(r0, arrived_r0), assembled(w0, arrived_w0)])
    ):
        rows_ref[at] = value
    arrived_w1 = exchange_end(2, halo)
    z2 = precondition(2, arrived_w1)
    grad2 = slopes(z2)
    total = sum_round_end(0, 1, ring)
    gamma0, delta0 = scalars(total, 2)
    alpha0 = gamma0 / delta0

    r1 = r0 - alpha0 * w0
    u1 = z0 - alpha0 * z1
    v1 = w0 - alpha0 * w1
    q = z1 - alpha0 * z2
    grad_q = grad1[0] - alpha0 * grad2[0]
    grad_qz = grad1[1] - alpha0 * grad2[1]
    slope_q = slopes_ref[...] * grad_q
    ring = sum_round_start(
        1, 0,
        partial_tile(
            [
                [(r1, u1)], [(v1, u1)], [(v1, q)], [(v1, z1)], [(w0, z1)],
                [
                    (slope_q[:32], grad_q[:32]), (slope_q[32:], grad_q[32:]),
                    (geometry[0] * grad_qz, grad_qz), (geometry[1] * q, q),
                ],
                [(w1, q)], [(w1, z1)],
            ]
        ),
    )
    sent += ring
    w2 = operate(z2, grad2)
    halo = exchange_start(3, w2)
    sent += halo
    for at, value in enumerate(to_rows([z2, assembled(w1, arrived_w1)])):
        rows_ref[4 + at] = value
    total = sum_round_end(1, 0, ring)
    ring = sum_round_start(1, 1, total)
    sent += ring
    arrived_w2 = exchange_end(3, halo)
    rows_w2, = to_rows([assembled(w2, arrived_w2)])
    rows_z0, rows_z1, rows_r0, rows_w0, rows_z2, rows_w1 = [rows_ref[at] for at in range(6)]
    rows_ref[1] = rows_z0 - alpha0 * rows_z1
    rows_ref[4] = rows_z1 - alpha0 * rows_z2
    rows_ref[2] = rows_r0 - alpha0 * rows_w0
    rows_ref[5] = rows_w0 - alpha0 * rows_w1
    rows_ref[6] = rows_w1 - alpha0 * rows_w2
    pressure_ref[...] = rows_z1
    residual_ref[...] = rows_w1
    total = sum_round_end(1, 1, ring)
    gamma1, delta1, vq, vz, wz0, yq, yz, wz1 = scalars(total, 8)

    beta1 = gamma1 / gamma0
    alpha1 = gamma1 / (delta1 - beta1 * gamma1 / alpha0)
    uz = -gamma1 / alpha0
    gamma2 = (
        gamma1 - 2.0 * alpha1 * (delta1 + beta1 * uz)
        + alpha1 * alpha1 * (vq + beta1 * (2.0 * vz + beta1 * wz0))
    )
    delta2 = (
        delta1 - 2.0 * alpha1 * (vq + beta1 * vz)
        + alpha1 * alpha1 * (yq + beta1 * (2.0 * yz + beta1 * wz1))
    )
    beta2 = gamma2 / gamma1
    alpha2 = gamma2 / (delta2 - beta2 * gamma2 / alpha1)
    rows_z0, rows_u1, rows_r1, rows_w0, rows_q, rows_v1, rows_y = [
        rows_ref[at] for at in range(7)
    ]
    rows_p1 = rows_u1 + beta1 * rows_z0
    rows_u2 = rows_u1 - alpha1 * (rows_q + beta1 * pressure_ref[...])
    rows_s1 = rows_v1 + beta1 * rows_w0
    rows_v2 = rows_v1 - alpha1 * (rows_y + beta1 * residual_ref[...])
    pressure_ref[...] = alpha0 * rows_z0 + alpha1 * rows_p1 + alpha2 * (rows_u2 + beta2 * rows_p1)
    residual_ref[...] = rows_r1 - alpha1 * rows_s1 - alpha2 * (rows_v2 + beta2 * rows_s1)
    for copy in sent:
        copy.wait_send()


def solution(mesh):
    nx, ny = mesh.shape["gx"], mesh.shape["gy"]
    lo = 8 if nx % 8 == 0 else 2
    consts = tables()
    vmem = pl.BlockSpec(memory_space=pltpu.VMEM)
    rows = jax.ShapeDtypeStruct((16, 512), jnp.float32)
    longest = max(nx // lo * (ny // 2), 2 * lo)
    shapes = dict(
        consts,
        load=rows,
        metric=jax.ShapeDtypeStruct((3, 16, 512), jnp.float32),
        mass=rows,
        smoother=jax.ShapeDtypeStruct((10, 10), jnp.float32),
        order=jax.ShapeDtypeStruct((16,), jnp.int32),
    )
    call = pl.pallas_call(
        functools.partial(kernel, nx, ny, lo),
        out_shape=(rows, rows),
        in_specs=[pl.BlockSpec(memory_space=pltpu.HBM)] * len(FETCHED),
        out_specs=(vmem, vmem),
        scratch_shapes=[
            (pltpu.SMEM if name == "order" else pltpu.VMEM)(shapes[name].shape, shapes[name].dtype)
            for name in FETCHED
        ]
        + [
            pltpu.SemaphoreType.DMA((len(FETCHED),)),
            pltpu.VMEM((512, 512), jnp.bfloat16),
            pltpu.VMEM((640, 256), jnp.bfloat16),
            pltpu.VMEM((640, 256), jnp.bfloat16),
            pltpu.VMEM((256, 384), jnp.bfloat16),
            pltpu.VMEM((256, 384), jnp.bfloat16),
            pltpu.VMEM((16, 128), jnp.float32),
            pltpu.VMEM((64, 256), jnp.float32),
            pltpu.VMEM((2, 32, 256), jnp.float32),
            pltpu.VMEM((32, 96), jnp.bfloat16),
            pltpu.VMEM((3, 32, 256), jnp.float32),
            pltpu.VMEM((7, 16, 512), jnp.float32),
            pltpu.VMEM((4, 5, 16, 128), jnp.float32),
            pltpu.VMEM((4, 8, 16, 128), jnp.float32),
            pltpu.SemaphoreType.DMA((4, 8)),
            pltpu.SemaphoreType.DMA((4, 8)),
            pltpu.VMEM((2, 2, longest, 8, 128), jnp.float32),
            pltpu.SemaphoreType.DMA((2, 2, longest)),
            pltpu.SemaphoreType.DMA((2, 2, longest)),
        ],
        compiler_params=pltpu.CompilerParams(
            collective_id=0, has_side_effects=True, vmem_limit_bytes=60 * 1024 * 1024
        ),
    )

    def on_device(load_nodes, metric, mass_nodes, smoother, element_order):
        given = dict(
            consts, load=load_nodes, metric=metric.transpose(1, 0, 2), mass=mass_nodes, smoother=smoother,
            order=element_order,
        )
        return call(*[jnp.asarray(given[name]) for name in FETCHED])

    return jax.shard_map(
        on_device,
        mesh=mesh,
        in_specs=(
            P(("gx", "gy"), None),
            P(("gx", "gy"), None, None),
            P(("gx", "gy"), None),
            P(),
            P(("gx", "gy")),
        ),
        out_specs=(P(("gx", "gy"), None), P(("gx", "gy"), None)),
        check_vma=False,
    )
```

```python
import functools

import jax
import jax.numpy as jnp
import ml_dtypes
import numpy as np
from jax import lax
from jax.experimental import pallas as pl
from jax.experimental.pallas import tpu as pltpu
from jax.sharding import PartitionSpec as P

NODES = 8
BF16 = ml_dtypes.bfloat16
MESH = pl.DeviceIdType.MESH


def derivative_table(node_count):
    degree = node_count - 1
    points = np.cos(np.pi * np.arange(node_count) / degree)
    weights = np.ones(node_count)
    weights[0] = 2.0
    weights[-1] = 2.0
    matrix = np.zeros((node_count, node_count))
    for row in range(node_count):
        for col in range(node_count):
            if row != col:
                matrix[row, col] = (
                    weights[row]
                    / weights[col]
                    * (-1.0) ** (row + col)
                    / (points[row] - points[col])
                )
        matrix[row, row] = -np.sum(matrix[row])
    return matrix


def split_const(matrix):
    full = np.asarray(matrix, np.float32)
    high = full.astype(BF16)
    return high, (full - high.astype(np.float32)).astype(BF16)


@functools.lru_cache(None)
def tables():
    node = np.array([7 * i + a for i in range(2) for a in range(8)])
    incidence = {}
    for box in (-1, 0, 1, 2):
        block = np.zeros((10, 16))
        for at in range(16):
            idx = node[at] - 7 * box + 1
            if 0 <= idx < 10:
                block[idx, at] = 1.0
        incidence[box] = block
    uc = np.zeros((24, 4, 16))
    uci = np.zeros((24, 16))
    rv = np.zeros((4, 16, 16))
    rvi = np.zeros((16, 16))
    re = np.zeros((16, 2, 16))
    rei = np.zeros((16, 32))
    ae = np.zeros((2, 16, 24))
    aei = np.zeros((32, 24))
    for at in range(16):
        for slot, box in enumerate((-1, 0, 1, 2)):
            uc[at, slot, :10] = incidence[box][:, at]
            rv[slot, :10, at] = incidence[box][:, at]
        re[at, 0, :10] = incidence[0][:, at]
        re[at, 1, :10] = incidence[1][:, at]
        rei[at, at] = 1.0
        aei[at, at] = 1.0
        for dim, where in enumerate((0, 1, 13, 14)):
            rvi[dim, at] = float(node[at] == where)
            rei[at, 16 + dim] = float(node[at] == where)
    uc[16, 2, 8] = uc[17, 2, 9] = uci[18, 2] = uci[19, 3] = 1.0
    uc[20, 1, 0] = uc[21, 1, 1] = uci[22, 0] = uci[23, 1] = 1.0
    aei[16, 16] = aei[17, 17] = ae[0, 0, 18] = ae[0, 1, 19] = 1.0
    aei[18, 20] = aei[19, 21] = ae[1, 8, 22] = ae[1, 9, 23] = 1.0
    assemble = np.zeros((24, 16))
    assemble[:16] = node[:, None] == node[None, :]
    assemble[16] = node == 14
    assemble[21] = node == 0

    lane = np.arange(256)
    xi = (lane // 128) * 8 + (lane // 8) % 8
    eta = ((lane // 64) % 2) * 8 + lane % 8
    mx, my = [], []
    for side in (16, 20):
        for q in range(4):
            for e in range(16):
                mx.append(side + q)
                my.append(e)
    for side in (16, 20):
        for e in range(16):
            for q in range(4):
                mx.append(e)
                my.append(side + q)
    for sx in (16, 20):
        for sy in (16, 20):
            for qx in range(4):
                for qy in range(4):
                    mx.append(sx + qx)
                    my.append(sy + qy)
    mx, my = np.array(mx), np.array(my)

    def padded(rows, index):
        return np.concatenate([rows[index], np.zeros((64,) + rows.shape[1:])], axis=0)

    allx = np.concatenate([xi, mx])
    ally = np.concatenate([eta, my])
    def kernel_side(index):
        rows = uc.reshape(24, 64)
        return padded(np.concatenate([rows, rows, uci], axis=1), index)

    def sending_side(index):
        rows = re.reshape(16, 32)[index]
        return np.concatenate([rows, rows, rei[index]], axis=1)

    spread_e = [padded(ae[box].T, m).T for m in (mx, my) for box in range(2)]
    spread_k = [rv[box][:, at] for at in (xi, eta) for box in range(4)]
    asm = padded(assemble, allx)[:, xi] * padded(assemble, ally)[:, eta]

    znode = np.array([7 * k + c for k in range(4) for c in range(8)])
    rz = np.zeros((4, 16, 32))
    for block in range(4):
        for at in range(32):
            idx = znode[at] - 7 * block + 1
            if 0 <= idx < 10:
                rz[block, idx, at] = 1.0
    spread_z = [np.concatenate([block] * 4, axis=1) for block in rz]
    rzt = rz.reshape(64, 32).T
    az = (znode[:, None] == znode[None, :]).astype(float)

    d = derivative_table(NODES).astype(np.float32)
    eye8 = np.eye(8)
    dx = np.kron(np.eye(2), np.kron(d.T, eye8))
    dy = np.kron(np.eye(2), np.kron(eye8, d.T))
    dxy_hi, dxy_lo = split_const(np.concatenate([dx, dy], axis=1))
    dz = np.kron(np.eye(4), d)
    dz_hi, dz_lo = split_const(dz)
    dzt_hi, dzt_lo = split_const(dz.T)

    b = lambda m: np.asarray(m, BF16)
    return dict(
        dxy_hi=dxy_hi,
        dxy_lo=dxy_lo,
        dxyt_hi=np.ascontiguousarray(dxy_hi.T),
        dxyt_lo=np.ascontiguousarray(dxy_lo.T),
        dz=np.concatenate([dz_hi, dz_hi, dz_lo], axis=1),
        dzt=np.concatenate([dzt_hi, dzt_hi, dzt_lo], axis=1),
        az=b(np.concatenate([az, az], axis=1)),
        uc=b(np.stack([kernel_side(allx), kernel_side(ally)])),
        rvi=b(np.stack([rvi[:, xi], rvi[:, eta]])),
        re=b(np.stack([sending_side(xi), sending_side(eta)])),
        aei=b(np.stack([padded(aei.T, mx).T, padded(aei.T, my).T])),
        spread_e=b(np.concatenate(spread_e, axis=1)),
        spread_k=b(np.concatenate(spread_k + spread_z, axis=1)),
        rzt=b(np.concatenate([rzt, rzt], axis=1)),
        asm=b(asm),
    )


FETCHED = (
    "order", "smoother", "load", "spread_e", "aei", "re", "spread_k", "rvi", "uc", "rzt",
    "metric", "mass", "dxy_hi", "dxy_lo", "dz", "dxyt_hi", "dxyt_lo", "dzt", "asm", "az",
)


def fdot(left, right):
    return jnp.dot(left, right, preferred_element_type=jnp.float32)


def split(value):
    high = value.astype(jnp.bfloat16)
    low = (value - high.astype(jnp.float32)).astype(jnp.bfloat16)
    return high, low


def right_dot(value, w_hi, w_lo):
    rows = value.shape[0]
    high, low = split(value)
    both = fdot(jnp.concatenate([high, low], axis=0), w_hi)
    return both[:rows] + both[rows:] + fdot(high, w_lo)


def left_dot(stacked, value):
    high, low = split(value)
    return fdot(stacked, jnp.concatenate([high, low, high], axis=0))


def offsets(first, second):
    def far(pair):
        return -min(pair[0], first - pair[0]) - min(pair[1], second - pair[1])

    pairs = [(a, b) for a in range(first) for b in range(second)]
    return sorted(pairs[1:], key=far)


def iota(shape, dim):
    return lax.broadcasted_iota(jnp.int32, shape, dim)


def half_roll(value):
    return pltpu.roll(value, 64, 1)


def local_sum(pairs):
    t = sum(first * second for first, second in pairs)
    t = t[0:8] + t[8:16] + t[16:24] + t[24:32]
    return t[:, :128] + t[:, 128:]


def kernel(
    nx, ny, lo,
    *refs,
):
    count = len(FETCHED)
    far = dict(zip(FETCHED, refs[:count]))
    near = dict(zip(FETCHED, refs[count + 2:2 * count + 2]))
    pressure_ref, residual_ref = refs[count:count + 2]
    (
        fetch_sem, sel, k_hi, k_lo, e_hi, e_lo, s_pad,
        slopes_ref, geometry, tz_ref, own_ref, rows_ref,
        halo_out, halo_in, halo_send, halo_recv,
        plane_in, plane_send, plane_recv, column_in, column_send, column_recv,
    ) = refs[2 * count + 2:]
    gx = lax.axis_index("gx")
    gy = lax.axis_index("gy")
    hi = nx // lo
    x_low, x_high = lax.rem(gx + nx - 1, nx), lax.rem(gx + 1, nx)
    y_low, y_high = lax.rem(gy + ny - 1, ny), lax.rem(gy + 1, ny)
    has_low_x, has_high_x = gx > 0, gx < nx - 1
    has_low_y, has_high_y = gy > 0, gy < ny - 1
    neighbours = (
        ((x_low, gy), 0, has_low_x), ((x_high, gy), 1, has_high_x),
        ((gx, y_low), 2, has_low_y), ((gx, y_high), 3, has_high_y),
        ((x_low, y_low), 4, has_low_x & has_low_y), ((x_low, y_high), 4, has_low_x & has_high_y),
        ((x_high, y_low), 4, has_high_x & has_low_y), ((x_high, y_high), 4, has_high_x & has_high_y),
    )
    filled = [neighbours[at][2] for at in (1, 0, 3, 2, 7, 6, 5, 4)]

    z_at, y_at = lax.rem(gx, lo), lax.div(gx, lo)
    x_at, core = lax.div(gy, 2), lax.rem(gy, 2)
    first_core = core == 0
    plane = [
        (lax.rem(y_at + a, hi) * lo + z_at, lax.rem(x_at + b, ny // 2) * 2)
        for a, b in offsets(hi, ny // 2)
    ]
    plane_from = [
        (lax.rem(y_at + hi - a, hi) * lo + z_at, lax.rem(x_at + ny // 2 - b, ny // 2) * 2)
        for a, b in offsets(hi, ny // 2)
    ]
    column = [(y_at * lo + lax.rem(z_at + a, lo), x_at * 2) for a, _ in offsets(lo, 1)]
    column_from = [(y_at * lo + lax.rem(z_at + lo - a, lo), x_at * 2) for a, _ in offsets(lo, 1)]

    barrier = pltpu.get_barrier_semaphore()

    def greet(peer, is_there=None):
        def signal():
            pl.semaphore_signal(barrier, inc=1, device_id=peer, device_id_type=MESH)

        if is_there is None:
            signal()
        else:
            pl.when(is_there)(signal)

    for peer in column_from:
        greet(peer)
    for peer, _, is_there in neighbours[::-1]:
        greet(peer, is_there)

    @pl.when(first_core)
    def _():
        for peer_x, peer_y in plane_from:
            greet((peer_x, peer_y + 1))
            greet((peer_x, peer_y))
        greet((gx, gy + 1))

    @pl.when(jnp.logical_not(first_core))
    def _():
        greet((gx, gy - 1))

    heard = len(plane) + jnp.where(first_core, 2 * len(column) + 1, 1)
    for _, _, is_there in neighbours:
        heard = heard + is_there.astype(jnp.int32)

    fetches = {}
    for at, name in enumerate(FETCHED):
        fetches[name] = pltpu.make_async_copy(far[name], near[name], fetch_sem.at[at])
        fetches[name].start()

    def c(name):
        if name in fetches:
            fetches.pop(name).wait()
        return near[name]

    col = iota((64, 512), 1)
    for block in range(8):
        at = iota((64, 512), 0) + block * 64
        sel[block * 64:block * 64 + 64] = (
            ((at & 7) * 64 + (at >> 3)) == col
        ).astype(jnp.float32).astype(jnp.bfloat16)

    lane1 = iota((1, 128), 1)
    order_ref = c("order")
    row16 = iota((16, 128), 0)
    along_lanes = jnp.zeros((1, 128), jnp.int32)
    along_rows = jnp.zeros((16, 128), jnp.int32)
    for at in range(16):
        along_lanes = jnp.where((lane1 & 15) == at, order_ref[at], along_lanes)
        along_rows = jnp.where(row16 == at, order_ref[at], along_rows)
    row = iota((128, 128), 0)
    place = (
        ((row >> 3) == along_lanes) & (((row & 7) >> 1) == ((lane1 & 63) >> 4))
    ).astype(jnp.float32).astype(jnp.bfloat16)
    lane16 = iota((16, 128), 1)
    unplace = jnp.concatenate(
        [((lane16 >> 3) == along_rows) & (((lane16 & 7) >> 1) == u) for u in range(4)], axis=0
    ).astype(jnp.float32).astype(jnp.bfloat16)

    row32 = iota((32, 128), 0)
    lane32 = iota((32, 128), 1)
    parity = row32 & 1
    left_half = lane32 < 64

    def from_rows(fields):
        count = len(fields)
        parts = [split(f) for f in fields]
        stacked = jnp.concatenate([p[0] for p in parts] + [p[1] for p in parts], axis=0)
        moved = fdot(stacked, sel[...]).astype(jnp.bfloat16)
        out = []
        for f in range(count):
            pieces = []
            for part in range(2):
                z = moved[(part * count + f) * 16:(part * count + f) * 16 + 16]
                pieces += [z[:, u * 128:u * 128 + 128] for u in range(4)]
            v = fdot(place, jnp.concatenate(pieces, axis=0))
            tiles = []
            for pair in range(2):
                picked = []
                for odd in range(2):
                    at = (pair * 2 + odd) * 32
                    block = v[at:at + 32]
                    picked.append(jnp.where(parity == odd, block, half_roll(block)))
                tiles.append(jnp.where(left_half, picked[0], picked[1]))
            out.append(jnp.concatenate(tiles, axis=1))
        return out

    def to_rows(values):
        count = len(values)
        highs, lows = [], []
        for value in values:
            blocks = []
            for ij in range(4):
                block = value[:, (ij // 2) * 128:(ij // 2) * 128 + 128]
                block = jnp.where(parity == (ij & 1), block, half_roll(block))
                blocks.append(jnp.where((lane32 >> 6) == parity, block, 0.0))
            high, low = split(jnp.concatenate(blocks, axis=0))
            highs.append(high)
            lows.append(low)
        o = fdot(unplace, jnp.concatenate(highs + lows, axis=1)).astype(jnp.bfloat16)
        rows = []
        for v in range(2 * count):
            rows.append(
                jnp.concatenate(
                    [o[u * 16:u * 16 + 16, v * 128:v * 128 + 128] for u in range(4)], axis=1
                )
            )
        n = lax.dot_general(
            jnp.concatenate(rows, axis=0), sel[...], (((1,), (1,)), ((), ())),
            preferred_element_type=jnp.float32,
        )
        return [
            n[v * 16:v * 16 + 16] + n[(count + v) * 16:(count + v) * 16 + 16]
            for v in range(count)
        ]

    for name in ("smoother", "load", "spread_e", "aei", "re"):
        c(name)
    s_pad[...] = jnp.zeros((16, 128), jnp.float32)
    s_pad[0:10, 0:10] = c("smoother")[...]
    both_parts = jnp.concatenate(split(s_pad[...]), axis=0)[:, 0:16]
    entries = fdot(both_parts, c("spread_e")[...]).astype(jnp.bfloat16)

    def stacked_entries(entries, at, width, number):
        blocks = [entries[:, at + b * width:at + (b + 1) * width] for b in range(number)]
        return [block[0:16] for block in blocks] + [block[16:32] for block in blocks]

    for axis in range(2):
        wide = fdot(
            c("re")[axis],
            jnp.concatenate(
                stacked_entries(entries, axis * 768, 384, 2) + [c("aei")[axis]], axis=0
            ),
        )
        enc = wide if axis == 0 else enc * wide
    high, low = split(enc)
    e_hi[...] = high
    e_lo[...] = low

    r0, = from_rows([c("load")[...]])

    low_x = (gx == 0).astype(jnp.float32)
    high_x = (gx == nx - 1).astype(jnp.float32)
    low_y = (gy == 0).astype(jnp.float32)
    high_y = (gy == ny - 1).astype(jnp.float32)
    left16 = lane16 < 64
    quarter = (lane16 & 63) >> 4

    for slot, is_filled in enumerate(filled):
        @pl.when(jnp.logical_not(is_filled))
        def _():
            for stage in range(4):
                halo_in[stage, slot] = jnp.zeros((16, 128), jnp.float32)

    pl.semaphore_wait(barrier, heard)

    sent = []

    def exchange_start(stage, value):
        m = right_dot(value, e_hi[...], e_lo[...])
        for pair in range(2):
            t = m[:, pair * 128:pair * 128 + 128]
            top, bottom = t[0:16], t[16:32]
            halo_out[stage, 2 * pair] = jnp.where(left16, top, half_roll(bottom))
            halo_out[stage, 2 * pair + 1] = jnp.where(left16, half_roll(top), bottom)
        t = m[:, 256:384]
        halo_out[stage, 4] = jnp.where(left16, t[0:16], half_roll(t[16:32]))
        copies = []
        for slot, (peer, part, is_there) in enumerate(neighbours):
            copy = pltpu.make_async_remote_copy(
                src_ref=halo_out.at[stage, part],
                dst_ref=halo_in.at[stage, slot],
                send_sem=halo_send.at[stage, slot],
                recv_sem=halo_recv.at[stage, slot],
                device_id=peer,
                device_id_type=MESH,
            )
            pl.when(is_there)(copy.start)
            copies.append(copy)
            sent.append((copy, is_there))
        return copies

    def exchange_end(stage, copies):
        for copy, is_filled in zip(copies, filled):
            pl.when(is_filled)(copy.wait_recv)
        tiles = []
        for pair in range(2):
            a, b = halo_in[stage, 2 * pair], halo_in[stage, 2 * pair + 1]
            tiles.append(
                jnp.concatenate(
                    [jnp.where(left16, a, half_roll(b)), jnp.where(left16, half_roll(a), b)],
                    axis=0,
                )
            )
        corner = jnp.where(
            quarter == 0, halo_in[stage, 4],
            jnp.where(
                quarter == 1, halo_in[stage, 5],
                jnp.where(quarter == 2, halo_in[stage, 6], halo_in[stage, 7]),
            ),
        )
        tiles.append(jnp.concatenate([corner, half_roll(corner)], axis=0))
        return jnp.concatenate(tiles, axis=1)

    def sum_copy(which, ring, source, slot, out, peer):
        near, send, receive = (
            (plane_in, plane_send, plane_recv) if ring == 0 else (column_in, column_send, column_recv)
        )
        return pltpu.make_async_remote_copy(
            src_ref=source,
            dst_ref=near.at[which, slot],
            send_sem=send.at[which, out],
            recv_sem=receive.at[which, slot],
            device_id=peer,
            device_id_type=MESH,
        )

    own_slot = 2 * len(plane)

    def sum_start(which, value):
        plane_in[which, own_slot] = value
        source = plane_in.at[which, own_slot]
        for at, peer in enumerate(plane):
            copy = sum_copy(which, 0, source, 2 * at + core, at, peer)
            copy.start()
            sent.append((copy, None))
        copy = sum_copy(which, 0, source, own_slot + 1, len(plane), (gx, gy - core))
        pl.when(jnp.logical_not(first_core))(copy.start)
        sent.append((copy, jnp.logical_not(first_core)))

    def sum_middle(which):
        @pl.when(first_core)
        def _():
            for slot in range(own_slot + 2):
                if slot != own_slot:
                    sum_copy(
                        which, 0, plane_in.at[which, own_slot], slot, 0, (gx, gy + 1)
                    ).wait_recv()
            parts = [plane_in[which, slot] for slot in range(own_slot + 2)]
            while len(parts) > 1:
                parts = [sum(parts[at:at + 2]) for at in range(0, len(parts), 2)]
            column_in[which, 0] = parts[0]
            source = column_in.at[which, 0]
            out = 0
            for at, (peer_x, peer_y) in enumerate(column):
                for other in (1, 0):
                    sum_copy(which, 1, source, at + 1, out, (peer_x, peer_y + other)).start()
                    out += 1
            sum_copy(which, 1, source, 0, out, (gx, gy + 1)).start()

    def sum_end(which):
        any_peer = (gx, gy + 1 - 2 * core)
        for at in range(len(column)):
            sum_copy(which, 1, column_in.at[which, 0], at + 1, 0, any_peer).wait_recv()
        own = sum_copy(which, 1, column_in.at[which, 0], 0, 0, any_peer)
        pl.when(jnp.logical_not(first_core))(own.wait_recv)
        parts = [column_in[which, slot] for slot in range(len(column) + 1)]
        while len(parts) > 1:
            parts = [sum(parts[at:at + 2]) for at in range(0, len(parts), 2)]
        return parts[0]

    row8 = iota((8, 128), 0)

    def partial_tile(pairs):
        tile = jnp.zeros((8, 128), jnp.float32)
        for q, products in enumerate(pairs):
            t = local_sum(products)
            for shift in (4, 2, 1):
                t = t + pltpu.roll(t, shift, 0)
            tile = jnp.where(row8 == q, t, tile)
        return tile

    def scalars(total, number):
        column = jnp.sum(total, axis=1, keepdims=True)
        return [column[q:q + 1] for q in range(number)]

    halo = exchange_start(0, r0)

    for name in ("spread_k", "rvi", "uc", "rzt", "metric", "mass"):
        c(name)
    entries = fdot(both_parts, c("spread_k")[...]).astype(jnp.bfloat16)
    for axis, low_edge, high_edge in ((0, low_x, high_x), (1, low_y, high_y)):
        blocks = stacked_entries(entries, axis * 1024, 256, 4)
        for at in (0, 4):
            blocks[at] = blocks[at] * (1.0 - low_edge).astype(jnp.bfloat16)
            blocks[at + 3] = blocks[at + 3] * (1.0 - high_edge).astype(jnp.bfloat16)
        wide = fdot(c("uc")[axis], jnp.concatenate(blocks + [c("rvi")[axis]], axis=0))
        kxy = wide if axis == 0 else kxy * wide
    high, low = split(kxy)
    k_hi[...] = high
    k_lo[...] = low
    tz = fdot(c("rzt")[...], jnp.concatenate(stacked_entries(entries, 2048, 128, 4), axis=0))
    tz_hi, tz_lo = split(tz[:, 0:96])
    tz = jnp.where(iota((32, 96), 1) < 64, tz_hi.astype(jnp.float32), tz_lo.astype(jnp.float32))
    tz_ref[...] = tz.astype(jnp.bfloat16)

    metric = c("metric")
    m0, m1, m2, mass = from_rows(
        [metric[0], metric[1], metric[2], c("mass")[...]]
    )
    slopes_ref[...] = jnp.concatenate(
        [
            jnp.concatenate([m0[:, :128], m1[:, :128]], axis=1),
            jnp.concatenate([m0[:, 128:], m1[:, 128:]], axis=1),
        ],
        axis=0,
    )

    geometry[0] = m2
    geometry[1] = mass

    def own_part(stage, value):
        own_ref[stage] = right_dot(value, k_hi[0:256], k_lo[0:256])

    def precondition(stage, arrived):
        return left_dot(
            tz_ref[...], own_ref[stage] + right_dot(arrived, k_hi[256:640], k_lo[256:640])
        )

    def slopes(u):
        tall = jnp.concatenate([u[:, :128], u[:, 128:]], axis=0)
        return right_dot(tall, c("dxy_hi")[...], c("dxy_lo")[...]), left_dot(c("dz")[...], u)

    def operate(u, grad):
        slope = slopes_ref[...] * grad[0]
        slope_z = geometry[0] * grad[1]
        tall = right_dot(slope, c("dxyt_hi")[...], c("dxyt_lo")[...])
        return (
            jnp.concatenate([tall[:32], tall[32:]], axis=1)
            + left_dot(c("dzt")[...], slope_z)
            + geometry[1] * u
        )

    def assembled(value, arrived):
        both = jnp.concatenate([value, arrived], axis=1)
        high, low = split(both)
        t = fdot(jnp.concatenate([high, low], axis=0), c("asm")[...])
        t = t[:32] + t[32:]
        high, low = split(t)
        return fdot(c("az")[...], jnp.concatenate([high, low], axis=0))

    own_part(0, r0)
    arrived_r0 = exchange_end(0, halo)
    z0 = precondition(0, arrived_r0)
    w0 = operate(z0, slopes(z0))

    halo = exchange_start(1, w0)
    sum_start(0, partial_tile([[(r0, z0)], [(w0, z0)]]))
    own_part(1, w0)
    arrived_w0 = exchange_end(1, halo)
    z1 = precondition(1, arrived_w0)
    grad1 = slopes(z1)
    w1 = operate(z1, grad1)
    halo = exchange_start(2, w1)
    sum_middle(0)
    own_part(2, w1)
    for at, value in enumerate(
        to_rows([z0, z1, assembled(r0, arrived_r0), assembled(w0, arrived_w0)])
    ):
        rows_ref[at] = value
    arrived_w1 = exchange_end(2, halo)
    z2 = precondition(2, arrived_w1)
    grad2 = slopes(z2)
    gamma0, delta0 = scalars(sum_end(0), 2)
    alpha0 = gamma0 / delta0

    r1 = r0 - alpha0 * w0
    u1 = z0 - alpha0 * z1
    v1 = w0 - alpha0 * w1
    q = z1 - alpha0 * z2
    grad_q = grad1[0] - alpha0 * grad2[0]
    grad_qz = grad1[1] - alpha0 * grad2[1]
    slope_q = slopes_ref[...] * grad_q
    sum_start(
        1,
        partial_tile(
            [
                [(r1, u1)], [(v1, u1)], [(v1, q)], [(v1, z1)], [(w0, z1)],
                [
                    (slope_q[:32], grad_q[:32]), (slope_q[32:], grad_q[32:]),
                    (geometry[0] * grad_qz, grad_qz), (geometry[1] * q, q),
                ],
                [(w1, q)], [(w1, z1)],
            ]
        ),
    )
    w2 = operate(z2, grad2)
    halo = exchange_start(3, w2)
    for at, value in enumerate(to_rows([z2, assembled(w1, arrived_w1)])):
        rows_ref[4 + at] = value
    sum_middle(1)
    arrived_w2 = exchange_end(3, halo)
    rows_w2, = to_rows([assembled(w2, arrived_w2)])
    rows_z0, rows_z1, rows_r0, rows_w0, rows_z2, rows_w1 = [rows_ref[at] for at in range(6)]
    rows_ref[1] = rows_z0 - alpha0 * rows_z1
    rows_ref[4] = rows_z1 - alpha0 * rows_z2
    rows_ref[2] = rows_r0 - alpha0 * rows_w0
    rows_ref[5] = rows_w0 - alpha0 * rows_w1
    rows_ref[6] = rows_w1 - alpha0 * rows_w2
    pressure_ref[...] = rows_z1
    residual_ref[...] = rows_w1
    gamma1, delta1, vq, vz, wz0, yq, yz, wz1 = scalars(sum_end(1), 8)

    beta1 = gamma1 / gamma0
    alpha1 = gamma1 / (delta1 - beta1 * gamma1 / alpha0)
    uz = -gamma1 / alpha0
    gamma2 = (
        gamma1 - 2.0 * alpha1 * (delta1 + beta1 * uz)
        + alpha1 * alpha1 * (vq + beta1 * (2.0 * vz + beta1 * wz0))
    )
    delta2 = (
        delta1 - 2.0 * alpha1 * (vq + beta1 * vz)
        + alpha1 * alpha1 * (yq + beta1 * (2.0 * yz + beta1 * wz1))
    )
    beta2 = gamma2 / gamma1
    alpha2 = gamma2 / (delta2 - beta2 * gamma2 / alpha1)
    rows_z0, rows_u1, rows_r1, rows_w0, rows_q, rows_v1, rows_y = [
        rows_ref[at] for at in range(7)
    ]
    rows_p1 = rows_u1 + beta1 * rows_z0
    rows_u2 = rows_u1 - alpha1 * (rows_q + beta1 * pressure_ref[...])
    rows_s1 = rows_v1 + beta1 * rows_w0
    rows_v2 = rows_v1 - alpha1 * (rows_y + beta1 * residual_ref[...])
    pressure_ref[...] = alpha0 * rows_z0 + alpha1 * rows_p1 + alpha2 * (rows_u2 + beta2 * rows_p1)
    residual_ref[...] = rows_r1 - alpha1 * rows_s1 - alpha2 * (rows_v2 + beta2 * rows_s1)
    for copy, is_there in sent:
        if is_there is None:
            copy.wait_send()
        else:
            pl.when(is_there)(copy.wait_send)

    @pl.when(first_core)
    def _():
        for which in range(2):
            for out in range(2 * len(column) + 1):
                sum_copy(
                    which, 1, column_in.at[which, 0], 0, out, (gx, gy + 1)
                ).wait_send()


def solution(mesh):
    nx, ny = mesh.shape["gx"], mesh.shape["gy"]
    lo = 8 if nx % 8 == 0 else 2
    consts = tables()
    vmem = pl.BlockSpec(memory_space=pltpu.VMEM)
    rows = jax.ShapeDtypeStruct((16, 512), jnp.float32)
    chips = nx // lo * (ny // 2)
    shapes = dict(
        consts,
        load=rows,
        metric=jax.ShapeDtypeStruct((3, 16, 512), jnp.float32),
        mass=rows,
        smoother=jax.ShapeDtypeStruct((10, 10), jnp.float32),
        order=jax.ShapeDtypeStruct((16,), jnp.int32),
    )
    call = pl.pallas_call(
        functools.partial(kernel, nx, ny, lo),
        out_shape=(rows, rows),
        in_specs=[pl.BlockSpec(memory_space=pltpu.HBM)] * len(FETCHED),
        out_specs=(vmem, vmem),
        scratch_shapes=[
            (pltpu.SMEM if name == "order" else pltpu.VMEM)(shapes[name].shape, shapes[name].dtype)
            for name in FETCHED
        ]
        + [
            pltpu.SemaphoreType.DMA((len(FETCHED),)),
            pltpu.VMEM((512, 512), jnp.bfloat16),
            pltpu.VMEM((640, 256), jnp.bfloat16),
            pltpu.VMEM((640, 256), jnp.bfloat16),
            pltpu.VMEM((256, 384), jnp.bfloat16),
            pltpu.VMEM((256, 384), jnp.bfloat16),
            pltpu.VMEM((16, 128), jnp.float32),
            pltpu.VMEM((64, 256), jnp.float32),
            pltpu.VMEM((2, 32, 256), jnp.float32),
            pltpu.VMEM((32, 96), jnp.bfloat16),
            pltpu.VMEM((3, 32, 256), jnp.float32),
            pltpu.VMEM((7, 16, 512), jnp.float32),
            pltpu.VMEM((4, 5, 16, 128), jnp.float32),
            pltpu.VMEM((4, 8, 16, 128), jnp.float32),
            pltpu.SemaphoreType.DMA((4, 8)),
            pltpu.SemaphoreType.DMA((4, 8)),
            pltpu.VMEM((2, 2 * chips, 8, 128), jnp.float32),
            pltpu.SemaphoreType.DMA((2, chips)),
            pltpu.SemaphoreType.DMA((2, 2 * chips)),
            pltpu.VMEM((2, lo, 8, 128), jnp.float32),
            pltpu.SemaphoreType.DMA((2, 2 * lo)),
            pltpu.SemaphoreType.DMA((2, lo)),
        ],
        compiler_params=pltpu.CompilerParams(
            collective_id=0, has_side_effects=True, vmem_limit_bytes=60 * 1024 * 1024
        ),
    )

    def on_device(load_nodes, metric, mass_nodes, smoother, element_order):
        given = dict(
            consts, load=load_nodes, metric=metric.transpose(1, 0, 2), mass=mass_nodes, smoother=smoother,
            order=element_order,
        )
        return call(*[jnp.asarray(given[name]) for name in FETCHED])

    return jax.shard_map(
        on_device,
        mesh=mesh,
        in_specs=(
            P(("gx", "gy"), None),
            P(("gx", "gy"), None, None),
            P(("gx", "gy"), None),
            P(),
            P(("gx", "gy")),
        ),
        out_specs=(P(("gx", "gy"), None), P(("gx", "gy"), None)),
        check_vma=False,
    )
```

```python
import functools

import jax
import jax.numpy as jnp
import ml_dtypes
import numpy as np
from jax import lax
from jax.experimental import pallas as pl
from jax.experimental.pallas import tpu as pltpu
from jax.sharding import PartitionSpec as P

NODES = 8
BF16 = ml_dtypes.bfloat16
MESH = pl.DeviceIdType.MESH


def derivative_table(node_count):
    degree = node_count - 1
    points = np.cos(np.pi * np.arange(node_count) / degree)
    weights = np.ones(node_count)
    weights[0] = 2.0
    weights[-1] = 2.0
    matrix = np.zeros((node_count, node_count))
    for row in range(node_count):
        for col in range(node_count):
            if row != col:
                matrix[row, col] = (
                    weights[row]
                    / weights[col]
                    * (-1.0) ** (row + col)
                    / (points[row] - points[col])
                )
        matrix[row, row] = -np.sum(matrix[row])
    return matrix


def split_const(matrix):
    full = np.asarray(matrix, np.float32)
    high = full.astype(BF16)
    return high, (full - high.astype(np.float32)).astype(BF16)


@functools.lru_cache(None)
def tables():
    node = np.array([7 * i + a for i in range(2) for a in range(8)])
    incidence = {}
    for box in (-1, 0, 1, 2):
        block = np.zeros((10, 16))
        for at in range(16):
            idx = node[at] - 7 * box + 1
            if 0 <= idx < 10:
                block[idx, at] = 1.0
        incidence[box] = block
    uc = np.zeros((24, 4, 16))
    uci = np.zeros((24, 16))
    rv = np.zeros((4, 16, 16))
    rvi = np.zeros((16, 16))
    re = np.zeros((16, 2, 16))
    rei = np.zeros((16, 32))
    ae = np.zeros((2, 16, 24))
    aei = np.zeros((32, 24))
    for at in range(16):
        for slot, box in enumerate((-1, 0, 1, 2)):
            uc[at, slot, :10] = incidence[box][:, at]
            rv[slot, :10, at] = incidence[box][:, at]
        re[at, 0, :10] = incidence[0][:, at]
        re[at, 1, :10] = incidence[1][:, at]
        rei[at, at] = 1.0
        aei[at, at] = 1.0
        for dim, where in enumerate((0, 1, 13, 14)):
            rvi[dim, at] = float(node[at] == where)
            rei[at, 16 + dim] = float(node[at] == where)
    uc[16, 2, 8] = uc[17, 2, 9] = uci[18, 2] = uci[19, 3] = 1.0
    uc[20, 1, 0] = uc[21, 1, 1] = uci[22, 0] = uci[23, 1] = 1.0
    aei[16, 16] = aei[17, 17] = ae[0, 0, 18] = ae[0, 1, 19] = 1.0
    aei[18, 20] = aei[19, 21] = ae[1, 8, 22] = ae[1, 9, 23] = 1.0
    assemble = np.zeros((24, 16))
    assemble[:16] = node[:, None] == node[None, :]
    assemble[16] = node == 14
    assemble[21] = node == 0

    lane = np.arange(256)
    xi = (lane // 128) * 8 + (lane // 8) % 8
    eta = ((lane // 64) % 2) * 8 + lane % 8
    mx, my = [], []
    for side in (16, 20):
        for q in range(4):
            for e in range(16):
                mx.append(side + q)
                my.append(e)
    for side in (16, 20):
        for e in range(16):
            for q in range(4):
                mx.append(e)
                my.append(side + q)
    for sx in (16, 20):
        for sy in (16, 20):
            for qx in range(4):
                for qy in range(4):
                    mx.append(sx + qx)
                    my.append(sy + qy)
    mx, my = np.array(mx), np.array(my)

    def padded(rows, index):
        return np.concatenate([rows[index], np.zeros((64,) + rows.shape[1:])], axis=0)

    allx = np.concatenate([xi, mx])
    ally = np.concatenate([eta, my])
    def kernel_side(index):
        rows = uc.reshape(24, 64)
        return padded(np.concatenate([rows, rows, uci], axis=1), index)

    def sending_side(index):
        rows = re.reshape(16, 32)[index]
        return np.concatenate([rows, rows, rei[index]], axis=1)

    spread_e = [padded(ae[box].T, m).T for m in (mx, my) for box in range(2)]
    spread_k = [rv[box][:, at] for at in (xi, eta) for box in range(4)]
    asm = padded(assemble, allx)[:, xi] * padded(assemble, ally)[:, eta]

    znode = np.array([7 * k + c for k in range(4) for c in range(8)])
    rz = np.zeros((4, 16, 32))
    for block in range(4):
        for at in range(32):
            idx = znode[at] - 7 * block + 1
            if 0 <= idx < 10:
                rz[block, idx, at] = 1.0
    spread_z = [np.concatenate([block] * 4, axis=1) for block in rz]
    rzt = rz.reshape(64, 32).T
    az = (znode[:, None] == znode[None, :]).astype(float)

    d = derivative_table(NODES).astype(np.float32)
    eye8 = np.eye(8)
    dx = np.kron(np.eye(2), np.kron(d.T, eye8))
    dy = np.kron(np.eye(2), np.kron(eye8, d.T))
    dxy_hi, dxy_lo = split_const(np.concatenate([dx, dy], axis=1))
    dz = np.kron(np.eye(4), d)
    dz_hi, dz_lo = split_const(dz)
    dzt_hi, dzt_lo = split_const(dz.T)

    b = lambda m: np.asarray(m, BF16)
    return dict(
        dxy_hi=dxy_hi,
        dxy_lo=dxy_lo,
        dxyt_hi=np.ascontiguousarray(dxy_hi.T),
        dxyt_lo=np.ascontiguousarray(dxy_lo.T),
        dz=np.concatenate([dz_hi, dz_hi, dz_lo], axis=1),
        dzt=np.concatenate([dzt_hi, dzt_hi, dzt_lo], axis=1),
        az=b(np.concatenate([az, az], axis=1)),
        uc=b(np.stack([kernel_side(allx), kernel_side(ally)])),
        rvi=b(np.stack([rvi[:, xi], rvi[:, eta]])),
        re=b(np.stack([sending_side(xi), sending_side(eta)])),
        aei=b(np.stack([padded(aei.T, mx).T, padded(aei.T, my).T])),
        spread_e=b(np.concatenate(spread_e, axis=1)),
        spread_k=b(np.concatenate(spread_k + spread_z, axis=1)),
        rzt=b(np.concatenate([rzt, rzt], axis=1)),
        asm=b(asm),
    )


FETCHED = (
    "order", "smoother", "load", "spread_e", "aei", "re", "spread_k", "rvi", "uc", "rzt",
    "metric", "mass", "dxy_hi", "dxy_lo", "dz", "dxyt_hi", "dxyt_lo", "dzt", "asm", "az",
)


def fdot(left, right):
    return jnp.dot(left, right, preferred_element_type=jnp.float32)


def split(value):
    high = value.astype(jnp.bfloat16)
    low = (value - high.astype(jnp.float32)).astype(jnp.bfloat16)
    return high, low


def right_dot(value, w_hi, w_lo):
    rows = value.shape[0]
    high, low = split(value)
    both = fdot(jnp.concatenate([high, low], axis=0), w_hi)
    return both[:rows] + both[rows:] + fdot(high, w_lo)


def left_dot(stacked, value):
    high, low = split(value)
    return fdot(stacked, jnp.concatenate([high, low, high], axis=0))


def offsets(first, second):
    def far(pair):
        return -min(pair[0], first - pair[0]) - min(pair[1], second - pair[1])

    pairs = [(a, b) for a in range(first) for b in range(second)]
    return sorted(pairs[1:], key=far)


def iota(shape, dim):
    return lax.broadcasted_iota(jnp.int32, shape, dim)


def half_roll(value):
    return pltpu.roll(value, 64, 1)


def local_sum(pairs):
    t = sum(first * second for first, second in pairs)
    t = t[0:8] + t[8:16] + t[16:24] + t[24:32]
    return t[:, :128] + t[:, 128:]


def kernel(
    nx, ny, lo,
    *refs,
):
    count = len(FETCHED)
    far = dict(zip(FETCHED, refs[:count]))
    near = dict(zip(FETCHED, refs[count + 2:2 * count + 2]))
    pressure_ref, residual_ref = refs[count:count + 2]
    (
        fetch_sem, sel, k_hi, k_lo, e_hi, e_lo, s_pad,
        slopes_ref, geometry, tz_ref, own_ref, rows_ref,
        halo_out, halo_in, halo_send, halo_recv,
        plane_in, plane_send, plane_recv, column_in, column_send, column_recv,
    ) = refs[2 * count + 2:]
    gx = lax.axis_index("gx")
    gy = lax.axis_index("gy")
    hi = nx // lo
    x_low, x_high = lax.rem(gx + nx - 1, nx), lax.rem(gx + 1, nx)
    y_low, y_high = lax.rem(gy + ny - 1, ny), lax.rem(gy + 1, ny)
    has_low_x, has_high_x = gx > 0, gx < nx - 1
    has_low_y, has_high_y = gy > 0, gy < ny - 1
    neighbours = (
        ((x_low, gy), 0, has_low_x), ((x_high, gy), 1, has_high_x),
        ((gx, y_low), 2, has_low_y), ((gx, y_high), 3, has_high_y),
        ((x_low, y_low), 4, has_low_x & has_low_y), ((x_low, y_high), 4, has_low_x & has_high_y),
        ((x_high, y_low), 4, has_high_x & has_low_y), ((x_high, y_high), 4, has_high_x & has_high_y),
    )
    inside = has_low_x & has_high_x & has_low_y & has_high_y

    def where_there(actions, there):
        @pl.when(inside)
        def _():
            for action in actions:
                action()

        @pl.when(jnp.logical_not(inside))
        def _():
            for action, is_there in zip(actions, there):
                pl.when(is_there)(action)

    filled = [neighbours[at][2] for at in (1, 0, 3, 2, 7, 6, 5, 4)]

    z_at, y_at = lax.rem(gx, lo), lax.div(gx, lo)
    x_at, core = lax.div(gy, 2), lax.rem(gy, 2)
    first_core = core == 0
    plane = [
        (lax.rem(y_at + a, hi) * lo + z_at, lax.rem(x_at + b, ny // 2) * 2)
        for a, b in offsets(hi, ny // 2)
    ]
    plane_from = [
        (lax.rem(y_at + hi - a, hi) * lo + z_at, lax.rem(x_at + ny // 2 - b, ny // 2) * 2)
        for a, b in offsets(hi, ny // 2)
    ]
    column = [(y_at * lo + lax.rem(z_at + a, lo), x_at * 2) for a, _ in offsets(lo, 1)]
    column_from = [(y_at * lo + lax.rem(z_at + lo - a, lo), x_at * 2) for a, _ in offsets(lo, 1)]

    barrier = pltpu.get_barrier_semaphore()

    def greet(peer, is_there=None):
        def signal():
            pl.semaphore_signal(barrier, inc=1, device_id=peer, device_id_type=MESH)

        if is_there is None:
            signal()
        else:
            pl.when(is_there)(signal)

    def greet_plane(peers):
        @pl.when(first_core)
        def _():
            for peer_x, peer_y in peers:
                greet((peer_x, peer_y + 1))
                greet((peer_x, peer_y))

    greet_plane(plane_from[:5])
    for peer in column_from[:3]:
        greet(peer)
    for peer, _, is_there in neighbours[::-1]:
        greet(peer, is_there)
    greet_plane(plane_from[5:])
    for peer in column_from[3:]:
        greet(peer)
    greet((gx, gy + 1 - 2 * core))

    heard = len(plane) + jnp.where(first_core, 2 * len(column) + 1, 1)
    for _, _, is_there in neighbours:
        heard = heard + is_there.astype(jnp.int32)

    fetches = {}
    for at, name in enumerate(FETCHED):
        fetches[name] = pltpu.make_async_copy(far[name], near[name], fetch_sem.at[at])
        fetches[name].start()

    def c(name):
        if name in fetches:
            fetches.pop(name).wait()
        return near[name]

    col = iota((64, 512), 1)
    for block in range(8):
        at = iota((64, 512), 0) + block * 64
        sel[block * 64:block * 64 + 64] = (
            ((at & 7) * 64 + (at >> 3)) == col
        ).astype(jnp.float32).astype(jnp.bfloat16)

    lane1 = iota((1, 128), 1)
    order_ref = c("order")
    row16 = iota((16, 128), 0)
    along_lanes = jnp.zeros((1, 128), jnp.int32)
    along_rows = jnp.zeros((16, 128), jnp.int32)
    for at in range(16):
        along_lanes = jnp.where((lane1 & 15) == at, order_ref[at], along_lanes)
        along_rows = jnp.where(row16 == at, order_ref[at], along_rows)
    row = iota((128, 128), 0)
    place = (
        ((row >> 3) == along_lanes) & (((row & 7) >> 1) == ((lane1 & 63) >> 4))
    ).astype(jnp.float32).astype(jnp.bfloat16)
    lane16 = iota((16, 128), 1)
    unplace = jnp.concatenate(
        [((lane16 >> 3) == along_rows) & (((lane16 & 7) >> 1) == u) for u in range(4)], axis=0
    ).astype(jnp.float32).astype(jnp.bfloat16)

    row32 = iota((32, 128), 0)
    lane32 = iota((32, 128), 1)
    parity = row32 & 1
    left_half = lane32 < 64

    def from_rows(fields):
        count = len(fields)
        parts = [split(f) for f in fields]
        stacked = jnp.concatenate([p[0] for p in parts] + [p[1] for p in parts], axis=0)
        moved = fdot(stacked, sel[...]).astype(jnp.bfloat16)
        out = []
        for f in range(count):
            pieces = []
            for part in range(2):
                z = moved[(part * count + f) * 16:(part * count + f) * 16 + 16]
                pieces += [z[:, u * 128:u * 128 + 128] for u in range(4)]
            v = fdot(place, jnp.concatenate(pieces, axis=0))
            tiles = []
            for pair in range(2):
                picked = []
                for odd in range(2):
                    at = (pair * 2 + odd) * 32
                    block = v[at:at + 32]
                    picked.append(jnp.where(parity == odd, block, half_roll(block)))
                tiles.append(jnp.where(left_half, picked[0], picked[1]))
            out.append(jnp.concatenate(tiles, axis=1))
        return out

    def to_rows(values):
        count = len(values)
        highs, lows = [], []
        for value in values:
            blocks = []
            for ij in range(4):
                block = value[:, (ij // 2) * 128:(ij // 2) * 128 + 128]
                block = jnp.where(parity == (ij & 1), block, half_roll(block))
                blocks.append(jnp.where((lane32 >> 6) == parity, block, 0.0))
            high, low = split(jnp.concatenate(blocks, axis=0))
            highs.append(high)
            lows.append(low)
        o = fdot(unplace, jnp.concatenate(highs + lows, axis=1)).astype(jnp.bfloat16)
        rows = []
        for v in range(2 * count):
            rows.append(
                jnp.concatenate(
                    [o[u * 16:u * 16 + 16, v * 128:v * 128 + 128] for u in range(4)], axis=1
                )
            )
        n = lax.dot_general(
            jnp.concatenate(rows, axis=0), sel[...], (((1,), (1,)), ((), ())),
            preferred_element_type=jnp.float32,
        )
        return [
            n[v * 16:v * 16 + 16] + n[(count + v) * 16:(count + v) * 16 + 16]
            for v in range(count)
        ]

    for name in ("smoother", "load", "spread_e", "aei", "re"):
        c(name)
    s_pad[...] = jnp.zeros((16, 128), jnp.float32)
    s_pad[0:10, 0:10] = c("smoother")[...]
    both_parts = jnp.concatenate(split(s_pad[...]), axis=0)[:, 0:16]
    entries = fdot(both_parts, c("spread_e")[...]).astype(jnp.bfloat16)

    def stacked_entries(entries, at, width, number):
        blocks = [entries[:, at + b * width:at + (b + 1) * width] for b in range(number)]
        return [block[0:16] for block in blocks] + [block[16:32] for block in blocks]

    for axis in range(2):
        wide = fdot(
            c("re")[axis],
            jnp.concatenate(
                stacked_entries(entries, axis * 768, 384, 2) + [c("aei")[axis]], axis=0
            ),
        )
        enc = wide if axis == 0 else enc * wide
    high, low = split(enc)
    e_hi[...] = high
    e_lo[...] = low

    r0, = from_rows([c("load")[...]])

    low_x = (gx == 0).astype(jnp.float32)
    high_x = (gx == nx - 1).astype(jnp.float32)
    low_y = (gy == 0).astype(jnp.float32)
    high_y = (gy == ny - 1).astype(jnp.float32)
    left16 = lane16 < 64
    quarter = (lane16 & 63) >> 4

    for slot, is_filled in enumerate(filled):
        @pl.when(jnp.logical_not(is_filled))
        def _():
            for stage in range(4):
                halo_in[stage, slot] = jnp.zeros((16, 128), jnp.float32)

    pl.semaphore_wait(barrier, heard)

    sent = []
    halos = []

    def exchange_start(stage, value):
        m = right_dot(value, e_hi[...], e_lo[...])
        for pair in range(2):
            t = m[:, pair * 128:pair * 128 + 128]
            top, bottom = t[0:16], t[16:32]
            halo_out[stage, 2 * pair] = jnp.where(left16, top, half_roll(bottom))
            halo_out[stage, 2 * pair + 1] = jnp.where(left16, half_roll(top), bottom)
        t = m[:, 256:384]
        halo_out[stage, 4] = jnp.where(left16, t[0:16], half_roll(t[16:32]))
        copies = []
        for slot in (0, 1, 4, 5, 6, 7, 2, 3):
            peer, part, is_there = neighbours[slot]
            copy = pltpu.make_async_remote_copy(
                src_ref=halo_out.at[stage, part],
                dst_ref=halo_in.at[stage, slot],
                send_sem=halo_send.at[stage, slot],
                recv_sem=halo_recv.at[stage, slot],
                device_id=peer,
                device_id_type=MESH,
            )
            copies.append((copy, is_there, filled[slot]))
        where_there([copy.start for copy, _, _ in copies], [there for _, there, _ in copies])
        halos.extend(copies)
        return copies

    def exchange_end(stage, copies):
        where_there([copy.wait_recv for copy, _, _ in copies], [full for _, _, full in copies])
        tiles = []
        for pair in range(2):
            a, b = halo_in[stage, 2 * pair], halo_in[stage, 2 * pair + 1]
            tiles.append(
                jnp.concatenate(
                    [jnp.where(left16, a, half_roll(b)), jnp.where(left16, half_roll(a), b)],
                    axis=0,
                )
            )
        corner = jnp.where(
            quarter == 0, halo_in[stage, 4],
            jnp.where(
                quarter == 1, halo_in[stage, 5],
                jnp.where(quarter == 2, halo_in[stage, 6], halo_in[stage, 7]),
            ),
        )
        tiles.append(jnp.concatenate([corner, half_roll(corner)], axis=0))
        return jnp.concatenate(tiles, axis=1)

    def sum_copy(which, ring, source, slot, out, peer):
        near, send, receive = (
            (plane_in, plane_send, plane_recv) if ring == 0 else (column_in, column_send, column_recv)
        )
        return pltpu.make_async_remote_copy(
            src_ref=source,
            dst_ref=near.at[which, slot],
            send_sem=send.at[which, out],
            recv_sem=receive.at[which, slot],
            device_id=peer,
            device_id_type=MESH,
        )

    own_slot = 2 * len(plane)

    def sum_start(which, value):
        plane_in[which, own_slot] = value
        source = plane_in.at[which, own_slot]
        for at, peer in enumerate(plane):
            copy = sum_copy(which, 0, source, 2 * at + core, at, peer)
            copy.start()
            sent.append((copy, None))
        copy = sum_copy(which, 0, source, own_slot + 1, len(plane), (gx, gy - core))
        pl.when(jnp.logical_not(first_core))(copy.start)
        sent.append((copy, jnp.logical_not(first_core)))

    def sum_middle(which):
        @pl.when(first_core)
        def _():
            for slot in range(own_slot + 2):
                if slot != own_slot:
                    sum_copy(
                        which, 0, plane_in.at[which, own_slot], slot, 0, (gx, gy + 1)
                    ).wait_recv()
            parts = [plane_in[which, slot] for slot in range(own_slot + 2)]
            while len(parts) > 1:
                parts = [sum(parts[at:at + 2]) for at in range(0, len(parts), 2)]
            column_in[which, 0] = parts[0]
            source = column_in.at[which, 0]
            out = 0
            for at, (peer_x, peer_y) in enumerate(column):
                for other in (1, 0):
                    sum_copy(which, 1, source, at + 1, out, (peer_x, peer_y + other)).start()
                    out += 1
            sum_copy(which, 1, source, 0, out, (gx, gy + 1)).start()

    def sum_end(which):
        any_peer = (gx, gy + 1 - 2 * core)
        for at in range(len(column)):
            sum_copy(which, 1, column_in.at[which, 0], at + 1, 0, any_peer).wait_recv()
        own = sum_copy(which, 1, column_in.at[which, 0], 0, 0, any_peer)
        pl.when(jnp.logical_not(first_core))(own.wait_recv)
        parts = [column_in[which, slot] for slot in range(len(column) + 1)]
        while len(parts) > 1:
            parts = [sum(parts[at:at + 2]) for at in range(0, len(parts), 2)]
        return parts[0]

    row8 = iota((8, 128), 0)

    def partial_tile(pairs):
        tile = jnp.zeros((8, 128), jnp.float32)
        for q, products in enumerate(pairs):
            t = local_sum(products)
            for shift in (4, 2, 1):
                t = t + pltpu.roll(t, shift, 0)
            tile = jnp.where(row8 == q, t, tile)
        return tile

    def scalars(total, number):
        column = jnp.sum(total, axis=1, keepdims=True)
        return [column[q:q + 1] for q in range(number)]

    halo = exchange_start(0, r0)

    for name in ("spread_k", "rvi", "uc", "rzt", "metric", "mass"):
        c(name)
    entries = fdot(both_parts, c("spread_k")[...]).astype(jnp.bfloat16)
    for axis, low_edge, high_edge in ((0, low_x, high_x), (1, low_y, high_y)):
        blocks = stacked_entries(entries, axis * 1024, 256, 4)
        for at in (0, 4):
            blocks[at] = blocks[at] * (1.0 - low_edge).astype(jnp.bfloat16)
            blocks[at + 3] = blocks[at + 3] * (1.0 - high_edge).astype(jnp.bfloat16)
        wide = fdot(c("uc")[axis], jnp.concatenate(blocks + [c("rvi")[axis]], axis=0))
        kxy = wide if axis == 0 else kxy * wide
    high, low = split(kxy)
    k_hi[...] = high
    k_lo[...] = low
    tz = fdot(c("rzt")[...], jnp.concatenate(stacked_entries(entries, 2048, 128, 4), axis=0))
    tz_hi, tz_lo = split(tz[:, 0:96])
    tz = jnp.where(iota((32, 96), 1) < 64, tz_hi.astype(jnp.float32), tz_lo.astype(jnp.float32))
    tz_ref[...] = tz.astype(jnp.bfloat16)

    metric = c("metric")
    m0, m1, m2, mass = from_rows(
        [metric[0], metric[1], metric[2], c("mass")[...]]
    )
    slopes_ref[...] = jnp.concatenate(
        [
            jnp.concatenate([m0[:, :128], m1[:, :128]], axis=1),
            jnp.concatenate([m0[:, 128:], m1[:, 128:]], axis=1),
        ],
        axis=0,
    )

    geometry[0] = m2
    geometry[1] = mass

    def own_part(stage, value):
        own_ref[stage] = right_dot(value, k_hi[0:256], k_lo[0:256])

    def precondition(stage, arrived):
        return left_dot(
            tz_ref[...], own_ref[stage] + right_dot(arrived, k_hi[256:640], k_lo[256:640])
        )

    def slopes(u):
        tall = jnp.concatenate([u[:, :128], u[:, 128:]], axis=0)
        return right_dot(tall, c("dxy_hi")[...], c("dxy_lo")[...]), left_dot(c("dz")[...], u)

    def operate(u, grad):
        slope = slopes_ref[...] * grad[0]
        slope_z = geometry[0] * grad[1]
        tall = right_dot(slope, c("dxyt_hi")[...], c("dxyt_lo")[...])
        return (
            jnp.concatenate([tall[:32], tall[32:]], axis=1)
            + left_dot(c("dzt")[...], slope_z)
            + geometry[1] * u
        )

    def assembled(value, arrived):
        both = jnp.concatenate([value, arrived], axis=1)
        high, low = split(both)
        t = fdot(jnp.concatenate([high, low], axis=0), c("asm")[...])
        t = t[:32] + t[32:]
        high, low = split(t)
        return fdot(c("az")[...], jnp.concatenate([high, low], axis=0))

    own_part(0, r0)
    arrived_r0 = exchange_end(0, halo)
    z0 = precondition(0, arrived_r0)
    w0 = operate(z0, slopes(z0))

    halo = exchange_start(1, w0)
    sum_start(0, partial_tile([[(r0, z0)], [(w0, z0)]]))
    own_part(1, w0)
    arrived_w0 = exchange_end(1, halo)
    z1 = precondition(1, arrived_w0)
    grad1 = slopes(z1)
    w1 = operate(z1, grad1)
    halo = exchange_start(2, w1)
    sum_middle(0)
    own_part(2, w1)
    for at, value in enumerate(
        to_rows([z0, z1, assembled(r0, arrived_r0), assembled(w0, arrived_w0)])
    ):
        rows_ref[at] = value
    arrived_w1 = exchange_end(2, halo)
    z2 = precondition(2, arrived_w1)
    grad2 = slopes(z2)
    gamma0, delta0 = scalars(sum_end(0), 2)
    alpha0 = gamma0 / delta0
    per_gamma0 = 1.0 / gamma0
    per_alpha0 = delta0 / gamma0

    r1 = r0 - alpha0 * w0
    u1 = z0 - alpha0 * z1
    v1 = w0 - alpha0 * w1
    q = z1 - alpha0 * z2
    grad_q = grad1[0] - alpha0 * grad2[0]
    grad_qz = grad1[1] - alpha0 * grad2[1]
    slope_q = slopes_ref[...] * grad_q
    sum_start(
        1,
        partial_tile(
            [
                [(r1, u1)], [(v1, u1)], [(v1, q)], [(v1, z1)], [(w0, z1)],
                [
                    (slope_q[:32], grad_q[:32]), (slope_q[32:], grad_q[32:]),
                    (geometry[0] * grad_qz, grad_qz), (geometry[1] * q, q),
                ],
                [(w1, q)], [(w1, z1)],
            ]
        ),
    )
    w2 = operate(z2, grad2)
    halo = exchange_start(3, w2)
    for at, value in enumerate(to_rows([z2, assembled(w1, arrived_w1)])):
        rows_ref[4 + at] = value
    sum_middle(1)
    arrived_w2 = exchange_end(3, halo)
    rows_w2, = to_rows([assembled(w2, arrived_w2)])
    rows_z0, rows_z1, rows_r0, rows_w0, rows_z2, rows_w1 = [rows_ref[at] for at in range(6)]
    rows_ref[1] = rows_z0 - alpha0 * rows_z1
    rows_ref[4] = rows_z1 - alpha0 * rows_z2
    rows_ref[2] = rows_r0 - alpha0 * rows_w0
    rows_ref[5] = rows_w0 - alpha0 * rows_w1
    rows_ref[6] = rows_w1 - alpha0 * rows_w2
    pressure_ref[...] = rows_z1
    residual_ref[...] = rows_w1
    gamma1, delta1, vq, vz, wz0, yq, yz, wz1 = scalars(sum_end(1), 8)

    beta1 = gamma1 * per_gamma0
    uz = -gamma1 * per_alpha0
    curve1 = delta1 + beta1 * uz
    alpha1 = gamma1 / curve1
    per_gamma1 = 1.0 / gamma1
    gamma2 = (
        gamma1 - 2.0 * alpha1 * (delta1 + beta1 * uz)
        + alpha1 * alpha1 * (vq + beta1 * (2.0 * vz + beta1 * wz0))
    )
    delta2 = (
        delta1 - 2.0 * alpha1 * (vq + beta1 * vz)
        + alpha1 * alpha1 * (yq + beta1 * (2.0 * yz + beta1 * wz1))
    )
    beta2 = gamma2 * per_gamma1
    alpha2 = gamma2 / (delta2 - beta2 * gamma2 * (curve1 * per_gamma1))
    rows_z0, rows_u1, rows_r1, rows_w0, rows_q, rows_v1, rows_y = [
        rows_ref[at] for at in range(7)
    ]
    rows_p1 = rows_u1 + beta1 * rows_z0
    rows_u2 = rows_u1 - alpha1 * (rows_q + beta1 * pressure_ref[...])
    rows_s1 = rows_v1 + beta1 * rows_w0
    rows_v2 = rows_v1 - alpha1 * (rows_y + beta1 * residual_ref[...])
    pressure_ref[...] = alpha0 * rows_z0 + alpha1 * rows_p1 + alpha2 * (rows_u2 + beta2 * rows_p1)
    residual_ref[...] = rows_r1 - alpha1 * rows_s1 - alpha2 * (rows_v2 + beta2 * rows_s1)
    where_there([copy.wait_send for copy, _, _ in halos], [there for _, there, _ in halos])
    for copy, is_there in sent:
        if is_there is None:
            copy.wait_send()
        else:
            pl.when(is_there)(copy.wait_send)

    @pl.when(first_core)
    def _():
        for which in range(2):
            for out in range(2 * len(column) + 1):
                sum_copy(
                    which, 1, column_in.at[which, 0], 0, out, (gx, gy + 1)
                ).wait_send()


def solution(mesh):
    nx, ny = mesh.shape["gx"], mesh.shape["gy"]
    lo = 8 if nx % 8 == 0 else 2
    consts = tables()
    vmem = pl.BlockSpec(memory_space=pltpu.VMEM)
    rows = jax.ShapeDtypeStruct((16, 512), jnp.float32)
    chips = nx // lo * (ny // 2)
    shapes = dict(
        consts,
        load=rows,
        metric=jax.ShapeDtypeStruct((3, 16, 512), jnp.float32),
        mass=rows,
        smoother=jax.ShapeDtypeStruct((10, 10), jnp.float32),
        order=jax.ShapeDtypeStruct((16,), jnp.int32),
    )
    call = pl.pallas_call(
        functools.partial(kernel, nx, ny, lo),
        out_shape=(pltpu.VMEM((16, 512), jnp.float32),) * 2,
        in_specs=[pl.BlockSpec(memory_space=pltpu.HBM)] * len(FETCHED),
        out_specs=(vmem, vmem),
        scratch_shapes=[
            (pltpu.SMEM if name == "order" else pltpu.VMEM)(shapes[name].shape, shapes[name].dtype)
            for name in FETCHED
        ]
        + [
            pltpu.SemaphoreType.DMA((len(FETCHED),)),
            pltpu.VMEM((512, 512), jnp.bfloat16),
            pltpu.VMEM((640, 256), jnp.bfloat16),
            pltpu.VMEM((640, 256), jnp.bfloat16),
            pltpu.VMEM((256, 384), jnp.bfloat16),
            pltpu.VMEM((256, 384), jnp.bfloat16),
            pltpu.VMEM((16, 128), jnp.float32),
            pltpu.VMEM((64, 256), jnp.float32),
            pltpu.VMEM((2, 32, 256), jnp.float32),
            pltpu.VMEM((32, 96), jnp.bfloat16),
            pltpu.VMEM((3, 32, 256), jnp.float32),
            pltpu.VMEM((7, 16, 512), jnp.float32),
            pltpu.VMEM((4, 5, 16, 128), jnp.float32),
            pltpu.VMEM((4, 8, 16, 128), jnp.float32),
            pltpu.SemaphoreType.DMA((4, 8)),
            pltpu.SemaphoreType.DMA((4, 8)),
            pltpu.VMEM((2, 2 * chips, 8, 128), jnp.float32),
            pltpu.SemaphoreType.DMA((2, chips)),
            pltpu.SemaphoreType.DMA((2, 2 * chips)),
            pltpu.VMEM((2, lo, 8, 128), jnp.float32),
            pltpu.SemaphoreType.DMA((2, 2 * lo)),
            pltpu.SemaphoreType.DMA((2, lo)),
        ],
        compiler_params=pltpu.CompilerParams(
            collective_id=0, has_side_effects=True, vmem_limit_bytes=60 * 1024 * 1024
        ),
    )

    def on_device(load_nodes, metric, mass_nodes, smoother, element_order):
        given = dict(
            consts, load=load_nodes, metric=metric.transpose(1, 0, 2), mass=mass_nodes, smoother=smoother,
            order=element_order,
        )
        return call(*[jnp.asarray(given[name]) for name in FETCHED])

    return jax.shard_map(
        on_device,
        mesh=mesh,
        in_specs=(
            P(("gx", "gy"), None),
            P(("gx", "gy"), None, None),
            P(("gx", "gy"), None),
            P(),
            P(("gx", "gy")),
        ),
        out_specs=(P(("gx", "gy"), None), P(("gx", "gy"), None)),
        check_vma=False,
    )
```

```python
import functools

import jax
import jax.numpy as jnp
import ml_dtypes
import numpy as np
from jax import lax
from jax.experimental import pallas as pl
from jax.experimental.pallas import tpu as pltpu
from jax.sharding import PartitionSpec as P

NODES = 8
BF16 = ml_dtypes.bfloat16
MESH = pl.DeviceIdType.MESH


def derivative_table(node_count):
    degree = node_count - 1
    points = np.cos(np.pi * np.arange(node_count) / degree)
    weights = np.ones(node_count)
    weights[0] = 2.0
    weights[-1] = 2.0
    matrix = np.zeros((node_count, node_count))
    for row in range(node_count):
        for col in range(node_count):
            if row != col:
                matrix[row, col] = (
                    weights[row]
                    / weights[col]
                    * (-1.0) ** (row + col)
                    / (points[row] - points[col])
                )
        matrix[row, row] = -np.sum(matrix[row])
    return matrix


def split_const(matrix):
    full = np.asarray(matrix, np.float32)
    high = full.astype(BF16)
    return high, (full - high.astype(np.float32)).astype(BF16)


@functools.lru_cache(None)
def tables():
    node = np.array([7 * i + a for i in range(2) for a in range(8)])
    incidence = {}
    for box in (-1, 0, 1, 2):
        block = np.zeros((10, 16))
        for at in range(16):
            idx = node[at] - 7 * box + 1
            if 0 <= idx < 10:
                block[idx, at] = 1.0
        incidence[box] = block
    uc = np.zeros((24, 4, 16))
    uci = np.zeros((24, 16))
    rv = np.zeros((4, 16, 16))
    rvi = np.zeros((16, 16))
    re = np.zeros((16, 2, 16))
    rei = np.zeros((16, 32))
    ae = np.zeros((2, 16, 24))
    aei = np.zeros((32, 24))
    for at in range(16):
        for slot, box in enumerate((-1, 0, 1, 2)):
            uc[at, slot, :10] = incidence[box][:, at]
            rv[slot, :10, at] = incidence[box][:, at]
        re[at, 0, :10] = incidence[0][:, at]
        re[at, 1, :10] = incidence[1][:, at]
        rei[at, at] = 1.0
        aei[at, at] = 1.0
        for dim, where in enumerate((0, 1, 13, 14)):
            rvi[dim, at] = float(node[at] == where)
            rei[at, 16 + dim] = float(node[at] == where)
    uc[16, 2, 8] = uc[17, 2, 9] = uci[18, 2] = uci[19, 3] = 1.0
    uc[20, 1, 0] = uc[21, 1, 1] = uci[22, 0] = uci[23, 1] = 1.0
    aei[16, 16] = aei[17, 17] = ae[0, 0, 18] = ae[0, 1, 19] = 1.0
    aei[18, 20] = aei[19, 21] = ae[1, 8, 22] = ae[1, 9, 23] = 1.0
    assemble = np.zeros((24, 16))
    assemble[:16] = node[:, None] == node[None, :]
    assemble[16] = node == 14
    assemble[21] = node == 0

    lane = np.arange(256)
    xi = (lane // 128) * 8 + (lane // 8) % 8
    eta = ((lane // 64) % 2) * 8 + lane % 8
    mx, my = [], []
    for side in (16, 20):
        for q in range(4):
            for e in range(16):
                mx.append(side + q)
                my.append(e)
    for side in (16, 20):
        for e in range(16):
            for q in range(4):
                mx.append(e)
                my.append(side + q)
    for sx in (16, 20):
        for sy in (16, 20):
            for qx in range(4):
                for qy in range(4):
                    mx.append(sx + qx)
                    my.append(sy + qy)
    mx, my = np.array(mx), np.array(my)

    def padded(rows, index):
        return np.concatenate([rows[index], np.zeros((64,) + rows.shape[1:])], axis=0)

    allx = np.concatenate([xi, mx])
    ally = np.concatenate([eta, my])
    def kernel_side(index):
        rows = uc.reshape(24, 64)
        return padded(np.concatenate([rows, rows, uci], axis=1), index)

    def sending_side(index):
        rows = re.reshape(16, 32)[index]
        return np.concatenate([rows, rows, rei[index]], axis=1)

    spread_e = [padded(ae[box].T, m).T for m in (mx, my) for box in range(2)]
    spread_k = [rv[box][:, at] for at in (xi, eta) for box in range(4)]
    asm = padded(assemble, allx)[:, xi] * padded(assemble, ally)[:, eta]

    znode = np.array([7 * k + c for k in range(4) for c in range(8)])
    rz = np.zeros((4, 16, 32))
    for block in range(4):
        for at in range(32):
            idx = znode[at] - 7 * block + 1
            if 0 <= idx < 10:
                rz[block, idx, at] = 1.0
    spread_z = [np.concatenate([block] * 4, axis=1) for block in rz]
    rzt = rz.reshape(64, 32).T
    az = (znode[:, None] == znode[None, :]).astype(float)

    d = derivative_table(NODES).astype(np.float32)
    eye8 = np.eye(8)
    dx = np.kron(np.eye(2), np.kron(d.T, eye8))
    dy = np.kron(np.eye(2), np.kron(eye8, d.T))
    dxy_hi, dxy_lo = split_const(np.concatenate([dx, dy], axis=1))
    dz = np.kron(np.eye(4), d)
    dz_hi, dz_lo = split_const(dz)
    dzt_hi, dzt_lo = split_const(dz.T)

    b = lambda m: np.asarray(m, BF16)
    return dict(
        dxy_hi=dxy_hi,
        dxy_lo=dxy_lo,
        dxyt_hi=np.ascontiguousarray(dxy_hi.T),
        dxyt_lo=np.ascontiguousarray(dxy_lo.T),
        dz=np.concatenate([dz_hi, dz_hi, dz_lo], axis=1),
        dzt=np.concatenate([dzt_hi, dzt_hi, dzt_lo], axis=1),
        az=b(np.concatenate([az, az], axis=1)),
        uc=b(np.stack([kernel_side(allx), kernel_side(ally)])),
        rvi=b(np.stack([rvi[:, xi], rvi[:, eta]])),
        re=b(np.stack([sending_side(xi), sending_side(eta)])),
        aei=b(np.stack([padded(aei.T, mx).T, padded(aei.T, my).T])),
        spread_e=b(np.concatenate(spread_e, axis=1)),
        spread_k=b(np.concatenate(spread_k + spread_z, axis=1)),
        rzt=b(np.concatenate([rzt, rzt], axis=1)),
        asm=b(asm),
    )


FETCHED = (
    "order", "smoother", "load", "spread_e", "aei", "re", "spread_k", "rvi", "uc", "rzt",
    "metric", "mass", "dxy_hi", "dxy_lo", "dz", "dxyt_hi", "dxyt_lo", "dzt", "asm", "az",
)


def fdot(left, right):
    return jnp.dot(left, right, preferred_element_type=jnp.float32)


def split(value):
    high = value.astype(jnp.bfloat16)
    low = (value - high.astype(jnp.float32)).astype(jnp.bfloat16)
    return high, low


def right_dot(value, w_hi, w_lo):
    rows = value.shape[0]
    high, low = split(value)
    both = fdot(jnp.concatenate([high, low], axis=0), w_hi)
    return both[:rows] + both[rows:] + fdot(high, w_lo)


def left_dot(stacked, value):
    high, low = split(value)
    return fdot(stacked, jnp.concatenate([high, low, high], axis=0))


def offsets(first, second):
    def far(pair):
        return -min(pair[0], first - pair[0]) - min(pair[1], second - pair[1])

    pairs = [(a, b) for a in range(first) for b in range(second)]
    return sorted(pairs[1:], key=far)


def iota(shape, dim):
    return lax.broadcasted_iota(jnp.int32, shape, dim)


def half_roll(value):
    return pltpu.roll(value, 64, 1)


def local_sum(pairs):
    t = sum(first * second for first, second in pairs)
    t = t[0:8] + t[8:16] + t[16:24] + t[24:32]
    return t[:, :128] + t[:, 128:]


def kernel(
    nx, ny, lo,
    *refs,
):
    count = len(FETCHED)
    far = dict(zip(FETCHED, refs[:count]))
    near = dict(zip(FETCHED, refs[count + 5:2 * count + 5]))
    pressure_ref, residual_ref, direction_ref, image_ref, alpha_ref = refs[count:count + 5]
    (
        fetch_sem, sel, k_hi, k_lo, e_hi, e_lo, s_pad,
        slopes_ref, geometry, tz_ref, own_ref, rows_ref,
        halo_out, halo_in, halo_send, halo_recv,
        plane_in, plane_send, plane_recv, column_in, column_send, column_recv,
    ) = refs[2 * count + 5:]
    gx = lax.axis_index("gx")
    gy = lax.axis_index("gy")
    hi = nx // lo
    x_low, x_high = lax.rem(gx + nx - 1, nx), lax.rem(gx + 1, nx)
    y_low, y_high = lax.rem(gy + ny - 1, ny), lax.rem(gy + 1, ny)
    has_low_x, has_high_x = gx > 0, gx < nx - 1
    has_low_y, has_high_y = gy > 0, gy < ny - 1
    neighbours = (
        ((x_low, gy), 0, has_low_x), ((x_high, gy), 1, has_high_x),
        ((gx, y_low), 2, has_low_y), ((gx, y_high), 3, has_high_y),
        ((x_low, y_low), 4, has_low_x & has_low_y), ((x_low, y_high), 4, has_low_x & has_high_y),
        ((x_high, y_low), 4, has_high_x & has_low_y), ((x_high, y_high), 4, has_high_x & has_high_y),
    )
    inside = has_low_x & has_high_x & has_low_y & has_high_y

    def where_there(actions, there):
        @pl.when(inside)
        def _():
            for action in actions:
                action()

        @pl.when(jnp.logical_not(inside))
        def _():
            for action, is_there in zip(actions, there):
                pl.when(is_there)(action)

    filled = [neighbours[at][2] for at in (1, 0, 3, 2, 7, 6, 5, 4)]

    z_at, y_at = lax.rem(gx, lo), lax.div(gx, lo)
    x_at, core = lax.div(gy, 2), lax.rem(gy, 2)
    first_core = core == 0
    plane = [
        (lax.rem(y_at + a, hi) * lo + z_at, lax.rem(x_at + b, ny // 2) * 2)
        for a, b in offsets(hi, ny // 2)
    ]
    plane_from = [
        (lax.rem(y_at + hi - a, hi) * lo + z_at, lax.rem(x_at + ny // 2 - b, ny // 2) * 2)
        for a, b in offsets(hi, ny // 2)
    ]
    column = [(y_at * lo + lax.rem(z_at + a, lo), x_at * 2) for a, _ in offsets(lo, 1)]
    column_from = [(y_at * lo + lax.rem(z_at + lo - a, lo), x_at * 2) for a, _ in offsets(lo, 1)]

    barrier = pltpu.get_barrier_semaphore()

    def greet(peer, is_there=None):
        def signal():
            pl.semaphore_signal(barrier, inc=1, device_id=peer, device_id_type=MESH)

        if is_there is None:
            signal()
        else:
            pl.when(is_there)(signal)

    def greet_plane(peers):
        @pl.when(first_core)
        def _():
            for peer_x, peer_y in peers:
                greet((peer_x, peer_y + 1))
                greet((peer_x, peer_y))

    greet_plane(plane_from[:5])
    for peer in column_from[:3]:
        greet(peer)
    for peer, _, is_there in neighbours[::-1]:
        greet(peer, is_there)
    greet_plane(plane_from[5:])
    for peer in column_from[3:]:
        greet(peer)
    greet((gx, gy + 1 - 2 * core))

    heard = len(plane) + jnp.where(first_core, 2 * len(column) + 1, 1)
    for _, _, is_there in neighbours:
        heard = heard + is_there.astype(jnp.int32)

    fetches = {}
    for at, name in enumerate(FETCHED):
        fetches[name] = pltpu.make_async_copy(far[name], near[name], fetch_sem.at[at])
        fetches[name].start()

    def c(name):
        if name in fetches:
            fetches.pop(name).wait()
        return near[name]

    col = iota((64, 512), 1)
    for block in range(8):
        at = iota((64, 512), 0) + block * 64
        sel[block * 64:block * 64 + 64] = (
            ((at & 7) * 64 + (at >> 3)) == col
        ).astype(jnp.float32).astype(jnp.bfloat16)

    lane1 = iota((1, 128), 1)
    order_ref = c("order")
    row16 = iota((16, 128), 0)
    along_lanes = jnp.zeros((1, 128), jnp.int32)
    along_rows = jnp.zeros((16, 128), jnp.int32)
    for at in range(16):
        along_lanes = jnp.where((lane1 & 15) == at, order_ref[at], along_lanes)
        along_rows = jnp.where(row16 == at, order_ref[at], along_rows)
    row = iota((128, 128), 0)
    place = (
        ((row >> 3) == along_lanes) & (((row & 7) >> 1) == ((lane1 & 63) >> 4))
    ).astype(jnp.float32).astype(jnp.bfloat16)
    lane16 = iota((16, 128), 1)
    unplace = jnp.concatenate(
        [((lane16 >> 3) == along_rows) & (((lane16 & 7) >> 1) == u) for u in range(4)], axis=0
    ).astype(jnp.float32).astype(jnp.bfloat16)

    row32 = iota((32, 128), 0)
    lane32 = iota((32, 128), 1)
    parity = row32 & 1
    left_half = lane32 < 64

    def from_rows(fields):
        count = len(fields)
        parts = [split(f) for f in fields]
        stacked = jnp.concatenate([p[0] for p in parts] + [p[1] for p in parts], axis=0)
        moved = fdot(stacked, sel[...]).astype(jnp.bfloat16)
        out = []
        for f in range(count):
            pieces = []
            for part in range(2):
                z = moved[(part * count + f) * 16:(part * count + f) * 16 + 16]
                pieces += [z[:, u * 128:u * 128 + 128] for u in range(4)]
            v = fdot(place, jnp.concatenate(pieces, axis=0))
            tiles = []
            for pair in range(2):
                picked = []
                for odd in range(2):
                    at = (pair * 2 + odd) * 32
                    block = v[at:at + 32]
                    picked.append(jnp.where(parity == odd, block, half_roll(block)))
                tiles.append(jnp.where(left_half, picked[0], picked[1]))
            out.append(jnp.concatenate(tiles, axis=1))
        return out

    def to_rows(values):
        count = len(values)
        highs, lows = [], []
        for value in values:
            blocks = []
            for ij in range(4):
                block = value[:, (ij // 2) * 128:(ij // 2) * 128 + 128]
                block = jnp.where(parity == (ij & 1), block, half_roll(block))
                blocks.append(jnp.where((lane32 >> 6) == parity, block, 0.0))
            high, low = split(jnp.concatenate(blocks, axis=0))
            highs.append(high)
            lows.append(low)
        o = fdot(unplace, jnp.concatenate(highs + lows, axis=1)).astype(jnp.bfloat16)
        rows = []
        for v in range(2 * count):
            rows.append(
                jnp.concatenate(
                    [o[u * 16:u * 16 + 16, v * 128:v * 128 + 128] for u in range(4)], axis=1
                )
            )
        n = lax.dot_general(
            jnp.concatenate(rows, axis=0), sel[...], (((1,), (1,)), ((), ())),
            preferred_element_type=jnp.float32,
        )
        return [
            n[v * 16:v * 16 + 16] + n[(count + v) * 16:(count + v) * 16 + 16]
            for v in range(count)
        ]

    for name in ("smoother", "load", "spread_e", "aei", "re"):
        c(name)
    s_pad[...] = jnp.zeros((16, 128), jnp.float32)
    s_pad[0:10, 0:10] = c("smoother")[...]
    both_parts = jnp.concatenate(split(s_pad[...]), axis=0)[:, 0:16]
    entries = fdot(both_parts, c("spread_e")[...]).astype(jnp.bfloat16)

    def stacked_entries(entries, at, width, number):
        blocks = [entries[:, at + b * width:at + (b + 1) * width] for b in range(number)]
        return [block[0:16] for block in blocks] + [block[16:32] for block in blocks]

    for axis in range(2):
        wide = fdot(
            c("re")[axis],
            jnp.concatenate(
                stacked_entries(entries, axis * 768, 384, 2) + [c("aei")[axis]], axis=0
            ),
        )
        enc = wide if axis == 0 else enc * wide
    high, low = split(enc)
    e_hi[...] = high
    e_lo[...] = low

    r0, = from_rows([c("load")[...]])

    low_x = (gx == 0).astype(jnp.float32)
    high_x = (gx == nx - 1).astype(jnp.float32)
    low_y = (gy == 0).astype(jnp.float32)
    high_y = (gy == ny - 1).astype(jnp.float32)
    left16 = lane16 < 64
    quarter = (lane16 & 63) >> 4

    for slot, is_filled in enumerate(filled):
        @pl.when(jnp.logical_not(is_filled))
        def _():
            for stage in range(4):
                halo_in[stage, slot] = jnp.zeros((16, 128), jnp.float32)

    pl.semaphore_wait(barrier, heard)

    sent = []
    halos = []

    def exchange_start(stage, value):
        m = right_dot(value, e_hi[...], e_lo[...])
        for pair in range(2):
            t = m[:, pair * 128:pair * 128 + 128]
            top, bottom = t[0:16], t[16:32]
            halo_out[stage, 2 * pair] = jnp.where(left16, top, half_roll(bottom))
            halo_out[stage, 2 * pair + 1] = jnp.where(left16, half_roll(top), bottom)
        t = m[:, 256:384]
        halo_out[stage, 4] = jnp.where(left16, t[0:16], half_roll(t[16:32]))
        copies = []
        for slot in (0, 1, 4, 5, 6, 7, 2, 3):
            peer, part, is_there = neighbours[slot]
            copy = pltpu.make_async_remote_copy(
                src_ref=halo_out.at[stage, part],
                dst_ref=halo_in.at[stage, slot],
                send_sem=halo_send.at[stage, slot],
                recv_sem=halo_recv.at[stage, slot],
                device_id=peer,
                device_id_type=MESH,
            )
            copies.append((copy, is_there, filled[slot]))
        where_there([copy.start for copy, _, _ in copies], [there for _, there, _ in copies])
        halos.extend(copies)
        return copies

    def exchange_end(stage, copies):
        where_there([copy.wait_recv for copy, _, _ in copies], [full for _, _, full in copies])
        tiles = []
        for pair in range(2):
            a, b = halo_in[stage, 2 * pair], halo_in[stage, 2 * pair + 1]
            tiles.append(
                jnp.concatenate(
                    [jnp.where(left16, a, half_roll(b)), jnp.where(left16, half_roll(a), b)],
                    axis=0,
                )
            )
        corner = jnp.where(
            quarter == 0, halo_in[stage, 4],
            jnp.where(
                quarter == 1, halo_in[stage, 5],
                jnp.where(quarter == 2, halo_in[stage, 6], halo_in[stage, 7]),
            ),
        )
        tiles.append(jnp.concatenate([corner, half_roll(corner)], axis=0))
        return jnp.concatenate(tiles, axis=1)

    def sum_copy(which, ring, source, slot, out, peer):
        near, send, receive = (
            (plane_in, plane_send, plane_recv) if ring == 0 else (column_in, column_send, column_recv)
        )
        return pltpu.make_async_remote_copy(
            src_ref=source,
            dst_ref=near.at[which, slot],
            send_sem=send.at[which, out],
            recv_sem=receive.at[which, slot],
            device_id=peer,
            device_id_type=MESH,
        )

    own_slot = 2 * len(plane)

    def sum_start(which, value):
        plane_in[which, own_slot] = value
        source = plane_in.at[which, own_slot]
        for at, peer in enumerate(plane):
            copy = sum_copy(which, 0, source, 2 * at + core, at, peer)
            copy.start()
            sent.append((copy, None))
        copy = sum_copy(which, 0, source, own_slot + 1, len(plane), (gx, gy - core))
        pl.when(jnp.logical_not(first_core))(copy.start)
        sent.append((copy, jnp.logical_not(first_core)))

    def sum_middle(which):
        @pl.when(first_core)
        def _():
            for slot in range(own_slot + 2):
                if slot != own_slot:
                    sum_copy(
                        which, 0, plane_in.at[which, own_slot], slot, 0, (gx, gy + 1)
                    ).wait_recv()
            parts = [plane_in[which, slot] for slot in range(own_slot + 2)]
            while len(parts) > 1:
                parts = [sum(parts[at:at + 2]) for at in range(0, len(parts), 2)]
            column_in[which, 0] = parts[0]
            source = column_in.at[which, 0]
            out = 0
            for at, (peer_x, peer_y) in enumerate(column):
                for other in (1, 0):
                    sum_copy(which, 1, source, at + 1, out, (peer_x, peer_y + other)).start()
                    out += 1
            sum_copy(which, 1, source, 0, out, (gx, gy + 1)).start()

    def sum_end(which):
        any_peer = (gx, gy + 1 - 2 * core)
        for at in range(len(column)):
            sum_copy(which, 1, column_in.at[which, 0], at + 1, 0, any_peer).wait_recv()
        own = sum_copy(which, 1, column_in.at[which, 0], 0, 0, any_peer)
        pl.when(jnp.logical_not(first_core))(own.wait_recv)
        parts = [column_in[which, slot] for slot in range(len(column) + 1)]
        while len(parts) > 1:
            parts = [sum(parts[at:at + 2]) for at in range(0, len(parts), 2)]
        return parts[0]

    row8 = iota((8, 128), 0)

    def partial_tile(pairs):
        tile = jnp.zeros((8, 128), jnp.float32)
        for q, products in enumerate(pairs):
            t = local_sum(products)
            for shift in (4, 2, 1):
                t = t + pltpu.roll(t, shift, 0)
            tile = jnp.where(row8 == q, t, tile)
        return tile

    def scalars(total, number):
        column = jnp.sum(total, axis=1, keepdims=True)
        return [column[q:q + 1] for q in range(number)]

    halo = exchange_start(0, r0)

    for name in ("spread_k", "rvi", "uc", "rzt", "metric", "mass"):
        c(name)
    entries = fdot(both_parts, c("spread_k")[...]).astype(jnp.bfloat16)
    for axis, low_edge, high_edge in ((0, low_x, high_x), (1, low_y, high_y)):
        blocks = stacked_entries(entries, axis * 1024, 256, 4)
        for at in (0, 4):
            blocks[at] = blocks[at] * (1.0 - low_edge).astype(jnp.bfloat16)
            blocks[at + 3] = blocks[at + 3] * (1.0 - high_edge).astype(jnp.bfloat16)
        wide = fdot(c("uc")[axis], jnp.concatenate(blocks + [c("rvi")[axis]], axis=0))
        kxy = wide if axis == 0 else kxy * wide
    high, low = split(kxy)
    k_hi[...] = high
    k_lo[...] = low
    tz = fdot(c("rzt")[...], jnp.concatenate(stacked_entries(entries, 2048, 128, 4), axis=0))
    tz_hi, tz_lo = split(tz[:, 0:96])
    tz = jnp.where(iota((32, 96), 1) < 64, tz_hi.astype(jnp.float32), tz_lo.astype(jnp.float32))
    tz_ref[...] = tz.astype(jnp.bfloat16)

    metric = c("metric")
    m0, m1, m2, mass = from_rows(
        [metric[0], metric[1], metric[2], c("mass")[...]]
    )
    slopes_ref[...] = jnp.concatenate(
        [
            jnp.concatenate([m0[:, :128], m1[:, :128]], axis=1),
            jnp.concatenate([m0[:, 128:], m1[:, 128:]], axis=1),
        ],
        axis=0,
    )

    geometry[0] = m2
    geometry[1] = mass

    def own_part(stage, value):
        own_ref[stage] = right_dot(value, k_hi[0:256], k_lo[0:256])

    def precondition(stage, arrived):
        return left_dot(
            tz_ref[...], own_ref[stage] + right_dot(arrived, k_hi[256:640], k_lo[256:640])
        )

    def slopes(u):
        tall = jnp.concatenate([u[:, :128], u[:, 128:]], axis=0)
        return right_dot(tall, c("dxy_hi")[...], c("dxy_lo")[...]), left_dot(c("dz")[...], u)

    def operate(u, grad):
        slope = slopes_ref[...] * grad[0]
        slope_z = geometry[0] * grad[1]
        tall = right_dot(slope, c("dxyt_hi")[...], c("dxyt_lo")[...])
        return (
            jnp.concatenate([tall[:32], tall[32:]], axis=1)
            + left_dot(c("dzt")[...], slope_z)
            + geometry[1] * u
        )

    def assembled(value, arrived):
        both = jnp.concatenate([value, arrived], axis=1)
        high, low = split(both)
        t = fdot(jnp.concatenate([high, low], axis=0), c("asm")[...])
        t = t[:32] + t[32:]
        high, low = split(t)
        return fdot(c("az")[...], jnp.concatenate([high, low], axis=0))

    own_part(0, r0)
    arrived_r0 = exchange_end(0, halo)
    z0 = precondition(0, arrived_r0)
    w0 = operate(z0, slopes(z0))

    halo = exchange_start(1, w0)
    sum_start(0, partial_tile([[(r0, z0)], [(w0, z0)]]))
    own_part(1, w0)
    arrived_w0 = exchange_end(1, halo)
    z1 = precondition(1, arrived_w0)
    grad1 = slopes(z1)
    w1 = operate(z1, grad1)
    halo = exchange_start(2, w1)
    sum_middle(0)
    own_part(2, w1)
    for at, value in enumerate(
        to_rows([z0, z1, assembled(r0, arrived_r0), assembled(w0, arrived_w0)])
    ):
        rows_ref[at] = value
    arrived_w1 = exchange_end(2, halo)
    z2 = precondition(2, arrived_w1)
    grad2 = slopes(z2)
    gamma0, delta0 = scalars(sum_end(0), 2)
    alpha0 = gamma0 / delta0
    per_gamma0 = 1.0 / gamma0
    per_alpha0 = delta0 / gamma0

    r1 = r0 - alpha0 * w0
    u1 = z0 - alpha0 * z1
    v1 = w0 - alpha0 * w1
    q = z1 - alpha0 * z2
    grad_q = grad1[0] - alpha0 * grad2[0]
    grad_qz = grad1[1] - alpha0 * grad2[1]
    slope_q = slopes_ref[...] * grad_q
    sum_start(
        1,
        partial_tile(
            [
                [(r1, u1)], [(v1, u1)], [(v1, q)], [(v1, z1)], [(w0, z1)],
                [
                    (slope_q[:32], grad_q[:32]), (slope_q[32:], grad_q[32:]),
                    (geometry[0] * grad_qz, grad_qz), (geometry[1] * q, q),
                ],
                [(w1, q)], [(w1, z1)],
            ]
        ),
    )
    w2 = operate(z2, grad2)
    halo = exchange_start(3, w2)
    for at, value in enumerate(to_rows([z2, assembled(w1, arrived_w1)])):
        rows_ref[4 + at] = value
    sum_middle(1)
    arrived_w2 = exchange_end(3, halo)
    rows_w2, = to_rows([assembled(w2, arrived_w2)])
    rows_z0, rows_z1, rows_r0, rows_w0, rows_z2, rows_w1 = [rows_ref[at] for at in range(6)]
    rows_ref[1] = rows_z0 - alpha0 * rows_z1
    rows_ref[4] = rows_z1 - alpha0 * rows_z2
    rows_ref[2] = rows_r0 - alpha0 * rows_w0
    rows_ref[5] = rows_w0 - alpha0 * rows_w1
    rows_ref[6] = rows_w1 - alpha0 * rows_w2
    pressure_ref[...] = rows_z1
    residual_ref[...] = rows_w1
    gamma1, delta1, vq, vz, wz0, yq, yz, wz1 = scalars(sum_end(1), 8)

    beta1 = gamma1 * per_gamma0
    uz = -gamma1 * per_alpha0
    curve1 = delta1 + beta1 * uz
    alpha1 = gamma1 / curve1
    per_gamma1 = 1.0 / gamma1
    gamma2 = (
        gamma1 - 2.0 * alpha1 * (delta1 + beta1 * uz)
        + alpha1 * alpha1 * (vq + beta1 * (2.0 * vz + beta1 * wz0))
    )
    delta2 = (
        delta1 - 2.0 * alpha1 * (vq + beta1 * vz)
        + alpha1 * alpha1 * (yq + beta1 * (2.0 * yz + beta1 * wz1))
    )
    beta2 = gamma2 * per_gamma1
    alpha2 = gamma2 / (delta2 - beta2 * gamma2 * (curve1 * per_gamma1))
    rows_z0, rows_u1, rows_r1, rows_w0, rows_q, rows_v1, rows_y = [
        rows_ref[at] for at in range(7)
    ]
    rows_p1 = rows_u1 + beta1 * rows_z0
    rows_u2 = rows_u1 - alpha1 * (rows_q + beta1 * pressure_ref[...])
    rows_s1 = rows_v1 + beta1 * rows_w0
    rows_v2 = rows_v1 - alpha1 * (rows_y + beta1 * residual_ref[...])
    pressure_ref[...] = alpha0 * rows_z0 + alpha1 * rows_p1
    residual_ref[...] = rows_r1 - alpha1 * rows_s1
    direction_ref[...] = rows_u2 + beta2 * rows_p1
    image_ref[...] = rows_v2 + beta2 * rows_s1
    alpha_ref[...] = jnp.broadcast_to(alpha2, (1, 512))
    where_there([copy.wait_send for copy, _, _ in halos], [there for _, there, _ in halos])
    for copy, is_there in sent:
        if is_there is None:
            copy.wait_send()
        else:
            pl.when(is_there)(copy.wait_send)

    @pl.when(first_core)
    def _():
        for which in range(2):
            for out in range(2 * len(column) + 1):
                sum_copy(
                    which, 1, column_in.at[which, 0], 0, out, (gx, gy + 1)
                ).wait_send()


def solution(mesh):
    nx, ny = mesh.shape["gx"], mesh.shape["gy"]
    lo = 8 if nx % 8 == 0 else 2
    consts = tables()
    vmem = pl.BlockSpec(memory_space=pltpu.VMEM)
    rows = jax.ShapeDtypeStruct((16, 512), jnp.float32)
    chips = nx // lo * (ny // 2)
    shapes = dict(
        consts,
        load=rows,
        metric=jax.ShapeDtypeStruct((3, 16, 512), jnp.float32),
        mass=rows,
        smoother=jax.ShapeDtypeStruct((10, 10), jnp.float32),
        order=jax.ShapeDtypeStruct((16,), jnp.int32),
    )
    call = pl.pallas_call(
        functools.partial(kernel, nx, ny, lo),
        out_shape=(pltpu.VMEM((16, 512), jnp.float32),) * 4 + (pltpu.VMEM((1, 512), jnp.float32),),
        in_specs=[pl.BlockSpec(memory_space=pltpu.HBM)] * len(FETCHED),
        out_specs=(vmem,) * 5,
        scratch_shapes=[
            (pltpu.SMEM if name == "order" else pltpu.VMEM)(shapes[name].shape, shapes[name].dtype)
            for name in FETCHED
        ]
        + [
            pltpu.SemaphoreType.DMA((len(FETCHED),)),
            pltpu.VMEM((512, 512), jnp.bfloat16),
            pltpu.VMEM((640, 256), jnp.bfloat16),
            pltpu.VMEM((640, 256), jnp.bfloat16),
            pltpu.VMEM((256, 384), jnp.bfloat16),
            pltpu.VMEM((256, 384), jnp.bfloat16),
            pltpu.VMEM((16, 128), jnp.float32),
            pltpu.VMEM((64, 256), jnp.float32),
            pltpu.VMEM((2, 32, 256), jnp.float32),
            pltpu.VMEM((32, 96), jnp.bfloat16),
            pltpu.VMEM((3, 32, 256), jnp.float32),
            pltpu.VMEM((7, 16, 512), jnp.float32),
            pltpu.VMEM((4, 5, 16, 128), jnp.float32),
            pltpu.VMEM((4, 8, 16, 128), jnp.float32),
            pltpu.SemaphoreType.DMA((4, 8)),
            pltpu.SemaphoreType.DMA((4, 8)),
            pltpu.VMEM((2, 2 * chips, 8, 128), jnp.float32),
            pltpu.SemaphoreType.DMA((2, chips)),
            pltpu.SemaphoreType.DMA((2, 2 * chips)),
            pltpu.VMEM((2, lo, 8, 128), jnp.float32),
            pltpu.SemaphoreType.DMA((2, 2 * lo)),
            pltpu.SemaphoreType.DMA((2, lo)),
        ],
        compiler_params=pltpu.CompilerParams(
            collective_id=0, has_side_effects=True, vmem_limit_bytes=60 * 1024 * 1024
        ),
    )

    def on_device(load_nodes, metric, mass_nodes, smoother, element_order):
        given = dict(
            consts, load=load_nodes, metric=metric.transpose(1, 0, 2), mass=mass_nodes, smoother=smoother,
            order=element_order,
        )
        pressure, residual, direction, image, alpha = call(
            *[jnp.asarray(given[name]) for name in FETCHED]
        )
        return pressure + alpha * direction, residual - alpha * image

    return jax.shard_map(
        on_device,
        mesh=mesh,
        in_specs=(
            P(("gx", "gy"), None),
            P(("gx", "gy"), None, None),
            P(("gx", "gy"), None),
            P(),
            P(("gx", "gy")),
        ),
        out_specs=(P(("gx", "gy"), None), P(("gx", "gy"), None)),
        check_vma=False,
    )
```

```python
import functools

import jax
import jax.numpy as jnp
import ml_dtypes
import numpy as np
from jax import lax
from jax.experimental import pallas as pl
from jax.experimental.pallas import tpu as pltpu
from jax.sharding import PartitionSpec as P

NODES = 8
BF16 = ml_dtypes.bfloat16
MESH = pl.DeviceIdType.MESH


def derivative_table(node_count):
    degree = node_count - 1
    points = np.cos(np.pi * np.arange(node_count) / degree)
    weights = np.ones(node_count)
    weights[0] = 2.0
    weights[-1] = 2.0
    matrix = np.zeros((node_count, node_count))
    for row in range(node_count):
        for col in range(node_count):
            if row != col:
                matrix[row, col] = (
                    weights[row]
                    / weights[col]
                    * (-1.0) ** (row + col)
                    / (points[row] - points[col])
                )
        matrix[row, row] = -np.sum(matrix[row])
    return matrix


def split_const(matrix):
    full = np.asarray(matrix, np.float32)
    high = full.astype(BF16)
    return high, (full - high.astype(np.float32)).astype(BF16)


@functools.lru_cache(None)
def tables():
    node = np.array([7 * i + a for i in range(2) for a in range(8)])
    incidence = {}
    for box in (-1, 0, 1, 2):
        block = np.zeros((10, 16))
        for at in range(16):
            idx = node[at] - 7 * box + 1
            if 0 <= idx < 10:
                block[idx, at] = 1.0
        incidence[box] = block
    uc = np.zeros((24, 4, 16))
    uci = np.zeros((24, 16))
    rv = np.zeros((4, 16, 16))
    rvi = np.zeros((16, 16))
    re = np.zeros((16, 2, 16))
    rei = np.zeros((16, 32))
    ae = np.zeros((2, 16, 24))
    aei = np.zeros((32, 24))
    for at in range(16):
        for slot, box in enumerate((-1, 0, 1, 2)):
            uc[at, slot, :10] = incidence[box][:, at]
            rv[slot, :10, at] = incidence[box][:, at]
        re[at, 0, :10] = incidence[0][:, at]
        re[at, 1, :10] = incidence[1][:, at]
        rei[at, at] = 1.0
        aei[at, at] = 1.0
        for dim, where in enumerate((0, 1, 13, 14)):
            rvi[dim, at] = float(node[at] == where)
            rei[at, 16 + dim] = float(node[at] == where)
    uc[16, 2, 8] = uc[17, 2, 9] = uci[18, 2] = uci[19, 3] = 1.0
    uc[20, 1, 0] = uc[21, 1, 1] = uci[22, 0] = uci[23, 1] = 1.0
    aei[16, 16] = aei[17, 17] = ae[0, 0, 18] = ae[0, 1, 19] = 1.0
    aei[18, 20] = aei[19, 21] = ae[1, 8, 22] = ae[1, 9, 23] = 1.0
    assemble = np.zeros((24, 16))
    assemble[:16] = node[:, None] == node[None, :]
    assemble[16] = node == 14
    assemble[21] = node == 0

    lane = np.arange(256)
    xi = (lane // 128) * 8 + (lane // 8) % 8
    eta = ((lane // 64) % 2) * 8 + lane % 8
    mx, my = [], []
    for side in (16, 20):
        for q in range(4):
            for e in range(16):
                mx.append(side + q)
                my.append(e)
    for side in (16, 20):
        for e in range(16):
            for q in range(4):
                mx.append(e)
                my.append(side + q)
    for sx in (16, 20):
        for sy in (16, 20):
            for qx in range(4):
                for qy in range(4):
                    mx.append(sx + qx)
                    my.append(sy + qy)
    mx, my = np.array(mx), np.array(my)

    def padded(rows, index):
        return np.concatenate([rows[index], np.zeros((64,) + rows.shape[1:])], axis=0)

    allx = np.concatenate([xi, mx])
    ally = np.concatenate([eta, my])
    def kernel_side(index):
        rows = uc.reshape(24, 64)
        return padded(np.concatenate([rows, rows, uci], axis=1), index)

    def sending_side(index):
        rows = re.reshape(16, 32)[index]
        return np.concatenate([rows, rows, rei[index]], axis=1)

    spread_e = [padded(ae[box].T, m).T for m in (mx, my) for box in range(2)]
    spread_k = [rv[box][:, at] for at in (xi, eta) for box in range(4)]
    asm = padded(assemble, allx)[:, xi] * padded(assemble, ally)[:, eta]

    znode = np.array([7 * k + c for k in range(4) for c in range(8)])
    rz = np.zeros((4, 16, 32))
    for block in range(4):
        for at in range(32):
            idx = znode[at] - 7 * block + 1
            if 0 <= idx < 10:
                rz[block, idx, at] = 1.0
    spread_z = [np.concatenate([block] * 4, axis=1) for block in rz]
    rzt = rz.reshape(64, 32).T
    az = (znode[:, None] == znode[None, :]).astype(float)

    d = derivative_table(NODES).astype(np.float32)
    eye8 = np.eye(8)
    dx = np.kron(np.eye(2), np.kron(d.T, eye8))
    dy = np.kron(np.eye(2), np.kron(eye8, d.T))
    dxy_hi, dxy_lo = split_const(np.concatenate([dx, dy], axis=1))
    dz = np.kron(np.eye(4), d)
    dz_hi, dz_lo = split_const(dz)
    dzt_hi, dzt_lo = split_const(dz.T)

    b = lambda m: np.asarray(m, BF16)
    return dict(
        dxy_hi=dxy_hi,
        dxy_lo=dxy_lo,
        dxyt_hi=np.ascontiguousarray(dxy_hi.T),
        dxyt_lo=np.ascontiguousarray(dxy_lo.T),
        dz=np.concatenate([dz_hi, dz_hi, dz_lo], axis=1),
        dzt=np.concatenate([dzt_hi, dzt_hi, dzt_lo], axis=1),
        az=b(np.concatenate([az, az], axis=1)),
        uc=b(np.stack([kernel_side(allx), kernel_side(ally)])),
        rvi=b(np.stack([rvi[:, xi], rvi[:, eta]])),
        re=b(np.stack([sending_side(xi), sending_side(eta)])),
        aei=b(np.stack([padded(aei.T, mx).T, padded(aei.T, my).T])),
        spread_e=b(np.concatenate(spread_e, axis=1)),
        spread_k=b(np.concatenate(spread_k + spread_z, axis=1)),
        rzt=b(np.concatenate([rzt, rzt], axis=1)),
        asm=b(asm),
    )


FETCHED = (
    "order", "smoother", "load", "spread_e", "aei", "re", "spread_k", "rvi", "uc", "rzt",
    "metric", "mass", "dxy_hi", "dxy_lo", "dz", "dxyt_hi", "dxyt_lo", "dzt", "asm", "az",
)


def fdot(left, right):
    return jnp.dot(left, right, preferred_element_type=jnp.float32)


def split(value):
    high = value.astype(jnp.bfloat16)
    low = (value - high.astype(jnp.float32)).astype(jnp.bfloat16)
    return high, low


def right_dot(value, w_hi, w_lo):
    rows = value.shape[0]
    high, low = split(value)
    both = fdot(jnp.concatenate([high, low], axis=0), w_hi)
    return both[:rows] + both[rows:] + fdot(high, w_lo)


def left_dot(stacked, value):
    high, low = split(value)
    return fdot(stacked, jnp.concatenate([high, low, high], axis=0))


def offsets(first, second):
    def far(pair):
        return -min(pair[0], first - pair[0]) - min(pair[1], second - pair[1])

    pairs = [(a, b) for a in range(first) for b in range(second)]
    return sorted(pairs[1:], key=far)


def iota(shape, dim):
    return lax.broadcasted_iota(jnp.int32, shape, dim)


def half_roll(value):
    return pltpu.roll(value, 64, 1)


def local_sum(pairs):
    t = sum(first * second for first, second in pairs)
    t = t[0:8] + t[8:16] + t[16:24] + t[24:32]
    return t[:, :128] + t[:, 128:]


def kernel(
    nx, ny, lo,
    *refs,
):
    count = len(FETCHED)
    far = dict(zip(FETCHED, refs[:count]))
    near = dict(zip(FETCHED, refs[count + 5:2 * count + 5]))
    pressure_ref, residual_ref, direction_ref, image_ref, alpha_ref = refs[count:count + 5]
    (
        fetch_sem, sel, k_hi, k_lo, e_hi, e_lo, s_pad,
        slopes_ref, geometry, tz_ref, own_ref, rows_ref,
        halo_out, halo_in, halo_send, halo_recv,
        plane_in, plane_send, plane_recv, column_in, column_send, column_recv,
    ) = refs[2 * count + 5:]
    gx = lax.axis_index("gx")
    gy = lax.axis_index("gy")
    hi = nx // lo
    x_low, x_high = lax.rem(gx + nx - 1, nx), lax.rem(gx + 1, nx)
    y_low, y_high = lax.rem(gy + ny - 1, ny), lax.rem(gy + 1, ny)
    has_low_x, has_high_x = gx > 0, gx < nx - 1
    has_low_y, has_high_y = gy > 0, gy < ny - 1
    neighbours = (
        ((x_low, gy), 0, has_low_x), ((x_high, gy), 1, has_high_x),
        ((gx, y_low), 2, has_low_y), ((gx, y_high), 3, has_high_y),
        ((x_low, y_low), 4, has_low_x & has_low_y), ((x_low, y_high), 4, has_low_x & has_high_y),
        ((x_high, y_low), 4, has_high_x & has_low_y), ((x_high, y_high), 4, has_high_x & has_high_y),
    )
    inside = has_low_x & has_high_x & has_low_y & has_high_y

    def where_there(actions, there):
        @pl.when(inside)
        def _():
            for action in actions:
                action()

        @pl.when(jnp.logical_not(inside))
        def _():
            for action, is_there in zip(actions, there):
                pl.when(is_there)(action)

    filled = [neighbours[at][2] for at in (1, 0, 3, 2, 7, 6, 5, 4)]

    z_at, y_at = lax.rem(gx, lo), lax.div(gx, lo)
    x_at, core = lax.div(gy, 2), lax.rem(gy, 2)
    first_core = core == 0
    plane = [
        (lax.rem(y_at + a, hi) * lo + z_at, lax.rem(x_at + b, ny // 2) * 2)
        for a, b in offsets(hi, ny // 2)
    ]
    plane_from = [
        (lax.rem(y_at + hi - a, hi) * lo + z_at, lax.rem(x_at + ny // 2 - b, ny // 2) * 2)
        for a, b in offsets(hi, ny // 2)
    ]
    column = [(y_at * lo + lax.rem(z_at + a, lo), x_at * 2) for a, _ in offsets(lo, 1)]
    column_from = [(y_at * lo + lax.rem(z_at + lo - a, lo), x_at * 2) for a, _ in offsets(lo, 1)]

    barrier = pltpu.get_barrier_semaphore()

    def greet(peer, is_there=None):
        def signal():
            pl.semaphore_signal(barrier, inc=1, device_id=peer, device_id_type=MESH)

        if is_there is None:
            signal()
        else:
            pl.when(is_there)(signal)

    def greet_plane(peers):
        @pl.when(first_core)
        def _():
            for peer_x, peer_y in peers:
                greet((peer_x, peer_y + 1))
                greet((peer_x, peer_y))

    greet_plane(plane_from[:5])
    for peer in column_from[:3]:
        greet(peer)
    for peer, _, is_there in neighbours[::-1]:
        greet(peer, is_there)
    greet_plane(plane_from[5:])
    for peer in column_from[3:]:
        greet(peer)
    greet((gx, gy + 1 - 2 * core))

    heard = len(plane) + jnp.where(first_core, 2 * len(column) + 1, 1)
    for _, _, is_there in neighbours:
        heard = heard + is_there.astype(jnp.int32)

    fetches = {}
    for at, name in enumerate(FETCHED):
        fetches[name] = pltpu.make_async_copy(far[name], near[name], fetch_sem.at[at])
        fetches[name].start()

    def c(name):
        if name in fetches:
            fetches.pop(name).wait()
        return near[name]

    col = iota((64, 512), 1)
    for block in range(8):
        at = iota((64, 512), 0) + block * 64
        sel[block * 64:block * 64 + 64] = (
            ((at & 7) * 64 + (at >> 3)) == col
        ).astype(jnp.float32).astype(jnp.bfloat16)

    lane1 = iota((1, 128), 1)
    order_ref = c("order")
    row16 = iota((16, 128), 0)
    along_lanes = jnp.zeros((1, 128), jnp.int32)
    along_rows = jnp.zeros((16, 128), jnp.int32)
    for at in range(16):
        along_lanes = jnp.where((lane1 & 15) == at, order_ref[at], along_lanes)
        along_rows = jnp.where(row16 == at, order_ref[at], along_rows)
    row = iota((128, 128), 0)
    place = (
        ((row >> 3) == along_lanes) & (((row & 7) >> 1) == ((lane1 & 63) >> 4))
    ).astype(jnp.float32).astype(jnp.bfloat16)
    lane16 = iota((16, 128), 1)
    unplace = jnp.concatenate(
        [((lane16 >> 3) == along_rows) & (((lane16 & 7) >> 1) == u) for u in range(4)], axis=0
    ).astype(jnp.float32).astype(jnp.bfloat16)

    row32 = iota((32, 128), 0)
    lane32 = iota((32, 128), 1)
    parity = row32 & 1
    left_half = lane32 < 64

    def from_rows(fields):
        count = len(fields)
        parts = [split(f) for f in fields]
        stacked = jnp.concatenate([p[0] for p in parts] + [p[1] for p in parts], axis=0)
        moved = fdot(stacked, sel[...]).astype(jnp.bfloat16)
        out = []
        for f in range(count):
            pieces = []
            for part in range(2):
                z = moved[(part * count + f) * 16:(part * count + f) * 16 + 16]
                pieces += [z[:, u * 128:u * 128 + 128] for u in range(4)]
            v = fdot(place, jnp.concatenate(pieces, axis=0))
            tiles = []
            for pair in range(2):
                picked = []
                for odd in range(2):
                    at = (pair * 2 + odd) * 32
                    block = v[at:at + 32]
                    picked.append(jnp.where(parity == odd, block, half_roll(block)))
                tiles.append(jnp.where(left_half, picked[0], picked[1]))
            out.append(jnp.concatenate(tiles, axis=1))
        return out

    def to_rows(values):
        count = len(values)
        highs, lows = [], []
        for value in values:
            blocks = []
            for ij in range(4):
                block = value[:, (ij // 2) * 128:(ij // 2) * 128 + 128]
                block = jnp.where(parity == (ij & 1), block, half_roll(block))
                blocks.append(jnp.where((lane32 >> 6) == parity, block, 0.0))
            high, low = split(jnp.concatenate(blocks, axis=0))
            highs.append(high)
            lows.append(low)
        o = fdot(unplace, jnp.concatenate(highs + lows, axis=1)).astype(jnp.bfloat16)
        rows = []
        for v in range(2 * count):
            rows.append(
                jnp.concatenate(
                    [o[u * 16:u * 16 + 16, v * 128:v * 128 + 128] for u in range(4)], axis=1
                )
            )
        n = lax.dot_general(
            jnp.concatenate(rows, axis=0), sel[...], (((1,), (1,)), ((), ())),
            preferred_element_type=jnp.float32,
        )
        return [
            n[v * 16:v * 16 + 16] + n[(count + v) * 16:(count + v) * 16 + 16]
            for v in range(count)
        ]

    for name in ("smoother", "load", "spread_e", "aei", "re"):
        c(name)
    s_pad[...] = jnp.zeros((16, 128), jnp.float32)
    s_pad[0:10, 0:10] = c("smoother")[...]
    both_parts = jnp.concatenate(split(s_pad[...]), axis=0)[:, 0:16]
    entries = fdot(both_parts, c("spread_e")[...]).astype(jnp.bfloat16)

    def stacked_entries(entries, at, width, number):
        blocks = [entries[:, at + b * width:at + (b + 1) * width] for b in range(number)]
        return [block[0:16] for block in blocks] + [block[16:32] for block in blocks]

    for axis in range(2):
        wide = fdot(
            c("re")[axis],
            jnp.concatenate(
                stacked_entries(entries, axis * 768, 384, 2) + [c("aei")[axis]], axis=0
            ),
        )
        enc = wide if axis == 0 else enc * wide
    high, low = split(enc)
    e_hi[...] = high
    e_lo[...] = low

    r0, = from_rows([c("load")[...]])

    low_x = (gx == 0).astype(jnp.float32)
    high_x = (gx == nx - 1).astype(jnp.float32)
    low_y = (gy == 0).astype(jnp.float32)
    high_y = (gy == ny - 1).astype(jnp.float32)
    left16 = lane16 < 64
    quarter = (lane16 & 63) >> 4

    for slot, is_filled in enumerate(filled):
        @pl.when(jnp.logical_not(is_filled))
        def _():
            for stage in range(4):
                halo_in[stage, slot] = jnp.zeros((16, 128), jnp.float32)

    pl.semaphore_wait(barrier, heard)

    halos = []

    def exchange_start(stage, value):
        m = right_dot(value, e_hi[...], e_lo[...])
        for pair in range(2):
            t = m[:, pair * 128:pair * 128 + 128]
            top, bottom = t[0:16], t[16:32]
            halo_out[stage, 2 * pair] = jnp.where(left16, top, half_roll(bottom))
            halo_out[stage, 2 * pair + 1] = jnp.where(left16, half_roll(top), bottom)
        t = m[:, 256:384]
        halo_out[stage, 4] = jnp.where(left16, t[0:16], half_roll(t[16:32]))
        copies = []
        for slot in (0, 1, 4, 5, 6, 7, 2, 3):
            peer, part, is_there = neighbours[slot]
            copy = pltpu.make_async_remote_copy(
                src_ref=halo_out.at[stage, part],
                dst_ref=halo_in.at[stage, slot],
                send_sem=halo_send.at[stage, slot],
                recv_sem=halo_recv.at[stage, slot],
                device_id=peer,
                device_id_type=MESH,
            )
            copies.append((copy, is_there, filled[slot]))
        where_there([copy.start for copy, _, _ in copies], [there for _, there, _ in copies])
        halos.extend(copies)
        return copies

    def exchange_end(stage, copies):
        where_there(
            [copy.wait_recv for copy, _, _ in copies[::-1]], [full for _, _, full in copies[::-1]]
        )
        tiles = []
        for pair in range(2):
            a, b = halo_in[stage, 2 * pair], halo_in[stage, 2 * pair + 1]
            tiles.append(
                jnp.concatenate(
                    [jnp.where(left16, a, half_roll(b)), jnp.where(left16, half_roll(a), b)],
                    axis=0,
                )
            )
        corner = jnp.where(
            quarter == 0, halo_in[stage, 4],
            jnp.where(
                quarter == 1, halo_in[stage, 5],
                jnp.where(quarter == 2, halo_in[stage, 6], halo_in[stage, 7]),
            ),
        )
        tiles.append(jnp.concatenate([corner, half_roll(corner)], axis=0))
        return jnp.concatenate(tiles, axis=1)

    others = 2 * len(plane) + 1
    sibling = (gx, gy + 1 - 2 * core)

    def plane_copy(which, target, peer, tiles=1):
        source = plane_in.at[which, pl.ds(others, 1)] if tiles == 1 else target
        return pltpu.make_async_remote_copy(
            src_ref=source,
            dst_ref=target,
            send_sem=plane_send.at[which],
            recv_sem=plane_recv.at[which],
            device_id=peer,
            device_id_type=MESH,
        )

    def column_copy(which, target, peer, tiles=1):
        source = column_in.at[which, pl.ds(0, 1)] if tiles == 1 else target
        return pltpu.make_async_remote_copy(
            src_ref=source,
            dst_ref=target,
            send_sem=column_send.at[which],
            recv_sem=column_recv.at[which],
            device_id=peer,
            device_id_type=MESH,
        )

    def tree_sum(parts):
        while len(parts) > 1:
            parts = [sum(parts[at:at + 2]) for at in range(0, len(parts), 2)]
        return parts[0]

    def sum_start(which, value):
        plane_in[which, others] = value
        for at, peer in enumerate(plane):
            plane_copy(which, plane_in.at[which, pl.ds(2 * at + core, 1)], peer).start()

        @pl.when(jnp.logical_not(first_core))
        def _():
            plane_copy(which, plane_in.at[which, pl.ds(others - 1, 1)], sibling).start()

    def sum_middle(which):
        @pl.when(first_core)
        def _():
            arrived = plane_in.at[which, pl.ds(0, others)]
            plane_copy(which, arrived, sibling, others).wait_recv()
            column_in[which, 0] = tree_sum([plane_in[which, slot] for slot in range(others + 1)])
            for at, (peer_x, peer_y) in enumerate(column):
                for other in (1, 0):
                    target = column_in.at[which, pl.ds(at + 1, 1)]
                    column_copy(which, target, (peer_x, peer_y + other)).start()
            column_copy(which, column_in.at[which, pl.ds(0, 1)], sibling).start()

    def sum_end(which):
        @pl.when(first_core)
        def _():
            arrived = column_in.at[which, pl.ds(1, len(column))]
            column_copy(which, arrived, sibling, len(column)).wait_recv()

        @pl.when(jnp.logical_not(first_core))
        def _():
            arrived = column_in.at[which, pl.ds(0, len(column) + 1)]
            column_copy(which, arrived, sibling, len(column) + 1).wait_recv()

        return tree_sum([column_in[which, slot] for slot in range(len(column) + 1)])

    def plane_sent(which):
        @pl.when(first_core)
        def _():
            leaving = plane_in.at[which, pl.ds(0, len(plane))]
            plane_copy(which, leaving, sibling, len(plane)).wait_send()

        @pl.when(jnp.logical_not(first_core))
        def _():
            leaving = plane_in.at[which, pl.ds(0, len(plane) + 1)]
            plane_copy(which, leaving, sibling, len(plane) + 1).wait_send()

    def column_sent(which):
        @pl.when(first_core)
        def _():
            number = 2 * len(column) + 1
            leaving = plane_in.at[which, pl.ds(0, number)]
            column_copy(which, leaving, sibling, number).wait_send()

    row8 = iota((8, 128), 0)

    def partial_tile(pairs):
        tile = jnp.zeros((8, 128), jnp.float32)
        for q, products in enumerate(pairs):
            t = local_sum(products)
            for shift in (4, 2, 1):
                t = t + pltpu.roll(t, shift, 0)
            tile = jnp.where(row8 == q, t, tile)
        return tile

    def scalars(total, number):
        column = jnp.sum(total, axis=1, keepdims=True)
        return [column[q:q + 1] for q in range(number)]

    halo = exchange_start(0, r0)

    for name in ("spread_k", "rvi", "uc", "rzt", "metric", "mass"):
        c(name)
    entries = fdot(both_parts, c("spread_k")[...]).astype(jnp.bfloat16)
    for axis, low_edge, high_edge in ((0, low_x, high_x), (1, low_y, high_y)):
        blocks = stacked_entries(entries, axis * 1024, 256, 4)
        for at in (0, 4):
            blocks[at] = blocks[at] * (1.0 - low_edge).astype(jnp.bfloat16)
            blocks[at + 3] = blocks[at + 3] * (1.0 - high_edge).astype(jnp.bfloat16)
        wide = fdot(c("uc")[axis], jnp.concatenate(blocks + [c("rvi")[axis]], axis=0))
        kxy = wide if axis == 0 else kxy * wide
    high, low = split(kxy)
    k_hi[...] = high
    k_lo[...] = low
    tz = fdot(c("rzt")[...], jnp.concatenate(stacked_entries(entries, 2048, 128, 4), axis=0))
    tz_hi, tz_lo = split(tz[:, 0:96])
    tz = jnp.where(iota((32, 96), 1) < 64, tz_hi.astype(jnp.float32), tz_lo.astype(jnp.float32))
    tz_ref[...] = tz.astype(jnp.bfloat16)

    metric = c("metric")
    m0, m1, m2, mass = from_rows(
        [metric[0], metric[1], metric[2], c("mass")[...]]
    )
    slopes_ref[...] = jnp.concatenate(
        [
            jnp.concatenate([m0[:, :128], m1[:, :128]], axis=1),
            jnp.concatenate([m0[:, 128:], m1[:, 128:]], axis=1),
        ],
        axis=0,
    )

    geometry[0] = m2
    geometry[1] = mass

    def own_part(stage, value):
        own_ref[stage] = right_dot(value, k_hi[0:256], k_lo[0:256])

    def precondition(stage, arrived):
        return left_dot(
            tz_ref[...], own_ref[stage] + right_dot(arrived, k_hi[256:640], k_lo[256:640])
        )

    def slopes(u):
        tall = jnp.concatenate([u[:, :128], u[:, 128:]], axis=0)
        return right_dot(tall, c("dxy_hi")[...], c("dxy_lo")[...]), left_dot(c("dz")[...], u)

    def operate(u, grad):
        slope = slopes_ref[...] * grad[0]
        slope_z = geometry[0] * grad[1]
        tall = right_dot(slope, c("dxyt_hi")[...], c("dxyt_lo")[...])
        return (
            jnp.concatenate([tall[:32], tall[32:]], axis=1)
            + left_dot(c("dzt")[...], slope_z)
            + geometry[1] * u
        )

    def assembled(value, arrived):
        both = jnp.concatenate([value, arrived], axis=1)
        high, low = split(both)
        t = fdot(jnp.concatenate([high, low], axis=0), c("asm")[...])
        t = t[:32] + t[32:]
        high, low = split(t)
        return fdot(c("az")[...], jnp.concatenate([high, low], axis=0))

    own_part(0, r0)
    arrived_r0 = exchange_end(0, halo)
    z0 = precondition(0, arrived_r0)
    w0 = operate(z0, slopes(z0))

    halo = exchange_start(1, w0)
    sum_start(0, partial_tile([[(r0, z0)], [(w0, z0)]]))
    own_part(1, w0)
    arrived_w0 = exchange_end(1, halo)
    z1 = precondition(1, arrived_w0)
    grad1 = slopes(z1)
    w1 = operate(z1, grad1)
    halo = exchange_start(2, w1)
    sum_middle(0)
    own_part(2, w1)
    for at, value in enumerate(
        to_rows([z0, z1, assembled(r0, arrived_r0), assembled(w0, arrived_w0)])
    ):
        rows_ref[at] = value
    arrived_w1 = exchange_end(2, halo)
    z2 = precondition(2, arrived_w1)
    grad2 = slopes(z2)
    gamma0, delta0 = scalars(sum_end(0), 2)
    alpha0 = gamma0 / delta0
    per_gamma0 = 1.0 / gamma0
    per_alpha0 = delta0 / gamma0

    r1 = r0 - alpha0 * w0
    u1 = z0 - alpha0 * z1
    v1 = w0 - alpha0 * w1
    q = z1 - alpha0 * z2
    grad_q = grad1[0] - alpha0 * grad2[0]
    grad_qz = grad1[1] - alpha0 * grad2[1]
    slope_q = slopes_ref[...] * grad_q
    sum_start(
        1,
        partial_tile(
            [
                [(r1, u1)], [(v1, u1)], [(v1, q)], [(v1, z1)], [(w0, z1)],
                [
                    (slope_q[:32], grad_q[:32]), (slope_q[32:], grad_q[32:]),
                    (geometry[0] * grad_qz, grad_qz), (geometry[1] * q, q),
                ],
                [(w1, q)], [(w1, z1)],
            ]
        ),
    )
    w2 = operate(z2, grad2)
    halo = exchange_start(3, w2)
    for at, value in enumerate(to_rows([z2, assembled(w1, arrived_w1)])):
        rows_ref[4 + at] = value
    sum_middle(1)
    arrived_w2 = exchange_end(3, halo)
    rows_w2, = to_rows([assembled(w2, arrived_w2)])
    rows_z0, rows_z1, rows_r0, rows_w0, rows_z2, rows_w1 = [rows_ref[at] for at in range(6)]
    rows_ref[1] = rows_z0 - alpha0 * rows_z1
    rows_ref[4] = rows_z1 - alpha0 * rows_z2
    rows_ref[2] = rows_r0 - alpha0 * rows_w0
    rows_ref[5] = rows_w0 - alpha0 * rows_w1
    rows_ref[6] = rows_w1 - alpha0 * rows_w2
    pressure_ref[...] = rows_z1
    residual_ref[...] = rows_w1
    where_there([copy.wait_send for copy, _, _ in halos], [there for _, there, _ in halos])
    plane_sent(0)
    plane_sent(1)
    column_sent(0)
    gamma1, delta1, vq, vz, wz0, yq, yz, wz1 = scalars(sum_end(1), 8)

    beta1 = gamma1 * per_gamma0
    uz = -gamma1 * per_alpha0
    curve1 = delta1 + beta1 * uz
    alpha1 = gamma1 / curve1
    per_gamma1 = 1.0 / gamma1
    gamma2 = (
        gamma1 - 2.0 * alpha1 * (delta1 + beta1 * uz)
        + alpha1 * alpha1 * (vq + beta1 * (2.0 * vz + beta1 * wz0))
    )
    delta2 = (
        delta1 - 2.0 * alpha1 * (vq + beta1 * vz)
        + alpha1 * alpha1 * (yq + beta1 * (2.0 * yz + beta1 * wz1))
    )
    beta2 = gamma2 * per_gamma1
    alpha2 = gamma2 / (delta2 - beta2 * gamma2 * (curve1 * per_gamma1))
    rows_z0, rows_u1, rows_r1, rows_w0, rows_q, rows_v1, rows_y = [
        rows_ref[at] for at in range(7)
    ]
    rows_p1 = rows_u1 + beta1 * rows_z0
    rows_u2 = rows_u1 - alpha1 * (rows_q + beta1 * pressure_ref[...])
    rows_s1 = rows_v1 + beta1 * rows_w0
    rows_v2 = rows_v1 - alpha1 * (rows_y + beta1 * residual_ref[...])
    pressure_ref[...] = alpha0 * rows_z0 + alpha1 * rows_p1
    residual_ref[...] = rows_r1 - alpha1 * rows_s1
    direction_ref[...] = rows_u2 + beta2 * rows_p1
    image_ref[...] = rows_v2 + beta2 * rows_s1
    alpha_ref[...] = jnp.broadcast_to(alpha2, (1, 512))
    column_sent(1)


def solution(mesh):
    nx, ny = mesh.shape["gx"], mesh.shape["gy"]
    lo = 8 if nx % 8 == 0 else 2
    consts = tables()
    vmem = pl.BlockSpec(memory_space=pltpu.VMEM)
    rows = jax.ShapeDtypeStruct((16, 512), jnp.float32)
    chips = nx // lo * (ny // 2)
    shapes = dict(
        consts,
        load=rows,
        metric=jax.ShapeDtypeStruct((3, 16, 512), jnp.float32),
        mass=rows,
        smoother=jax.ShapeDtypeStruct((10, 10), jnp.float32),
        order=jax.ShapeDtypeStruct((16,), jnp.int32),
    )
    call = pl.pallas_call(
        functools.partial(kernel, nx, ny, lo),
        out_shape=(pltpu.VMEM((16, 512), jnp.float32),) * 4 + (pltpu.VMEM((1, 512), jnp.float32),),
        in_specs=[pl.BlockSpec(memory_space=pltpu.HBM)] * len(FETCHED),
        out_specs=(vmem,) * 5,
        scratch_shapes=[
            (pltpu.SMEM if name == "order" else pltpu.VMEM)(shapes[name].shape, shapes[name].dtype)
            for name in FETCHED
        ]
        + [
            pltpu.SemaphoreType.DMA((len(FETCHED),)),
            pltpu.VMEM((512, 512), jnp.bfloat16),
            pltpu.VMEM((640, 256), jnp.bfloat16),
            pltpu.VMEM((640, 256), jnp.bfloat16),
            pltpu.VMEM((256, 384), jnp.bfloat16),
            pltpu.VMEM((256, 384), jnp.bfloat16),
            pltpu.VMEM((16, 128), jnp.float32),
            pltpu.VMEM((64, 256), jnp.float32),
            pltpu.VMEM((2, 32, 256), jnp.float32),
            pltpu.VMEM((32, 96), jnp.bfloat16),
            pltpu.VMEM((3, 32, 256), jnp.float32),
            pltpu.VMEM((7, 16, 512), jnp.float32),
            pltpu.VMEM((4, 5, 16, 128), jnp.float32),
            pltpu.VMEM((4, 8, 16, 128), jnp.float32),
            pltpu.SemaphoreType.DMA((4, 8)),
            pltpu.SemaphoreType.DMA((4, 8)),
            pltpu.VMEM((2, 2 * chips, 8, 128), jnp.float32),
            pltpu.SemaphoreType.DMA((2,)),
            pltpu.SemaphoreType.DMA((2,)),
            pltpu.VMEM((2, lo, 8, 128), jnp.float32),
            pltpu.SemaphoreType.DMA((2,)),
            pltpu.SemaphoreType.DMA((2,)),
        ],
        compiler_params=pltpu.CompilerParams(
            collective_id=0, has_side_effects=True, vmem_limit_bytes=60 * 1024 * 1024
        ),
    )

    def on_device(load_nodes, metric, mass_nodes, smoother, element_order):
        given = dict(
            consts, load=load_nodes, metric=metric.transpose(1, 0, 2), mass=mass_nodes, smoother=smoother,
            order=element_order,
        )
        pressure, residual, direction, image, alpha = call(
            *[jnp.asarray(given[name]) for name in FETCHED]
        )
        return pressure + alpha * direction, residual - alpha * image

    return jax.shard_map(
        on_device,
        mesh=mesh,
        in_specs=(
            P(("gx", "gy"), None),
            P(("gx", "gy"), None, None),
            P(("gx", "gy"), None),
            P(),
            P(("gx", "gy")),
        ),
        out_specs=(P(("gx", "gy"), None), P(("gx", "gy"), None)),
        check_vma=False,
    )
```

```python
import functools

import jax
import jax.numpy as jnp
import ml_dtypes
import numpy as np
from jax import lax
from jax.experimental import pallas as pl
from jax.experimental.pallas import tpu as pltpu
from jax.sharding import PartitionSpec as P

NODES = 8
BF16 = ml_dtypes.bfloat16
MESH = pl.DeviceIdType.MESH


def derivative_table(node_count):
    degree = node_count - 1
    points = np.cos(np.pi * np.arange(node_count) / degree)
    weights = np.ones(node_count)
    weights[0] = 2.0
    weights[-1] = 2.0
    matrix = np.zeros((node_count, node_count))
    for row in range(node_count):
        for col in range(node_count):
            if row != col:
                matrix[row, col] = (
                    weights[row]
                    / weights[col]
                    * (-1.0) ** (row + col)
                    / (points[row] - points[col])
                )
        matrix[row, row] = -np.sum(matrix[row])
    return matrix


def split_const(matrix):
    full = np.asarray(matrix, np.float32)
    high = full.astype(BF16)
    return high, (full - high.astype(np.float32)).astype(BF16)


@functools.lru_cache(None)
def tables():
    node = np.array([7 * i + a for i in range(2) for a in range(8)])
    incidence = {}
    for box in (-1, 0, 1, 2):
        block = np.zeros((10, 16))
        for at in range(16):
            idx = node[at] - 7 * box + 1
            if 0 <= idx < 10:
                block[idx, at] = 1.0
        incidence[box] = block
    uc = np.zeros((24, 4, 16))
    uci = np.zeros((24, 16))
    rv = np.zeros((4, 16, 16))
    rvi = np.zeros((16, 16))
    re = np.zeros((16, 2, 16))
    rei = np.zeros((16, 32))
    ae = np.zeros((2, 16, 24))
    aei = np.zeros((32, 24))
    for at in range(16):
        for slot, box in enumerate((-1, 0, 1, 2)):
            uc[at, slot, :10] = incidence[box][:, at]
            rv[slot, :10, at] = incidence[box][:, at]
        re[at, 0, :10] = incidence[0][:, at]
        re[at, 1, :10] = incidence[1][:, at]
        rei[at, at] = 1.0
        aei[at, at] = 1.0
        for dim, where in enumerate((0, 1, 13, 14)):
            rvi[dim, at] = float(node[at] == where)
            rei[at, 16 + dim] = float(node[at] == where)
    uc[16, 2, 8] = uc[17, 2, 9] = uci[18, 2] = uci[19, 3] = 1.0
    uc[20, 1, 0] = uc[21, 1, 1] = uci[22, 0] = uci[23, 1] = 1.0
    aei[16, 16] = aei[17, 17] = ae[0, 0, 18] = ae[0, 1, 19] = 1.0
    aei[18, 20] = aei[19, 21] = ae[1, 8, 22] = ae[1, 9, 23] = 1.0
    assemble = np.zeros((24, 16))
    assemble[:16] = node[:, None] == node[None, :]
    assemble[16] = node == 14
    assemble[21] = node == 0

    lane = np.arange(256)
    xi = (lane // 128) * 8 + (lane // 8) % 8
    eta = ((lane // 64) % 2) * 8 + lane % 8
    mx, my = [], []
    for side in (16, 20):
        for q in range(4):
            for e in range(16):
                mx.append(side + q)
                my.append(e)
    for side in (16, 20):
        for e in range(16):
            for q in range(4):
                mx.append(e)
                my.append(side + q)
    for sx in (16, 20):
        for sy in (16, 20):
            for qx in range(4):
                for qy in range(4):
                    mx.append(sx + qx)
                    my.append(sy + qy)
    mx, my = np.array(mx), np.array(my)

    def padded(rows, index):
        return np.concatenate([rows[index], np.zeros((64,) + rows.shape[1:])], axis=0)

    allx = np.concatenate([xi, mx])
    ally = np.concatenate([eta, my])
    def kernel_side(index):
        rows = uc.reshape(24, 64)
        return padded(np.concatenate([rows, rows, uci], axis=1), index)

    def sending_side(index):
        rows = re.reshape(16, 32)[index]
        return np.concatenate([rows, rows, rei[index]], axis=1)

    spread_e = [padded(ae[box].T, m).T for m in (mx, my) for box in range(2)]
    spread_k = [rv[box][:, at] for at in (xi, eta) for box in range(4)]
    asm = padded(assemble, allx)[:, xi] * padded(assemble, ally)[:, eta]

    znode = np.array([7 * k + c for k in range(4) for c in range(8)])
    rz = np.zeros((4, 16, 32))
    for block in range(4):
        for at in range(32):
            idx = znode[at] - 7 * block + 1
            if 0 <= idx < 10:
                rz[block, idx, at] = 1.0
    spread_z = [np.concatenate([block] * 4, axis=1) for block in rz]
    rzt = rz.reshape(64, 32).T
    az = (znode[:, None] == znode[None, :]).astype(float)

    d = derivative_table(NODES).astype(np.float32)
    eye8 = np.eye(8)
    dx = np.kron(np.eye(2), np.kron(d.T, eye8))
    dy = np.kron(np.eye(2), np.kron(eye8, d.T))
    dxy_hi, dxy_lo = split_const(np.concatenate([dx, dy], axis=1))
    dz = np.kron(np.eye(4), d)
    dz_hi, dz_lo = split_const(dz)
    dzt_hi, dzt_lo = split_const(dz.T)

    b = lambda m: np.asarray(m, BF16)
    return dict(
        dxy_hi=dxy_hi,
        dxy_lo=dxy_lo,
        dxyt_hi=np.ascontiguousarray(dxy_hi.T),
        dxyt_lo=np.ascontiguousarray(dxy_lo.T),
        dz=np.concatenate([dz_hi, dz_hi, dz_lo], axis=1),
        dzt=np.concatenate([dzt_hi, dzt_hi, dzt_lo], axis=1),
        az=b(np.concatenate([az, az], axis=1)),
        uc=b(np.stack([kernel_side(allx), kernel_side(ally)])),
        rvi=b(np.stack([rvi[:, xi], rvi[:, eta]])),
        re=b(np.stack([sending_side(xi), sending_side(eta)])),
        aei=b(np.stack([padded(aei.T, mx).T, padded(aei.T, my).T])),
        spread_e=b(np.concatenate(spread_e, axis=1)),
        spread_k=b(np.concatenate(spread_k + spread_z, axis=1)),
        rzt=b(np.concatenate([rzt, rzt], axis=1)),
        asm=b(asm),
    )


FETCHED = (
    "order", "smoother", "load", "spread_e", "aei", "re", "spread_k", "rvi", "uc", "rzt",
    "metric", "mass", "dxy_hi", "dxy_lo", "dz", "dxyt_hi", "dxyt_lo", "dzt", "asm", "az",
)


def fdot(left, right):
    return jnp.dot(left, right, preferred_element_type=jnp.float32)


def split(value):
    high = value.astype(jnp.bfloat16)
    low = (value - high.astype(jnp.float32)).astype(jnp.bfloat16)
    return high, low


def right_dot(value, w_hi, w_lo):
    rows = value.shape[0]
    high, low = split(value)
    both = fdot(jnp.concatenate([high, low], axis=0), w_hi)
    return both[:rows] + both[rows:] + fdot(high, w_lo)


def left_dot(stacked, value):
    high, low = split(value)
    return fdot(stacked, jnp.concatenate([high, low, high], axis=0))


def offsets(first, second):
    def far(pair):
        return -min(pair[0], first - pair[0]) - min(pair[1], second - pair[1])

    pairs = [(a, b) for a in range(first) for b in range(second)]
    return sorted(pairs[1:], key=far)


def iota(shape, dim):
    return lax.broadcasted_iota(jnp.int32, shape, dim)


def half_roll(value):
    return pltpu.roll(value, 64, 1)


def local_sum(pairs):
    t = sum(first * second for first, second in pairs)
    t = t[0:8] + t[8:16] + t[16:24] + t[24:32]
    return t[:, :128] + t[:, 128:]


def kernel(
    nx, ny, lo,
    *refs,
):
    count = len(FETCHED)
    far = dict(zip(FETCHED, refs[:count]))
    near = dict(zip(FETCHED, refs[count + 5:2 * count + 5]))
    pressure_ref, residual_ref, direction_ref, image_ref, alpha_ref = refs[count:count + 5]
    (
        fetch_sem, sel, k_hi, k_lo, e_hi, e_lo, s_pad,
        slopes_ref, geometry, tz_ref, own_ref, rows_ref,
        halo_out, halo_in, halo_send, halo_recv,
        plane_in, plane_send, plane_recv, column_in, column_send, column_recv,
    ) = refs[2 * count + 5:]
    gx = lax.axis_index("gx")
    gy = lax.axis_index("gy")
    hi = nx // lo
    x_low, x_high = lax.rem(gx + nx - 1, nx), lax.rem(gx + 1, nx)
    y_low, y_high = lax.rem(gy + ny - 1, ny), lax.rem(gy + 1, ny)
    has_low_x, has_high_x = gx > 0, gx < nx - 1
    has_low_y, has_high_y = gy > 0, gy < ny - 1
    neighbours = (
        ((x_low, gy), 0, has_low_x), ((x_high, gy), 1, has_high_x),
        ((gx, y_low), 2, has_low_y), ((gx, y_high), 3, has_high_y),
        ((x_low, y_low), 4, has_low_x & has_low_y), ((x_low, y_high), 4, has_low_x & has_high_y),
        ((x_high, y_low), 4, has_high_x & has_low_y), ((x_high, y_high), 4, has_high_x & has_high_y),
    )
    inside_x, inside_y = has_low_x & has_high_x, has_low_y & has_high_y
    inside = inside_x & inside_y
    at_corner = jnp.logical_not(inside_x | inside_y)
    at_edge = jnp.logical_not(inside | at_corner)

    def where_there(actions, there):
        @pl.when(inside)
        def _():
            for action in actions:
                action()

        @pl.when(jnp.logical_not(inside))
        def _():
            for action, is_there in zip(actions, there):
                pl.when(is_there)(action)

    filled = [neighbours[at][2] for at in (1, 0, 3, 2, 7, 6, 5, 4)]

    z_at, y_at = lax.rem(gx, lo), lax.div(gx, lo)
    x_at, core = lax.div(gy, 2), lax.rem(gy, 2)
    first_core = core == 0
    sibling = (gx, gy + 1 - 2 * core)
    plane = [
        (lax.rem(y_at + a, hi) * lo + z_at, lax.rem(x_at + b, ny // 2) * 2)
        for a, b in offsets(hi, ny // 2)
    ]
    plane_from = [
        (lax.rem(y_at + hi - a, hi) * lo + z_at, lax.rem(x_at + ny // 2 - b, ny // 2) * 2)
        for a, b in offsets(hi, ny // 2)
    ]
    column = [(y_at * lo + lax.rem(z_at + a, lo), x_at * 2) for a, _ in offsets(lo, 1)]
    column_from = [(y_at * lo + lax.rem(z_at + lo - a, lo), x_at * 2) for a, _ in offsets(lo, 1)]

    barrier = pltpu.get_barrier_semaphore()

    def greet(peer, is_there=None):
        def signal():
            pl.semaphore_signal(barrier, inc=1, device_id=peer, device_id_type=MESH)

        if is_there is None:
            signal()
        else:
            pl.when(is_there)(signal)

    def greet_plane(peers):
        @pl.when(first_core)
        def _():
            for peer_x, peer_y in peers:
                greet((peer_x, peer_y + 1))
                greet((peer_x, peer_y))

    greet_plane(plane_from[:5])
    for peer in column_from[:3]:
        greet(peer)
    for peer, _, is_there in neighbours[::-1]:
        greet(peer, is_there)
    greet_plane(plane_from[5:])
    for peer in column_from[3:]:
        greet(peer)
    greet((gx, gy + 1 - 2 * core))

    heard = len(plane) + jnp.where(first_core, 2 * len(column) + 1, 1)
    for _, _, is_there in neighbours:
        heard = heard + is_there.astype(jnp.int32)

    fetches = {}
    for at, name in enumerate(FETCHED):
        fetches[name] = pltpu.make_async_copy(far[name], near[name], fetch_sem.at[at])
        fetches[name].start()

    def c(name):
        if name in fetches:
            fetches.pop(name).wait()
        return near[name]

    col = iota((64, 512), 1)
    for block in range(8):
        at = iota((64, 512), 0) + block * 64
        sel[block * 64:block * 64 + 64] = (
            ((at & 7) * 64 + (at >> 3)) == col
        ).astype(jnp.float32).astype(jnp.bfloat16)

    lane1 = iota((1, 128), 1)
    order_ref = c("order")
    row16 = iota((16, 128), 0)
    along_lanes = jnp.zeros((1, 128), jnp.int32)
    along_rows = jnp.zeros((16, 128), jnp.int32)
    for at in range(16):
        along_lanes = jnp.where((lane1 & 15) == at, order_ref[at], along_lanes)
        along_rows = jnp.where(row16 == at, order_ref[at], along_rows)
    row = iota((128, 128), 0)
    place = (
        ((row >> 3) == along_lanes) & (((row & 7) >> 1) == ((lane1 & 63) >> 4))
    ).astype(jnp.float32).astype(jnp.bfloat16)
    lane16 = iota((16, 128), 1)
    unplace = jnp.concatenate(
        [((lane16 >> 3) == along_rows) & (((lane16 & 7) >> 1) == u) for u in range(4)], axis=0
    ).astype(jnp.float32).astype(jnp.bfloat16)

    row32 = iota((32, 128), 0)
    lane32 = iota((32, 128), 1)
    parity = row32 & 1
    left_half = lane32 < 64

    def from_rows(fields):
        count = len(fields)
        parts = [split(f) for f in fields]
        stacked = jnp.concatenate([p[0] for p in parts] + [p[1] for p in parts], axis=0)
        moved = fdot(stacked, sel[...]).astype(jnp.bfloat16)
        out = []
        for f in range(count):
            pieces = []
            for part in range(2):
                z = moved[(part * count + f) * 16:(part * count + f) * 16 + 16]
                pieces += [z[:, u * 128:u * 128 + 128] for u in range(4)]
            v = fdot(place, jnp.concatenate(pieces, axis=0))
            tiles = []
            for pair in range(2):
                picked = []
                for odd in range(2):
                    at = (pair * 2 + odd) * 32
                    block = v[at:at + 32]
                    picked.append(jnp.where(parity == odd, block, half_roll(block)))
                tiles.append(jnp.where(left_half, picked[0], picked[1]))
            out.append(jnp.concatenate(tiles, axis=1))
        return out

    def to_rows(values):
        count = len(values)
        highs, lows = [], []
        for value in values:
            blocks = []
            for ij in range(4):
                block = value[:, (ij // 2) * 128:(ij // 2) * 128 + 128]
                block = jnp.where(parity == (ij & 1), block, half_roll(block))
                blocks.append(jnp.where((lane32 >> 6) == parity, block, 0.0))
            high, low = split(jnp.concatenate(blocks, axis=0))
            highs.append(high)
            lows.append(low)
        o = fdot(unplace, jnp.concatenate(highs + lows, axis=1)).astype(jnp.bfloat16)
        rows = []
        for v in range(2 * count):
            rows.append(
                jnp.concatenate(
                    [o[u * 16:u * 16 + 16, v * 128:v * 128 + 128] for u in range(4)], axis=1
                )
            )
        n = lax.dot_general(
            jnp.concatenate(rows, axis=0), sel[...], (((1,), (1,)), ((), ())),
            preferred_element_type=jnp.float32,
        )
        return [
            n[v * 16:v * 16 + 16] + n[(count + v) * 16:(count + v) * 16 + 16]
            for v in range(count)
        ]

    for name in ("smoother", "load", "spread_e", "aei", "re"):
        c(name)
    s_pad[...] = jnp.zeros((16, 128), jnp.float32)
    s_pad[0:10, 0:10] = c("smoother")[...]
    both_parts = jnp.concatenate(split(s_pad[...]), axis=0)[:, 0:16]
    entries = fdot(both_parts, c("spread_e")[...]).astype(jnp.bfloat16)

    def stacked_entries(entries, at, width, number):
        blocks = [entries[:, at + b * width:at + (b + 1) * width] for b in range(number)]
        return [block[0:16] for block in blocks] + [block[16:32] for block in blocks]

    for axis in range(2):
        wide = fdot(
            c("re")[axis],
            jnp.concatenate(
                stacked_entries(entries, axis * 768, 384, 2) + [c("aei")[axis]], axis=0
            ),
        )
        enc = wide if axis == 0 else enc * wide
    high, low = split(enc)
    e_hi[...] = high
    e_lo[...] = low

    r0, = from_rows([c("load")[...]])

    low_x = (gx == 0).astype(jnp.float32)
    high_x = (gx == nx - 1).astype(jnp.float32)
    low_y = (gy == 0).astype(jnp.float32)
    high_y = (gy == ny - 1).astype(jnp.float32)
    left16 = lane16 < 64
    quarter = (lane16 & 63) >> 4

    for slot, is_filled in enumerate(filled):
        @pl.when(jnp.logical_not(is_filled))
        def _():
            for stage in range(4):
                halo_in[stage, slot] = jnp.zeros((16, 128), jnp.float32)

    pl.semaphore_wait(barrier, heard)

    halos = []

    def exchange_start(stage, value):
        m = right_dot(value, e_hi[...], e_lo[...])
        for pair in range(2):
            t = m[:, pair * 128:pair * 128 + 128]
            top, bottom = t[0:16], t[16:32]
            halo_out[stage, 2 * pair] = jnp.where(left16, top, half_roll(bottom))
            halo_out[stage, 2 * pair + 1] = jnp.where(left16, half_roll(top), bottom)
        t = m[:, 256:384]
        halo_out[stage, 4] = jnp.where(left16, t[0:16], half_roll(t[16:32]))
        copies = []
        for slot in (0, 1, 4, 5, 6, 7, 2, 3):
            peer, part, is_there = neighbours[slot]
            copy = pltpu.make_async_remote_copy(
                src_ref=halo_out.at[stage, part],
                dst_ref=halo_in.at[stage, slot],
                send_sem=halo_send.at[stage, slot],
                recv_sem=halo_recv.at[stage],
                device_id=peer,
                device_id_type=MESH,
            )
            copies.append((copy, is_there))
        where_there([copy.start for copy, _ in copies], [there for _, there in copies])
        halos.extend(copies)

    def exchange_end(stage):
        for number, here in ((8, inside), (5, at_edge), (3, at_corner)):
            arrived = halo_in.at[stage, pl.ds(0, number)]
            pl.when(here)(
                pltpu.make_async_remote_copy(
                    src_ref=arrived,
                    dst_ref=arrived,
                    send_sem=halo_send.at[stage, 0],
                    recv_sem=halo_recv.at[stage],
                    device_id=sibling,
                    device_id_type=MESH,
                ).wait_recv
            )
        tiles = []
        for pair in range(2):
            a, b = halo_in[stage, 2 * pair], halo_in[stage, 2 * pair + 1]
            tiles.append(
                jnp.concatenate(
                    [jnp.where(left16, a, half_roll(b)), jnp.where(left16, half_roll(a), b)],
                    axis=0,
                )
            )
        corner = jnp.where(
            quarter == 0, halo_in[stage, 4],
            jnp.where(
                quarter == 1, halo_in[stage, 5],
                jnp.where(quarter == 2, halo_in[stage, 6], halo_in[stage, 7]),
            ),
        )
        tiles.append(jnp.concatenate([corner, half_roll(corner)], axis=0))
        return jnp.concatenate(tiles, axis=1)

    others = 2 * len(plane) + 1

    def plane_copy(which, target, peer, tiles=1):
        source = plane_in.at[which, pl.ds(others, 1)] if tiles == 1 else target
        return pltpu.make_async_remote_copy(
            src_ref=source,
            dst_ref=target,
            send_sem=plane_send.at[which],
            recv_sem=plane_recv.at[which],
            device_id=peer,
            device_id_type=MESH,
        )

    def column_copy(which, target, peer, tiles=1):
        source = column_in.at[which, pl.ds(0, 1)] if tiles == 1 else target
        return pltpu.make_async_remote_copy(
            src_ref=source,
            dst_ref=target,
            send_sem=column_send.at[which],
            recv_sem=column_recv.at[which],
            device_id=peer,
            device_id_type=MESH,
        )

    def tree_sum(parts):
        while len(parts) > 1:
            parts = [sum(parts[at:at + 2]) for at in range(0, len(parts), 2)]
        return parts[0]

    def sum_start(which, value):
        plane_in[which, others] = value
        for at, peer in enumerate(plane):
            plane_copy(which, plane_in.at[which, pl.ds(2 * at + core, 1)], peer).start()

        @pl.when(jnp.logical_not(first_core))
        def _():
            plane_copy(which, plane_in.at[which, pl.ds(others - 1, 1)], sibling).start()

    def sum_middle(which):
        @pl.when(first_core)
        def _():
            arrived = plane_in.at[which, pl.ds(0, others)]
            plane_copy(which, arrived, sibling, others).wait_recv()
            column_in[which, 0] = tree_sum([plane_in[which, slot] for slot in range(others + 1)])
            for at, (peer_x, peer_y) in enumerate(column):
                for other in (1, 0):
                    target = column_in.at[which, pl.ds(at + 1, 1)]
                    column_copy(which, target, (peer_x, peer_y + other)).start()
            column_copy(which, column_in.at[which, pl.ds(0, 1)], sibling).start()

    def sum_end(which):
        @pl.when(first_core)
        def _():
            arrived = column_in.at[which, pl.ds(1, len(column))]
            column_copy(which, arrived, sibling, len(column)).wait_recv()

        @pl.when(jnp.logical_not(first_core))
        def _():
            arrived = column_in.at[which, pl.ds(0, len(column) + 1)]
            column_copy(which, arrived, sibling, len(column) + 1).wait_recv()

        return tree_sum([column_in[which, slot] for slot in range(len(column) + 1)])

    def plane_sent(which):
        @pl.when(first_core)
        def _():
            leaving = plane_in.at[which, pl.ds(0, len(plane))]
            plane_copy(which, leaving, sibling, len(plane)).wait_send()

        @pl.when(jnp.logical_not(first_core))
        def _():
            leaving = plane_in.at[which, pl.ds(0, len(plane) + 1)]
            plane_copy(which, leaving, sibling, len(plane) + 1).wait_send()

    def column_sent(which):
        @pl.when(first_core)
        def _():
            number = 2 * len(column) + 1
            leaving = plane_in.at[which, pl.ds(0, number)]
            column_copy(which, leaving, sibling, number).wait_send()

    row8 = iota((8, 128), 0)

    def partial_tile(pairs):
        tile = jnp.zeros((8, 128), jnp.float32)
        for q, products in enumerate(pairs):
            t = local_sum(products)
            for shift in (4, 2, 1):
                t = t + pltpu.roll(t, shift, 0)
            tile = jnp.where(row8 == q, t, tile)
        return tile

    def scalars(total, number):
        column = jnp.sum(total, axis=1, keepdims=True)
        return [column[q:q + 1] for q in range(number)]

    exchange_start(0, r0)

    for name in ("spread_k", "rvi", "uc", "rzt", "metric", "mass"):
        c(name)
    entries = fdot(both_parts, c("spread_k")[...]).astype(jnp.bfloat16)
    for axis, low_edge, high_edge in ((0, low_x, high_x), (1, low_y, high_y)):
        blocks = stacked_entries(entries, axis * 1024, 256, 4)
        for at in (0, 4):
            blocks[at] = blocks[at] * (1.0 - low_edge).astype(jnp.bfloat16)
            blocks[at + 3] = blocks[at + 3] * (1.0 - high_edge).astype(jnp.bfloat16)
        wide = fdot(c("uc")[axis], jnp.concatenate(blocks + [c("rvi")[axis]], axis=0))
        kxy = wide if axis == 0 else kxy * wide
    high, low = split(kxy)
    k_hi[...] = high
    k_lo[...] = low
    tz = fdot(c("rzt")[...], jnp.concatenate(stacked_entries(entries, 2048, 128, 4), axis=0))
    tz_hi, tz_lo = split(tz[:, 0:96])
    tz = jnp.where(iota((32, 96), 1) < 64, tz_hi.astype(jnp.float32), tz_lo.astype(jnp.float32))
    tz_ref[...] = tz.astype(jnp.bfloat16)

    metric = c("metric")
    m0, m1, m2, mass = from_rows(
        [metric[0], metric[1], metric[2], c("mass")[...]]
    )
    slopes_ref[...] = jnp.concatenate(
        [
            jnp.concatenate([m0[:, :128], m1[:, :128]], axis=1),
            jnp.concatenate([m0[:, 128:], m1[:, 128:]], axis=1),
        ],
        axis=0,
    )

    geometry[0] = m2
    geometry[1] = mass

    def own_part(stage, value):
        own_ref[stage] = right_dot(value, k_hi[0:256], k_lo[0:256])

    def precondition(stage, arrived):
        return left_dot(
            tz_ref[...], own_ref[stage] + right_dot(arrived, k_hi[256:640], k_lo[256:640])
        )

    def slopes(u):
        tall = jnp.concatenate([u[:, :128], u[:, 128:]], axis=0)
        return right_dot(tall, c("dxy_hi")[...], c("dxy_lo")[...]), left_dot(c("dz")[...], u)

    def operate(u, grad):
        slope = slopes_ref[...] * grad[0]
        slope_z = geometry[0] * grad[1]
        tall = right_dot(slope, c("dxyt_hi")[...], c("dxyt_lo")[...])
        return (
            jnp.concatenate([tall[:32], tall[32:]], axis=1)
            + left_dot(c("dzt")[...], slope_z)
            + geometry[1] * u
        )

    def assembled(value, arrived):
        both = jnp.concatenate([value, arrived], axis=1)
        high, low = split(both)
        t = fdot(jnp.concatenate([high, low], axis=0), c("asm")[...])
        t = t[:32] + t[32:]
        high, low = split(t)
        return fdot(c("az")[...], jnp.concatenate([high, low], axis=0))

    own_part(0, r0)
    for name in ("dxy_hi", "dxy_lo", "dz", "dxyt_hi", "dxyt_lo", "dzt", "asm", "az"):
        c(name)
    arrived_r0 = exchange_end(0)
    z0 = precondition(0, arrived_r0)
    w0 = operate(z0, slopes(z0))

    exchange_start(1, w0)
    sum_start(0, partial_tile([[(r0, z0)], [(w0, z0)]]))
    own_part(1, w0)
    arrived_w0 = exchange_end(1)
    z1 = precondition(1, arrived_w0)
    grad1 = slopes(z1)
    w1 = operate(z1, grad1)
    exchange_start(2, w1)
    sum_middle(0)
    own_part(2, w1)
    for at, value in enumerate(
        to_rows([z0, z1, assembled(r0, arrived_r0), assembled(w0, arrived_w0)])
    ):
        rows_ref[at] = value
    arrived_w1 = exchange_end(2)
    z2 = precondition(2, arrived_w1)
    grad2 = slopes(z2)
    gamma0, delta0 = scalars(sum_end(0), 2)
    alpha0 = gamma0 / delta0
    per_gamma0 = 1.0 / gamma0
    per_alpha0 = delta0 / gamma0

    r1 = r0 - alpha0 * w0
    u1 = z0 - alpha0 * z1
    v1 = w0 - alpha0 * w1
    q = z1 - alpha0 * z2
    grad_q = grad1[0] - alpha0 * grad2[0]
    grad_qz = grad1[1] - alpha0 * grad2[1]
    slope_q = slopes_ref[...] * grad_q
    sum_start(
        1,
        partial_tile(
            [
                [(r1, u1)], [(v1, u1)], [(v1, q)], [(v1, z1)], [(w0, z1)],
                [
                    (slope_q[:32], grad_q[:32]), (slope_q[32:], grad_q[32:]),
                    (geometry[0] * grad_qz, grad_qz), (geometry[1] * q, q),
                ],
                [(w1, q)], [(w1, z1)],
            ]
        ),
    )
    w2 = operate(z2, grad2)
    exchange_start(3, w2)
    for at, value in enumerate(to_rows([z2, assembled(w1, arrived_w1)])):
        rows_ref[4 + at] = value
    sum_middle(1)
    arrived_w2 = exchange_end(3)
    rows_w2, = to_rows([assembled(w2, arrived_w2)])
    rows_z0, rows_z1, rows_r0, rows_w0, rows_z2, rows_w1 = [rows_ref[at] for at in range(6)]
    rows_ref[1] = rows_z0 - alpha0 * rows_z1
    rows_ref[4] = rows_z1 - alpha0 * rows_z2
    rows_ref[2] = rows_r0 - alpha0 * rows_w0
    rows_ref[5] = rows_w0 - alpha0 * rows_w1
    rows_ref[6] = rows_w1 - alpha0 * rows_w2
    pressure_ref[...] = rows_z1
    residual_ref[...] = rows_w1
    where_there([copy.wait_send for copy, _ in halos], [there for _, there in halos])
    plane_sent(0)
    plane_sent(1)
    column_sent(0)
    gamma1, delta1, vq, vz, wz0, yq, yz, wz1 = scalars(sum_end(1), 8)

    beta1 = gamma1 * per_gamma0
    uz = -gamma1 * per_alpha0
    curve1 = delta1 + beta1 * uz
    alpha1 = gamma1 / curve1
    per_gamma1 = 1.0 / gamma1
    gamma2 = (
        gamma1 - 2.0 * alpha1 * (delta1 + beta1 * uz)
        + alpha1 * alpha1 * (vq + beta1 * (2.0 * vz + beta1 * wz0))
    )
    delta2 = (
        delta1 - 2.0 * alpha1 * (vq + beta1 * vz)
        + alpha1 * alpha1 * (yq + beta1 * (2.0 * yz + beta1 * wz1))
    )
    beta2 = gamma2 * per_gamma1
    alpha2 = gamma2 / (delta2 - beta2 * gamma2 * (curve1 * per_gamma1))
    rows_z0, rows_u1, rows_r1, rows_w0, rows_q, rows_v1, rows_y = [
        rows_ref[at] for at in range(7)
    ]
    rows_p1 = rows_u1 + beta1 * rows_z0
    rows_u2 = rows_u1 - alpha1 * (rows_q + beta1 * pressure_ref[...])
    rows_s1 = rows_v1 + beta1 * rows_w0
    rows_v2 = rows_v1 - alpha1 * (rows_y + beta1 * residual_ref[...])
    pressure_ref[...] = alpha0 * rows_z0 + alpha1 * rows_p1
    residual_ref[...] = rows_r1 - alpha1 * rows_s1
    direction_ref[...] = rows_u2 + beta2 * rows_p1
    image_ref[...] = rows_v2 + beta2 * rows_s1
    alpha_ref[...] = jnp.broadcast_to(alpha2, (1, 512))
    column_sent(1)


def solution(mesh):
    nx, ny = mesh.shape["gx"], mesh.shape["gy"]
    lo = 8 if nx % 8 == 0 else 2
    consts = tables()
    vmem = pl.BlockSpec(memory_space=pltpu.VMEM)
    rows = jax.ShapeDtypeStruct((16, 512), jnp.float32)
    chips = nx // lo * (ny // 2)
    shapes = dict(
        consts,
        load=rows,
        metric=jax.ShapeDtypeStruct((3, 16, 512), jnp.float32),
        mass=rows,
        smoother=jax.ShapeDtypeStruct((10, 10), jnp.float32),
        order=jax.ShapeDtypeStruct((16,), jnp.int32),
    )
    call = pl.pallas_call(
        functools.partial(kernel, nx, ny, lo),
        out_shape=(pltpu.VMEM((16, 512), jnp.float32),) * 4 + (pltpu.VMEM((1, 512), jnp.float32),),
        in_specs=[pl.BlockSpec(memory_space=pltpu.HBM)] * len(FETCHED),
        out_specs=(vmem,) * 5,
        scratch_shapes=[
            (pltpu.SMEM if name == "order" else pltpu.VMEM)(shapes[name].shape, shapes[name].dtype)
            for name in FETCHED
        ]
        + [
            pltpu.SemaphoreType.DMA((len(FETCHED),)),
            pltpu.VMEM((512, 512), jnp.bfloat16),
            pltpu.VMEM((640, 256), jnp.bfloat16),
            pltpu.VMEM((640, 256), jnp.bfloat16),
            pltpu.VMEM((256, 384), jnp.bfloat16),
            pltpu.VMEM((256, 384), jnp.bfloat16),
            pltpu.VMEM((16, 128), jnp.float32),
            pltpu.VMEM((64, 256), jnp.float32),
            pltpu.VMEM((2, 32, 256), jnp.float32),
            pltpu.VMEM((32, 96), jnp.bfloat16),
            pltpu.VMEM((3, 32, 256), jnp.float32),
            pltpu.VMEM((7, 16, 512), jnp.float32),
            pltpu.VMEM((4, 5, 16, 128), jnp.float32),
            pltpu.VMEM((4, 8, 16, 128), jnp.float32),
            pltpu.SemaphoreType.DMA((4, 8)),
            pltpu.SemaphoreType.DMA((4,)),
            pltpu.VMEM((2, 2 * chips, 8, 128), jnp.float32),
            pltpu.SemaphoreType.DMA((2,)),
            pltpu.SemaphoreType.DMA((2,)),
            pltpu.VMEM((2, lo, 8, 128), jnp.float32),
            pltpu.SemaphoreType.DMA((2,)),
            pltpu.SemaphoreType.DMA((2,)),
        ],
        compiler_params=pltpu.CompilerParams(
            collective_id=0, has_side_effects=True, vmem_limit_bytes=60 * 1024 * 1024
        ),
    )

    def on_device(load_nodes, metric, mass_nodes, smoother, element_order):
        given = dict(
            consts, load=load_nodes, metric=metric.transpose(1, 0, 2), mass=mass_nodes, smoother=smoother,
            order=element_order,
        )
        pressure, residual, direction, image, alpha = call(
            *[jnp.asarray(given[name]) for name in FETCHED]
        )
        return pressure + alpha * direction, residual - alpha * image

    return jax.shard_map(
        on_device,
        mesh=mesh,
        in_specs=(
            P(("gx", "gy"), None),
            P(("gx", "gy"), None, None),
            P(("gx", "gy"), None),
            P(),
            P(("gx", "gy")),
        ),
        out_specs=(P(("gx", "gy"), None), P(("gx", "gy"), None)),
        check_vma=False,
    )
```

```python
import functools

import jax
import jax.numpy as jnp
import ml_dtypes
import numpy as np
from jax import lax
from jax.experimental import pallas as pl
from jax.experimental.pallas import tpu as pltpu
from jax.sharding import PartitionSpec as P

NODES = 8
BF16 = ml_dtypes.bfloat16
MESH = pl.DeviceIdType.MESH


def derivative_table(node_count):
    degree = node_count - 1
    points = np.cos(np.pi * np.arange(node_count) / degree)
    weights = np.ones(node_count)
    weights[0] = 2.0
    weights[-1] = 2.0
    matrix = np.zeros((node_count, node_count))
    for row in range(node_count):
        for col in range(node_count):
            if row != col:
                matrix[row, col] = (
                    weights[row]
                    / weights[col]
                    * (-1.0) ** (row + col)
                    / (points[row] - points[col])
                )
        matrix[row, row] = -np.sum(matrix[row])
    return matrix


def split_const(matrix):
    full = np.asarray(matrix, np.float32)
    high = full.astype(BF16)
    return high, (full - high.astype(np.float32)).astype(BF16)


@functools.lru_cache(None)
def tables():
    node = np.array([7 * i + a for i in range(2) for a in range(8)])
    incidence = {}
    for box in (-1, 0, 1, 2):
        block = np.zeros((10, 16))
        for at in range(16):
            idx = node[at] - 7 * box + 1
            if 0 <= idx < 10:
                block[idx, at] = 1.0
        incidence[box] = block
    uc = np.zeros((24, 4, 16))
    uci = np.zeros((24, 16))
    rv = np.zeros((4, 16, 16))
    rvi = np.zeros((16, 16))
    re = np.zeros((16, 2, 16))
    rei = np.zeros((16, 32))
    ae = np.zeros((2, 16, 24))
    aei = np.zeros((32, 24))
    for at in range(16):
        for slot, box in enumerate((-1, 0, 1, 2)):
            uc[at, slot, :10] = incidence[box][:, at]
            rv[slot, :10, at] = incidence[box][:, at]
        re[at, 0, :10] = incidence[0][:, at]
        re[at, 1, :10] = incidence[1][:, at]
        rei[at, at] = 1.0
        aei[at, at] = 1.0
        for dim, where in enumerate((0, 1, 13, 14)):
            rvi[dim, at] = float(node[at] == where)
            rei[at, 16 + dim] = float(node[at] == where)
    uc[16, 2, 8] = uc[17, 2, 9] = uci[18, 2] = uci[19, 3] = 1.0
    uc[20, 1, 0] = uc[21, 1, 1] = uci[22, 0] = uci[23, 1] = 1.0
    aei[16, 16] = aei[17, 17] = ae[0, 0, 18] = ae[0, 1, 19] = 1.0
    aei[18, 20] = aei[19, 21] = ae[1, 8, 22] = ae[1, 9, 23] = 1.0
    assemble = np.zeros((24, 16))
    assemble[:16] = node[:, None] == node[None, :]
    assemble[16] = node == 14
    assemble[21] = node == 0

    lane = np.arange(256)
    xi = (lane // 128) * 8 + (lane // 8) % 8
    eta = ((lane // 64) % 2) * 8 + lane % 8
    mx, my = [], []
    for side in (16, 20):
        for q in range(4):
            for e in range(16):
                mx.append(side + q)
                my.append(e)
    for side in (16, 20):
        for e in range(16):
            for q in range(4):
                mx.append(e)
                my.append(side + q)
    for sx in (16, 20):
        for sy in (16, 20):
            for qx in range(4):
                for qy in range(4):
                    mx.append(sx + qx)
                    my.append(sy + qy)
    mx, my = np.array(mx), np.array(my)

    def padded(rows, index):
        return np.concatenate([rows[index], np.zeros((64,) + rows.shape[1:])], axis=0)

    allx = np.concatenate([xi, mx])
    ally = np.concatenate([eta, my])
    def kernel_side(index):
        rows = uc.reshape(24, 64)
        return padded(np.concatenate([rows, rows, uci], axis=1), index)

    def sending_side(index):
        rows = re.reshape(16, 32)[index]
        return np.concatenate([rows, rows, rei[index]], axis=1)

    spread_e = [padded(ae[box].T, m).T for m in (mx, my) for box in range(2)]
    spread_k = [rv[box][:, at] for at in (xi, eta) for box in range(4)]
    asm = padded(assemble, allx)[:, xi] * padded(assemble, ally)[:, eta]

    znode = np.array([7 * k + c for k in range(4) for c in range(8)])
    rz = np.zeros((4, 16, 32))
    for block in range(4):
        for at in range(32):
            idx = znode[at] - 7 * block + 1
            if 0 <= idx < 10:
                rz[block, idx, at] = 1.0
    spread_z = [np.concatenate([block] * 4, axis=1) for block in rz]
    rzt = rz.reshape(64, 32).T
    az = (znode[:, None] == znode[None, :]).astype(float)

    d = derivative_table(NODES).astype(np.float32)
    eye8 = np.eye(8)
    dx = np.kron(np.eye(2), np.kron(d.T, eye8))
    dy = np.kron(np.eye(2), np.kron(eye8, d.T))
    dxy_hi, dxy_lo = split_const(np.concatenate([dx, dy], axis=1))
    dz = np.kron(np.eye(4), d)
    dz_hi, dz_lo = split_const(dz)
    dzt_hi, dzt_lo = split_const(dz.T)

    b = lambda m: np.asarray(m, BF16)
    return dict(
        dxy_hi=dxy_hi,
        dxy_lo=dxy_lo,
        dxyt_hi=np.ascontiguousarray(dxy_hi.T),
        dxyt_lo=np.ascontiguousarray(dxy_lo.T),
        dz=np.concatenate([dz_hi, dz_hi, dz_lo], axis=1),
        dzt=np.concatenate([dzt_hi, dzt_hi, dzt_lo], axis=1),
        az=b(np.concatenate([az, az], axis=1)),
        uc=b(np.stack([kernel_side(allx), kernel_side(ally)])),
        rvi=b(np.stack([rvi[:, xi], rvi[:, eta]])),
        re=b(np.stack([sending_side(xi), sending_side(eta)])),
        aei=b(np.stack([padded(aei.T, mx).T, padded(aei.T, my).T])),
        spread_e=b(np.concatenate(spread_e, axis=1)),
        spread_k=b(np.concatenate(spread_k + spread_z, axis=1)),
        rzt=b(np.concatenate([rzt, rzt], axis=1)),
        asm=b(asm),
    )


FETCHED = (
    "order", "smoother", "load", "spread_e", "aei", "re", "spread_k", "rvi", "uc", "rzt",
    "metric", "mass", "dxy_hi", "dxy_lo", "dz", "dxyt_hi", "dxyt_lo", "dzt", "asm", "az",
)


def fdot(left, right):
    return jnp.dot(left, right, preferred_element_type=jnp.float32)


def split(value):
    high = value.astype(jnp.bfloat16)
    low = (value - high.astype(jnp.float32)).astype(jnp.bfloat16)
    return high, low


def right_dot(value, w_hi, w_lo):
    rows = value.shape[0]
    high, low = split(value)
    both = fdot(jnp.concatenate([high, low], axis=0), w_hi)
    return both[:rows] + both[rows:] + fdot(high, w_lo)


def left_dot(stacked, value):
    high, low = split(value)
    return fdot(stacked, jnp.concatenate([high, low, high], axis=0))


def offsets(first, second):
    def far(pair):
        return -min(pair[0], first - pair[0]) - min(pair[1], second - pair[1])

    pairs = [(a, b) for a in range(first) for b in range(second)]
    return sorted(pairs[1:], key=far)


def iota(shape, dim):
    return lax.broadcasted_iota(jnp.int32, shape, dim)


def half_roll(value):
    return pltpu.roll(value, 64, 1)


def local_sum(pairs):
    t = sum(first * second for first, second in pairs)
    t = t[0:8] + t[8:16] + t[16:24] + t[24:32]
    return t[:, :128] + t[:, 128:]


def kernel(
    nx, ny, lo,
    *refs,
):
    count = len(FETCHED)
    far = dict(zip(FETCHED, refs[:count]))
    near = dict(zip(FETCHED, refs[count + 5:2 * count + 5]))
    pressure_ref, residual_ref, direction_ref, image_ref, alpha_ref = refs[count:count + 5]
    (
        fetch_sem, sel, k_hi, k_lo, e_hi, e_lo, s_pad,
        slopes_ref, geometry, tz_ref, own_ref, rows_ref,
        halo_out, halo_in, halo_send, halo_recv,
        plane_in, plane_send, plane_recv, column_in, column_send, column_recv,
    ) = refs[2 * count + 5:]
    gx = lax.axis_index("gx")
    gy = lax.axis_index("gy")
    hi = nx // lo
    x_low, x_high = lax.rem(gx + nx - 1, nx), lax.rem(gx + 1, nx)
    y_low, y_high = lax.rem(gy + ny - 1, ny), lax.rem(gy + 1, ny)
    has_low_x, has_high_x = gx > 0, gx < nx - 1
    has_low_y, has_high_y = gy > 0, gy < ny - 1
    neighbours = (
        ((x_low, gy), 0, has_low_x), ((x_high, gy), 1, has_high_x),
        ((gx, y_low), 2, has_low_y), ((gx, y_high), 3, has_high_y),
        ((x_low, y_low), 4, has_low_x & has_low_y), ((x_low, y_high), 4, has_low_x & has_high_y),
        ((x_high, y_low), 4, has_high_x & has_low_y), ((x_high, y_high), 4, has_high_x & has_high_y),
    )
    inside_x, inside_y = has_low_x & has_high_x, has_low_y & has_high_y
    inside = inside_x & inside_y
    at_corner = jnp.logical_not(inside_x | inside_y)
    at_edge = jnp.logical_not(inside | at_corner)

    def where_there(actions, there):
        @pl.when(inside)
        def _():
            for action in actions:
                action()

        @pl.when(jnp.logical_not(inside))
        def _():
            for action, is_there in zip(actions, there):
                pl.when(is_there)(action)

    filled = [neighbours[at][2] for at in (1, 0, 3, 2, 7, 6, 5, 4)]

    z_at, y_at = lax.rem(gx, lo), lax.div(gx, lo)
    x_at, core = lax.div(gy, 2), lax.rem(gy, 2)
    first_core = core == 0
    sibling = (gx, gy + 1 - 2 * core)
    plane = [
        (lax.rem(y_at + a, hi) * lo + z_at, lax.rem(x_at + b, ny // 2) * 2)
        for a, b in offsets(hi, ny // 2)
    ]
    plane_from = [
        (lax.rem(y_at + hi - a, hi) * lo + z_at, lax.rem(x_at + ny // 2 - b, ny // 2) * 2)
        for a, b in offsets(hi, ny // 2)
    ]
    column = [(y_at * lo + lax.rem(z_at + a, lo), x_at * 2) for a, _ in offsets(lo, 1)]
    column_from = [(y_at * lo + lax.rem(z_at + lo - a, lo), x_at * 2) for a, _ in offsets(lo, 1)]

    barrier = pltpu.get_barrier_semaphore()

    def greet(peer):
        pl.semaphore_signal(barrier, inc=1, device_id=peer, device_id_type=MESH)

    where_there(
        [functools.partial(greet, peer) for peer, _, _ in neighbours[::-1]],
        [is_there for _, _, is_there in neighbours[::-1]],
    )
    for peer in column_from:
        greet(peer)

    @pl.when(first_core)
    def _():
        for peer_x, peer_y in plane_from:
            greet((peer_x, peer_y + 1))
            greet((peer_x, peer_y))

    greet(sibling)

    heard = len(plane) + jnp.where(first_core, 2 * len(column) + 1, 1)
    for _, _, is_there in neighbours:
        heard = heard + is_there.astype(jnp.int32)

    fetches = {}
    for at, name in enumerate(FETCHED):
        fetches[name] = pltpu.make_async_copy(far[name], near[name], fetch_sem.at[at])
        fetches[name].start()

    def c(name):
        if name in fetches:
            fetches.pop(name).wait()
        return near[name]

    col = iota((64, 512), 1)
    for block in range(8):
        at = iota((64, 512), 0) + block * 64
        sel[block * 64:block * 64 + 64] = (
            ((at & 7) * 64 + (at >> 3)) == col
        ).astype(jnp.float32).astype(jnp.bfloat16)

    lane1 = iota((1, 128), 1)
    order_ref = c("order")
    row16 = iota((16, 128), 0)
    along_lanes = jnp.zeros((1, 128), jnp.int32)
    along_rows = jnp.zeros((16, 128), jnp.int32)
    for at in range(16):
        along_lanes = jnp.where((lane1 & 15) == at, order_ref[at], along_lanes)
        along_rows = jnp.where(row16 == at, order_ref[at], along_rows)
    row = iota((128, 128), 0)
    place = (
        ((row >> 3) == along_lanes) & (((row & 7) >> 1) == ((lane1 & 63) >> 4))
    ).astype(jnp.float32).astype(jnp.bfloat16)
    lane16 = iota((16, 128), 1)
    unplace = jnp.concatenate(
        [((lane16 >> 3) == along_rows) & (((lane16 & 7) >> 1) == u) for u in range(4)], axis=0
    ).astype(jnp.float32).astype(jnp.bfloat16)

    row32 = iota((32, 128), 0)
    lane32 = iota((32, 128), 1)
    parity = row32 & 1
    left_half = lane32 < 64

    def from_rows(fields):
        count = len(fields)
        parts = [split(f) for f in fields]
        stacked = jnp.concatenate([p[0] for p in parts] + [p[1] for p in parts], axis=0)
        moved = fdot(stacked, sel[...]).astype(jnp.bfloat16)
        out = []
        for f in range(count):
            pieces = []
            for part in range(2):
                z = moved[(part * count + f) * 16:(part * count + f) * 16 + 16]
                pieces += [z[:, u * 128:u * 128 + 128] for u in range(4)]
            v = fdot(place, jnp.concatenate(pieces, axis=0))
            tiles = []
            for pair in range(2):
                picked = []
                for odd in range(2):
                    at = (pair * 2 + odd) * 32
                    block = v[at:at + 32]
                    picked.append(jnp.where(parity == odd, block, half_roll(block)))
                tiles.append(jnp.where(left_half, picked[0], picked[1]))
            out.append(jnp.concatenate(tiles, axis=1))
        return out

    def to_rows(values):
        count = len(values)
        highs, lows = [], []
        for value in values:
            blocks = []
            for ij in range(4):
                block = value[:, (ij // 2) * 128:(ij // 2) * 128 + 128]
                block = jnp.where(parity == (ij & 1), block, half_roll(block))
                blocks.append(jnp.where((lane32 >> 6) == parity, block, 0.0))
            high, low = split(jnp.concatenate(blocks, axis=0))
            highs.append(high)
            lows.append(low)
        o = fdot(unplace, jnp.concatenate(highs + lows, axis=1)).astype(jnp.bfloat16)
        rows = []
        for v in range(2 * count):
            rows.append(
                jnp.concatenate(
                    [o[u * 16:u * 16 + 16, v * 128:v * 128 + 128] for u in range(4)], axis=1
                )
            )
        n = lax.dot_general(
            jnp.concatenate(rows, axis=0), sel[...], (((1,), (1,)), ((), ())),
            preferred_element_type=jnp.float32,
        )
        return [
            n[v * 16:v * 16 + 16] + n[(count + v) * 16:(count + v) * 16 + 16]
            for v in range(count)
        ]

    for name in ("smoother", "load", "spread_e", "aei", "re"):
        c(name)
    s_pad[...] = jnp.zeros((16, 128), jnp.float32)
    s_pad[0:10, 0:10] = c("smoother")[...]
    both_parts = jnp.concatenate(split(s_pad[...]), axis=0)[:, 0:16]
    entries = fdot(both_parts, c("spread_e")[...]).astype(jnp.bfloat16)

    def stacked_entries(entries, at, width, number):
        blocks = [entries[:, at + b * width:at + (b + 1) * width] for b in range(number)]
        return [block[0:16] for block in blocks] + [block[16:32] for block in blocks]

    for axis in range(2):
        wide = fdot(
            c("re")[axis],
            jnp.concatenate(
                stacked_entries(entries, axis * 768, 384, 2) + [c("aei")[axis]], axis=0
            ),
        )
        enc = wide if axis == 0 else enc * wide
    high, low = split(enc)
    e_hi[...] = high
    e_lo[...] = low

    r0, = from_rows([c("load")[...]])

    low_x = (gx == 0).astype(jnp.float32)
    high_x = (gx == nx - 1).astype(jnp.float32)
    low_y = (gy == 0).astype(jnp.float32)
    high_y = (gy == ny - 1).astype(jnp.float32)
    left16 = lane16 < 64
    quarter = (lane16 & 63) >> 4

    @pl.when(jnp.logical_not(inside))
    def _():
        for slot, is_filled in enumerate(filled):
            @pl.when(jnp.logical_not(is_filled))
            def _():
                for stage in range(4):
                    halo_in[stage, slot] = jnp.zeros((16, 128), jnp.float32)

    pl.semaphore_wait(barrier, heard)

    def exchange_start(stage, value):
        m = right_dot(value, e_hi[...], e_lo[...])
        for pair in range(2):
            t = m[:, pair * 128:pair * 128 + 128]
            top, bottom = t[0:16], t[16:32]
            halo_out[stage, 2 * pair] = jnp.where(left16, top, half_roll(bottom))
            halo_out[stage, 2 * pair + 1] = jnp.where(left16, half_roll(top), bottom)
        t = m[:, 256:384]
        halo_out[stage, 4] = jnp.where(left16, t[0:16], half_roll(t[16:32]))
        copies = []
        for slot in (0, 1, 4, 5, 6, 7, 2, 3):
            peer, part, is_there = neighbours[slot]
            copy = pltpu.make_async_remote_copy(
                src_ref=halo_out.at[stage, part],
                dst_ref=halo_in.at[stage, slot],
                send_sem=halo_send.at[stage],
                recv_sem=halo_recv.at[stage],
                device_id=peer,
                device_id_type=MESH,
            )
            copies.append((copy, is_there))
        where_there([copy.start for copy, _ in copies], [there for _, there in copies])

    def halo_wait(stage, receiving):
        for number, here in ((8, inside), (5, at_edge), (3, at_corner)):
            moved = halo_in.at[stage, pl.ds(0, number)]
            copy = pltpu.make_async_remote_copy(
                src_ref=moved,
                dst_ref=moved,
                send_sem=halo_send.at[stage],
                recv_sem=halo_recv.at[stage],
                device_id=sibling,
                device_id_type=MESH,
            )
            pl.when(here)(copy.wait_recv if receiving else copy.wait_send)

    def exchange_end(stage):
        halo_wait(stage, True)
        tiles = []
        for pair in range(2):
            a, b = halo_in[stage, 2 * pair], halo_in[stage, 2 * pair + 1]
            tiles.append(
                jnp.concatenate(
                    [jnp.where(left16, a, half_roll(b)), jnp.where(left16, half_roll(a), b)],
                    axis=0,
                )
            )
        corner = jnp.where(
            quarter == 0, halo_in[stage, 4],
            jnp.where(
                quarter == 1, halo_in[stage, 5],
                jnp.where(quarter == 2, halo_in[stage, 6], halo_in[stage, 7]),
            ),
        )
        tiles.append(jnp.concatenate([corner, half_roll(corner)], axis=0))
        return jnp.concatenate(tiles, axis=1)

    others = 2 * len(plane) + 1

    def plane_copy(which, target, peer, tiles=1):
        source = plane_in.at[which, pl.ds(others, 1)] if tiles == 1 else target
        return pltpu.make_async_remote_copy(
            src_ref=source,
            dst_ref=target,
            send_sem=plane_send.at[which],
            recv_sem=plane_recv.at[which],
            device_id=peer,
            device_id_type=MESH,
        )

    def column_copy(which, target, peer, tiles=1):
        source = column_in.at[which, pl.ds(0, 1)] if tiles == 1 else target
        return pltpu.make_async_remote_copy(
            src_ref=source,
            dst_ref=target,
            send_sem=column_send.at[which],
            recv_sem=column_recv.at[which],
            device_id=peer,
            device_id_type=MESH,
        )

    def tree_sum(parts):
        while len(parts) > 1:
            parts = [sum(parts[at:at + 2]) for at in range(0, len(parts), 2)]
        return parts[0]

    def sum_start(which, value):
        plane_in[which, others] = value
        for at, peer in enumerate(plane):
            plane_copy(which, plane_in.at[which, pl.ds(2 * at + core, 1)], peer).start()

        @pl.when(jnp.logical_not(first_core))
        def _():
            plane_copy(which, plane_in.at[which, pl.ds(others - 1, 1)], sibling).start()

    def sum_middle(which):
        @pl.when(first_core)
        def _():
            arrived = plane_in.at[which, pl.ds(0, others)]
            plane_copy(which, arrived, sibling, others).wait_recv()
            column_in[which, 0] = tree_sum([plane_in[which, slot] for slot in range(others + 1)])
            for at, (peer_x, peer_y) in enumerate(column):
                for other in (1, 0):
                    target = column_in.at[which, pl.ds(at + 1, 1)]
                    column_copy(which, target, (peer_x, peer_y + other)).start()
            column_copy(which, column_in.at[which, pl.ds(0, 1)], sibling).start()

    def sum_end(which):
        @pl.when(first_core)
        def _():
            arrived = column_in.at[which, pl.ds(1, len(column))]
            column_copy(which, arrived, sibling, len(column)).wait_recv()

        @pl.when(jnp.logical_not(first_core))
        def _():
            arrived = column_in.at[which, pl.ds(0, len(column) + 1)]
            column_copy(which, arrived, sibling, len(column) + 1).wait_recv()

        return tree_sum([column_in[which, slot] for slot in range(len(column) + 1)])

    def plane_sent(which):
        @pl.when(first_core)
        def _():
            leaving = plane_in.at[which, pl.ds(0, len(plane))]
            plane_copy(which, leaving, sibling, len(plane)).wait_send()

        @pl.when(jnp.logical_not(first_core))
        def _():
            leaving = plane_in.at[which, pl.ds(0, len(plane) + 1)]
            plane_copy(which, leaving, sibling, len(plane) + 1).wait_send()

    def column_sent(which):
        @pl.when(first_core)
        def _():
            number = 2 * len(column) + 1
            leaving = plane_in.at[which, pl.ds(0, number)]
            column_copy(which, leaving, sibling, number).wait_send()

    row8 = iota((8, 128), 0)

    def partial_tile(pairs):
        tile = jnp.zeros((8, 128), jnp.float32)
        for q, products in enumerate(pairs):
            t = local_sum(products)
            for shift in (4, 2, 1):
                t = t + pltpu.roll(t, shift, 0)
            tile = jnp.where(row8 == q, t, tile)
        return tile

    def scalars(total, number):
        column = jnp.sum(total, axis=1, keepdims=True)
        return [column[q:q + 1] for q in range(number)]

    exchange_start(0, r0)

    for name in ("spread_k", "rvi", "uc", "rzt", "metric", "mass"):
        c(name)
    entries = fdot(both_parts, c("spread_k")[...]).astype(jnp.bfloat16)
    for axis, low_edge, high_edge in ((0, low_x, high_x), (1, low_y, high_y)):
        blocks = stacked_entries(entries, axis * 1024, 256, 4)
        for at in (0, 4):
            blocks[at] = blocks[at] * (1.0 - low_edge).astype(jnp.bfloat16)
            blocks[at + 3] = blocks[at + 3] * (1.0 - high_edge).astype(jnp.bfloat16)
        wide = fdot(c("uc")[axis], jnp.concatenate(blocks + [c("rvi")[axis]], axis=0))
        kxy = wide if axis == 0 else kxy * wide
    high, low = split(kxy)
    k_hi[...] = high
    k_lo[...] = low
    tz = fdot(c("rzt")[...], jnp.concatenate(stacked_entries(entries, 2048, 128, 4), axis=0))
    tz_hi, tz_lo = split(tz[:, 0:96])
    tz = jnp.where(iota((32, 96), 1) < 64, tz_hi.astype(jnp.float32), tz_lo.astype(jnp.float32))
    tz_ref[...] = tz.astype(jnp.bfloat16)

    metric = c("metric")
    m0, m1, m2, mass = from_rows(
        [metric[0], metric[1], metric[2], c("mass")[...]]
    )
    slopes_ref[...] = jnp.concatenate(
        [
            jnp.concatenate([m0[:, :128], m1[:, :128]], axis=1),
            jnp.concatenate([m0[:, 128:], m1[:, 128:]], axis=1),
        ],
        axis=0,
    )

    geometry[0] = m2
    geometry[1] = mass

    def own_part(stage, value):
        own_ref[stage] = right_dot(value, k_hi[0:256], k_lo[0:256])

    def precondition(stage, arrived):
        return left_dot(
            tz_ref[...], own_ref[stage] + right_dot(arrived, k_hi[256:640], k_lo[256:640])
        )

    def slopes(u):
        tall = jnp.concatenate([u[:, :128], u[:, 128:]], axis=0)
        return right_dot(tall, c("dxy_hi")[...], c("dxy_lo")[...]), left_dot(c("dz")[...], u)

    def operate(u, grad):
        slope = slopes_ref[...] * grad[0]
        slope_z = geometry[0] * grad[1]
        tall = right_dot(slope, c("dxyt_hi")[...], c("dxyt_lo")[...])
        return (
            jnp.concatenate([tall[:32], tall[32:]], axis=1)
            + left_dot(c("dzt")[...], slope_z)
            + geometry[1] * u
        )

    def assembled(value, arrived):
        both = jnp.concatenate([value, arrived], axis=1)
        high, low = split(both)
        t = fdot(jnp.concatenate([high, low], axis=0), c("asm")[...])
        t = t[:32] + t[32:]
        high, low = split(t)
        return fdot(c("az")[...], jnp.concatenate([high, low], axis=0))

    own_part(0, r0)
    for name in ("dxy_hi", "dxy_lo", "dz", "dxyt_hi", "dxyt_lo", "dzt", "asm", "az"):
        c(name)
    arrived_r0 = exchange_end(0)
    z0 = precondition(0, arrived_r0)
    w0 = operate(z0, slopes(z0))

    exchange_start(1, w0)
    sum_start(0, partial_tile([[(r0, z0)], [(w0, z0)]]))
    own_part(1, w0)
    arrived_w0 = exchange_end(1)
    z1 = precondition(1, arrived_w0)
    grad1 = slopes(z1)
    w1 = operate(z1, grad1)
    exchange_start(2, w1)
    sum_middle(0)
    own_part(2, w1)
    for at, value in enumerate(
        to_rows([z0, z1, assembled(r0, arrived_r0), assembled(w0, arrived_w0)])
    ):
        rows_ref[at] = value
    arrived_w1 = exchange_end(2)
    z2 = precondition(2, arrived_w1)
    grad2 = slopes(z2)
    gamma0, delta0 = scalars(sum_end(0), 2)
    alpha0 = gamma0 / delta0
    per_gamma0 = 1.0 / gamma0
    per_alpha0 = delta0 / gamma0

    r1 = r0 - alpha0 * w0
    u1 = z0 - alpha0 * z1
    v1 = w0 - alpha0 * w1
    q = z1 - alpha0 * z2
    grad_q = grad1[0] - alpha0 * grad2[0]
    grad_qz = grad1[1] - alpha0 * grad2[1]
    slope_q = slopes_ref[...] * grad_q
    sum_start(
        1,
        partial_tile(
            [
                [(r1, u1)], [(v1, u1)], [(v1, q)], [(v1, z1)], [(w0, z1)],
                [
                    (slope_q[:32], grad_q[:32]), (slope_q[32:], grad_q[32:]),
                    (geometry[0] * grad_qz, grad_qz), (geometry[1] * q, q),
                ],
                [(w1, q)], [(w1, z1)],
            ]
        ),
    )
    w2 = operate(z2, grad2)
    exchange_start(3, w2)
    for at, value in enumerate(to_rows([z2, assembled(w1, arrived_w1)])):
        rows_ref[4 + at] = value
    sum_middle(1)
    arrived_w2 = exchange_end(3)
    rows_w2, = to_rows([assembled(w2, arrived_w2)])
    rows_z0, rows_z1, rows_r0, rows_w0, rows_z2, rows_w1 = [rows_ref[at] for at in range(6)]
    rows_ref[1] = rows_z0 - alpha0 * rows_z1
    rows_ref[4] = rows_z1 - alpha0 * rows_z2
    rows_ref[2] = rows_r0 - alpha0 * rows_w0
    rows_ref[5] = rows_w0 - alpha0 * rows_w1
    rows_ref[6] = rows_w1 - alpha0 * rows_w2
    pressure_ref[...] = rows_z1
    residual_ref[...] = rows_w1
    for stage in range(4):
        halo_wait(stage, False)
    plane_sent(0)
    plane_sent(1)
    column_sent(0)
    gamma1, delta1, vq, vz, wz0, yq, yz, wz1 = scalars(sum_end(1), 8)

    beta1 = gamma1 * per_gamma0
    uz = -gamma1 * per_alpha0
    curve1 = delta1 + beta1 * uz
    alpha1 = gamma1 / curve1
    per_gamma1 = 1.0 / gamma1
    gamma2 = (
        gamma1 - 2.0 * alpha1 * (delta1 + beta1 * uz)
        + alpha1 * alpha1 * (vq + beta1 * (2.0 * vz + beta1 * wz0))
    )
    delta2 = (
        delta1 - 2.0 * alpha1 * (vq + beta1 * vz)
        + alpha1 * alpha1 * (yq + beta1 * (2.0 * yz + beta1 * wz1))
    )
    beta2 = gamma2 * per_gamma1
    alpha2 = gamma2 / (delta2 - beta2 * gamma2 * (curve1 * per_gamma1))
    rows_z0, rows_u1, rows_r1, rows_w0, rows_q, rows_v1, rows_y = [
        rows_ref[at] for at in range(7)
    ]
    rows_p1 = rows_u1 + beta1 * rows_z0
    rows_u2 = rows_u1 - alpha1 * (rows_q + beta1 * pressure_ref[...])
    rows_s1 = rows_v1 + beta1 * rows_w0
    rows_v2 = rows_v1 - alpha1 * (rows_y + beta1 * residual_ref[...])
    pressure_ref[...] = alpha0 * rows_z0 + alpha1 * rows_p1
    residual_ref[...] = rows_r1 - alpha1 * rows_s1
    direction_ref[...] = rows_u2 + beta2 * rows_p1
    image_ref[...] = rows_v2 + beta2 * rows_s1
    alpha_ref[...] = jnp.broadcast_to(alpha2, (1, 512))
    column_sent(1)


def solution(mesh):
    nx, ny = mesh.shape["gx"], mesh.shape["gy"]
    lo = 8 if nx % 8 == 0 else 2
    consts = tables()
    vmem = pl.BlockSpec(memory_space=pltpu.VMEM)
    rows = jax.ShapeDtypeStruct((16, 512), jnp.float32)
    chips = nx // lo * (ny // 2)
    shapes = dict(
        consts,
        load=rows,
        metric=jax.ShapeDtypeStruct((3, 16, 512), jnp.float32),
        mass=rows,
        smoother=jax.ShapeDtypeStruct((10, 10), jnp.float32),
        order=jax.ShapeDtypeStruct((16,), jnp.int32),
    )
    call = pl.pallas_call(
        functools.partial(kernel, nx, ny, lo),
        out_shape=(pltpu.VMEM((16, 512), jnp.float32),) * 4 + (pltpu.VMEM((1, 512), jnp.float32),),
        in_specs=[pl.BlockSpec(memory_space=pltpu.HBM)] * len(FETCHED),
        out_specs=(vmem,) * 5,
        scratch_shapes=[
            (pltpu.SMEM if name == "order" else pltpu.VMEM)(shapes[name].shape, shapes[name].dtype)
            for name in FETCHED
        ]
        + [
            pltpu.SemaphoreType.DMA((len(FETCHED),)),
            pltpu.VMEM((512, 512), jnp.bfloat16),
            pltpu.VMEM((640, 256), jnp.bfloat16),
            pltpu.VMEM((640, 256), jnp.bfloat16),
            pltpu.VMEM((256, 384), jnp.bfloat16),
            pltpu.VMEM((256, 384), jnp.bfloat16),
            pltpu.VMEM((16, 128), jnp.float32),
            pltpu.VMEM((64, 256), jnp.float32),
            pltpu.VMEM((2, 32, 256), jnp.float32),
            pltpu.VMEM((32, 96), jnp.bfloat16),
            pltpu.VMEM((3, 32, 256), jnp.float32),
            pltpu.VMEM((7, 16, 512), jnp.float32),
            pltpu.VMEM((4, 5, 16, 128), jnp.float32),
            pltpu.VMEM((4, 8, 16, 128), jnp.float32),
            pltpu.SemaphoreType.DMA((4,)),
            pltpu.SemaphoreType.DMA((4,)),
            pltpu.VMEM((2, 2 * chips, 8, 128), jnp.float32),
            pltpu.SemaphoreType.DMA((2,)),
            pltpu.SemaphoreType.DMA((2,)),
            pltpu.VMEM((2, lo, 8, 128), jnp.float32),
            pltpu.SemaphoreType.DMA((2,)),
            pltpu.SemaphoreType.DMA((2,)),
        ],
        compiler_params=pltpu.CompilerParams(
            collective_id=0, has_side_effects=True, vmem_limit_bytes=60 * 1024 * 1024
        ),
    )

    def on_device(load_nodes, metric, mass_nodes, smoother, element_order):
        given = dict(
            consts, load=load_nodes, metric=metric.transpose(1, 0, 2), mass=mass_nodes, smoother=smoother,
            order=element_order,
        )
        pressure, residual, direction, image, alpha = call(
            *[jnp.asarray(given[name]) for name in FETCHED]
        )
        return pressure + alpha * direction, residual - alpha * image

    return jax.shard_map(
        on_device,
        mesh=mesh,
        in_specs=(
            P(("gx", "gy"), None),
            P(("gx", "gy"), None, None),
            P(("gx", "gy"), None),
            P(),
            P(("gx", "gy")),
        ),
        out_specs=(P(("gx", "gy"), None), P(("gx", "gy"), None)),
        check_vma=False,
    )
```

```python
import functools

import jax
import jax.numpy as jnp
import ml_dtypes
import numpy as np
from jax import lax
from jax.experimental import pallas as pl
from jax.experimental.pallas import tpu as pltpu
from jax.sharding import PartitionSpec as P

NODES = 8
BF16 = ml_dtypes.bfloat16
MESH = pl.DeviceIdType.MESH


def derivative_table(node_count):
    degree = node_count - 1
    points = np.cos(np.pi * np.arange(node_count) / degree)
    weights = np.ones(node_count)
    weights[0] = 2.0
    weights[-1] = 2.0
    matrix = np.zeros((node_count, node_count))
    for row in range(node_count):
        for col in range(node_count):
            if row != col:
                matrix[row, col] = (
                    weights[row]
                    / weights[col]
                    * (-1.0) ** (row + col)
                    / (points[row] - points[col])
                )
        matrix[row, row] = -np.sum(matrix[row])
    return matrix


def split_const(matrix):
    full = np.asarray(matrix, np.float32)
    high = full.astype(BF16)
    return high, (full - high.astype(np.float32)).astype(BF16)


@functools.lru_cache(None)
def tables():
    node = np.array([7 * i + a for i in range(2) for a in range(8)])
    incidence = {}
    for box in (-1, 0, 1, 2):
        block = np.zeros((10, 16))
        for at in range(16):
            idx = node[at] - 7 * box + 1
            if 0 <= idx < 10:
                block[idx, at] = 1.0
        incidence[box] = block
    uc = np.zeros((24, 4, 16))
    uci = np.zeros((24, 16))
    rv = np.zeros((4, 16, 16))
    rvi = np.zeros((16, 16))
    re = np.zeros((16, 2, 16))
    rei = np.zeros((16, 32))
    ae = np.zeros((2, 16, 24))
    aei = np.zeros((32, 24))
    for at in range(16):
        for slot, box in enumerate((-1, 0, 1, 2)):
            uc[at, slot, :10] = incidence[box][:, at]
            rv[slot, :10, at] = incidence[box][:, at]
        re[at, 0, :10] = incidence[0][:, at]
        re[at, 1, :10] = incidence[1][:, at]
        rei[at, at] = 1.0
        aei[at, at] = 1.0
        for dim, where in enumerate((0, 1, 13, 14)):
            rvi[dim, at] = float(node[at] == where)
            rei[at, 16 + dim] = float(node[at] == where)
    uc[16, 2, 8] = uc[17, 2, 9] = uci[18, 2] = uci[19, 3] = 1.0
    uc[20, 1, 0] = uc[21, 1, 1] = uci[22, 0] = uci[23, 1] = 1.0
    aei[16, 16] = aei[17, 17] = ae[0, 0, 18] = ae[0, 1, 19] = 1.0
    aei[18, 20] = aei[19, 21] = ae[1, 8, 22] = ae[1, 9, 23] = 1.0
    assemble = np.zeros((24, 16))
    assemble[:16] = node[:, None] == node[None, :]
    assemble[16] = node == 14
    assemble[21] = node == 0

    lane = np.arange(256)
    xi = (lane // 128) * 8 + (lane // 8) % 8
    eta = ((lane // 64) % 2) * 8 + lane % 8
    mx, my = [], []
    for side in (16, 20):
        for q in range(4):
            for e in range(16):
                mx.append(side + q)
                my.append(e)
    for side in (16, 20):
        for e in range(16):
            for q in range(4):
                mx.append(e)
                my.append(side + q)
    for sx in (16, 20):
        for sy in (16, 20):
            for qx in range(4):
                for qy in range(4):
                    mx.append(sx + qx)
                    my.append(sy + qy)
    mx, my = np.array(mx), np.array(my)

    def padded(rows, index):
        return np.concatenate([rows[index], np.zeros((64,) + rows.shape[1:])], axis=0)

    allx = np.concatenate([xi, mx])
    ally = np.concatenate([eta, my])
    def kernel_side(index):
        rows = uc.reshape(24, 64)
        return padded(np.concatenate([rows, rows, uci], axis=1), index)

    def sending_side(index):
        rows = re.reshape(16, 32)[index]
        return np.concatenate([rows, rows, rei[index]], axis=1)

    spread_e = [padded(ae[box].T, m).T for m in (mx, my) for box in range(2)]
    spread_k = [rv[box][:, at] for at in (xi, eta) for box in range(4)]
    asm = padded(assemble, allx)[:, xi] * padded(assemble, ally)[:, eta]

    znode = np.array([7 * k + c for k in range(4) for c in range(8)])
    rz = np.zeros((4, 16, 32))
    for block in range(4):
        for at in range(32):
            idx = znode[at] - 7 * block + 1
            if 0 <= idx < 10:
                rz[block, idx, at] = 1.0
    spread_z = [np.concatenate([block] * 4, axis=1) for block in rz]
    rzt = rz.reshape(64, 32).T
    az = (znode[:, None] == znode[None, :]).astype(float)

    d = derivative_table(NODES).astype(np.float32)
    eye8 = np.eye(8)
    dx = np.kron(np.eye(2), np.kron(d.T, eye8))
    dy = np.kron(np.eye(2), np.kron(eye8, d.T))
    dxy_hi, dxy_lo = split_const(np.concatenate([dx, dy], axis=1))
    dz = np.kron(np.eye(4), d)
    dz_hi, dz_lo = split_const(dz)
    dzt_hi, dzt_lo = split_const(dz.T)

    b = lambda m: np.asarray(m, BF16)
    return dict(
        dxy_hi=dxy_hi,
        dxy_lo=dxy_lo,
        dxyt_hi=np.ascontiguousarray(dxy_hi.T),
        dxyt_lo=np.ascontiguousarray(dxy_lo.T),
        dz=np.concatenate([dz_hi, dz_hi, dz_lo], axis=1),
        dzt=np.concatenate([dzt_hi, dzt_hi, dzt_lo], axis=1),
        az=b(np.concatenate([az, az], axis=1)),
        uc=b(np.stack([kernel_side(allx), kernel_side(ally)])),
        rvi=b(np.stack([rvi[:, xi], rvi[:, eta]])),
        re=b(np.stack([sending_side(xi), sending_side(eta)])),
        aei=b(np.stack([padded(aei.T, mx).T, padded(aei.T, my).T])),
        spread_e=b(np.concatenate(spread_e, axis=1)),
        spread_k=b(np.concatenate(spread_k + spread_z, axis=1)),
        rzt=b(np.concatenate([rzt, rzt], axis=1)),
        asm=b(asm),
    )


FETCHED = (
    "order", "smoother", "load", "spread_e", "aei", "re", "spread_k", "rvi", "uc", "rzt",
    "metric", "mass", "dxy_hi", "dxy_lo", "dz", "dxyt_hi", "dxyt_lo", "dzt", "asm", "az",
)


EARLY = FETCHED.index("re") + 1


def fdot(left, right):
    return jnp.dot(left, right, preferred_element_type=jnp.float32)


def split(value):
    high = value.astype(jnp.bfloat16)
    low = (value - high.astype(jnp.float32)).astype(jnp.bfloat16)
    return high, low


def right_dot(value, w_hi, w_lo):
    rows = value.shape[0]
    high, low = split(value)
    both = fdot(jnp.concatenate([high, low], axis=0), w_hi)
    return both[:rows] + both[rows:] + fdot(high, w_lo)


def left_dot(stacked, value):
    high, low = split(value)
    return fdot(stacked, jnp.concatenate([high, low, high], axis=0))


def offsets(first, second):
    def far(pair):
        return -min(pair[0], first - pair[0]) - min(pair[1], second - pair[1])

    pairs = [(a, b) for a in range(first) for b in range(second)]
    return sorted(pairs[1:], key=far)


def iota(shape, dim):
    return lax.broadcasted_iota(jnp.int32, shape, dim)


def half_roll(value):
    return pltpu.roll(value, 64, 1)


def local_sum(pairs):
    t = sum(first * second for first, second in pairs)
    t = t[0:8] + t[8:16] + t[16:24] + t[24:32]
    return t[:, :128] + t[:, 128:]


def kernel(
    nx, ny, lo,
    *refs,
):
    count = len(FETCHED)
    far = dict(zip(FETCHED, refs[:count]))
    near = dict(zip(FETCHED, refs[count + 5:2 * count + 5]))
    pressure_ref, residual_ref, direction_ref, image_ref, alpha_ref = refs[count:count + 5]
    (
        fetch_sem, sel, k_hi, k_lo, e_hi, e_lo, s_pad,
        slopes_ref, geometry, tz_ref, own_ref, rows_ref,
        halo_out, halo_in, halo_send, halo_recv,
        plane_in, plane_send, plane_recv, column_in, column_send, column_recv,
    ) = refs[2 * count + 5:]
    gx = lax.axis_index("gx")
    gy = lax.axis_index("gy")
    hi = nx // lo
    x_low, x_high = lax.rem(gx + nx - 1, nx), lax.rem(gx + 1, nx)
    y_low, y_high = lax.rem(gy + ny - 1, ny), lax.rem(gy + 1, ny)
    has_low_x, has_high_x = gx > 0, gx < nx - 1
    has_low_y, has_high_y = gy > 0, gy < ny - 1
    neighbours = (
        ((x_low, gy), 0, has_low_x), ((x_high, gy), 1, has_high_x),
        ((gx, y_low), 2, has_low_y), ((gx, y_high), 3, has_high_y),
        ((x_low, y_low), 4, has_low_x & has_low_y), ((x_low, y_high), 4, has_low_x & has_high_y),
        ((x_high, y_low), 4, has_high_x & has_low_y), ((x_high, y_high), 4, has_high_x & has_high_y),
    )
    inside_x, inside_y = has_low_x & has_high_x, has_low_y & has_high_y
    inside = inside_x & inside_y
    at_corner = jnp.logical_not(inside_x | inside_y)
    at_edge = jnp.logical_not(inside | at_corner)

    def where_there(actions, there):
        @pl.when(inside)
        def _():
            for action in actions:
                action()

        @pl.when(jnp.logical_not(inside))
        def _():
            for action, is_there in zip(actions, there):
                pl.when(is_there)(action)

    filled = [neighbours[at][2] for at in (1, 0, 3, 2, 7, 6, 5, 4)]

    z_at, y_at = lax.rem(gx, lo), lax.div(gx, lo)
    x_at, core = lax.div(gy, 2), lax.rem(gy, 2)
    first_core = core == 0
    sibling = (gx, gy + 1 - 2 * core)
    plane = [
        (lax.rem(y_at + a, hi) * lo + z_at, lax.rem(x_at + b, ny // 2) * 2)
        for a, b in offsets(hi, ny // 2)
    ]
    plane_from = [
        (lax.rem(y_at + hi - a, hi) * lo + z_at, lax.rem(x_at + ny // 2 - b, ny // 2) * 2)
        for a, b in offsets(hi, ny // 2)
    ]
    column = [(y_at * lo + lax.rem(z_at + a, lo), x_at * 2) for a, _ in offsets(lo, 1)]
    column_from = [(y_at * lo + lax.rem(z_at + lo - a, lo), x_at * 2) for a, _ in offsets(lo, 1)]

    barrier = pltpu.get_barrier_semaphore()

    def greet(peer):
        pl.semaphore_signal(barrier, inc=1, device_id=peer, device_id_type=MESH)

    where_there(
        [functools.partial(greet, peer) for peer, _, _ in neighbours[::-1]],
        [is_there for _, _, is_there in neighbours[::-1]],
    )
    for peer in column_from:
        greet(peer)

    @pl.when(first_core)
    def _():
        for peer_x, peer_y in plane_from:
            greet((peer_x, peer_y + 1))
            greet((peer_x, peer_y))

    greet(sibling)

    heard = len(plane) + jnp.where(first_core, 2 * len(column) + 1, 1)
    for _, _, is_there in neighbours:
        heard = heard + is_there.astype(jnp.int32)

    fetches = {}
    for at, name in enumerate(FETCHED):
        fetches[name] = pltpu.make_async_copy(far[name], near[name], fetch_sem.at[at])
        if at < EARLY:
            fetches[name].start()

    def c(name):
        if name in fetches:
            fetches.pop(name).wait()
        return near[name]

    col = iota((64, 512), 1)
    for block in range(8):
        at = iota((64, 512), 0) + block * 64
        sel[block * 64:block * 64 + 64] = (
            ((at & 7) * 64 + (at >> 3)) == col
        ).astype(jnp.float32).astype(jnp.bfloat16)

    lane1 = iota((1, 128), 1)
    order_ref = c("order")
    row16 = iota((16, 128), 0)
    along_lanes = jnp.zeros((1, 128), jnp.int32)
    along_rows = jnp.zeros((16, 128), jnp.int32)
    for at in range(16):
        along_lanes = jnp.where((lane1 & 15) == at, order_ref[at], along_lanes)
        along_rows = jnp.where(row16 == at, order_ref[at], along_rows)
    row = iota((128, 128), 0)
    place = (
        ((row >> 3) == along_lanes) & (((row & 7) >> 1) == ((lane1 & 63) >> 4))
    ).astype(jnp.float32).astype(jnp.bfloat16)
    lane16 = iota((16, 128), 1)
    unplace = jnp.concatenate(
        [((lane16 >> 3) == along_rows) & (((lane16 & 7) >> 1) == u) for u in range(4)], axis=0
    ).astype(jnp.float32).astype(jnp.bfloat16)

    row32 = iota((32, 128), 0)
    lane32 = iota((32, 128), 1)
    parity = row32 & 1
    left_half = lane32 < 64

    def from_rows(fields):
        count = len(fields)
        parts = [split(f) for f in fields]
        stacked = jnp.concatenate([p[0] for p in parts] + [p[1] for p in parts], axis=0)
        moved = fdot(stacked, sel[...]).astype(jnp.bfloat16)
        out = []
        for f in range(count):
            pieces = []
            for part in range(2):
                z = moved[(part * count + f) * 16:(part * count + f) * 16 + 16]
                pieces += [z[:, u * 128:u * 128 + 128] for u in range(4)]
            v = fdot(place, jnp.concatenate(pieces, axis=0))
            tiles = []
            for pair in range(2):
                picked = []
                for odd in range(2):
                    at = (pair * 2 + odd) * 32
                    block = v[at:at + 32]
                    picked.append(jnp.where(parity == odd, block, half_roll(block)))
                tiles.append(jnp.where(left_half, picked[0], picked[1]))
            out.append(jnp.concatenate(tiles, axis=1))
        return out

    def to_rows(values):
        count = len(values)
        highs, lows = [], []
        for value in values:
            blocks = []
            for ij in range(4):
                block = value[:, (ij // 2) * 128:(ij // 2) * 128 + 128]
                block = jnp.where(parity == (ij & 1), block, half_roll(block))
                blocks.append(jnp.where((lane32 >> 6) == parity, block, 0.0))
            high, low = split(jnp.concatenate(blocks, axis=0))
            highs.append(high)
            lows.append(low)
        o = fdot(unplace, jnp.concatenate(highs + lows, axis=1)).astype(jnp.bfloat16)
        rows = []
        for v in range(2 * count):
            rows.append(
                jnp.concatenate(
                    [o[u * 16:u * 16 + 16, v * 128:v * 128 + 128] for u in range(4)], axis=1
                )
            )
        n = lax.dot_general(
            jnp.concatenate(rows, axis=0), sel[...], (((1,), (1,)), ((), ())),
            preferred_element_type=jnp.float32,
        )
        return [
            n[v * 16:v * 16 + 16] + n[(count + v) * 16:(count + v) * 16 + 16]
            for v in range(count)
        ]

    for name in ("smoother", "load", "spread_e", "aei", "re"):
        c(name)
    s_pad[...] = jnp.zeros((16, 128), jnp.float32)
    s_pad[0:10, 0:10] = c("smoother")[...]
    both_parts = jnp.concatenate(split(s_pad[...]), axis=0)[:, 0:16]
    entries = fdot(both_parts, c("spread_e")[...]).astype(jnp.bfloat16)

    def stacked_entries(entries, at, width, number):
        blocks = [entries[:, at + b * width:at + (b + 1) * width] for b in range(number)]
        return [block[0:16] for block in blocks] + [block[16:32] for block in blocks]

    for axis in range(2):
        wide = fdot(
            c("re")[axis],
            jnp.concatenate(
                stacked_entries(entries, axis * 768, 384, 2) + [c("aei")[axis]], axis=0
            ),
        )
        enc = wide if axis == 0 else enc * wide
    high, low = split(enc)
    e_hi[...] = high
    e_lo[...] = low

    r0, = from_rows([c("load")[...]])
    for name in FETCHED[EARLY:]:
        fetches[name].start()

    low_x = (gx == 0).astype(jnp.float32)
    high_x = (gx == nx - 1).astype(jnp.float32)
    low_y = (gy == 0).astype(jnp.float32)
    high_y = (gy == ny - 1).astype(jnp.float32)
    left16 = lane16 < 64
    quarter = (lane16 & 63) >> 4

    @pl.when(jnp.logical_not(inside))
    def _():
        for slot, is_filled in enumerate(filled):
            @pl.when(jnp.logical_not(is_filled))
            def _():
                for stage in range(4):
                    halo_in[stage, slot] = jnp.zeros((16, 128), jnp.float32)

    pl.semaphore_wait(barrier, heard)

    def exchange_start(stage, value):
        m = right_dot(value, e_hi[...], e_lo[...])
        for pair in range(2):
            t = m[:, pair * 128:pair * 128 + 128]
            top, bottom = t[0:16], t[16:32]
            halo_out[stage, 2 * pair] = jnp.where(left16, top, half_roll(bottom))
            halo_out[stage, 2 * pair + 1] = jnp.where(left16, half_roll(top), bottom)
        t = m[:, 256:384]
        halo_out[stage, 4] = jnp.where(left16, t[0:16], half_roll(t[16:32]))
        copies = []
        for slot in (0, 1, 4, 5, 6, 7, 2, 3):
            peer, part, is_there = neighbours[slot]
            copy = pltpu.make_async_remote_copy(
                src_ref=halo_out.at[stage, part],
                dst_ref=halo_in.at[stage, slot],
                send_sem=halo_send.at[stage],
                recv_sem=halo_recv.at[stage],
                device_id=peer,
                device_id_type=MESH,
            )
            copies.append((copy, is_there))
        where_there([copy.start for copy, _ in copies], [there for _, there in copies])

    def halo_wait(stage, receiving):
        for number, here in ((8, inside), (5, at_edge), (3, at_corner)):
            moved = halo_in.at[stage, pl.ds(0, number)]
            copy = pltpu.make_async_remote_copy(
                src_ref=moved,
                dst_ref=moved,
                send_sem=halo_send.at[stage],
                recv_sem=halo_recv.at[stage],
                device_id=sibling,
                device_id_type=MESH,
            )
            pl.when(here)(copy.wait_recv if receiving else copy.wait_send)

    def exchange_end(stage):
        halo_wait(stage, True)
        tiles = []
        for pair in range(2):
            a, b = halo_in[stage, 2 * pair], halo_in[stage, 2 * pair + 1]
            tiles.append(
                jnp.concatenate(
                    [jnp.where(left16, a, half_roll(b)), jnp.where(left16, half_roll(a), b)],
                    axis=0,
                )
            )
        corner = jnp.where(
            quarter == 0, halo_in[stage, 4],
            jnp.where(
                quarter == 1, halo_in[stage, 5],
                jnp.where(quarter == 2, halo_in[stage, 6], halo_in[stage, 7]),
            ),
        )
        tiles.append(jnp.concatenate([corner, half_roll(corner)], axis=0))
        return jnp.concatenate(tiles, axis=1)

    others = 2 * len(plane) + 1

    def plane_copy(which, target, peer, tiles=1):
        source = plane_in.at[which, pl.ds(others, 1)] if tiles == 1 else target
        return pltpu.make_async_remote_copy(
            src_ref=source,
            dst_ref=target,
            send_sem=plane_send.at[which],
            recv_sem=plane_recv.at[which],
            device_id=peer,
            device_id_type=MESH,
        )

    def column_copy(which, target, peer, tiles=1):
        source = column_in.at[which, pl.ds(0, 1)] if tiles == 1 else target
        return pltpu.make_async_remote_copy(
            src_ref=source,
            dst_ref=target,
            send_sem=column_send.at[which],
            recv_sem=column_recv.at[which],
            device_id=peer,
            device_id_type=MESH,
        )

    def tree_sum(parts):
        while len(parts) > 1:
            parts = [sum(parts[at:at + 2]) for at in range(0, len(parts), 2)]
        return parts[0]

    def sum_start(which, value):
        plane_in[which, others] = value
        for at, peer in enumerate(plane):
            plane_copy(which, plane_in.at[which, pl.ds(2 * at + core, 1)], peer).start()

        @pl.when(jnp.logical_not(first_core))
        def _():
            plane_copy(which, plane_in.at[which, pl.ds(others - 1, 1)], sibling).start()

    def sum_middle(which):
        @pl.when(first_core)
        def _():
            arrived = plane_in.at[which, pl.ds(0, others)]
            plane_copy(which, arrived, sibling, others).wait_recv()
            column_in[which, 0] = tree_sum([plane_in[which, slot] for slot in range(others + 1)])
            for at, (peer_x, peer_y) in enumerate(column):
                for other in (1, 0):
                    target = column_in.at[which, pl.ds(at + 1, 1)]
                    column_copy(which, target, (peer_x, peer_y + other)).start()
            column_copy(which, column_in.at[which, pl.ds(0, 1)], sibling).start()

    def sum_end(which):
        @pl.when(first_core)
        def _():
            arrived = column_in.at[which, pl.ds(1, len(column))]
            column_copy(which, arrived, sibling, len(column)).wait_recv()

        @pl.when(jnp.logical_not(first_core))
        def _():
            arrived = column_in.at[which, pl.ds(0, len(column) + 1)]
            column_copy(which, arrived, sibling, len(column) + 1).wait_recv()

        return tree_sum([column_in[which, slot] for slot in range(len(column) + 1)])

    def plane_sent(which):
        @pl.when(first_core)
        def _():
            leaving = plane_in.at[which, pl.ds(0, len(plane))]
            plane_copy(which, leaving, sibling, len(plane)).wait_send()

        @pl.when(jnp.logical_not(first_core))
        def _():
            leaving = plane_in.at[which, pl.ds(0, len(plane) + 1)]
            plane_copy(which, leaving, sibling, len(plane) + 1).wait_send()

    def column_sent(which):
        @pl.when(first_core)
        def _():
            number = 2 * len(column) + 1
            leaving = plane_in.at[which, pl.ds(0, number)]
            column_copy(which, leaving, sibling, number).wait_send()

    row8 = iota((8, 128), 0)

    def partial_tile(pairs):
        tile = jnp.zeros((8, 128), jnp.float32)
        for q, products in enumerate(pairs):
            t = local_sum(products)
            for shift in (4, 2, 1):
                t = t + pltpu.roll(t, shift, 0)
            tile = jnp.where(row8 == q, t, tile)
        return tile

    def scalars(total, number):
        column = jnp.sum(total, axis=1, keepdims=True)
        return [column[q:q + 1] for q in range(number)]

    exchange_start(0, r0)

    for name in ("spread_k", "rvi", "uc", "rzt", "metric", "mass"):
        c(name)
    entries = fdot(both_parts, c("spread_k")[...]).astype(jnp.bfloat16)
    for axis, low_edge, high_edge in ((0, low_x, high_x), (1, low_y, high_y)):
        blocks = stacked_entries(entries, axis * 1024, 256, 4)
        for at in (0, 4):
            blocks[at] = blocks[at] * (1.0 - low_edge).astype(jnp.bfloat16)
            blocks[at + 3] = blocks[at + 3] * (1.0 - high_edge).astype(jnp.bfloat16)
        wide = fdot(c("uc")[axis], jnp.concatenate(blocks + [c("rvi")[axis]], axis=0))
        kxy = wide if axis == 0 else kxy * wide
    high, low = split(kxy)
    k_hi[...] = high
    k_lo[...] = low
    tz = fdot(c("rzt")[...], jnp.concatenate(stacked_entries(entries, 2048, 128, 4), axis=0))
    tz_hi, tz_lo = split(tz[:, 0:96])
    tz = jnp.where(iota((32, 96), 1) < 64, tz_hi.astype(jnp.float32), tz_lo.astype(jnp.float32))
    tz_ref[...] = tz.astype(jnp.bfloat16)

    metric = c("metric")
    m0, m1, m2, mass = from_rows(
        [metric[0], metric[1], metric[2], c("mass")[...]]
    )
    slopes_ref[...] = jnp.concatenate(
        [
            jnp.concatenate([m0[:, :128], m1[:, :128]], axis=1),
            jnp.concatenate([m0[:, 128:], m1[:, 128:]], axis=1),
        ],
        axis=0,
    )

    geometry[0] = m2
    geometry[1] = mass

    def own_part(stage, value):
        own_ref[stage] = right_dot(value, k_hi[0:256], k_lo[0:256])

    def precondition(stage, arrived):
        return left_dot(
            tz_ref[...], own_ref[stage] + right_dot(arrived, k_hi[256:640], k_lo[256:640])
        )

    def slopes(u):
        tall = jnp.concatenate([u[:, :128], u[:, 128:]], axis=0)
        return right_dot(tall, c("dxy_hi")[...], c("dxy_lo")[...]), left_dot(c("dz")[...], u)

    def operate(u, grad):
        slope = slopes_ref[...] * grad[0]
        slope_z = geometry[0] * grad[1]
        tall = right_dot(slope, c("dxyt_hi")[...], c("dxyt_lo")[...])
        return (
            jnp.concatenate([tall[:32], tall[32:]], axis=1)
            + left_dot(c("dzt")[...], slope_z)
            + geometry[1] * u
        )

    def assembled(value, arrived):
        both = jnp.concatenate([value, arrived], axis=1)
        high, low = split(both)
        t = fdot(jnp.concatenate([high, low], axis=0), c("asm")[...])
        t = t[:32] + t[32:]
        high, low = split(t)
        return fdot(c("az")[...], jnp.concatenate([high, low], axis=0))

    own_part(0, r0)
    for name in ("dxy_hi", "dxy_lo", "dz", "dxyt_hi", "dxyt_lo", "dzt", "asm", "az"):
        c(name)
    arrived_r0 = exchange_end(0)
    z0 = precondition(0, arrived_r0)
    w0 = operate(z0, slopes(z0))

    exchange_start(1, w0)
    sum_start(0, partial_tile([[(r0, z0)], [(w0, z0)]]))
    own_part(1, w0)
    arrived_w0 = exchange_end(1)
    z1 = precondition(1, arrived_w0)
    grad1 = slopes(z1)
    w1 = operate(z1, grad1)
    exchange_start(2, w1)
    sum_middle(0)
    own_part(2, w1)
    for at, value in enumerate(
        to_rows([z0, z1, assembled(r0, arrived_r0), assembled(w0, arrived_w0)])
    ):
        rows_ref[at] = value
    arrived_w1 = exchange_end(2)
    z2 = precondition(2, arrived_w1)
    grad2 = slopes(z2)
    gamma0, delta0 = scalars(sum_end(0), 2)
    alpha0 = gamma0 / delta0
    per_gamma0 = 1.0 / gamma0
    per_alpha0 = delta0 / gamma0

    r1 = r0 - alpha0 * w0
    u1 = z0 - alpha0 * z1
    v1 = w0 - alpha0 * w1
    q = z1 - alpha0 * z2
    grad_q = grad1[0] - alpha0 * grad2[0]
    grad_qz = grad1[1] - alpha0 * grad2[1]
    slope_q = slopes_ref[...] * grad_q
    sum_start(
        1,
        partial_tile(
            [
                [(r1, u1)], [(v1, u1)], [(v1, q)], [(v1, z1)], [(w0, z1)],
                [
                    (slope_q[:32], grad_q[:32]), (slope_q[32:], grad_q[32:]),
                    (geometry[0] * grad_qz, grad_qz), (geometry[1] * q, q),
                ],
                [(w1, q)], [(w1, z1)],
            ]
        ),
    )
    w2 = operate(z2, grad2)
    exchange_start(3, w2)
    for at, value in enumerate(to_rows([z2, assembled(w1, arrived_w1)])):
        rows_ref[4 + at] = value
    sum_middle(1)
    arrived_w2 = exchange_end(3)
    rows_w2, = to_rows([assembled(w2, arrived_w2)])
    rows_z0, rows_z1, rows_r0, rows_w0, rows_z2, rows_w1 = [rows_ref[at] for at in range(6)]
    rows_ref[1] = rows_z0 - alpha0 * rows_z1
    rows_ref[4] = rows_z1 - alpha0 * rows_z2
    rows_ref[2] = rows_r0 - alpha0 * rows_w0
    rows_ref[5] = rows_w0 - alpha0 * rows_w1
    rows_ref[6] = rows_w1 - alpha0 * rows_w2
    pressure_ref[...] = rows_z1
    residual_ref[...] = rows_w1
    for stage in range(4):
        halo_wait(stage, False)
    plane_sent(0)
    plane_sent(1)
    column_sent(0)
    gamma1, delta1, vq, vz, wz0, yq, yz, wz1 = scalars(sum_end(1), 8)

    beta1 = gamma1 * per_gamma0
    uz = -gamma1 * per_alpha0
    curve1 = delta1 + beta1 * uz
    alpha1 = gamma1 / curve1
    per_gamma1 = 1.0 / gamma1
    gamma2 = (
        gamma1 - 2.0 * alpha1 * (delta1 + beta1 * uz)
        + alpha1 * alpha1 * (vq + beta1 * (2.0 * vz + beta1 * wz0))
    )
    delta2 = (
        delta1 - 2.0 * alpha1 * (vq + beta1 * vz)
        + alpha1 * alpha1 * (yq + beta1 * (2.0 * yz + beta1 * wz1))
    )
    beta2 = gamma2 * per_gamma1
    alpha2 = gamma2 / (delta2 - beta2 * gamma2 * (curve1 * per_gamma1))
    rows_z0, rows_u1, rows_r1, rows_w0, rows_q, rows_v1, rows_y = [
        rows_ref[at] for at in range(7)
    ]
    rows_p1 = rows_u1 + beta1 * rows_z0
    rows_u2 = rows_u1 - alpha1 * (rows_q + beta1 * pressure_ref[...])
    rows_s1 = rows_v1 + beta1 * rows_w0
    rows_v2 = rows_v1 - alpha1 * (rows_y + beta1 * residual_ref[...])
    pressure_ref[...] = alpha0 * rows_z0 + alpha1 * rows_p1
    residual_ref[...] = rows_r1 - alpha1 * rows_s1
    direction_ref[...] = rows_u2 + beta2 * rows_p1
    image_ref[...] = rows_v2 + beta2 * rows_s1
    alpha_ref[...] = jnp.broadcast_to(alpha2, (1, 512))
    column_sent(1)


def solution(mesh):
    nx, ny = mesh.shape["gx"], mesh.shape["gy"]
    lo = 8 if nx % 8 == 0 else 2
    consts = tables()
    vmem = pl.BlockSpec(memory_space=pltpu.VMEM)
    rows = jax.ShapeDtypeStruct((16, 512), jnp.float32)
    chips = nx // lo * (ny // 2)
    shapes = dict(
        consts,
        load=rows,
        metric=jax.ShapeDtypeStruct((3, 16, 512), jnp.float32),
        mass=rows,
        smoother=jax.ShapeDtypeStruct((10, 10), jnp.float32),
        order=jax.ShapeDtypeStruct((16,), jnp.int32),
    )
    call = pl.pallas_call(
        functools.partial(kernel, nx, ny, lo),
        out_shape=(pltpu.VMEM((16, 512), jnp.float32),) * 4 + (pltpu.VMEM((1, 512), jnp.float32),),
        in_specs=[pl.BlockSpec(memory_space=pltpu.HBM)] * len(FETCHED),
        out_specs=(vmem,) * 5,
        scratch_shapes=[
            (pltpu.SMEM if name == "order" else pltpu.VMEM)(shapes[name].shape, shapes[name].dtype)
            for name in FETCHED
        ]
        + [
            pltpu.SemaphoreType.DMA((len(FETCHED),)),
            pltpu.VMEM((512, 512), jnp.bfloat16),
            pltpu.VMEM((640, 256), jnp.bfloat16),
            pltpu.VMEM((640, 256), jnp.bfloat16),
            pltpu.VMEM((256, 384), jnp.bfloat16),
            pltpu.VMEM((256, 384), jnp.bfloat16),
            pltpu.VMEM((16, 128), jnp.float32),
            pltpu.VMEM((64, 256), jnp.float32),
            pltpu.VMEM((2, 32, 256), jnp.float32),
            pltpu.VMEM((32, 96), jnp.bfloat16),
            pltpu.VMEM((3, 32, 256), jnp.float32),
            pltpu.VMEM((7, 16, 512), jnp.float32),
            pltpu.VMEM((4, 5, 16, 128), jnp.float32),
            pltpu.VMEM((4, 8, 16, 128), jnp.float32),
            pltpu.SemaphoreType.DMA((4,)),
            pltpu.SemaphoreType.DMA((4,)),
            pltpu.VMEM((2, 2 * chips, 8, 128), jnp.float32),
            pltpu.SemaphoreType.DMA((2,)),
            pltpu.SemaphoreType.DMA((2,)),
            pltpu.VMEM((2, lo, 8, 128), jnp.float32),
            pltpu.SemaphoreType.DMA((2,)),
            pltpu.SemaphoreType.DMA((2,)),
        ],
        compiler_params=pltpu.CompilerParams(
            collective_id=0, has_side_effects=True, vmem_limit_bytes=60 * 1024 * 1024
        ),
    )

    def on_device(load_nodes, metric, mass_nodes, smoother, element_order):
        given = dict(
            consts, load=load_nodes, metric=metric.transpose(1, 0, 2), mass=mass_nodes, smoother=smoother,
            order=element_order,
        )
        pressure, residual, direction, image, alpha = call(
            *[jnp.asarray(given[name]) for name in FETCHED]
        )
        return pressure + alpha * direction, residual - alpha * image

    return jax.shard_map(
        on_device,
        mesh=mesh,
        in_specs=(
            P(("gx", "gy"), None),
            P(("gx", "gy"), None, None),
            P(("gx", "gy"), None),
            P(),
            P(("gx", "gy")),
        ),
        out_specs=(P(("gx", "gy"), None), P(("gx", "gy"), None)),
        check_vma=False,
    )
```

```python
import functools

import jax
import jax.numpy as jnp
import ml_dtypes
import numpy as np
from jax import lax
from jax.experimental import pallas as pl
from jax.experimental.pallas import tpu as pltpu
from jax.sharding import PartitionSpec as P

NODES = 8
BF16 = ml_dtypes.bfloat16
MESH = pl.DeviceIdType.MESH


def derivative_table(node_count):
    degree = node_count - 1
    points = np.cos(np.pi * np.arange(node_count) / degree)
    weights = np.ones(node_count)
    weights[0] = 2.0
    weights[-1] = 2.0
    matrix = np.zeros((node_count, node_count))
    for row in range(node_count):
        for col in range(node_count):
            if row != col:
                matrix[row, col] = (
                    weights[row]
                    / weights[col]
                    * (-1.0) ** (row + col)
                    / (points[row] - points[col])
                )
        matrix[row, row] = -np.sum(matrix[row])
    return matrix


def split_const(matrix):
    full = np.asarray(matrix, np.float32)
    high = full.astype(BF16)
    return high, (full - high.astype(np.float32)).astype(BF16)


@functools.lru_cache(None)
def tables():
    node = np.array([7 * i + a for i in range(2) for a in range(8)])
    incidence = {}
    for box in (-1, 0, 1, 2):
        block = np.zeros((10, 16))
        for at in range(16):
            idx = node[at] - 7 * box + 1
            if 0 <= idx < 10:
                block[idx, at] = 1.0
        incidence[box] = block
    uc = np.zeros((24, 4, 16))
    uci = np.zeros((24, 16))
    rv = np.zeros((4, 16, 16))
    rvi = np.zeros((16, 16))
    re = np.zeros((16, 2, 16))
    rei = np.zeros((16, 32))
    ae = np.zeros((2, 16, 24))
    aei = np.zeros((32, 24))
    for at in range(16):
        for slot, box in enumerate((-1, 0, 1, 2)):
            uc[at, slot, :10] = incidence[box][:, at]
            rv[slot, :10, at] = incidence[box][:, at]
        re[at, 0, :10] = incidence[0][:, at]
        re[at, 1, :10] = incidence[1][:, at]
        rei[at, at] = 1.0
        aei[at, at] = 1.0
        for dim, where in enumerate((0, 1, 13, 14)):
            rvi[dim, at] = float(node[at] == where)
            rei[at, 16 + dim] = float(node[at] == where)
    uc[16, 2, 8] = uc[17, 2, 9] = uci[18, 2] = uci[19, 3] = 1.0
    uc[20, 1, 0] = uc[21, 1, 1] = uci[22, 0] = uci[23, 1] = 1.0
    aei[16, 16] = aei[17, 17] = ae[0, 0, 18] = ae[0, 1, 19] = 1.0
    aei[18, 20] = aei[19, 21] = ae[1, 8, 22] = ae[1, 9, 23] = 1.0
    assemble = np.zeros((24, 16))
    assemble[:16] = node[:, None] == node[None, :]
    assemble[16] = node == 14
    assemble[21] = node == 0

    lane = np.arange(256)
    xi = (lane // 128) * 8 + (lane // 8) % 8
    eta = ((lane // 64) % 2) * 8 + lane % 8
    mx, my = [], []
    for side in (16, 20):
        for q in range(4):
            for e in range(16):
                mx.append(side + q)
                my.append(e)
    for side in (16, 20):
        for e in range(16):
            for q in range(4):
                mx.append(e)
                my.append(side + q)
    for sx in (16, 20):
        for sy in (16, 20):
            for qx in range(4):
                for qy in range(4):
                    mx.append(sx + qx)
                    my.append(sy + qy)
    mx, my = np.array(mx), np.array(my)

    def padded(rows, index):
        return np.concatenate([rows[index], np.zeros((64,) + rows.shape[1:])], axis=0)

    allx = np.concatenate([xi, mx])
    ally = np.concatenate([eta, my])
    def kernel_side(index):
        rows = uc.reshape(24, 64)
        return padded(np.concatenate([rows, rows, uci], axis=1), index)

    def sending_side(index):
        rows = re.reshape(16, 32)[index]
        return np.concatenate([rows, rows, rei[index]], axis=1)

    spread_e = [padded(ae[box].T, m).T for m in (mx, my) for box in range(2)]
    spread_k = [rv[box][:, at] for at in (xi, eta) for box in range(4)]
    asm = padded(assemble, allx)[:, xi] * padded(assemble, ally)[:, eta]

    znode = np.array([7 * k + c for k in range(4) for c in range(8)])
    rz = np.zeros((4, 16, 32))
    for block in range(4):
        for at in range(32):
            idx = znode[at] - 7 * block + 1
            if 0 <= idx < 10:
                rz[block, idx, at] = 1.0
    spread_z = [np.concatenate([block] * 4, axis=1) for block in rz]
    rzt = rz.reshape(64, 32).T
    az = (znode[:, None] == znode[None, :]).astype(float)

    d = derivative_table(NODES).astype(np.float32)
    eye8 = np.eye(8)
    dx = np.kron(np.eye(2), np.kron(d.T, eye8))
    dy = np.kron(np.eye(2), np.kron(eye8, d.T))
    dxy_hi, dxy_lo = split_const(np.concatenate([dx, dy], axis=1))
    dz = np.kron(np.eye(4), d)
    dz_hi, dz_lo = split_const(dz)
    dzt_hi, dzt_lo = split_const(dz.T)

    b = lambda m: np.asarray(m, BF16)
    return dict(
        dxy_hi=dxy_hi,
        dxy_lo=dxy_lo,
        dxyt_hi=np.ascontiguousarray(dxy_hi.T),
        dxyt_lo=np.ascontiguousarray(dxy_lo.T),
        dz=np.concatenate([dz_hi, dz_hi, dz_lo], axis=1),
        dzt=np.concatenate([dzt_hi, dzt_hi, dzt_lo], axis=1),
        az=b(np.concatenate([az, az], axis=1)),
        uc=b(np.stack([kernel_side(allx), kernel_side(ally)])),
        rvi=b(np.stack([rvi[:, xi], rvi[:, eta]])),
        re=b(np.stack([sending_side(xi), sending_side(eta)])),
        aei=b(np.stack([padded(aei.T, mx).T, padded(aei.T, my).T])),
        spread_e=b(np.concatenate(spread_e, axis=1)),
        spread_k=b(np.concatenate(spread_k + spread_z, axis=1)),
        rzt=b(np.concatenate([rzt, rzt], axis=1)),
        asm=b(asm),
    )


FETCHED = (
    "order", "smoother", "load", "spread_e", "aei", "re", "spread_k", "rvi", "uc", "rzt",
    "metric", "mass", "dxy_hi", "dxy_lo", "dz", "dxyt_hi", "dxyt_lo", "dzt", "asm", "az",
)


EARLY = FETCHED.index("re") + 1


def fdot(left, right):
    return jnp.dot(left, right, preferred_element_type=jnp.float32)


def split(value):
    high = value.astype(jnp.bfloat16)
    low = (value - high.astype(jnp.float32)).astype(jnp.bfloat16)
    return high, low


def right_dot(value, w_hi, w_lo):
    rows = value.shape[0]
    high, low = split(value)
    both = fdot(jnp.concatenate([high, low], axis=0), w_hi)
    return both[:rows] + both[rows:] + fdot(high, w_lo)


def left_dot(stacked, value):
    high, low = split(value)
    return fdot(stacked, jnp.concatenate([high, low, high], axis=0))


def offsets(first, second):
    def far(pair):
        return -min(pair[0], first - pair[0]) - min(pair[1], second - pair[1])

    pairs = [(a, b) for a in range(first) for b in range(second)]
    return sorted(pairs[1:], key=far)


def iota(shape, dim):
    return lax.broadcasted_iota(jnp.int32, shape, dim)


def half_roll(value):
    return pltpu.roll(value, 64, 1)


def local_sum(pairs):
    t = sum(first * second for first, second in pairs)
    t = t[0:8] + t[8:16] + t[16:24] + t[24:32]
    return t[:, :128] + t[:, 128:]


def kernel(
    nx, ny, lo,
    *refs,
):
    count = len(FETCHED)
    far = dict(zip(FETCHED, refs[:count]))
    near = dict(zip(FETCHED, refs[count + 5:2 * count + 5]))
    pressure_ref, residual_ref, direction_ref, image_ref, alpha_ref = refs[count:count + 5]
    (
        fetch_sem, sel, k_hi, k_lo, e_hi, e_lo, s_pad,
        slopes_ref, geometry, tz_ref, own_ref, rows_ref,
        halo_out, halo_in, halo_send, halo_recv,
        plane_in, plane_send, plane_recv, column_in, column_send, column_recv,
    ) = refs[2 * count + 5:]
    gx = lax.axis_index("gx")
    gy = lax.axis_index("gy")
    hi = nx // lo
    x_low, x_high = lax.rem(gx + nx - 1, nx), lax.rem(gx + 1, nx)
    y_low, y_high = lax.rem(gy + ny - 1, ny), lax.rem(gy + 1, ny)
    has_low_x, has_high_x = gx > 0, gx < nx - 1
    has_low_y, has_high_y = gy > 0, gy < ny - 1
    neighbours = (
        ((x_low, gy), 0, has_low_x), ((x_high, gy), 1, has_high_x),
        ((gx, y_low), 2, has_low_y), ((gx, y_high), 3, has_high_y),
        ((x_low, y_low), 4, has_low_x & has_low_y), ((x_low, y_high), 4, has_low_x & has_high_y),
        ((x_high, y_low), 4, has_high_x & has_low_y), ((x_high, y_high), 4, has_high_x & has_high_y),
    )
    inside_x, inside_y = has_low_x & has_high_x, has_low_y & has_high_y
    inside = inside_x & inside_y
    at_corner = jnp.logical_not(inside_x | inside_y)
    at_edge = jnp.logical_not(inside | at_corner)

    def where_there(actions, there):
        @pl.when(inside)
        def _():
            for action in actions:
                action()

        @pl.when(jnp.logical_not(inside))
        def _():
            for action, is_there in zip(actions, there):
                pl.when(is_there)(action)

    filled = [neighbours[at][2] for at in (1, 0, 3, 2, 7, 6, 5, 4)]

    z_at, y_at = lax.rem(gx, lo), lax.div(gx, lo)
    x_at, core = lax.div(gy, 2), lax.rem(gy, 2)
    first_core = core == 0
    sibling = (gx, gy + 1 - 2 * core)
    plane = [
        (lax.rem(y_at + a, hi) * lo + z_at, lax.rem(x_at + b, ny // 2) * 2)
        for a, b in offsets(hi, ny // 2)
    ]
    plane_from = [
        (lax.rem(y_at + hi - a, hi) * lo + z_at, lax.rem(x_at + ny // 2 - b, ny // 2) * 2)
        for a, b in offsets(hi, ny // 2)
    ]
    column = [(y_at * lo + lax.rem(z_at + a, lo), x_at * 2) for a, _ in offsets(lo, 1)]
    column_from = [(y_at * lo + lax.rem(z_at + lo - a, lo), x_at * 2) for a, _ in offsets(lo, 1)]

    barrier = pltpu.get_barrier_semaphore()

    def greet(peer):
        pl.semaphore_signal(barrier, inc=1, device_id=peer, device_id_type=MESH)

    where_there(
        [functools.partial(greet, peer) for peer, _, _ in neighbours[::-1]],
        [is_there for _, _, is_there in neighbours[::-1]],
    )
    for peer in column_from:
        greet(peer)

    @pl.when(first_core)
    def _():
        for peer_x, peer_y in plane_from:
            greet((peer_x, peer_y + 1))
            greet((peer_x, peer_y))

    greet(sibling)

    heard = len(plane) + jnp.where(first_core, 2 * len(column) + 1, 1)
    for _, _, is_there in neighbours:
        heard = heard + is_there.astype(jnp.int32)

    fetches = {}
    for at, name in enumerate(FETCHED):
        fetches[name] = pltpu.make_async_copy(far[name], near[name], fetch_sem.at[at])
        if at < EARLY:
            fetches[name].start()

    def c(name):
        if name in fetches:
            fetches.pop(name).wait()
        return near[name]

    col = iota((64, 512), 1)
    for block in range(8):
        at = iota((64, 512), 0) + block * 64
        sel[block * 64:block * 64 + 64] = (
            ((at & 7) * 64 + (at >> 3)) == col
        ).astype(jnp.float32).astype(jnp.bfloat16)

    lane1 = iota((1, 128), 1)
    order_ref = c("order")
    row16 = iota((16, 128), 0)
    along_lanes = jnp.zeros((1, 128), jnp.int32)
    along_rows = jnp.zeros((16, 128), jnp.int32)
    for at in range(16):
        along_lanes = jnp.where((lane1 & 15) == at, order_ref[at], along_lanes)
        along_rows = jnp.where(row16 == at, order_ref[at], along_rows)
    row = iota((128, 128), 0)
    place = (
        ((row >> 3) == along_lanes) & (((row & 7) >> 1) == ((lane1 & 63) >> 4))
    ).astype(jnp.float32).astype(jnp.bfloat16)
    lane16 = iota((16, 128), 1)
    unplace = jnp.concatenate(
        [((lane16 >> 3) == along_rows) & (((lane16 & 7) >> 1) == u) for u in range(4)], axis=0
    ).astype(jnp.float32).astype(jnp.bfloat16)

    row32 = iota((32, 128), 0)
    lane32 = iota((32, 128), 1)
    parity = row32 & 1
    left_half = lane32 < 64

    def from_rows(fields):
        count = len(fields)
        parts = [split(f) for f in fields]
        stacked = jnp.concatenate([p[0] for p in parts] + [p[1] for p in parts], axis=0)
        moved = fdot(stacked, sel[...]).astype(jnp.bfloat16)
        out = []
        for f in range(count):
            pieces = []
            for part in range(2):
                z = moved[(part * count + f) * 16:(part * count + f) * 16 + 16]
                pieces += [z[:, u * 128:u * 128 + 128] for u in range(4)]
            v = fdot(place, jnp.concatenate(pieces, axis=0))
            tiles = []
            for pair in range(2):
                picked = []
                for odd in range(2):
                    at = (pair * 2 + odd) * 32
                    block = v[at:at + 32]
                    picked.append(jnp.where(parity == odd, block, half_roll(block)))
                tiles.append(jnp.where(left_half, picked[0], picked[1]))
            out.append(jnp.concatenate(tiles, axis=1))
        return out

    def to_rows(values):
        count = len(values)
        highs, lows = [], []
        for value in values:
            blocks = []
            for ij in range(4):
                block = value[:, (ij // 2) * 128:(ij // 2) * 128 + 128]
                block = jnp.where(parity == (ij & 1), block, half_roll(block))
                blocks.append(jnp.where((lane32 >> 6) == parity, block, 0.0))
            high, low = split(jnp.concatenate(blocks, axis=0))
            highs.append(high)
            lows.append(low)
        o = fdot(unplace, jnp.concatenate(highs + lows, axis=1)).astype(jnp.bfloat16)
        rows = []
        for v in range(2 * count):
            rows.append(
                jnp.concatenate(
                    [o[u * 16:u * 16 + 16, v * 128:v * 128 + 128] for u in range(4)], axis=1
                )
            )
        n = lax.dot_general(
            jnp.concatenate(rows, axis=0), sel[...], (((1,), (1,)), ((), ())),
            preferred_element_type=jnp.float32,
        )
        return [
            n[v * 16:v * 16 + 16] + n[(count + v) * 16:(count + v) * 16 + 16]
            for v in range(count)
        ]

    for name in ("smoother", "load", "spread_e", "aei", "re"):
        c(name)
    s_pad[...] = jnp.zeros((16, 128), jnp.float32)
    s_pad[0:10, 0:10] = c("smoother")[...]
    both_parts = jnp.concatenate(split(s_pad[...]), axis=0)[:, 0:16]
    entries = fdot(both_parts, c("spread_e")[...]).astype(jnp.bfloat16)

    def stacked_entries(entries, at, width, number):
        blocks = [entries[:, at + b * width:at + (b + 1) * width] for b in range(number)]
        return [block[0:16] for block in blocks] + [block[16:32] for block in blocks]

    for axis in range(2):
        wide = fdot(
            c("re")[axis],
            jnp.concatenate(
                stacked_entries(entries, axis * 768, 384, 2) + [c("aei")[axis]], axis=0
            ),
        )
        enc = wide if axis == 0 else enc * wide
    high, low = split(enc)
    e_hi[...] = high
    e_lo[...] = low

    r0, = from_rows([c("load")[...]])
    for name in FETCHED[EARLY:]:
        fetches[name].start()

    low_x = (gx == 0).astype(jnp.float32)
    high_x = (gx == nx - 1).astype(jnp.float32)
    low_y = (gy == 0).astype(jnp.float32)
    high_y = (gy == ny - 1).astype(jnp.float32)
    left16 = lane16 < 64
    quarter = (lane16 & 63) >> 4

    @pl.when(jnp.logical_not(inside))
    def _():
        for slot, is_filled in enumerate(filled):
            @pl.when(jnp.logical_not(is_filled))
            def _():
                for stage in range(4):
                    halo_in[stage, slot] = jnp.zeros((16, 128), jnp.float32)

    pl.semaphore_wait(barrier, heard)

    def exchange_start(stage, value):
        m = right_dot(value, e_hi[...], e_lo[...])

        def pack(pair):
            t = m[:, pair * 128:pair * 128 + 128]
            top, bottom = t[0:16], t[16:32]
            halo_out[stage, 2 * pair] = jnp.where(left16, top, half_roll(bottom))
            if pair < 2:
                halo_out[stage, 2 * pair + 1] = jnp.where(left16, half_roll(top), bottom)

        def send(slots):
            copies = [
                pltpu.make_async_remote_copy(
                    src_ref=halo_out.at[stage, neighbours[slot][1]],
                    dst_ref=halo_in.at[stage, slot],
                    send_sem=halo_send.at[stage],
                    recv_sem=halo_recv.at[stage],
                    device_id=neighbours[slot][0],
                    device_id_type=MESH,
                )
                for slot in slots
            ]
            where_there([copy.start for copy in copies], [neighbours[slot][2] for slot in slots])

        pack(0)
        pack(2)
        send((0, 1, 4, 5, 6, 7))
        pack(1)
        send((2, 3))

    def halo_wait(stage, receiving):
        for number, here in ((8, inside), (5, at_edge), (3, at_corner)):
            moved = halo_in.at[stage, pl.ds(0, number)]
            copy = pltpu.make_async_remote_copy(
                src_ref=moved,
                dst_ref=moved,
                send_sem=halo_send.at[stage],
                recv_sem=halo_recv.at[stage],
                device_id=sibling,
                device_id_type=MESH,
            )
            pl.when(here)(copy.wait_recv if receiving else copy.wait_send)

    def exchange_end(stage):
        halo_wait(stage, True)
        tiles = []
        for pair in range(2):
            a, b = halo_in[stage, 2 * pair], halo_in[stage, 2 * pair + 1]
            tiles.append(
                jnp.concatenate(
                    [jnp.where(left16, a, half_roll(b)), jnp.where(left16, half_roll(a), b)],
                    axis=0,
                )
            )
        corner = jnp.where(
            quarter == 0, halo_in[stage, 4],
            jnp.where(
                quarter == 1, halo_in[stage, 5],
                jnp.where(quarter == 2, halo_in[stage, 6], halo_in[stage, 7]),
            ),
        )
        tiles.append(jnp.concatenate([corner, half_roll(corner)], axis=0))
        return jnp.concatenate(tiles, axis=1)

    others = 2 * len(plane) + 1

    def plane_copy(which, target, peer, tiles=1):
        source = plane_in.at[which, pl.ds(others, 1)] if tiles == 1 else target
        return pltpu.make_async_remote_copy(
            src_ref=source,
            dst_ref=target,
            send_sem=plane_send.at[which],
            recv_sem=plane_recv.at[which],
            device_id=peer,
            device_id_type=MESH,
        )

    def column_copy(which, target, peer, tiles=1):
        source = column_in.at[which, pl.ds(0, 1)] if tiles == 1 else target
        return pltpu.make_async_remote_copy(
            src_ref=source,
            dst_ref=target,
            send_sem=column_send.at[which],
            recv_sem=column_recv.at[which],
            device_id=peer,
            device_id_type=MESH,
        )

    def tree_sum(parts):
        while len(parts) > 1:
            parts = [sum(parts[at:at + 2]) for at in range(0, len(parts), 2)]
        return parts[0]

    def sum_start(which, value):
        plane_in[which, others] = value
        for at, peer in enumerate(plane):
            plane_copy(which, plane_in.at[which, pl.ds(2 * at + core, 1)], peer).start()

        @pl.when(jnp.logical_not(first_core))
        def _():
            plane_copy(which, plane_in.at[which, pl.ds(others - 1, 1)], sibling).start()

    def sum_middle(which):
        @pl.when(first_core)
        def _():
            arrived = plane_in.at[which, pl.ds(0, others)]
            plane_copy(which, arrived, sibling, others).wait_recv()
            column_in[which, 0] = tree_sum([plane_in[which, slot] for slot in range(others + 1)])
            for at, (peer_x, peer_y) in enumerate(column):
                for other in (1, 0):
                    target = column_in.at[which, pl.ds(at + 1, 1)]
                    column_copy(which, target, (peer_x, peer_y + other)).start()
            column_copy(which, column_in.at[which, pl.ds(0, 1)], sibling).start()

    def sum_end(which):
        @pl.when(first_core)
        def _():
            arrived = column_in.at[which, pl.ds(1, len(column))]
            column_copy(which, arrived, sibling, len(column)).wait_recv()

        @pl.when(jnp.logical_not(first_core))
        def _():
            arrived = column_in.at[which, pl.ds(0, len(column) + 1)]
            column_copy(which, arrived, sibling, len(column) + 1).wait_recv()

        return tree_sum([column_in[which, slot] for slot in range(len(column) + 1)])

    def plane_sent(which):
        @pl.when(first_core)
        def _():
            leaving = plane_in.at[which, pl.ds(0, len(plane))]
            plane_copy(which, leaving, sibling, len(plane)).wait_send()

        @pl.when(jnp.logical_not(first_core))
        def _():
            leaving = plane_in.at[which, pl.ds(0, len(plane) + 1)]
            plane_copy(which, leaving, sibling, len(plane) + 1).wait_send()

    def column_sent(which):
        @pl.when(first_core)
        def _():
            number = 2 * len(column) + 1
            leaving = plane_in.at[which, pl.ds(0, number)]
            column_copy(which, leaving, sibling, number).wait_send()

    row8 = iota((8, 128), 0)

    def partial_tile(pairs):
        tile = jnp.zeros((8, 128), jnp.float32)
        for q, products in enumerate(pairs):
            t = local_sum(products)
            for shift in (4, 2, 1):
                t = t + pltpu.roll(t, shift, 0)
            tile = jnp.where(row8 == q, t, tile)
        return tile

    def scalars(total, number):
        column = jnp.sum(total, axis=1, keepdims=True)
        return [column[q:q + 1] for q in range(number)]

    exchange_start(0, r0)

    for name in ("spread_k", "rvi", "uc", "rzt", "metric", "mass"):
        c(name)
    entries = fdot(both_parts, c("spread_k")[...]).astype(jnp.bfloat16)
    for axis, low_edge, high_edge in ((0, low_x, high_x), (1, low_y, high_y)):
        blocks = stacked_entries(entries, axis * 1024, 256, 4)
        for at in (0, 4):
            blocks[at] = blocks[at] * (1.0 - low_edge).astype(jnp.bfloat16)
            blocks[at + 3] = blocks[at + 3] * (1.0 - high_edge).astype(jnp.bfloat16)
        wide = fdot(c("uc")[axis], jnp.concatenate(blocks + [c("rvi")[axis]], axis=0))
        kxy = wide if axis == 0 else kxy * wide
    high, low = split(kxy)
    k_hi[...] = high
    k_lo[...] = low
    tz = fdot(c("rzt")[...], jnp.concatenate(stacked_entries(entries, 2048, 128, 4), axis=0))
    tz_hi, tz_lo = split(tz[:, 0:96])
    tz = jnp.where(iota((32, 96), 1) < 64, tz_hi.astype(jnp.float32), tz_lo.astype(jnp.float32))
    tz_ref[...] = tz.astype(jnp.bfloat16)

    metric = c("metric")
    m0, m1, m2, mass = from_rows(
        [metric[0], metric[1], metric[2], c("mass")[...]]
    )
    slopes_ref[...] = jnp.concatenate(
        [
            jnp.concatenate([m0[:, :128], m1[:, :128]], axis=1),
            jnp.concatenate([m0[:, 128:], m1[:, 128:]], axis=1),
        ],
        axis=0,
    )

    geometry[0] = m2
    geometry[1] = mass

    def own_part(stage, value):
        own_ref[stage] = right_dot(value, k_hi[0:256], k_lo[0:256])

    def precondition(stage, arrived):
        return left_dot(
            tz_ref[...], own_ref[stage] + right_dot(arrived, k_hi[256:640], k_lo[256:640])
        )

    def slopes(u):
        tall = jnp.concatenate([u[:, :128], u[:, 128:]], axis=0)
        return right_dot(tall, c("dxy_hi")[...], c("dxy_lo")[...]), left_dot(c("dz")[...], u)

    def operate(u, grad):
        slope = slopes_ref[...] * grad[0]
        slope_z = geometry[0] * grad[1]
        tall = right_dot(slope, c("dxyt_hi")[...], c("dxyt_lo")[...])
        return (
            jnp.concatenate([tall[:32], tall[32:]], axis=1)
            + left_dot(c("dzt")[...], slope_z)
            + geometry[1] * u
        )

    def assembled(value, arrived):
        both = jnp.concatenate([value, arrived], axis=1)
        high, low = split(both)
        t = fdot(jnp.concatenate([high, low], axis=0), c("asm")[...])
        t = t[:32] + t[32:]
        high, low = split(t)
        return fdot(c("az")[...], jnp.concatenate([high, low], axis=0))

    own_part(0, r0)
    for name in ("dxy_hi", "dxy_lo", "dz", "dxyt_hi", "dxyt_lo", "dzt", "asm", "az"):
        c(name)
    arrived_r0 = exchange_end(0)
    z0 = precondition(0, arrived_r0)
    w0 = operate(z0, slopes(z0))

    exchange_start(1, w0)
    sum_start(0, partial_tile([[(r0, z0)], [(w0, z0)]]))
    own_part(1, w0)
    arrived_w0 = exchange_end(1)
    z1 = precondition(1, arrived_w0)
    grad1 = slopes(z1)
    w1 = operate(z1, grad1)
    exchange_start(2, w1)
    sum_middle(0)
    own_part(2, w1)
    for at, value in enumerate(
        to_rows([z0, z1, assembled(r0, arrived_r0), assembled(w0, arrived_w0)])
    ):
        rows_ref[at] = value
    arrived_w1 = exchange_end(2)
    z2 = precondition(2, arrived_w1)
    grad2 = slopes(z2)
    gamma0, delta0 = scalars(sum_end(0), 2)
    alpha0 = gamma0 / delta0
    per_gamma0 = 1.0 / gamma0
    per_alpha0 = delta0 / gamma0

    r1 = r0 - alpha0 * w0
    u1 = z0 - alpha0 * z1
    v1 = w0 - alpha0 * w1
    q = z1 - alpha0 * z2
    grad_q = grad1[0] - alpha0 * grad2[0]
    grad_qz = grad1[1] - alpha0 * grad2[1]
    slope_q = slopes_ref[...] * grad_q
    sum_start(
        1,
        partial_tile(
            [
                [(r1, u1)], [(v1, u1)], [(v1, q)], [(v1, z1)], [(w0, z1)],
                [
                    (slope_q[:32], grad_q[:32]), (slope_q[32:], grad_q[32:]),
                    (geometry[0] * grad_qz, grad_qz), (geometry[1] * q, q),
                ],
                [(w1, q)], [(w1, z1)],
            ]
        ),
    )
    w2 = operate(z2, grad2)
    exchange_start(3, w2)
    for at, value in enumerate(to_rows([z2, assembled(w1, arrived_w1)])):
        rows_ref[4 + at] = value
    sum_middle(1)
    arrived_w2 = exchange_end(3)
    rows_w2, = to_rows([assembled(w2, arrived_w2)])
    rows_z0, rows_z1, rows_r0, rows_w0, rows_z2, rows_w1 = [rows_ref[at] for at in range(6)]
    rows_ref[1] = rows_z0 - alpha0 * rows_z1
    rows_ref[4] = rows_z1 - alpha0 * rows_z2
    rows_ref[2] = rows_r0 - alpha0 * rows_w0
    rows_ref[5] = rows_w0 - alpha0 * rows_w1
    rows_ref[6] = rows_w1 - alpha0 * rows_w2
    pressure_ref[...] = rows_z1
    residual_ref[...] = rows_w1
    for stage in range(4):
        halo_wait(stage, False)
    plane_sent(0)
    plane_sent(1)
    column_sent(0)
    gamma1, delta1, vq, vz, wz0, yq, yz, wz1 = scalars(sum_end(1), 8)

    beta1 = gamma1 * per_gamma0
    uz = -gamma1 * per_alpha0
    curve1 = delta1 + beta1 * uz
    alpha1 = gamma1 / curve1
    per_gamma1 = 1.0 / gamma1
    gamma2 = (
        gamma1 - 2.0 * alpha1 * (delta1 + beta1 * uz)
        + alpha1 * alpha1 * (vq + beta1 * (2.0 * vz + beta1 * wz0))
    )
    delta2 = (
        delta1 - 2.0 * alpha1 * (vq + beta1 * vz)
        + alpha1 * alpha1 * (yq + beta1 * (2.0 * yz + beta1 * wz1))
    )
    beta2 = gamma2 * per_gamma1
    alpha2 = gamma2 / (delta2 - beta2 * gamma2 * (curve1 * per_gamma1))
    rows_z0, rows_u1, rows_r1, rows_w0, rows_q, rows_v1, rows_y = [
        rows_ref[at] for at in range(7)
    ]
    rows_p1 = rows_u1 + beta1 * rows_z0
    rows_u2 = rows_u1 - alpha1 * (rows_q + beta1 * pressure_ref[...])
    rows_s1 = rows_v1 + beta1 * rows_w0
    rows_v2 = rows_v1 - alpha1 * (rows_y + beta1 * residual_ref[...])
    pressure_ref[...] = alpha0 * rows_z0 + alpha1 * rows_p1
    residual_ref[...] = rows_r1 - alpha1 * rows_s1
    direction_ref[...] = rows_u2 + beta2 * rows_p1
    image_ref[...] = rows_v2 + beta2 * rows_s1
    alpha_ref[...] = jnp.broadcast_to(alpha2, (1, 512))
    column_sent(1)


def solution(mesh):
    nx, ny = mesh.shape["gx"], mesh.shape["gy"]
    lo = 8 if nx % 8 == 0 else 2
    consts = tables()
    vmem = pl.BlockSpec(memory_space=pltpu.VMEM)
    rows = jax.ShapeDtypeStruct((16, 512), jnp.float32)
    chips = nx // lo * (ny // 2)
    shapes = dict(
        consts,
        load=rows,
        metric=jax.ShapeDtypeStruct((3, 16, 512), jnp.float32),
        mass=rows,
        smoother=jax.ShapeDtypeStruct((10, 10), jnp.float32),
        order=jax.ShapeDtypeStruct((16,), jnp.int32),
    )
    call = pl.pallas_call(
        functools.partial(kernel, nx, ny, lo),
        out_shape=(pltpu.VMEM((16, 512), jnp.float32),) * 4 + (pltpu.VMEM((1, 512), jnp.float32),),
        in_specs=[pl.BlockSpec(memory_space=pltpu.HBM)] * len(FETCHED),
        out_specs=(vmem,) * 5,
        scratch_shapes=[
            (pltpu.SMEM if name == "order" else pltpu.VMEM)(shapes[name].shape, shapes[name].dtype)
            for name in FETCHED
        ]
        + [
            pltpu.SemaphoreType.DMA((len(FETCHED),)),
            pltpu.VMEM((512, 512), jnp.bfloat16),
            pltpu.VMEM((640, 256), jnp.bfloat16),
            pltpu.VMEM((640, 256), jnp.bfloat16),
            pltpu.VMEM((256, 384), jnp.bfloat16),
            pltpu.VMEM((256, 384), jnp.bfloat16),
            pltpu.VMEM((16, 128), jnp.float32),
            pltpu.VMEM((64, 256), jnp.float32),
            pltpu.VMEM((2, 32, 256), jnp.float32),
            pltpu.VMEM((32, 96), jnp.bfloat16),
            pltpu.VMEM((3, 32, 256), jnp.float32),
            pltpu.VMEM((7, 16, 512), jnp.float32),
            pltpu.VMEM((4, 5, 16, 128), jnp.float32),
            pltpu.VMEM((4, 8, 16, 128), jnp.float32),
            pltpu.SemaphoreType.DMA((4,)),
            pltpu.SemaphoreType.DMA((4,)),
            pltpu.VMEM((2, 2 * chips, 8, 128), jnp.float32),
            pltpu.SemaphoreType.DMA((2,)),
            pltpu.SemaphoreType.DMA((2,)),
            pltpu.VMEM((2, lo, 8, 128), jnp.float32),
            pltpu.SemaphoreType.DMA((2,)),
            pltpu.SemaphoreType.DMA((2,)),
        ],
        compiler_params=pltpu.CompilerParams(
            collective_id=0, has_side_effects=True, vmem_limit_bytes=60 * 1024 * 1024
        ),
    )

    def on_device(load_nodes, metric, mass_nodes, smoother, element_order):
        given = dict(
            consts, load=load_nodes, metric=metric.transpose(1, 0, 2), mass=mass_nodes, smoother=smoother,
            order=element_order,
        )
        pressure, residual, direction, image, alpha = call(
            *[jnp.asarray(given[name]) for name in FETCHED]
        )
        return pressure + alpha * direction, residual - alpha * image

    return jax.shard_map(
        on_device,
        mesh=mesh,
        in_specs=(
            P(("gx", "gy"), None),
            P(("gx", "gy"), None, None),
            P(("gx", "gy"), None),
            P(),
            P(("gx", "gy")),
        ),
        out_specs=(P(("gx", "gy"), None), P(("gx", "gy"), None)),
        check_vma=False,
    )
```
